32 devices in a mesh: dp: 8 (over y, x, core), tensor: 4 (over z).
Axes of the slice: x: 2, y: 2, z: 4, core: 2. Of those that a mesh axis runs over, the one named last changes fastest.
Arguments:
- tokens: bfloat16 [10240, 1536], P('dp'), may hold values from -6 to 6
- cotangent: bfloat16 [10240, 1536], P('dp'), may hold values from -6 to 6
- routes: int32 [10240, 8], P('dp'), may hold values from 0 to 15, all different within a row; in each aligned block of 640 rows (0 to 639, 640 to 1279, ...) at most 512 rows name the same one
- inproj_weight: float32 [1536, 8, 320], P('dp', 'tensor'), may hold values from -0.15625 to 0.15625
- inproj_first: float32 [1536, 8, 320], P('dp', 'tensor'), may hold values from -64 to 64
- inproj_second: float32 [1536, 8, 320], P('dp', 'tensor'), may hold values from 307.2 to 4096
- outproj_weight: float32 [8, 192, 1536], P('tensor', None, 'dp'), may hold values from -2.5 to 2.5
- outproj_first: float32 [8, 192, 1536], P('tensor', None, 'dp'), may hold values from -7 to 7
- outproj_second: float32 [8, 192, 1536], P('tensor', None, 'dp'), may hold values from 3.072 to 40.96
- gateup_weight: float32 [16, 1536, 2, 512], P(None, 'dp', None, 'tensor'), may hold values from -0.15625 to 0.15625
- gateup_first: float32 [16, 1536, 2, 512], P(None, 'dp', None, 'tensor'), may hold values from -10 to 10
- gateup_second: float32 [16, 1536, 2, 512], P(None, 'dp', None, 'tensor'), may hold values from 6.144 to 81.92
- down_weight: float32 [16, 512, 1536], P(None, 'tensor', 'dp'), may hold values from -0.5 to 0.5
- down_first: float32 [16, 512, 1536], P(None, 'tensor', 'dp'), may hold values from -4 to 4
- down_second: float32 [16, 512, 1536], P(None, 'tensor', 'dp'), may hold values from 1.024 to 13.312
- router_weight: float32 [1536, 16], P('dp'), may hold values from -0.078125 to 0.078125
- router_first: float32 [1536, 16], P('dp'), may hold values from -256 to 256
- router_second: float32 [1536, 16], P('dp'), may hold values from 4915.2 to 65536
- gains: float32 [2, 1536], P(None, 'dp'), may hold values from 0.5 to 1.5
- gains_first: float32 [2, 1536], P(None, 'dp'), may hold values from -64 to 64
- gains_second: float32 [2, 1536], P(None, 'dp'), may hold values from 307.2 to 4096
Outputs:
- block_out: bfloat16 [10240, 1536], P('dp')
- tokens_grad: float32 [10240, 1536], P('dp')
- inproj_next: float32 [1536, 8, 320], P('dp', 'tensor')
- inproj_first_next: float32 [1536, 8, 320], P('dp', 'tensor')
- inproj_second_next: float32 [1536, 8, 320], P('dp', 'tensor')
- outproj_next: float32 [8, 192, 1536], P('tensor', None, 'dp')
- outproj_first_next: float32 [8, 192, 1536], P('tensor', None, 'dp')
- outproj_second_next: float32 [8, 192, 1536], P('tensor', None, 'dp')
- gateup_next: float32 [16, 1536, 2, 512], P(None, 'dp', None, 'tensor')
- gateup_first_next: float32 [16, 1536, 2, 512], P(None, 'dp', None, 'tensor')
- gateup_second_next: float32 [16, 1536, 2, 512], P(None, 'dp', None, 'tensor')
- down_next: float32 [16, 512, 1536], P(None, 'tensor', 'dp')
- down_first_next: float32 [16, 512, 1536], P(None, 'tensor', 'dp')
- down_second_next: float32 [16, 512, 1536], P(None, 'tensor', 'dp')
- router_next: float32 [1536, 16], P('dp')
- router_first_next: float32 [1536, 16], P('dp')
- router_second_next: float32 [1536, 16], P('dp')
- gains_next: float32 [2, 1536], P(None, 'dp')
- gains_first_next: float32 [2, 1536], P(None, 'dp')
- gains_second_next: float32 [2, 1536], P(None, 'dp')
The draws below stay inside these ranges and needn't reach their ends.
Inputs may be any that keep to these rules, and one draw needn't show every extreme that they name: `routes`: in each block of 640 rows no expert is named by more than 512 rows, and in every draw some expert of some block by exactly 512; the 8 experts of a row differ.
All inputs are finite; a program needn't handle non-finite values.
Results may differ from the reference program's by a relative error of at most 0.015.
Values may be sent and summed in bfloat16 or wider, within the bound.
A program may use at most 576 MiB of HBM per device.

```python
import math
import jax
import jax.numpy as jnp
import numpy as np
from jax import lax

D = 1536
HEADS = 24
KV_HEADS = 8
HEAD_DIM = 64
FF = 512
TOPK = 8
EXPERTS = 16
PROMPT_DEV = 128
CONT = 512
MICRO = 2
STEP = 10
GROUP = 3
TOK_MB = 640
TOKENS = 10240
CAP = 512
N_DP = 8


def block_levels(rng, dims, split, smallest, high):
    loudness = 1.0
    for dim, parts in split:
        steps = jax.random.uniform(jax.random.fold_in(jax.random.fold_in(rng, 6), dim), (parts,), jnp.float32, smallest / len(split), high / len(split))
        loudness = loudness * jnp.repeat(jnp.exp(steps), dims[dim] // parts).reshape((-1,) + (1,) * (len(dims) - 1 - dim))
    return loudness


def shared_out(stream_key, own, number, rows, number_of, top, most, lean):
    sequence = jax.random.permutation(stream_key, number_of)
    heavy_load, ordinary = shares(number_of, rows * top, most, lean, True), shares(number_of, rows * top, most, lean, False)
    places = jnp.arange(number_of)

    def named(sizes, offset_by):
        used = int((sizes > 0).sum())
        fixed = max(1, used // 4)
        passed = fixed + (places - fixed + offset_by * (used - fixed)) % max(1, number_of - fixed)
        return jnp.zeros((number_of,), jnp.int32).at[sequence[jnp.where(places < fixed, places, passed)]].set(jnp.asarray(sizes, jnp.int32))

    sizes = jnp.where(number % 4 == 0, named(heavy_load, number // 4), named(ordinary, number - number // 4 - 1))
    mixed = jax.random.permutation(jax.random.fold_in(own, 3), number_of)
    donor, taker = mixed[0:number_of // 2 * 2:2], mixed[1:number_of // 2 * 2:2]
    slack = jnp.minimum(sizes[donor] - 1, most - sizes[taker]) // 2
    slack = jnp.where((donor == sequence[0]) | (taker == sequence[0]) | (sizes[taker] == 0), 0, jnp.maximum(slack, 0))
    passed = jax.random.randint(jax.random.fold_in(own, 4), (number_of // 2,), 0, 1 << 20) % (slack + 1)
    sizes = sizes.at[donor].add(-passed).at[taker].add(passed)
    labels = jnp.searchsorted(jnp.cumsum(sizes), jnp.arange(rows * top), side="right").astype(jnp.int32)
    table = labels.reshape(top, rows).T
    table = table[jax.random.permutation(jax.random.fold_in(own, 1), rows)]
    offset_by = jax.random.randint(jax.random.fold_in(own, 2), (rows, 1), 0, top)
    return jnp.take_along_axis(table, (jnp.arange(top)[None, :] + offset_by) % top, axis=1)


def shares(count, total, reach, skew, full):
    weights = [(1 << 20) // math.isqrt(standing ** skew) + 1 for standing in range(1, count + 1)]
    largest = reach if full else min(reach, max(-(-total // count), total * weights[0] // sum(weights)))
    least = 1 if total - largest >= count - 1 else 0
    holding, rest = [largest] + [least] * (count - 1), total - largest - least * (count - 1)
    while rest > 0:
        movable = [i for i in range(1, count) if holding[i] < largest] or [i for i in range(1, count) if holding[i] < reach]
        pool, left = sum([weights[i] for i in movable]), rest
        for i in movable:
            extra = min(reach - holding[i], max(1, left * weights[i] // pool), rest)
            holding[i] = holding[i] + extra
            rest = rest - extra
    return np.array(holding)


def scatter_about(own_key, shape, scale, bound, cuts=(), kind=jnp.bfloat16):
    factor_of = block_levels(own_key, shape, cuts, -0.22, 0.18) if cuts else 1.0
    drawn = jax.random.normal(own_key, shape, jnp.float32) * scale * factor_of
    return jnp.minimum(jnp.maximum(drawn, -bound), bound).astype(kind)


def setup_inputs(seed: int = 0) -> dict:
    splits = jax.random.split(jax.random.key(seed), 22)
    tokens = scatter_about(splits[0], (TOKENS, D), 1.0, 6.0, ((0, 8),))
    cotangent = scatter_about(splits[1], (TOKENS, D), 1.0, 6.0, ((0, 8),))
    routes_keys = jax.random.split(jax.random.fold_in(splits[2], 1), TOKENS // TOK_MB)
    routes_turns = jax.random.permutation(jax.random.fold_in(splits[2], 3), TOKENS // TOK_MB)
    routes = jax.vmap(lambda own, number: shared_out(jax.random.fold_in(splits[2], 2), own, number, TOK_MB, EXPERTS, TOPK, CAP, 1))(routes_keys, routes_turns).reshape((TOKENS, TOPK))
    inproj_weight = scatter_about(splits[3], (D, KV_HEADS, (GROUP + 2) * HEAD_DIM), D ** -0.5, 0.15625, ((0, 8), (1, 4)), jnp.float32)
    inproj_first = scatter_about(splits[4], (D, KV_HEADS, (GROUP + 2) * HEAD_DIM), (0.11 * TOKENS ** 0.5), 64.0, ((0, 8), (1, 4)), jnp.float32)
    inproj_second = jnp.clip(jnp.exp(math.log(4096.0) - 2.5902671 * jax.random.uniform(splits[5], (D, KV_HEADS, (GROUP + 2) * HEAD_DIM), jnp.float32) ** block_levels(splits[5], (D, KV_HEADS, (GROUP + 2) * HEAD_DIM), ((0, 8), (1, 4)), -0.2, 0.2)), 307.2, 4096.0)
    outproj_weight = scatter_about(splits[6], (KV_HEADS, GROUP * HEAD_DIM, D), (max(HEADS * HEAD_DIM // 256, 1)) ** -0.5, 2.5, ((0, 4), (2, 8)), jnp.float32)
    outproj_first = scatter_about(splits[7], (KV_HEADS, GROUP * HEAD_DIM, D), (0.011 * TOKENS ** 0.5), 7.0, ((0, 4), (2, 8)), jnp.float32)
    outproj_second = jnp.clip(jnp.exp(math.log(40.96) - 2.5902671 * jax.random.uniform(splits[8], (KV_HEADS, GROUP * HEAD_DIM, D), jnp.float32) ** block_levels(splits[8], (KV_HEADS, GROUP * HEAD_DIM, D), ((0, 4), (2, 8)), -0.2, 0.2)), 3.072, 40.96)
    gateup_weight = scatter_about(splits[9], (EXPERTS, D, 2, FF), D ** -0.5, 0.15625, ((1, 8), (3, 4)), jnp.float32)
    gateup_first = scatter_about(splits[10], (EXPERTS, D, 2, FF), (0.022 * (TOKENS * TOPK // EXPERTS) ** 0.5), 10.0, ((1, 8), (3, 4)), jnp.float32)
    gateup_second = jnp.clip(jnp.exp(math.log(81.92) - 2.5902671 * jax.random.uniform(splits[11], (EXPERTS, D, 2, FF), jnp.float32) ** block_levels(splits[11], (EXPERTS, D, 2, FF), ((1, 8), (3, 4)), -0.2, 0.2)), 6.144, 81.92)
    down_weight = scatter_about(splits[12], (EXPERTS, FF, D), (max(FF // 4, 1)) ** -0.5, 0.5, ((1, 4), (2, 8)), jnp.float32)
    down_first = scatter_about(splits[13], (EXPERTS, FF, D), (0.009 * (TOKENS * TOPK // EXPERTS) ** 0.5), 4.0, ((1, 4), (2, 8)), jnp.float32)
    down_second = jnp.clip(jnp.exp(math.log(13.312) - 2.5649493 * jax.random.uniform(splits[14], (EXPERTS, FF, D), jnp.float32) ** block_levels(splits[14], (EXPERTS, FF, D), ((1, 4), (2, 8)), -0.2, 0.2)), 1.024, 13.312)
    router_weight = scatter_about(splits[15], (D, EXPERTS), (4 * D) ** -0.5, 0.078125, ((0, 8),), jnp.float32)
    router_first = scatter_about(splits[16], (D, EXPERTS), (0.44 * TOKENS ** 0.5), 256.0, ((0, 8),), jnp.float32)
    router_second = jnp.clip(jnp.exp(math.log(65536.0) - 2.5902671 * jax.random.uniform(splits[17], (D, EXPERTS), jnp.float32) ** block_levels(splits[17], (D, EXPERTS), ((0, 8),), -0.2, 0.2)), 4915.2, 65536.0)
    gains = jnp.clip(1.0 + 0.1 * jax.random.normal(splits[18], (2, D), jnp.float32), 0.5, 1.5)
    gains_first = scatter_about(splits[19], (2, D), (0.11 * TOKENS ** 0.5), 64.0, ((1, 8),), jnp.float32)
    gains_second = jnp.clip(jnp.exp(math.log(4096.0) - 2.5902671 * jax.random.uniform(splits[20], (2, D), jnp.float32) ** block_levels(splits[20], (2, D), ((1, 8),), -0.2, 0.2)), 307.2, 4096.0)
    return {"tokens": tokens, "cotangent": cotangent, "routes": routes, "inproj_weight": inproj_weight, "inproj_first": inproj_first, "inproj_second": inproj_second, "outproj_weight": outproj_weight, "outproj_first": outproj_first, "outproj_second": outproj_second, "gateup_weight": gateup_weight, "gateup_first": gateup_first, "gateup_second": gateup_second, "down_weight": down_weight, "down_first": down_first, "down_second": down_second, "router_weight": router_weight, "router_first": router_first, "router_second": router_second, "gains": gains, "gains_first": gains_first, "gains_second": gains_second}


@jax.custom_vjp
def low(v):
    return lax.optimization_barrier(v.astype(jnp.bfloat16)).astype(jnp.float32)

@jax.custom_vjp
def low_back(v):
    return v

def low_keep(v):
    return (low(v), None)

def low_pass(kept, grad):
    return (grad,)

def back_keep(v):
    return (v, None)

def back_low(kept, grad):
    return (low(grad),)
low.defvjp(low_keep, low_pass)
low_back.defvjp(back_keep, back_low)
eps_norm = 1e-05
learn_rates = (0.05, 0.3, 0.05, 0.05, 0.05, 0.4)
beta_first = 0.9
beta_second = 0.95
adam_eps = 1e-08
weight_decay = 0.1
highest = lax.Precision.HIGHEST

def rms_norm(values, gain):
    inverse = lax.rsqrt(lax.optimization_barrier(jnp.mean(values * values, axis=-1, keepdims=True)) + eps_norm)
    return values * inverse * gain

def angles_for(positions, head_size):
    half_dim = head_size // 2
    freqs = 10000.0 ** (-2.0 * jnp.arange(half_dim, dtype=jnp.float32) / head_size)
    angles = positions.astype(jnp.float32)[..., None] * freqs
    return (jnp.cos(angles), jnp.sin(angles))

def rotate(values, cosine, sine):
    half_dim = values.shape[-1] // 2
    first_half = values[..., :half_dim]
    second_half = values[..., half_dim:]
    return jnp.concatenate([first_half * cosine - second_half * sine, second_half * cosine + first_half * sine], axis=-1)

def attend(queries, keys, values, allowed):
    factor = queries.shape[-1] ** (-0.5)
    scores = low_back(jnp.einsum('tkgd,skd->kgts', queries, keys, precision=highest) * factor)
    scores = jnp.where(allowed, scores, -1e+30)
    row_max = lax.optimization_barrier(jnp.max(scores, axis=-1, keepdims=True))
    exponent = jnp.exp(scores - row_max)
    softened = exponent / lax.optimization_barrier(jnp.sum(exponent, axis=-1, keepdims=True))
    return jnp.einsum('kgts,skd->tkgd', low(softened), values, precision=highest)

def group_attention(queries, keys, values):
    prompt_total = PROMPT_DEV * N_DP
    prompt_keys = keys[:, :PROMPT_DEV].reshape((prompt_total,) + keys.shape[2:])
    prompt_values = values[:, :PROMPT_DEV].reshape((prompt_total,) + values.shape[2:])
    prompt_queries = queries[:, :PROMPT_DEV].reshape((prompt_total,) + queries.shape[2:])
    block_rows = math.gcd(prompt_total, 512)
    key_index = jnp.arange(prompt_total, dtype=jnp.int32)

    def prompt_block(block_index):
        start = (block_index * block_rows).astype(jnp.int32)
        block_queries = lax.dynamic_slice_in_dim(prompt_queries, start, block_rows, 0)
        query_index = start + jnp.arange(block_rows, dtype=jnp.int32)
        allowed = key_index[None, :] <= query_index[:, None]
        return attend(block_queries, prompt_keys, prompt_values, allowed)
    prompt_out = lax.map(jax.checkpoint(prompt_block), jnp.arange(prompt_total // block_rows, dtype=jnp.int32))
    prompt_out = prompt_out.reshape((N_DP, PROMPT_DEV) + queries.shape[2:])
    cont_index = jnp.arange(CONT, dtype=jnp.int32)
    allowed_cont = jnp.concatenate([jnp.ones((CONT, prompt_total), jnp.bool_), cont_index[None, :] <= cont_index[:, None]], axis=1)

    def cont_block(pieces):
        block_queries, own_keys, own_values = pieces
        keys_all = jnp.concatenate([prompt_keys, own_keys], axis=0)
        values_all = jnp.concatenate([prompt_values, own_values], axis=0)
        return attend(block_queries, keys_all, values_all, allowed_cont)
    cont_out = lax.map(jax.checkpoint(cont_block), (queries[:, PROMPT_DEV:], keys[:, PROMPT_DEV:], values[:, PROMPT_DEV:]))
    return jnp.concatenate([prompt_out, cont_out], axis=1)

def expert_slots(route_rows):
    flat_routes = route_rows.reshape(-1).astype(jnp.int32)
    onehot = (flat_routes[:, None] == jnp.arange(EXPERTS, dtype=jnp.int32)[None, :]).astype(jnp.int32)
    earlier = jnp.cumsum(onehot, axis=0, dtype=jnp.int32) - onehot
    slot_index = lax.optimization_barrier(jnp.sum(earlier * onehot, axis=1, dtype=jnp.int32))
    destination = (flat_routes * CAP + slot_index).astype(jnp.int32)
    source = jnp.zeros((EXPERTS * CAP,), jnp.int32).at[destination].set(jnp.arange(flat_routes.shape[0], dtype=jnp.int32))
    filled = jnp.zeros((EXPERTS * CAP,), jnp.float32).at[destination].set(1.0)
    return (destination, source, filled)

def expert_block(normed, gates, route_rows, gateup_low, down_low):
    destination, source, filled = expert_slots(route_rows)
    model_width = normed.shape[-1]
    gathered = normed[source // TOPK].reshape(EXPERTS, CAP, model_width)
    hidden = low_back(jnp.einsum('ecd,edf->ecf', gathered, gateup_low.reshape(EXPERTS, model_width, -1), precision=highest))
    hidden_units = down_low.shape[1]
    active = low(jax.nn.silu(hidden[..., :hidden_units]) * hidden[..., hidden_units:])
    result = low_back(jnp.einsum('ecf,efd->ecd', active, down_low, precision=highest))
    picked = result.reshape(EXPERTS * CAP, model_width)[destination].reshape(gates.shape + (model_width,))
    return lax.optimization_barrier(jnp.sum(picked * gates[..., None], axis=1))

def forward(inputs, inproj, outproj, gateup, down, router, gain_pair, route_blocks):
    model_width = inputs.shape[-1]
    normed_first = low(rms_norm(inputs, gain_pair[0]))
    mixed = low_back(jnp.einsum('nmtd,dkc->nmtkc', normed_first, low(inproj), precision=highest))
    query_width = GROUP * HEAD_DIM
    queries_raw = mixed[..., :query_width].reshape(mixed.shape[:4] + (GROUP, HEAD_DIM))
    keys_raw = mixed[..., query_width:query_width + HEAD_DIM]
    values = low(mixed[..., query_width + HEAD_DIM:])
    device_index = jnp.arange(N_DP, dtype=jnp.int32)[:, None]
    inner = jnp.arange(TOK_MB, dtype=jnp.int32)[None, :]
    positions = jnp.where(inner < PROMPT_DEV, device_index * PROMPT_DEV + inner, PROMPT_DEV * N_DP + inner - PROMPT_DEV)
    cosine, sine = angles_for(positions, HEAD_DIM)
    cosine = cosine[:, None, :, None, :]
    sine = sine[:, None, :, None, :]
    keys_rot = low(rotate(keys_raw, cosine, sine))
    queries_rot = low(rotate(queries_raw, cosine[..., None, :], sine[..., None, :]))
    attended = jnp.stack([group_attention(queries_rot[:, micro_index], keys_rot[:, micro_index], values[:, micro_index]) for micro_index in range(MICRO)], axis=1)
    attended = low(low_back(attended)).reshape(attended.shape[:4] + (-1,))
    branch = low_back(jnp.einsum('nmtkc,kcd->nmtd', attended, low(outproj), precision=highest))
    middle = inputs + branch
    normed_second = low(rms_norm(middle, gain_pair[1]))
    logits = low_back(jnp.einsum('nmtd,de->nmte', normed_second, low(router), precision=highest))
    onehot = (route_blocks[..., None] == jnp.arange(EXPERTS, dtype=jnp.int32)).astype(jnp.float32)
    chosen = lax.optimization_barrier(jnp.sum(onehot * logits[..., None, :], axis=-1))
    gates = jax.nn.softmax(chosen, axis=-1)
    block_count = N_DP * MICRO
    gateup_low = low(gateup)
    down_low = low(down)

    def one_block(pieces):
        return expert_block(pieces[0], pieces[1], pieces[2], gateup_low, down_low)
    mixture = lax.map(jax.checkpoint(one_block), (normed_second.reshape(block_count, TOK_MB, model_width), gates.reshape(block_count, TOK_MB, TOPK), route_blocks.reshape(block_count, TOK_MB, TOPK)))
    return middle + mixture.reshape(middle.shape)

def adam_update(weight, moment_one, moment_two, gradient, decay_rate, learn_rate):
    first_next = beta_first * moment_one + (1.0 - beta_first) * gradient
    second_next = beta_second * moment_two + (1.0 - beta_second) * gradient * gradient
    corr_first = 1.0 - beta_first ** STEP
    corr_second = 1.0 - beta_second ** STEP
    update = first_next / corr_first / (jnp.sqrt(second_next / corr_second) + adam_eps)
    return (weight - learn_rate * (update + decay_rate * weight), first_next, second_next)

def reference(tokens, cotangent, routes, inproj_weight, inproj_first, inproj_second, outproj_weight, outproj_first, outproj_second, gateup_weight, gateup_first, gateup_second, down_weight, down_first, down_second, router_weight, router_first, router_second, gains, gains_first, gains_second):
    inputs = tokens.astype(jnp.float32).reshape(N_DP, MICRO, TOK_MB, D)
    route_blocks = routes.reshape(N_DP, MICRO, TOK_MB, TOPK).astype(jnp.int32)

    def closed(inputs_in, inproj, outproj, gateup, down, router, gain_pair):
        return forward(inputs_in, inproj, outproj, gateup, down, router, gain_pair, route_blocks)
    output, pullback = jax.vjp(closed, inputs, inproj_weight, outproj_weight, gateup_weight, down_weight, router_weight, gains)
    grads = pullback(cotangent.astype(jnp.float32).reshape(output.shape))
    triples = ((inproj_weight, inproj_first, inproj_second), (outproj_weight, outproj_first, outproj_second), (gateup_weight, gateup_first, gateup_second), (down_weight, down_first, down_second), (router_weight, router_first, router_second), (gains, gains_first, gains_second))
    decays = (weight_decay, weight_decay, weight_decay, weight_decay, weight_decay, 0.0)
    results = [output.reshape(TOKENS, D).astype(jnp.bfloat16), grads[0].reshape(TOKENS, D)]
    for triple, gradient, decay_rate, learn_rate in zip(triples, grads[1:], decays, learn_rates):
        results.extend(adam_update(triple[0], triple[1], triple[2], gradient, decay_rate, learn_rate))
    return tuple(results)
```

```python
import functools

import jax
import jax.numpy as jnp
from jax import lax
from jax.experimental import pallas as pl
from jax.experimental.pallas import tpu as pltpu
from jax.sharding import PartitionSpec as P

HEAD_DIM = 64
TOPK = 8
EXPERTS = 16
PROMPT_DEV = 128
CONT = 512
MICRO = 2
STEP = 10
GROUP = 3
TOK_MB = 640

eps_norm = 1e-05
beta_first = 0.9
beta_second = 0.95
adam_eps = 1e-08
weight_decay = 0.1
bf16 = jnp.bfloat16
f32 = jnp.float32
MESH = pl.DeviceIdType.MESH


def angles_for(positions, head_size):
    half_dim = head_size // 2
    freqs = 10000.0 ** (-2.0 * jnp.arange(half_dim, dtype=f32) / head_size)
    angles = positions.astype(f32)[..., None] * freqs
    return (jnp.cos(angles), jnp.sin(angles))


def rotate(values, cosine, sine):
    half_dim = values.shape[-1] // 2
    first_half = values[..., :half_dim]
    second_half = values[..., half_dim:]
    return jnp.concatenate(
        [first_half * cosine - second_half * sine, second_half * cosine + first_half * sine],
        axis=-1,
    )


def adam_update(weight, moment_one, moment_two, gradient, decay_rate, learn_rate):
    first_next = beta_first * moment_one + (1.0 - beta_first) * gradient
    second_next = beta_second * moment_two + (1.0 - beta_second) * gradient * gradient
    corr_first = 1.0 - beta_first**STEP
    corr_second = 1.0 - beta_second**STEP
    update = first_next / corr_first / (jnp.sqrt(second_next / corr_second) + adam_eps)
    return (weight - learn_rate * (update + decay_rate * weight), first_next, second_next)


def line_sum_kernel(n, chunks, x_ref, o_ref, held, send_red, recv_red, send_out, recv_out):
    me = lax.axis_index("tensor")
    rows = x_ref.shape[0] // (2 * chunks)
    low, high = me - 1, me + 1

    barrier = pltpu.get_barrier_semaphore()

    @pl.when(me > 0)
    def _():
        pl.semaphore_signal(barrier, inc=1, device_id={"tensor": low}, device_id_type=MESH)

    @pl.when(me < n - 1)
    def _():
        pl.semaphore_signal(barrier, inc=1, device_id={"tensor": high}, device_id_type=MESH)

    pl.semaphore_wait(barrier, jnp.where((me > 0) & (me < n - 1), 2, 1))

    def part(half, c):
        return pl.ds(pl.multiple_of((half * chunks + c) * rows, 16), rows)

    def reduce_copy(half, c, src):
        to = low if half == 0 else high
        return pltpu.make_async_remote_copy(
            src_ref=src.at[part(half, c)],
            dst_ref=held.at[part(half, c)],
            send_sem=send_red.at[half, c],
            recv_sem=recv_red.at[half, c],
            device_id={"tensor": to},
            device_id_type=MESH,
        )

    def out_copy(half, c):
        to = high if half == 0 else low
        return pltpu.make_async_remote_copy(
            src_ref=o_ref.at[part(half, c)],
            dst_ref=o_ref.at[part(half, c)],
            send_sem=send_out.at[half, c],
            recv_sem=recv_out.at[half, c],
            device_id={"tensor": to},
            device_id_type=MESH,
        )

    def place(half):
        return n - 1 - me if half == 0 else me

    def step(s, carry):
        for half in (0, 1):
            at = place(half)

            @pl.when(s < chunks)
            def _():
                @pl.when(at == 0)
                def _():
                    reduce_copy(half, s, x_ref).start()

                @pl.when(at > 0)
                def _():
                    reduce_copy(half, s, held).wait_recv()
                    total = x_ref[part(half, s)].astype(f32) + held[part(half, s)].astype(f32)

                    @pl.when(at < n - 1)
                    def _():
                        held[part(half, s)] = total.astype(held.dtype)
                        reduce_copy(half, s, held).start()

                    @pl.when(at == n - 1)
                    def _():
                        o_ref[part(half, s)] = total.astype(o_ref.dtype)
                        out_copy(half, s).start()

            c = s - 2 * (n - 1 - at)

            @pl.when((at < n - 1) & (c >= 0) & (c < chunks))
            def _():
                out_copy(half, c).wait_recv()

                @pl.when(at > 0)
                def _():
                    out_copy(half, c).start()

        return carry

    lax.fori_loop(0, chunks + 2 * (n - 1), step, 0)

    def finish(c, carry):
        for half in (0, 1):
            at = place(half)

            @pl.when(at < n - 1)
            def _():
                reduce_copy(half, c, held).wait_send()

            @pl.when(at > 0)
            def _():
                out_copy(half, c).wait_send()

        return carry

    lax.fori_loop(0, chunks, finish, 0)


def line_sum(x, n, barrier_id):
    rows, width = x.shape
    chunks = 8
    return pl.pallas_call(
        functools.partial(line_sum_kernel, n, chunks),
        out_shape=jax.ShapeDtypeStruct(x.shape, x.dtype),
        in_specs=[pl.BlockSpec(memory_space=pltpu.VMEM)],
        out_specs=pl.BlockSpec(memory_space=pltpu.VMEM),
        scratch_shapes=[pltpu.VMEM(x.shape, x.dtype)]
        + [pltpu.SemaphoreType.DMA((2, chunks)) for _ in range(4)],
        compiler_params=pltpu.CompilerParams(
            collective_id=barrier_id, has_side_effects=True, vmem_limit_bytes=24 * 2**20
        ),
        cost_estimate=pl.CostEstimate(
            flops=rows * width, bytes_accessed=100 * rows * width, transcendentals=0
        ),
    )(x)


def expert_kernel(group, rows_ref, outgrad_ref, gates_ref, gu_ref, down_ref,
                  active_ref, hidden_ref, gate_grad_ref):
    step = pl.program_id(0)
    tile = 256
    width = gu_ref.shape[1] // 2
    hidden = width // group
    lane = lax.broadcasted_iota(jnp.int32, (tile, 128), 1)
    column = lax.broadcasted_iota(jnp.int32, (tile, width), 1)

    @pl.when(step == 0)
    def _():
        gate_grad_ref[...] = jnp.zeros_like(gate_grad_ref)

    def one(t, carry):
        at = pl.ds(pl.multiple_of(t * tile, tile), tile)
        h = jnp.dot(rows_ref[at], gu_ref[...], preferred_element_type=f32)
        back = jnp.dot(outgrad_ref[at], down_ref[...], preferred_element_type=f32)
        gates = gates_ref[at]
        wide = jnp.zeros((tile, width), f32)
        for j in range(group):
            g = jnp.sum(jnp.where(lane == step * group + j, gates, 0.0), axis=1, keepdims=True)
            wide = g + wide if group == 1 else jnp.where(column // hidden == j, g, wide)
        gate, up = h[:, :width], h[:, width:]
        sig = 1.0 / (1.0 + jnp.exp(-gate))
        silu = gate * sig
        active = (silu * up).astype(bf16).astype(f32)
        active_ref[at] = (active * wide).astype(bf16)
        product = active * back
        grads = gate_grad_ref[at]
        for j in range(group):
            s = jnp.sum(jnp.where(column // hidden == j, product, 0.0), axis=1, keepdims=True)
            grads = jnp.where(lane == step * group + j, s, grads)
        gate_grad_ref[at] = grads
        back = back * wide
        hidden_ref[at, :width] = (back * up * sig * (1.0 + gate * (1.0 - sig))).astype(bf16)
        hidden_ref[at, width:] = (back * silu).astype(bf16)
        return carry

    lax.fori_loop(0, rows_ref.shape[0] // tile, one, 0)


def expert_call(rows, outgrad, gates, gu, down, group):
    tokens, model = rows.shape
    width = gu.shape[1] // (EXPERTS // group)
    steps = EXPERTS // group
    return pl.pallas_call(
        functools.partial(expert_kernel, group),
        grid=(steps,),
        in_specs=[
            pl.BlockSpec((tokens, model), lambda p: (0, 0)),
            pl.BlockSpec((tokens, model), lambda p: (0, 0)),
            pl.BlockSpec((tokens, 128), lambda p: (0, 0)),
            pl.BlockSpec((model, width), lambda p: (0, p)),
            pl.BlockSpec((model, width // 2), lambda p: (0, p)),
        ],
        out_specs=[
            pl.BlockSpec((tokens, width // 2), lambda p: (0, p)),
            pl.BlockSpec((tokens, width), lambda p: (0, p)),
            pl.BlockSpec((tokens, 128), lambda p: (0, 0)),
        ],
        out_shape=[
            jax.ShapeDtypeStruct((tokens, steps * width // 2), bf16),
            jax.ShapeDtypeStruct((tokens, steps * width), bf16),
            jax.ShapeDtypeStruct((tokens, 128), f32),
        ],
        compiler_params=pltpu.CompilerParams(vmem_limit_bytes=48 * 2**20),
        cost_estimate=pl.CostEstimate(
            flops=2 * tokens * model * steps * width * 3 // 2,
            bytes_accessed=2 * (model * steps * width * 3 // 2 + tokens * steps * width * 3 // 2),
            transcendentals=tokens * steps * width // 2,
        ),
    )(rows, outgrad, gates, gu, down)


def attend(queries, keys_all, values_all, allowed):
    factor = HEAD_DIM ** (-0.5)
    scores = jnp.einsum("tkgd,skd->kgts", queries, keys_all, preferred_element_type=f32) * factor
    scores = jnp.where(allowed, scores, -1e30)
    row_max = jnp.max(scores, axis=-1, keepdims=True)
    exponent = jnp.exp(scores - row_max)
    softened = exponent / jnp.sum(exponent, axis=-1, keepdims=True)
    soft_low = softened.astype(bf16)
    attended = jnp.einsum("kgts,skd->tkgd", soft_low, values_all, preferred_element_type=f32)
    return attended.astype(bf16), softened, soft_low


def attend_back(queries, keys_all, values_all, softened, soft_low, attended_grad):
    factor = HEAD_DIM ** (-0.5)
    soft_grad = jnp.einsum("tkgd,skd->kgts", attended_grad, values_all, preferred_element_type=f32)
    values_grad = jnp.einsum("kgts,tkgd->skd", soft_low, attended_grad, preferred_element_type=f32)
    row_delta = jnp.sum(softened * soft_grad, axis=-1, keepdims=True)
    scores_grad = (softened * (soft_grad - row_delta)).astype(bf16)
    queries_grad = (
        jnp.einsum("kgts,skd->tkgd", scores_grad, keys_all, preferred_element_type=f32) * factor
    )
    keys_grad = (
        jnp.einsum("kgts,tkgd->skd", scores_grad, queries, preferred_element_type=f32) * factor
    )
    return queries_grad, keys_grad, values_grad


def shards(
    tokens, cotangent, routes,
    inproj_weight, inproj_first, inproj_second,
    outproj_weight, outproj_first, outproj_second,
    gateup_weight, gateup_first, gateup_second,
    down_weight, down_first, down_second,
    router_weight, router_first, router_second,
    gains, gains_first, gains_second,
):
    n_dp = lax.axis_size("dp")
    n_tensor = lax.axis_size("tensor")
    depth = inproj_weight.shape[0]
    kv_local = inproj_weight.shape[1]
    hidden = down_weight.shape[1]
    group = max(1, 256 // hidden)
    groups = EXPERTS // group
    in_width = inproj_weight.shape[1] * inproj_weight.shape[2]
    out_width = outproj_weight.shape[0] * outproj_weight.shape[1]
    prompt_total = PROMPT_DEV * n_dp
    count = tokens.shape[0]

    def gateup_flat(w):
        w = w.reshape(groups, group, depth, 2, hidden)
        return w.transpose(2, 0, 3, 1, 4).reshape(depth, 2 * EXPERTS * hidden)

    def gateup_back(w):
        w = w.reshape(depth, groups, 2, group, hidden)
        return w.transpose(1, 3, 0, 2, 4).reshape(EXPERTS, depth, 2, hidden)

    gains_high = gains.astype(bf16)
    gains_low = (gains - gains_high.astype(f32)).astype(bf16)
    attn_local = jnp.concatenate(
        [
            inproj_weight.reshape(depth, in_width).astype(bf16),
            outproj_weight.reshape(out_width, depth).T.astype(bf16),
            jnp.concatenate(
                [
                    router_weight.astype(bf16),
                    gains_high.T,
                    gains_low.T,
                    jnp.zeros((depth, 128 - EXPERTS - 4), bf16),
                ],
                axis=1,
            ),
        ],
        axis=1,
    )
    attn_full = lax.all_gather(attn_local, "dp", axis=0, tiled=True)
    gu_full = lax.all_gather(gateup_flat(gateup_weight.astype(bf16)), "dp", axis=0, tiled=True)
    down_full = lax.all_gather(
        down_weight.reshape(EXPERTS * hidden, depth).T.astype(bf16), "dp", axis=0, tiled=True
    )
    inproj_full = attn_full[:, :in_width]
    outproj_full = attn_full[:, in_width : in_width + out_width]
    small_full = attn_full[:, in_width + out_width :]
    router_full = small_full[:, :EXPERTS]
    small_t = small_full[:, EXPERTS : EXPERTS + 4].astype(f32).T
    gain_first = small_t[0:1] + small_t[2:3]
    gain_second = small_t[1:2] + small_t[3:4]

    device_index = lax.axis_index("dp")
    inner = jnp.arange(TOK_MB, dtype=jnp.int32)
    positions = jnp.where(
        inner < PROMPT_DEV, device_index * PROMPT_DEV + inner, prompt_total + inner - PROMPT_DEV
    )
    cosine, sine = angles_for(positions, HEAD_DIM)
    cosine = jnp.tile(cosine, (MICRO, 1))
    sine = jnp.tile(sine, (MICRO, 1))
    key_index = jnp.arange(prompt_total + CONT, dtype=jnp.int32)
    allowed = (key_index[None, :] <= positions[:, None]) & (
        (key_index[None, :] < prompt_total) | (inner[:, None] >= PROMPT_DEV)
    )
    query_width = GROUP * HEAD_DIM
    cos_query, sin_query = cosine[:, None, None, :], sine[:, None, None, :]
    cos_key, sin_key = cosine[:, None, :], sine[:, None, :]

    inputs = tokens.astype(f32)
    inverse_first = lax.rsqrt(jnp.mean(inputs * inputs, axis=-1, keepdims=True) + eps_norm)
    norm_first = inputs * inverse_first
    normed_first = (norm_first * gain_first).astype(bf16)
    mixed = jnp.dot(normed_first, inproj_full, preferred_element_type=f32).reshape(
        count, kv_local, -1
    )
    queries = rotate(
        mixed[..., :query_width].reshape(count, kv_local, GROUP, HEAD_DIM), cos_query, sin_query
    ).astype(bf16)
    keys = rotate(mixed[..., query_width : query_width + HEAD_DIM], cos_key, sin_key)
    both = jnp.concatenate([keys, mixed[..., query_width + HEAD_DIM :]], axis=-1).astype(bf16)
    both = both.reshape(MICRO, TOK_MB, kv_local * 2 * HEAD_DIM)
    prompt_both = lax.all_gather(both[:, :PROMPT_DEV], "dp", axis=1, tiled=True)
    both_all = jnp.concatenate([prompt_both, both[:, PROMPT_DEV:]], axis=1).reshape(
        MICRO, prompt_total + CONT, kv_local, 2 * HEAD_DIM
    )
    kept = []
    attended = []
    for m in range(MICRO):
        q = queries[m * TOK_MB : (m + 1) * TOK_MB]
        k, v = both_all[m, :, :, :HEAD_DIM], both_all[m, :, :, HEAD_DIM:]
        out, softened, soft_low = attend(q, k, v, allowed)
        attended.append(out.reshape(TOK_MB, -1))
        kept.append((q, k, v, softened, soft_low))
    attended = jnp.concatenate(attended, axis=0)
    branch = lax.dot_general(
        attended, outproj_full, (((1,), (1,)), ((), ())), preferred_element_type=f32
    ).astype(bf16)
    branch = line_sum(branch, n_tensor, 1)

    middle = inputs + branch.astype(f32)
    inverse_second = lax.rsqrt(jnp.mean(middle * middle, axis=-1, keepdims=True) + eps_norm)
    norm_second = middle * inverse_second
    normed_second = (norm_second * gain_second).astype(bf16)
    logits = jnp.dot(normed_second, router_full, preferred_element_type=f32)
    named = jnp.any(routes[:, :, None] == jnp.arange(EXPERTS, dtype=jnp.int32), axis=1)
    top = jnp.max(jnp.where(named, logits, -jnp.inf), axis=-1, keepdims=True)
    weights = jnp.where(named, jnp.exp(jnp.where(named, logits, top) - top), 0.0)
    gates = weights / jnp.sum(weights, axis=-1, keepdims=True)
    gates_wide = jnp.pad(gates, ((0, 0), (0, 128 - EXPERTS)))
    active, hidden_grad, gate_grad = expert_call(
        normed_second, cotangent, gates_wide, gu_full, down_full, group
    )
    contract_last = (((1,), (1,)), ((), ()))
    rows_grad = lax.dot_general(
        hidden_grad, gu_full, contract_last, preferred_element_type=f32
    ).astype(bf16)
    summed = line_sum(jnp.concatenate([rows_grad, gate_grad.astype(bf16)], axis=1), n_tensor, 2)
    mixture = lax.dot_general(active, down_full, contract_last, preferred_element_type=f32).astype(
        bf16
    )
    mixture = line_sum(mixture, n_tensor, 1)
    block_out = (middle + mixture.astype(f32)).astype(bf16)
    contract_first = (((0,), (0,)), ((), ()))
    down_grad = lax.dot_general(
        cotangent, active, contract_first, preferred_element_type=f32
    ).astype(bf16)
    gateup_grad = lax.dot_general(
        normed_second, hidden_grad, contract_first, preferred_element_type=f32
    ).astype(bf16)
    down_grad = lax.psum_scatter(down_grad, "dp", scatter_dimension=0, tiled=True)
    gateup_grad = lax.psum_scatter(gateup_grad, "dp", scatter_dimension=0, tiled=True)

    model = tokens.shape[1]
    gate_grad = summed[:, model : model + EXPERTS].astype(f32)
    outgrad = cotangent.astype(f32)
    chosen_grad = gates * (gate_grad - jnp.sum(gates * gate_grad, axis=-1, keepdims=True))
    logits_grad = chosen_grad.astype(bf16)
    router_grad = lax.dot_general(
        normed_second, logits_grad, contract_first, preferred_element_type=f32
    )
    normed_second_grad = summed[:, :model].astype(f32) + lax.dot_general(
        logits_grad, router_full, contract_last, preferred_element_type=f32
    )
    norm_second_grad = normed_second_grad * gain_second
    gain_second_grad = jnp.sum(normed_second_grad * norm_second, axis=0)
    middle_grad = outgrad + inverse_second * (
        norm_second_grad
        - norm_second * jnp.mean(norm_second_grad * norm_second, axis=-1, keepdims=True)
    )

    branch_own = middle_grad.astype(bf16)
    outproj_grad = lax.dot_general(
        branch_own, attended, contract_first, preferred_element_type=f32
    )
    attended_grad = (
        jnp.dot(branch_own, outproj_full, preferred_element_type=f32)
        .astype(bf16)
        .reshape(count, kv_local, GROUP, HEAD_DIM)
    )
    queries_grad, both_grad = [], []
    for m in range(MICRO):
        q, k, v, softened, soft_low = kept[m]
        dq, dk, dv = attend_back(
            q, k, v, softened, soft_low, attended_grad[m * TOK_MB : (m + 1) * TOK_MB]
        )
        queries_grad.append(dq)
        both_grad.append(
            jnp.concatenate([dk, dv], axis=-1).reshape(
                prompt_total + CONT, kv_local * 2 * HEAD_DIM
            )
        )
    queries_grad = jnp.concatenate(queries_grad, axis=0)
    both_grad = jnp.stack(both_grad)
    prompt_grad = lax.psum_scatter(
        both_grad[:, :prompt_total].astype(bf16), "dp", scatter_dimension=1, tiled=True
    ).astype(f32)
    both_grad = jnp.concatenate([prompt_grad, both_grad[:, prompt_total:]], axis=1).reshape(
        count, kv_local, 2 * HEAD_DIM
    )
    keys_grad, values_grad = both_grad[..., :HEAD_DIM], both_grad[..., HEAD_DIM:]
    queries_raw_grad = rotate(queries_grad, cos_query, -sin_query).reshape(count, kv_local, -1)
    keys_raw_grad = rotate(keys_grad, cos_key, -sin_key)
    mixed_grad = (
        jnp.concatenate([queries_raw_grad, keys_raw_grad, values_grad], axis=-1)
        .astype(bf16)
        .reshape(count, -1)
    )
    normed_first_grad = lax.dot_general(
        mixed_grad, inproj_full, contract_last, preferred_element_type=f32
    ).astype(bf16)
    normed_first_grad = line_sum(normed_first_grad, n_tensor, 1).astype(f32)
    inproj_grad = lax.dot_general(
        normed_first, mixed_grad, contract_first, preferred_element_type=f32
    )
    norm_first_grad = normed_first_grad * gain_first
    gain_first_grad = jnp.sum(normed_first_grad * norm_first, axis=0)
    tokens_grad = middle_grad + inverse_first * (
        norm_first_grad
        - norm_first * jnp.mean(norm_first_grad * norm_first, axis=-1, keepdims=True)
    )

    attn_grad = lax.psum_scatter(
        jnp.concatenate([inproj_grad, outproj_grad], axis=1).astype(bf16),
        "dp",
        scatter_dimension=0,
        tiled=True,
    ).astype(f32)
    small_grad = lax.psum_scatter(
        jnp.concatenate(
            [router_grad, gain_first_grad[:, None], gain_second_grad[:, None]], axis=1
        ),
        "dp",
        scatter_dimension=0,
        tiled=True,
    )
    reduced = (
        attn_grad[:, :in_width].reshape(inproj_weight.shape),
        attn_grad[:, in_width:].T.reshape(outproj_weight.shape),
        gateup_back(gateup_grad).astype(f32),
        down_grad.T.reshape(down_weight.shape).astype(f32),
        small_grad[:, :EXPERTS],
        small_grad[:, EXPERTS:].T,
    )
    triples = (
        (inproj_weight, inproj_first, inproj_second, weight_decay, 0.05),
        (outproj_weight, outproj_first, outproj_second, weight_decay, 0.3),
        (gateup_weight, gateup_first, gateup_second, weight_decay, 0.05),
        (down_weight, down_first, down_second, weight_decay, 0.05),
        (router_weight, router_first, router_second, weight_decay, 0.05),
        (gains, gains_first, gains_second, 0.0, 0.4),
    )
    results = [block_out, tokens_grad]
    for (weight, first, second, decay, rate), gradient in zip(triples, reduced):
        results.extend(adam_update(weight, first, second, gradient, decay, rate))
    return tuple(results)


def solution(mesh):
    row = P("dp", None)
    inproj = P("dp", "tensor", None)
    outproj = P("tensor", None, "dp")
    gateup = P(None, "dp", None, "tensor")
    down = P(None, "tensor", "dp")
    gain = P(None, "dp")
    weights = (inproj,) * 3 + (outproj,) * 3 + (gateup,) * 3 + (down,) * 3 + (row,) * 3 + (gain,) * 3
    return jax.shard_map(
        shards,
        mesh=mesh,
        in_specs=(row, row, row) + weights,
        out_specs=(row, row) + weights,
        check_vma=False,
    )
```

```python
import functools

import jax
import jax.numpy as jnp
from jax import lax
from jax.experimental import pallas as pl
from jax.experimental.pallas import tpu as pltpu
from jax.sharding import PartitionSpec as P

HEAD_DIM = 64
TOPK = 8
EXPERTS = 16
PROMPT_DEV = 128
CONT = 512
MICRO = 2
STEP = 10
GROUP = 3
TOK_MB = 640

eps_norm = 1e-05
beta_first = 0.9
beta_second = 0.95
adam_eps = 1e-08
weight_decay = 0.1
bf16 = jnp.bfloat16
f32 = jnp.float32
line_chunks = 10
MESH = pl.DeviceIdType.MESH


def angles_for(positions, head_size):
    half_dim = head_size // 2
    freqs = 10000.0 ** (-2.0 * jnp.arange(half_dim, dtype=f32) / head_size)
    angles = positions.astype(f32)[..., None] * freqs
    return (jnp.cos(angles), jnp.sin(angles))


def rotate(values, cosine, sine):
    half_dim = values.shape[-1] // 2
    first_half = values[..., :half_dim]
    second_half = values[..., half_dim:]
    return jnp.concatenate(
        [first_half * cosine - second_half * sine, second_half * cosine + first_half * sine],
        axis=-1,
    )


def adam_update(weight, moment_one, moment_two, gradient, decay_rate, learn_rate):
    first_next = beta_first * moment_one + (1.0 - beta_first) * gradient
    second_next = beta_second * moment_two + (1.0 - beta_second) * gradient * gradient
    corr_first = 1.0 - beta_first**STEP
    corr_second = 1.0 - beta_second**STEP
    update = first_next / corr_first / (jnp.sqrt(second_next / corr_second) + adam_eps)
    return (weight - learn_rate * (update + decay_rate * weight), first_next, second_next)


def line_sum_kernel(n, chunks, x_ref, o_ref, held, send_red, recv_red, send_out, recv_out):
    me = lax.axis_index("tensor")
    rows = x_ref.shape[0] // (2 * chunks)
    low, high = me - 1, me + 1

    barrier = pltpu.get_barrier_semaphore()

    @pl.when(me > 0)
    def _():
        pl.semaphore_signal(barrier, inc=1, device_id={"tensor": low}, device_id_type=MESH)

    @pl.when(me < n - 1)
    def _():
        pl.semaphore_signal(barrier, inc=1, device_id={"tensor": high}, device_id_type=MESH)

    pl.semaphore_wait(barrier, jnp.where((me > 0) & (me < n - 1), 2, 1))

    def part(half, c):
        return pl.ds(pl.multiple_of((half * chunks + c) * rows, 16), rows)

    def reduce_copy(half, c, src):
        to = low if half == 0 else high
        return pltpu.make_async_remote_copy(
            src_ref=src.at[part(half, c)],
            dst_ref=held.at[part(half, c)],
            send_sem=send_red.at[half, c],
            recv_sem=recv_red.at[half, c],
            device_id={"tensor": to},
            device_id_type=MESH,
        )

    def out_copy(half, c):
        to = high if half == 0 else low
        return pltpu.make_async_remote_copy(
            src_ref=o_ref.at[part(half, c)],
            dst_ref=o_ref.at[part(half, c)],
            send_sem=send_out.at[half, c],
            recv_sem=recv_out.at[half, c],
            device_id={"tensor": to},
            device_id_type=MESH,
        )

    def place(half):
        return n - 1 - me if half == 0 else me

    def step(t, carry):
        for half in (0, 1):
            at = place(half)
            c = t - at

            @pl.when((c >= 0) & (c < chunks))
            def _():
                @pl.when(at == 0)
                def _():
                    reduce_copy(half, c, x_ref).start()

                @pl.when(at > 0)
                def _():
                    reduce_copy(half, c, held).wait_recv()
                    total = x_ref[part(half, c)].astype(f32) + held[part(half, c)].astype(f32)

                    @pl.when(at < n - 1)
                    def _():
                        held[part(half, c)] = total.astype(held.dtype)
                        reduce_copy(half, c, held).start()

                    @pl.when(at == n - 1)
                    def _():
                        o_ref[part(half, c)] = total.astype(o_ref.dtype)
                        out_copy(half, c).start()

        for half in (0, 1):
            at = place(half)
            c = t - 2 * (n - 1) + at

            @pl.when((at < n - 1) & (c >= 0) & (c < chunks))
            def _():
                out_copy(half, c).wait_recv()

                @pl.when(at > 0)
                def _():
                    out_copy(half, c).start()

        return carry

    lax.fori_loop(0, chunks + 2 * (n - 1), step, 0)

    def finish(c, carry):
        for half in (0, 1):
            at = place(half)

            @pl.when(at < n - 1)
            def _():
                reduce_copy(half, c, held).wait_send()

            @pl.when(at > 0)
            def _():
                out_copy(half, c).wait_send()

        return carry

    lax.fori_loop(0, chunks, finish, 0)


def line_sum(x, n, barrier_id):
    rows, width = x.shape
    chunks = line_chunks
    return pl.pallas_call(
        functools.partial(line_sum_kernel, n, chunks),
        out_shape=jax.ShapeDtypeStruct(x.shape, x.dtype),
        in_specs=[pl.BlockSpec(memory_space=pltpu.VMEM)],
        out_specs=pl.BlockSpec(memory_space=pltpu.VMEM),
        scratch_shapes=[pltpu.VMEM(x.shape, x.dtype)]
        + [pltpu.SemaphoreType.DMA((2, chunks)) for _ in range(4)],
        compiler_params=pltpu.CompilerParams(
            collective_id=barrier_id, has_side_effects=True, vmem_limit_bytes=24 * 2**20
        ),
        cost_estimate=pl.CostEstimate(
            flops=rows * width, bytes_accessed=100 * rows * width, transcendentals=0
        ),
    )(x)


def expert_kernel(group, rows_ref, outgrad_ref, gates_ref, gu_ref, down_ref,
                  active_ref, hidden_ref, gate_grad_ref):
    step = pl.program_id(0)
    tile = 256
    width = gu_ref.shape[1] // 2
    hidden = width // group
    lane = lax.broadcasted_iota(jnp.int32, (tile, 128), 1)
    column = lax.broadcasted_iota(jnp.int32, (tile, width), 1)

    @pl.when(step == 0)
    def _():
        gate_grad_ref[...] = jnp.zeros_like(gate_grad_ref)

    def one(t, carry):
        at = pl.ds(pl.multiple_of(t * tile, tile), tile)
        h = jnp.dot(rows_ref[at], gu_ref[...], preferred_element_type=f32)
        back = jnp.dot(outgrad_ref[at], down_ref[...], preferred_element_type=f32)
        gates = gates_ref[at]
        wide = jnp.zeros((tile, width), f32)
        for j in range(group):
            g = jnp.sum(jnp.where(lane == step * group + j, gates, 0.0), axis=1, keepdims=True)
            wide = g + wide if group == 1 else jnp.where(column // hidden == j, g, wide)
        gate, up = h[:, :width], h[:, width:]
        sig = 1.0 / (1.0 + jnp.exp(-gate))
        silu = gate * sig
        active = (silu * up).astype(bf16).astype(f32)
        active_ref[at] = (active * wide).astype(bf16)
        product = active * back
        grads = gate_grad_ref[at]
        for j in range(group):
            s = jnp.sum(jnp.where(column // hidden == j, product, 0.0), axis=1, keepdims=True)
            grads = jnp.where(lane == step * group + j, s, grads)
        gate_grad_ref[at] = grads
        back = back * wide
        hidden_ref[at, :width] = (back * up * sig * (1.0 + gate * (1.0 - sig))).astype(bf16)
        hidden_ref[at, width:] = (back * silu).astype(bf16)
        return carry

    lax.fori_loop(0, rows_ref.shape[0] // tile, one, 0)


def expert_call(rows, outgrad, gates, gu, down, group):
    tokens, model = rows.shape
    width = gu.shape[1] // (EXPERTS // group)
    steps = EXPERTS // group
    return pl.pallas_call(
        functools.partial(expert_kernel, group),
        grid=(steps,),
        in_specs=[
            pl.BlockSpec((tokens, model), lambda p: (0, 0)),
            pl.BlockSpec((tokens, model), lambda p: (0, 0)),
            pl.BlockSpec((tokens, 128), lambda p: (0, 0)),
            pl.BlockSpec((model, width), lambda p: (0, p)),
            pl.BlockSpec((model, width // 2), lambda p: (0, p)),
        ],
        out_specs=[
            pl.BlockSpec((tokens, width // 2), lambda p: (0, p)),
            pl.BlockSpec((tokens, width), lambda p: (0, p)),
            pl.BlockSpec((tokens, 128), lambda p: (0, 0)),
        ],
        out_shape=[
            jax.ShapeDtypeStruct((tokens, steps * width // 2), bf16),
            jax.ShapeDtypeStruct((tokens, steps * width), bf16),
            jax.ShapeDtypeStruct((tokens, 128), f32),
        ],
        compiler_params=pltpu.CompilerParams(vmem_limit_bytes=48 * 2**20),
        cost_estimate=pl.CostEstimate(
            flops=2 * tokens * model * steps * width * 3 // 2,
            bytes_accessed=2 * (model * steps * width * 3 // 2 + tokens * steps * width * 3 // 2),
            transcendentals=tokens * steps * width // 2,
        ),
    )(rows, outgrad, gates, gu, down)


def turn(u, cosine, sine):
    lane = lax.broadcasted_iota(jnp.int32, u.shape, 1) % HEAD_DIM
    other = jnp.where(lane < HEAD_DIM // 2, pltpu.roll(u, 96, 1), pltpu.roll(u, 32, 1))
    return u * cosine + other * sine


def project_kernel(x_ref, gain_ref, w_ref, cos_ref, sin_ref, normed_ref, q_ref, kv_ref):
    x = x_ref[...].astype(f32)
    inverse = lax.rsqrt(jnp.mean(x * x, axis=-1, keepdims=True) + eps_norm)
    normed = (x * inverse * gain_ref[0:1]).astype(bf16)
    normed_ref[...] = normed
    mixed = jnp.dot(normed, w_ref[...], preferred_element_type=f32)
    cosine, sine = cos_ref[...], sin_ref[...]
    turned = q_ref.shape[1] // 128
    for c in range(turned):
        q_ref[:, c * 128 : (c + 1) * 128] = turn(
            mixed[:, c * 128 : (c + 1) * 128], cosine, sine
        ).astype(bf16)
    start = turned * 128
    kv_ref[:, :128] = turn(mixed[:, start : start + 128], cosine, sine).astype(bf16)
    kv_ref[:, 128:] = mixed[:, start + 128 :].astype(bf16)


def project_call(tokens, gain, w, cosine, sine):
    count, model = tokens.shape
    tile = 256
    width = w.shape[1]
    row = lambda n: pl.BlockSpec((tile, n), lambda i: (i, 0))
    return pl.pallas_call(
        project_kernel,
        grid=(count // tile,),
        in_specs=[
            row(model),
            pl.BlockSpec((8, model), lambda i: (0, 0)),
            pl.BlockSpec((model, width), lambda i: (0, 0)),
            row(128),
            row(128),
        ],
        out_specs=[row(model), row(width - 256), row(256)],
        out_shape=[
            jax.ShapeDtypeStruct((count, model), bf16),
            jax.ShapeDtypeStruct((count, width - 256), bf16),
            jax.ShapeDtypeStruct((count, 256), bf16),
        ],
        compiler_params=pltpu.CompilerParams(vmem_limit_bytes=32 * 2**20),
        cost_estimate=pl.CostEstimate(
            flops=2 * count * model * width, bytes_accessed=6 * count * model, transcendentals=count
        ),
    )(tokens, gain, w, cosine, sine)


def head_places(heads):
    return [(h // GROUP, h % 2, h // 2) for h in range(heads)]


def spread(kv, scale):
    lane = lax.broadcasted_iota(jnp.int32, kv.shape, 1)
    kv = kv * scale
    turned = pltpu.roll(kv, HEAD_DIM, 1)
    first = lane < HEAD_DIM
    zero = jnp.zeros_like(kv)
    return {
        (0, 0): jnp.where(first, kv, zero).astype(bf16),
        (0, 1): jnp.where(first, zero, turned).astype(bf16),
        (1, 0): jnp.where(first, turned, zero).astype(bf16),
        (1, 1): jnp.where(first, zero, kv).astype(bf16),
    }


def row_tiles(prompt_total):
    tiles = [(0, PROMPT_DEV, prompt_total)]
    for start in range(0, CONT, 256):
        tiles.append((PROMPT_DEV + start, 256, prompt_total + start + 256))
    return tiles


nt = (((1,), (1,)), ((), ()))


def attention_kernel(heads, dp, q_ref, kv_ref, o_ref, lse_ref, k_ref, v_ref):
    prompt_total = kv_ref.shape[1] - CONT
    me = lax.axis_index(dp)
    keys = spread(kv_ref[0, :, :128].astype(f32), HEAD_DIM**-0.5)
    values = spread(kv_ref[0, :, 128:].astype(f32), 1.0)
    for i, place in enumerate(keys):
        k_ref[i] = keys[place]
        v_ref[i] = values[place]
    index = {place: i for i, place in enumerate(keys)}
    lane = lax.broadcasted_iota(jnp.int32, (1, 128), 1)
    for start, rows, length in row_tiles(prompt_total):
        row = lax.broadcasted_iota(jnp.int32, (rows, 1), 0)
        if start == 0:
            masked = 0
            reach = row + me * PROMPT_DEV
        else:
            masked = length - 256
            reach = row
        column = lax.broadcasted_iota(jnp.int32, (rows, length - masked), 1)
        lse = jnp.zeros((rows, 128), f32)
        pair_out = None
        for h, (kv, half, pair) in enumerate(head_places(heads)):
            q = q_ref[start : start + rows, pair * 128 : (pair + 1) * 128]
            i = index[kv, half]
            tail = lax.dot_general(q, k_ref[i, masked:length], nt, preferred_element_type=f32)
            tail = jnp.where(column <= reach, tail, -1e30)
            top = jnp.max(tail, axis=1, keepdims=True)
            if masked:
                head = lax.dot_general(q, k_ref[i, :masked], nt, preferred_element_type=f32)
                top = jnp.maximum(top, jnp.max(head, axis=1, keepdims=True))
                p_head = jnp.exp(head - top)
            p_tail = jnp.exp(tail - top)
            total = jnp.sum(p_tail, axis=1, keepdims=True)
            out = jnp.dot(
                p_tail.astype(bf16), v_ref[i, masked:length], preferred_element_type=f32
            )
            if masked:
                total = total + jnp.sum(p_head, axis=1, keepdims=True)
                out = out + jnp.dot(
                    p_head.astype(bf16), v_ref[i, :masked], preferred_element_type=f32
                )
            out = out / total
            lse = jnp.where(lane == h, top + jnp.log(total), lse)
            if half == 0:
                pair_out = out
            else:
                o_ref[start : start + rows, pair * 128 : (pair + 1) * 128] = (
                    pair_out + out
                ).astype(bf16)
        lse_ref[start : start + rows] = lse


def attention_call(q, kv, dp):
    count, width = q.shape
    keys = kv.shape[1]
    heads = width // HEAD_DIM
    return pl.pallas_call(
        functools.partial(attention_kernel, heads, dp),
        grid=(MICRO,),
        in_specs=[
            pl.BlockSpec((TOK_MB, width), lambda m: (m, 0)),
            pl.BlockSpec((1, keys, 256), lambda m: (m, 0, 0)),
        ],
        out_specs=[
            pl.BlockSpec((TOK_MB, width), lambda m: (m, 0)),
            pl.BlockSpec((TOK_MB, 128), lambda m: (m, 0)),
        ],
        out_shape=[
            jax.ShapeDtypeStruct((count, width), bf16),
            jax.ShapeDtypeStruct((count, 128), f32),
        ],
        scratch_shapes=[pltpu.VMEM((4, keys, 128), bf16), pltpu.VMEM((4, keys, 128), bf16)],
        compiler_params=pltpu.CompilerParams(vmem_limit_bytes=48 * 2**20),
        cost_estimate=pl.CostEstimate(
            flops=16 * count * keys * width,
            bytes_accessed=8 * count * width,
            transcendentals=count * keys * heads,
        ),
    )(q, kv)


def attention_back_kernel(
    heads, dp, q_ref, kv_ref, do_ref, o_ref, lse_ref, cos_ref, sin_ref, row_cos_ref, row_sin_ref,
    dq_ref, dkv_ref, k_ref, v_ref, kt_ref, dk_ref, dv_ref,
):
    prompt_total = kv_ref.shape[1] - CONT
    me = lax.axis_index(dp)
    keys = spread(kv_ref[0, :, :128].astype(f32), HEAD_DIM**-0.5)
    values = spread(kv_ref[0, :, 128:].astype(f32), 1.0)
    for i, place in enumerate(keys):
        k_ref[i] = keys[place]
        v_ref[i] = values[place]
        kt_ref[i] = keys[place].astype(f32).T.astype(bf16)
    index = {place: i for i, place in enumerate(keys)}
    dk_ref[...] = jnp.zeros_like(dk_ref)
    dv_ref[...] = jnp.zeros_like(dv_ref)
    half_rows = (
        lax.broadcasted_iota(jnp.int32, (8, 128), 1) // HEAD_DIM
        == lax.broadcasted_iota(jnp.int32, (8, 128), 0)
    ).astype(f32)
    for start, rows, length in row_tiles(prompt_total):
        at = slice(start, start + rows)
        column = lax.broadcasted_iota(jnp.int32, (1, rows), 1)
        if start == 0:
            masked = 0
            reach = column + me * PROMPT_DEV
        else:
            masked = length - 256
            reach = column
        key = lax.broadcasted_iota(jnp.int32, (length - masked, rows), 0)
        back = None
        for h, (kv, half, pair) in enumerate(head_places(heads)):
            lanes = slice(pair * 128, (pair + 1) * 128)
            i = index[kv, half]
            q, do = q_ref[at, lanes], do_ref[at, lanes]
            if half == 0:
                delta_pair = lax.dot_general(
                    half_rows,
                    do.astype(f32) * o_ref[at, lanes].astype(f32),
                    nt,
                    precision=lax.Precision.HIGHEST,
                    preferred_element_type=f32,
                )
            delta = delta_pair[half : half + 1]
            lse = lse_ref[0, h : h + 1, at]
            for low, high in ((0, masked), (masked, length)):
                if low == high:
                    continue
                s = lax.dot_general(k_ref[i, low:high], q, nt, preferred_element_type=f32)
                if low == masked:
                    s = jnp.where(key <= reach, s, -1e30)
                p = jnp.exp(s - lse)
                dp_ = lax.dot_general(v_ref[i, low:high], do, nt, preferred_element_type=f32)
                ds = (p * (dp_ - delta)).astype(bf16)
                dv_ref[i, low:high] += jnp.dot(
                    p.astype(bf16), do, preferred_element_type=f32
                )
                dk_ref[i, low:high] += jnp.dot(ds, q, preferred_element_type=f32)
                term = jnp.dot(kt_ref[i, :, low:high], ds, preferred_element_type=f32)
                back = term if back is None else back + term
            if half == 1:
                dq_ref[at, lanes] = turn(
                    back.T, row_cos_ref[at], -row_sin_ref[at]
                ).astype(bf16)
                back = None
    lane = lax.broadcasted_iota(jnp.int32, (kv_ref.shape[1], 128), 1)

    def joined(acc):
        get = lambda place: acc[index[place]]
        return jnp.where(
            lane < HEAD_DIM,
            get((0, 0)) + pltpu.roll(get((0, 1)), HEAD_DIM, 1),
            get((1, 1)) + pltpu.roll(get((1, 0)), HEAD_DIM, 1),
        )

    dk = joined(dk_ref) * HEAD_DIM**-0.5
    dkv_ref[0, :, :128] = turn(dk, cos_ref[...], -sin_ref[...]).astype(bf16)
    dkv_ref[0, :, 128:] = joined(dv_ref).astype(bf16)


def attention_back_call(q, kv, do, o, lse, cosine, sine, row_cos, row_sin, dp):
    count, width = q.shape
    keys = kv.shape[1]
    heads = width // HEAD_DIM
    rows = pl.BlockSpec((TOK_MB, width), lambda m: (m, 0))
    return pl.pallas_call(
        functools.partial(attention_back_kernel, heads, dp),
        grid=(MICRO,),
        in_specs=[
            rows,
            pl.BlockSpec((1, keys, 256), lambda m: (m, 0, 0)),
            rows,
            rows,
            pl.BlockSpec((1, 8, TOK_MB), lambda m: (m, 0, 0)),
            pl.BlockSpec((keys, 128), lambda m: (0, 0)),
            pl.BlockSpec((keys, 128), lambda m: (0, 0)),
            pl.BlockSpec((TOK_MB, 128), lambda m: (0, 0)),
            pl.BlockSpec((TOK_MB, 128), lambda m: (0, 0)),
        ],
        out_specs=[rows, pl.BlockSpec((1, keys, 256), lambda m: (m, 0, 0))],
        out_shape=[
            jax.ShapeDtypeStruct((count, width), bf16),
            jax.ShapeDtypeStruct((MICRO, keys, 256), bf16),
        ],
        scratch_shapes=[
            pltpu.VMEM((4, keys, 128), bf16),
            pltpu.VMEM((4, keys, 128), bf16),
            pltpu.VMEM((4, 128, keys), bf16),
            pltpu.VMEM((4, keys, 128), f32),
            pltpu.VMEM((4, keys, 128), f32),
        ],
        compiler_params=pltpu.CompilerParams(vmem_limit_bytes=56 * 2**20),
        cost_estimate=pl.CostEstimate(
            flops=40 * count * keys * width,
            bytes_accessed=12 * count * width,
            transcendentals=count * keys * heads,
        ),
    )(q, kv, do, o, lse, cosine, sine, row_cos, row_sin)


def attend(queries, keys_all, values_all, allowed):
    factor = HEAD_DIM ** (-0.5)
    scores = jnp.einsum("tkgd,skd->kgts", queries, keys_all, preferred_element_type=f32) * factor
    scores = jnp.where(allowed, scores, -1e30)
    row_max = jnp.max(scores, axis=-1, keepdims=True)
    exponent = jnp.exp(scores - row_max)
    softened = exponent / jnp.sum(exponent, axis=-1, keepdims=True)
    soft_low = softened.astype(bf16)
    attended = jnp.einsum("kgts,skd->tkgd", soft_low, values_all, preferred_element_type=f32)
    return attended.astype(bf16), softened, soft_low


def attend_back(queries, keys_all, values_all, softened, soft_low, attended_grad):
    factor = HEAD_DIM ** (-0.5)
    soft_grad = jnp.einsum("tkgd,skd->kgts", attended_grad, values_all, preferred_element_type=f32)
    values_grad = jnp.einsum("kgts,tkgd->skd", soft_low, attended_grad, preferred_element_type=f32)
    row_delta = jnp.sum(softened * soft_grad, axis=-1, keepdims=True)
    scores_grad = (softened * (soft_grad - row_delta)).astype(bf16)
    queries_grad = (
        jnp.einsum("kgts,skd->tkgd", scores_grad, keys_all, preferred_element_type=f32) * factor
    )
    keys_grad = (
        jnp.einsum("kgts,tkgd->skd", scores_grad, queries, preferred_element_type=f32) * factor
    )
    return queries_grad, keys_grad, values_grad


def shards(
    tokens, cotangent, routes,
    inproj_weight, inproj_first, inproj_second,
    outproj_weight, outproj_first, outproj_second,
    gateup_weight, gateup_first, gateup_second,
    down_weight, down_first, down_second,
    router_weight, router_first, router_second,
    gains, gains_first, gains_second,
):
    n_dp = lax.axis_size("dp")
    n_tensor = lax.axis_size("tensor")
    depth = inproj_weight.shape[0]
    kv_local = inproj_weight.shape[1]
    hidden = down_weight.shape[1]
    group = max(1, 256 // hidden)
    groups = EXPERTS // group
    in_width = inproj_weight.shape[1] * inproj_weight.shape[2]
    out_width = outproj_weight.shape[0] * outproj_weight.shape[1]
    prompt_total = PROMPT_DEV * n_dp
    count = tokens.shape[0]

    def gateup_flat(w):
        w = w.reshape(groups, group, depth, 2, hidden)
        return w.transpose(2, 0, 3, 1, 4).reshape(depth, 2 * EXPERTS * hidden)

    def gateup_back(w):
        w = w.reshape(depth, groups, 2, group, hidden)
        return w.transpose(1, 3, 0, 2, 4).reshape(EXPERTS, depth, 2, hidden)

    query_width = GROUP * HEAD_DIM

    def inproj_flat(w):
        w = w.reshape(depth, kv_local, query_width + 2 * HEAD_DIM)
        parts = (w[:, :, :query_width], w[:, :, query_width:-HEAD_DIM], w[:, :, -HEAD_DIM:])
        return jnp.concatenate([p.reshape(depth, -1) for p in parts], axis=1)

    def inproj_back(w):
        q, k, v = jnp.split(w, [kv_local * query_width, kv_local * (query_width + HEAD_DIM)], axis=1)
        return jnp.concatenate([p.reshape(depth, kv_local, -1) for p in (q, k, v)], axis=2)

    gains_high = gains.astype(bf16)
    gains_low = (gains - gains_high.astype(f32)).astype(bf16)
    attn_local = jnp.concatenate(
        [
            inproj_flat(inproj_weight.astype(bf16)),
            outproj_weight.reshape(out_width, depth).T.astype(bf16),
            jnp.concatenate(
                [
                    router_weight.astype(bf16),
                    gains_high.T,
                    gains_low.T,
                    jnp.zeros((depth, 128 - EXPERTS - 4), bf16),
                ],
                axis=1,
            ),
        ],
        axis=1,
    )
    attn_full = lax.all_gather(attn_local, "dp", axis=0, tiled=True)
    gu_full = lax.all_gather(gateup_flat(gateup_weight.astype(bf16)), "dp", axis=0, tiled=True)
    down_full = lax.all_gather(
        down_weight.reshape(EXPERTS * hidden, depth).T.astype(bf16), "dp", axis=0, tiled=True
    )
    inproj_full = attn_full[:, :in_width]
    outproj_full = attn_full[:, in_width : in_width + out_width]
    small_full = attn_full[:, in_width + out_width :]
    router_full = small_full[:, :EXPERTS]
    small_t = small_full[:, EXPERTS : EXPERTS + 4].astype(f32).T
    gain_first = small_t[0:1] + small_t[2:3]
    gain_second = small_t[1:2] + small_t[3:4]

    device_index = lax.axis_index("dp")
    inputs = tokens.astype(f32)
    inverse_first = lax.rsqrt(jnp.mean(inputs * inputs, axis=-1, keepdims=True) + eps_norm)
    norm_first = inputs * inverse_first
    cosine, sine = angles_for(jnp.arange(prompt_total + CONT), HEAD_DIM)

    def of_rows(table):
        own = lax.dynamic_slice_in_dim(table, device_index * PROMPT_DEV, PROMPT_DEV, 0)
        return jnp.concatenate([own, table[prompt_total:]], axis=0)

    in_kernels = kv_local * HEAD_DIM == 128
    queries_width = kv_local * query_width
    both_width = kv_local * 2 * HEAD_DIM
    if in_kernels:
        cos_all = jnp.concatenate([cosine] * 4, axis=1)
        sin_all = jnp.concatenate([-sine, sine] * 2, axis=1)
        cos_row, sin_row = of_rows(cos_all), of_rows(sin_all)
        normed_first, queries, both = project_call(
            tokens,
            jnp.pad(gain_first, ((0, 7), (0, 0))),
            inproj_full,
            jnp.concatenate([cos_row] * MICRO, axis=0),
            jnp.concatenate([sin_row] * MICRO, axis=0),
        )
    else:
        cosine, sine = (jnp.tile(of_rows(t), (MICRO, 1))[:, None, :] for t in (cosine, sine))
        normed_first = (norm_first * gain_first).astype(bf16)
        mixed = jnp.dot(normed_first, inproj_full, preferred_element_type=f32)
        queries = rotate(
            mixed[:, :queries_width].reshape(count, -1, HEAD_DIM), cosine, sine
        ).astype(bf16)
        keys = rotate(
            mixed[:, queries_width : queries_width + kv_local * HEAD_DIM].reshape(
                count, -1, HEAD_DIM
            ),
            cosine,
            sine,
        )
        both = jnp.concatenate(
            [keys.reshape(count, -1), mixed[:, queries_width + kv_local * HEAD_DIM :]], axis=1
        ).astype(bf16)
    both = both.reshape(MICRO, TOK_MB, both_width)
    prompt_both = lax.all_gather(both[:, :PROMPT_DEV], "dp", axis=1, tiled=True)
    both_all = jnp.concatenate([prompt_both, both[:, PROMPT_DEV:]], axis=1)
    if in_kernels:
        attended, lse = attention_call(queries, both_all, "dp")
    else:
        inner = jnp.arange(TOK_MB, dtype=jnp.int32)
        positions = jnp.where(
            inner < PROMPT_DEV, device_index * PROMPT_DEV + inner, prompt_total + inner - PROMPT_DEV
        )
        key_index = jnp.arange(prompt_total + CONT, dtype=jnp.int32)
        allowed = (key_index[None, :] <= positions[:, None]) & (
            (key_index[None, :] < prompt_total) | (inner[:, None] >= PROMPT_DEV)
        )
        kept = []
        attended = []
        for m in range(MICRO):
            q = queries[m * TOK_MB : (m + 1) * TOK_MB].reshape(TOK_MB, kv_local, GROUP, HEAD_DIM)
            k, v = (
                t.reshape(-1, kv_local, HEAD_DIM) for t in jnp.split(both_all[m], 2, axis=1)
            )
            out, softened, soft_low = attend(q, k, v, allowed)
            attended.append(out.reshape(TOK_MB, -1))
            kept.append((q, k, v, softened, soft_low))
        attended = jnp.concatenate(attended, axis=0)
    branch = lax.dot_general(
        attended, outproj_full, (((1,), (1,)), ((), ())), preferred_element_type=f32
    ).astype(bf16)
    branch = line_sum(branch, n_tensor, 1)

    middle = inputs + branch.astype(f32)
    inverse_second = lax.rsqrt(jnp.mean(middle * middle, axis=-1, keepdims=True) + eps_norm)
    norm_second = middle * inverse_second
    normed_second = (norm_second * gain_second).astype(bf16)
    logits = jnp.dot(normed_second, router_full, preferred_element_type=f32)
    named = jnp.any(routes[:, :, None] == jnp.arange(EXPERTS, dtype=jnp.int32), axis=1)
    top = jnp.max(jnp.where(named, logits, -jnp.inf), axis=-1, keepdims=True)
    weights = jnp.where(named, jnp.exp(jnp.where(named, logits, top) - top), 0.0)
    gates = weights / jnp.sum(weights, axis=-1, keepdims=True)
    gates_wide = jnp.pad(gates, ((0, 0), (0, 128 - EXPERTS)))
    active, hidden_grad, gate_grad = expert_call(
        normed_second, cotangent, gates_wide, gu_full, down_full, group
    )
    contract_last = (((1,), (1,)), ((), ()))
    contract_first = (((0,), (0,)), ((), ()))
    down_grad = lax.dot_general(
        cotangent, active, contract_first, preferred_element_type=f32
    ).astype(bf16)
    gateup_grad = lax.dot_general(
        normed_second, hidden_grad, contract_first, preferred_element_type=f32
    ).astype(bf16)
    hidden_grad, down_grad, gateup_grad = lax.optimization_barrier(
        (hidden_grad, down_grad, gateup_grad)
    )
    down_grad = lax.psum_scatter(down_grad, "dp", scatter_dimension=0, tiled=True)
    gateup_grad = lax.psum_scatter(gateup_grad, "dp", scatter_dimension=0, tiled=True)
    rows_grad = lax.dot_general(
        hidden_grad, gu_full, contract_last, preferred_element_type=f32
    ).astype(bf16)
    mixture = lax.dot_general(active, down_full, contract_last, preferred_element_type=f32).astype(
        bf16
    )
    summed = line_sum(jnp.concatenate([rows_grad, gate_grad.astype(bf16)], axis=1), n_tensor, 2)

    model = tokens.shape[1]
    gate_grad = summed[:, model : model + EXPERTS].astype(f32)
    outgrad = cotangent.astype(f32)
    chosen_grad = gates * (gate_grad - jnp.sum(gates * gate_grad, axis=-1, keepdims=True))
    logits_grad = chosen_grad.astype(bf16)
    router_grad = lax.dot_general(
        normed_second, logits_grad, contract_first, preferred_element_type=f32
    )
    normed_second_grad = summed[:, :model].astype(f32) + lax.dot_general(
        logits_grad, router_full, contract_last, preferred_element_type=f32
    )
    norm_second_grad = normed_second_grad * gain_second
    gain_second_grad = jnp.sum(normed_second_grad * norm_second, axis=0)
    middle_grad = outgrad + inverse_second * (
        norm_second_grad
        - norm_second * jnp.mean(norm_second_grad * norm_second, axis=-1, keepdims=True)
    )

    branch_own = middle_grad.astype(bf16)
    outproj_grad = lax.dot_general(
        branch_own, attended, contract_first, preferred_element_type=f32
    )
    attended_grad = jnp.dot(branch_own, outproj_full, preferred_element_type=f32).astype(bf16)
    attended_grad, down_grad, gateup_grad, mixture = lax.optimization_barrier(
        (attended_grad, down_grad, gateup_grad, mixture)
    )
    if in_kernels:
        lse_rows = lse[:, :8].reshape(MICRO, TOK_MB, 8).transpose(0, 2, 1)
        queries_grad, both_grad = attention_back_call(
            queries, both_all, attended_grad, attended, lse_rows,
            cos_all, sin_all, cos_row, sin_row, "dp",
        )
    else:
        queries_grad, both_grad = [], []
        for m in range(MICRO):
            q, k, v, softened, soft_low = kept[m]
            dout = attended_grad[m * TOK_MB : (m + 1) * TOK_MB].reshape(q.shape)
            dq, dk, dv = attend_back(q, k, v, softened, soft_low, dout)
            queries_grad.append(dq.reshape(TOK_MB, -1, HEAD_DIM))
            both_grad.append(jnp.concatenate([t.reshape(-1, both_width // 2) for t in (dk, dv)], 1))
        queries_grad = rotate(jnp.concatenate(queries_grad, axis=0), cosine, -sine)
        queries_grad = queries_grad.reshape(count, -1).astype(bf16)
        both_grad = jnp.stack(both_grad)
    both_grad, mixture = lax.optimization_barrier((both_grad, mixture))
    mixture = lax.psum(mixture, "tensor")
    block_out = (middle + mixture.astype(f32)).astype(bf16)
    prompt_grad = lax.psum_scatter(
        both_grad[:, :prompt_total].astype(bf16), "dp", scatter_dimension=1, tiled=True
    )
    both_grad = jnp.concatenate(
        [prompt_grad.astype(both_grad.dtype), both_grad[:, prompt_total:]], axis=1
    ).reshape(count, both_width)
    if not in_kernels:
        keys_grad = rotate(
            both_grad[:, : both_width // 2].reshape(count, -1, HEAD_DIM), cosine, -sine
        )
        both_grad = jnp.concatenate(
            [keys_grad.reshape(count, -1), both_grad[:, both_width // 2 :]], axis=1
        ).astype(bf16)
    mixed_grad = jnp.concatenate([queries_grad, both_grad], axis=1)
    normed_first_grad = lax.dot_general(
        mixed_grad, inproj_full, contract_last, preferred_element_type=f32
    ).astype(bf16)
    inproj_grad = lax.dot_general(
        normed_first, mixed_grad, contract_first, preferred_element_type=f32
    )
    attn_grad = jnp.concatenate(
        [
            inproj_grad,
            outproj_grad,
            router_grad,
            gain_second_grad[:, None],
            jnp.zeros((model, 127 - EXPERTS), f32),
        ],
        axis=1,
    ).astype(bf16)
    down_next = adam_update(
        down_weight, down_first, down_second,
        down_grad.T.reshape(down_weight.shape).astype(f32), weight_decay, 0.05,
    )
    gateup_next = adam_update(
        gateup_weight, gateup_first, gateup_second,
        gateup_back(gateup_grad).astype(f32), weight_decay, 0.05,
    )
    normed_first_grad, attn_grad, down_next, gateup_next = lax.optimization_barrier(
        (normed_first_grad, attn_grad, down_next, gateup_next)
    )
    attn_grad = lax.psum_scatter(attn_grad, "dp", scatter_dimension=0, tiled=True).astype(f32)
    normed_first_grad = line_sum(normed_first_grad, n_tensor, 1).astype(f32)
    norm_first_grad = normed_first_grad * gain_first
    gain_first_grad = jnp.sum(normed_first_grad * norm_first, axis=0)
    tokens_grad = middle_grad + inverse_first * (
        norm_first_grad
        - norm_first * jnp.mean(norm_first_grad * norm_first, axis=-1, keepdims=True)
    )

    gain_first_parts = lax.all_gather(gain_first_grad, "dp")
    gain_first_grad = lax.dynamic_slice_in_dim(
        jnp.sum(gain_first_parts, axis=0), device_index * depth, depth, 0
    )
    split = (in_width, in_width + out_width, in_width + out_width + EXPERTS)
    inproj_grad, outproj_grad, router_grad, gain_second_grad = (
        attn_grad[:, : split[0]],
        attn_grad[:, split[0] : split[1]],
        attn_grad[:, split[1] : split[2]],
        attn_grad[:, split[2]],
    )
    updates = (
        adam_update(
            inproj_weight, inproj_first, inproj_second, inproj_back(inproj_grad), weight_decay, 0.05
        ),
        adam_update(
            outproj_weight, outproj_first, outproj_second,
            outproj_grad.T.reshape(outproj_weight.shape), weight_decay, 0.3,
        ),
        gateup_next,
        down_next,
        adam_update(router_weight, router_first, router_second, router_grad, weight_decay, 0.05),
        adam_update(
            gains, gains_first, gains_second,
            jnp.stack([gain_first_grad, gain_second_grad]), 0.0, 0.4,
        ),
    )
    return (block_out, tokens_grad) + sum(updates, ())


def solution(mesh):
    row = P("dp", None)
    inproj = P("dp", "tensor", None)
    outproj = P("tensor", None, "dp")
    gateup = P(None, "dp", None, "tensor")
    down = P(None, "tensor", "dp")
    gain = P(None, "dp")
    weights = (inproj,) * 3 + (outproj,) * 3 + (gateup,) * 3 + (down,) * 3 + (row,) * 3 + (gain,) * 3
    return jax.shard_map(
        shards,
        mesh=mesh,
        in_specs=(row, row, row) + weights,
        out_specs=(row, row) + weights,
        check_vma=False,
    )
```

```python
import functools

import jax
import jax.numpy as jnp
from jax import lax
from jax.experimental import pallas as pl
from jax.experimental.pallas import tpu as pltpu
from jax.sharding import PartitionSpec as P

HEAD_DIM = 64
TOPK = 8
EXPERTS = 16
PROMPT_DEV = 128
CONT = 512
MICRO = 2
STEP = 10
GROUP = 3
TOK_MB = 640

eps_norm = 1e-05
beta_first = 0.9
beta_second = 0.95
adam_eps = 1e-08
weight_decay = 0.1
bf16 = jnp.bfloat16
f32 = jnp.float32
line_chunks = 20
line_lag = 2
MESH = pl.DeviceIdType.MESH


def angles_for(positions, head_size):
    half_dim = head_size // 2
    freqs = 10000.0 ** (-2.0 * jnp.arange(half_dim, dtype=f32) / head_size)
    angles = positions.astype(f32)[..., None] * freqs
    return (jnp.cos(angles), jnp.sin(angles))


def rotate(values, cosine, sine):
    half_dim = values.shape[-1] // 2
    first_half = values[..., :half_dim]
    second_half = values[..., half_dim:]
    return jnp.concatenate(
        [first_half * cosine - second_half * sine, second_half * cosine + first_half * sine],
        axis=-1,
    )


def adam_update(weight, moment_one, moment_two, gradient, decay_rate, learn_rate):
    first_next = beta_first * moment_one + (1.0 - beta_first) * gradient
    second_next = beta_second * moment_two + (1.0 - beta_second) * gradient * gradient
    corr_first = 1.0 - beta_first**STEP
    corr_second = 1.0 - beta_second**STEP
    update = first_next / corr_first / (jnp.sqrt(second_next / corr_second) + adam_eps)
    return (weight - learn_rate * (update + decay_rate * weight), first_next, second_next)


def line_sum_kernel(n, chunks, x_ref, o_ref, held, send_red, recv_red, send_out, recv_out):
    me = lax.axis_index("tensor")
    rows = x_ref.shape[0] // (2 * chunks)
    low, high = me - 1, me + 1

    barrier = pltpu.get_barrier_semaphore()

    @pl.when(me > 0)
    def _():
        pl.semaphore_signal(barrier, inc=1, device_id={"tensor": low}, device_id_type=MESH)

    @pl.when(me < n - 1)
    def _():
        pl.semaphore_signal(barrier, inc=1, device_id={"tensor": high}, device_id_type=MESH)

    pl.semaphore_wait(barrier, jnp.where((me > 0) & (me < n - 1), 2, 1))

    def part(half, c):
        return pl.ds(pl.multiple_of((half * chunks + c) * rows, 16), rows)

    def reduce_copy(half, c, src):
        to = low if half == 0 else high
        return pltpu.make_async_remote_copy(
            src_ref=src.at[part(half, c)],
            dst_ref=held.at[part(half, c)],
            send_sem=send_red.at[half, c],
            recv_sem=recv_red.at[half, c],
            device_id={"tensor": to},
            device_id_type=MESH,
        )

    def out_copy(half, c):
        to = high if half == 0 else low
        return pltpu.make_async_remote_copy(
            src_ref=o_ref.at[part(half, c)],
            dst_ref=o_ref.at[part(half, c)],
            send_sem=send_out.at[half, c],
            recv_sem=recv_out.at[half, c],
            device_id={"tensor": to},
            device_id_type=MESH,
        )

    def place(half):
        return n - 1 - me if half == 0 else me

    def step(t, carry):
        for half in (0, 1):
            at = place(half)
            c = t - line_lag * at

            @pl.when((c >= 0) & (c < chunks))
            def _():
                @pl.when(at == 0)
                def _():
                    reduce_copy(half, c, x_ref).start()

                @pl.when(at > 0)
                def _():
                    reduce_copy(half, c, held).wait_recv()
                    total = x_ref[part(half, c)].astype(f32) + held[part(half, c)].astype(f32)

                    @pl.when(at < n - 1)
                    def _():
                        held[part(half, c)] = total.astype(held.dtype)
                        reduce_copy(half, c, held).start()

                    @pl.when(at == n - 1)
                    def _():
                        o_ref[part(half, c)] = total.astype(o_ref.dtype)
                        out_copy(half, c).start()

        for half in (0, 1):
            at = place(half)
            c = t - line_lag * (2 * (n - 1) - at)

            @pl.when((at < n - 1) & (c >= 0) & (c < chunks))
            def _():
                out_copy(half, c).wait_recv()

                @pl.when(at > 0)
                def _():
                    out_copy(half, c).start()

        return carry

    lax.fori_loop(0, chunks + 2 * (n - 1) * line_lag, step, 0)

    def finish(c, carry):
        for half in (0, 1):
            at = place(half)

            @pl.when(at < n - 1)
            def _():
                reduce_copy(half, c, held).wait_send()

            @pl.when(at > 0)
            def _():
                out_copy(half, c).wait_send()

        return carry

    lax.fori_loop(0, chunks, finish, 0)


def line_sum(x, n, barrier_id):
    rows, width = x.shape
    chunks = line_chunks
    return pl.pallas_call(
        functools.partial(line_sum_kernel, n, chunks),
        out_shape=jax.ShapeDtypeStruct(x.shape, x.dtype),
        in_specs=[pl.BlockSpec(memory_space=pltpu.VMEM)],
        out_specs=pl.BlockSpec(memory_space=pltpu.VMEM),
        scratch_shapes=[pltpu.VMEM(x.shape, x.dtype)]
        + [pltpu.SemaphoreType.DMA((2, chunks)) for _ in range(4)],
        compiler_params=pltpu.CompilerParams(
            collective_id=barrier_id, has_side_effects=True, vmem_limit_bytes=24 * 2**20
        ),
        cost_estimate=pl.CostEstimate(
            flops=rows * width, bytes_accessed=100 * rows * width, transcendentals=0
        ),
    )(x)


def expert_kernel(group, rows_ref, outgrad_ref, gates_ref, gu_ref, down_ref,
                  active_ref, hidden_ref, gate_grad_ref):
    step = pl.program_id(0)
    tile = 256
    width = gu_ref.shape[1] // 2
    hidden = width // group
    lane = lax.broadcasted_iota(jnp.int32, (tile, 128), 1)
    column = lax.broadcasted_iota(jnp.int32, (tile, width), 1)

    @pl.when(step == 0)
    def _():
        gate_grad_ref[...] = jnp.zeros_like(gate_grad_ref)

    def one(t, carry):
        at = pl.ds(pl.multiple_of(t * tile, tile), tile)
        h = jnp.dot(rows_ref[at], gu_ref[...], preferred_element_type=f32)
        back = jnp.dot(outgrad_ref[at], down_ref[...], preferred_element_type=f32)
        gates = gates_ref[at]
        wide = jnp.zeros((tile, width), f32)
        for j in range(group):
            g = jnp.sum(jnp.where(lane == step * group + j, gates, 0.0), axis=1, keepdims=True)
            wide = g + wide if group == 1 else jnp.where(column // hidden == j, g, wide)
        gate, up = h[:, :width], h[:, width:]
        sig = 1.0 / (1.0 + jnp.exp(-gate))
        silu = gate * sig
        active = (silu * up).astype(bf16).astype(f32)
        active_ref[at] = (active * wide).astype(bf16)
        product = active * back
        grads = gate_grad_ref[at]
        for j in range(group):
            s = jnp.sum(jnp.where(column // hidden == j, product, 0.0), axis=1, keepdims=True)
            grads = jnp.where(lane == step * group + j, s, grads)
        gate_grad_ref[at] = grads
        back = back * wide
        hidden_ref[at, :width] = (back * up * sig * (1.0 + gate * (1.0 - sig))).astype(bf16)
        hidden_ref[at, width:] = (back * silu).astype(bf16)
        return carry

    lax.fori_loop(0, rows_ref.shape[0] // tile, one, 0)


def expert_call(rows, outgrad, gates, gu, down, group):
    tokens, model = rows.shape
    width = gu.shape[1] // (EXPERTS // group)
    steps = EXPERTS // group
    return pl.pallas_call(
        functools.partial(expert_kernel, group),
        grid=(steps,),
        in_specs=[
            pl.BlockSpec((tokens, model), lambda p: (0, 0)),
            pl.BlockSpec((tokens, model), lambda p: (0, 0)),
            pl.BlockSpec((tokens, 128), lambda p: (0, 0)),
            pl.BlockSpec((model, width), lambda p: (0, p)),
            pl.BlockSpec((model, width // 2), lambda p: (0, p)),
        ],
        out_specs=[
            pl.BlockSpec((tokens, width // 2), lambda p: (0, p)),
            pl.BlockSpec((tokens, width), lambda p: (0, p)),
            pl.BlockSpec((tokens, 128), lambda p: (0, 0)),
        ],
        out_shape=[
            jax.ShapeDtypeStruct((tokens, steps * width // 2), bf16),
            jax.ShapeDtypeStruct((tokens, steps * width), bf16),
            jax.ShapeDtypeStruct((tokens, 128), f32),
        ],
        compiler_params=pltpu.CompilerParams(vmem_limit_bytes=48 * 2**20),
        cost_estimate=pl.CostEstimate(
            flops=2 * tokens * model * steps * width * 3 // 2,
            bytes_accessed=2 * (model * steps * width * 3 // 2 + tokens * steps * width * 3 // 2),
            transcendentals=tokens * steps * width // 2,
        ),
    )(rows, outgrad, gates, gu, down)


def turn(u, cosine, sine):
    lane = lax.broadcasted_iota(jnp.int32, u.shape, 1) % HEAD_DIM
    other = jnp.where(lane < HEAD_DIM // 2, pltpu.roll(u, 96, 1), pltpu.roll(u, 32, 1))
    return u * cosine + other * sine


def project_kernel(x_ref, gain_ref, w_ref, cos_ref, sin_ref, normed_ref, q_ref, kv_ref):
    x = x_ref[...].astype(f32)
    inverse = lax.rsqrt(jnp.mean(x * x, axis=-1, keepdims=True) + eps_norm)
    normed = (x * inverse * gain_ref[0:1]).astype(bf16)
    normed_ref[...] = normed
    mixed = jnp.dot(normed, w_ref[...], preferred_element_type=f32)
    cosine, sine = cos_ref[...], sin_ref[...]
    turned = q_ref.shape[1] // 128
    for c in range(turned):
        q_ref[:, c * 128 : (c + 1) * 128] = turn(
            mixed[:, c * 128 : (c + 1) * 128], cosine, sine
        ).astype(bf16)
    start = turned * 128
    kv_ref[:, :128] = turn(mixed[:, start : start + 128], cosine, sine).astype(bf16)
    kv_ref[:, 128:] = mixed[:, start + 128 :].astype(bf16)


def project_call(tokens, gain, w, cosine, sine):
    count, model = tokens.shape
    tile = 256
    width = w.shape[1]
    row = lambda n: pl.BlockSpec((tile, n), lambda i: (i, 0))
    return pl.pallas_call(
        project_kernel,
        grid=(count // tile,),
        in_specs=[
            row(model),
            pl.BlockSpec((8, model), lambda i: (0, 0)),
            pl.BlockSpec((model, width), lambda i: (0, 0)),
            row(128),
            row(128),
        ],
        out_specs=[row(model), row(width - 256), row(256)],
        out_shape=[
            jax.ShapeDtypeStruct((count, model), bf16),
            jax.ShapeDtypeStruct((count, width - 256), bf16),
            jax.ShapeDtypeStruct((count, 256), bf16),
        ],
        compiler_params=pltpu.CompilerParams(vmem_limit_bytes=32 * 2**20),
        cost_estimate=pl.CostEstimate(
            flops=2 * count * model * width, bytes_accessed=6 * count * model, transcendentals=count
        ),
    )(tokens, gain, w, cosine, sine)


def head_places(heads):
    return [(h // GROUP, h % 2, h // 2) for h in range(heads)]


def spread(kv, scale):
    lane = lax.broadcasted_iota(jnp.int32, kv.shape, 1)
    kv = kv * scale
    turned = pltpu.roll(kv, HEAD_DIM, 1)
    first = lane < HEAD_DIM
    zero = jnp.zeros_like(kv)
    return {
        (0, 0): jnp.where(first, kv, zero).astype(bf16),
        (0, 1): jnp.where(first, zero, turned).astype(bf16),
        (1, 0): jnp.where(first, turned, zero).astype(bf16),
        (1, 1): jnp.where(first, zero, kv).astype(bf16),
    }


def row_tiles(prompt_total):
    tiles = [(0, PROMPT_DEV, prompt_total)]
    for start in range(0, CONT, 256):
        tiles.append((PROMPT_DEV + start, 256, prompt_total + start + 256))
    return tiles


nt = (((1,), (1,)), ((), ()))


def meet(me, n):
    barrier = pltpu.get_barrier_semaphore()

    def greet(k, carry):
        pl.semaphore_signal(
            barrier, inc=1, device_id={"dp": lax.rem(me + k, n)}, device_id_type=MESH
        )
        return carry

    lax.fori_loop(1, n, greet, 0)
    pl.semaphore_wait(barrier, n - 1)


def load_spread(m, all_ref, kv_ref, k_ref, v_ref, kt_ref=None):
    total = all_ref.shape[1]
    own = pl.ds(pl.multiple_of(m * TOK_MB + PROMPT_DEV, 16), CONT)
    for low, high, rows in ((0, total, all_ref[m]), (total, total + CONT, kv_ref[own])):
        keys = spread(rows[:, :128].astype(f32), HEAD_DIM**-0.5)
        values = spread(rows[:, 128:].astype(f32), 1.0)
        for i, place in enumerate(keys):
            k_ref[i, low:high] = keys[place]
            v_ref[i, low:high] = values[place]
            if kt_ref is not None:
                kt_ref[i, :, low:high] = keys[place].astype(f32).T.astype(bf16)
    return {place: i for i, place in enumerate(keys)}


def attention_kernel(heads, n, q_ref, kv_ref, o_ref, lse_ref, all_ref, k_ref, v_ref, send, recv):
    prompt_total = all_ref.shape[1]
    me = lax.axis_index("dp")

    def piece(m, k):
        rows = all_ref.at[m, pl.ds(pl.multiple_of(me * PROMPT_DEV, PROMPT_DEV), PROMPT_DEV)]
        return pltpu.make_async_remote_copy(
            src_ref=rows,
            dst_ref=rows,
            send_sem=send.at[m, k],
            recv_sem=recv.at[m, k],
            device_id={"dp": lax.rem(me + k, n)},
            device_id_type=MESH,
        )

    for m in range(MICRO):
        all_ref[m, pl.ds(pl.multiple_of(me * PROMPT_DEV, PROMPT_DEV), PROMPT_DEV)] = kv_ref[
            m * TOK_MB : m * TOK_MB + PROMPT_DEV
        ]
    meet(me, n)

    def every(m, act):
        def one(k, carry):
            act(piece(m, k))
            return carry

        lax.fori_loop(1, n, one, 0)

    for m in range(MICRO):
        every(m, lambda copy: copy.start())

    def micro(m, carry):
        every(m, lambda copy: copy.wait_recv())
        index = load_spread(m, all_ref, kv_ref, k_ref, v_ref)
        lane = lax.broadcasted_iota(jnp.int32, (1, 128), 1)
        for start, rows, length in row_tiles(prompt_total):
            at = pl.ds(pl.multiple_of(m * TOK_MB + start, 128), rows)
            row = lax.broadcasted_iota(jnp.int32, (rows, 1), 0)
            if start == 0:
                masked = 0
                reach = row + me * PROMPT_DEV
            else:
                masked = length - 256
                reach = row
            column = lax.broadcasted_iota(jnp.int32, (rows, length - masked), 1)
            lse = jnp.zeros((rows, 128), f32)
            pair_out = None
            for h, (kv, half, pair) in enumerate(head_places(heads)):
                q = q_ref[at, pair * 128 : (pair + 1) * 128]
                i = index[kv, half]
                tail = lax.dot_general(q, k_ref[i, masked:length], nt, preferred_element_type=f32)
                tail = jnp.where(column <= reach, tail, -1e30)
                top = jnp.max(tail, axis=1, keepdims=True)
                if masked:
                    head = lax.dot_general(q, k_ref[i, :masked], nt, preferred_element_type=f32)
                    top = jnp.maximum(top, jnp.max(head, axis=1, keepdims=True))
                    p_head = jnp.exp(head - top)
                p_tail = jnp.exp(tail - top)
                total = jnp.sum(p_tail, axis=1, keepdims=True)
                out = jnp.dot(
                    p_tail.astype(bf16), v_ref[i, masked:length], preferred_element_type=f32
                )
                if masked:
                    total = total + jnp.sum(p_head, axis=1, keepdims=True)
                    out = out + jnp.dot(
                        p_head.astype(bf16), v_ref[i, :masked], preferred_element_type=f32
                    )
                out = out / total
                lse = jnp.where(lane == h, top + jnp.log(total), lse)
                if half == 0:
                    pair_out = out
                else:
                    o_ref[at, pair * 128 : (pair + 1) * 128] = (pair_out + out).astype(bf16)
            lse_ref[at] = lse
        return carry

    lax.fori_loop(0, MICRO, micro, 0)
    for m in range(MICRO):
        every(m, lambda copy: copy.wait_send())


def attention_call(q, kv, n):
    count, width = q.shape
    keys = PROMPT_DEV * n + CONT
    heads = width // HEAD_DIM
    whole = pl.BlockSpec(memory_space=pltpu.VMEM)
    return pl.pallas_call(
        functools.partial(attention_kernel, heads, n),
        in_specs=[whole] * 2,
        out_specs=[whole] * 3,
        out_shape=[
            jax.ShapeDtypeStruct((count, width), bf16),
            jax.ShapeDtypeStruct((count, 128), f32),
            jax.ShapeDtypeStruct((MICRO, PROMPT_DEV * n, 256), bf16),
        ],
        scratch_shapes=[
            pltpu.VMEM((4, keys, 128), bf16),
            pltpu.VMEM((4, keys, 128), bf16),
            pltpu.SemaphoreType.DMA((MICRO, n)),
            pltpu.SemaphoreType.DMA((MICRO, n)),
        ],
        compiler_params=pltpu.CompilerParams(
            collective_id=3, has_side_effects=True, vmem_limit_bytes=48 * 2**20
        ),
        cost_estimate=pl.CostEstimate(
            flops=16 * count * keys * width,
            bytes_accessed=8 * count * width,
            transcendentals=count * keys * heads,
        ),
    )(q, kv)


def attention_back_kernel(
    heads, n, q_ref, kv_ref, all_ref, do_ref, o_ref, lse_ref,
    cos_ref, sin_ref, row_cos_ref, row_sin_ref,
    grad_ref, k_ref, v_ref, kt_ref, dk_ref, dv_ref, sent_ref, got_ref, send, recv,
):
    prompt_total = all_ref.shape[1]
    me = lax.axis_index("dp")
    width = heads * HEAD_DIM

    def piece(m, k):
        to = lax.rem(me + k, n)
        return pltpu.make_async_remote_copy(
            src_ref=sent_ref.at[m, pl.ds(pl.multiple_of(to * PROMPT_DEV, PROMPT_DEV), PROMPT_DEV)],
            dst_ref=got_ref.at[m, k],
            send_sem=send.at[m, k],
            recv_sem=recv.at[m, k],
            device_id={"dp": to},
            device_id_type=MESH,
        )

    def every(m, act):
        def one(k, carry):
            act(piece(m, k))
            return carry

        lax.fori_loop(1, n, one, 0)

    meet(me, n)
    half_rows = (
        lax.broadcasted_iota(jnp.int32, (8, 128), 1) // HEAD_DIM
        == lax.broadcasted_iota(jnp.int32, (8, 128), 0)
    ).astype(f32)

    def micro(m, carry):
        index = load_spread(m, all_ref, kv_ref, k_ref, v_ref, kt_ref)
        dk_ref[...] = jnp.zeros_like(dk_ref)
        dv_ref[...] = jnp.zeros_like(dv_ref)
        for start, rows, length in row_tiles(prompt_total):
            at = pl.ds(pl.multiple_of(m * TOK_MB + start, 128), rows)
            inner = slice(start, start + rows)
            column = lax.broadcasted_iota(jnp.int32, (1, rows), 1)
            if start == 0:
                masked = 0
                reach = column + me * PROMPT_DEV
            else:
                masked = length - 256
                reach = column
            key = lax.broadcasted_iota(jnp.int32, (length - masked, rows), 0)
            back = None
            for h, (kv, half, pair) in enumerate(head_places(heads)):
                lanes = slice(pair * 128, (pair + 1) * 128)
                i = index[kv, half]
                q, do = q_ref[at, lanes], do_ref[at, lanes]
                if half == 0:
                    delta_pair = lax.dot_general(
                        half_rows,
                        do.astype(f32) * o_ref[at, lanes].astype(f32),
                        nt,
                        precision=lax.Precision.HIGHEST,
                        preferred_element_type=f32,
                    )
                delta = delta_pair[half : half + 1]
                lse = lse_ref[m, h : h + 1, inner]
                for low, high in ((0, masked), (masked, length)):
                    if low == high:
                        continue
                    s = lax.dot_general(k_ref[i, low:high], q, nt, preferred_element_type=f32)
                    if low == masked:
                        s = jnp.where(key <= reach, s, -1e30)
                    p = jnp.exp(s - lse)
                    dp_ = lax.dot_general(v_ref[i, low:high], do, nt, preferred_element_type=f32)
                    ds = (p * (dp_ - delta)).astype(bf16)
                    dv_ref[i, low:high] += jnp.dot(
                        p.astype(bf16), do, preferred_element_type=f32
                    )
                    dk_ref[i, low:high] += jnp.dot(ds, q, preferred_element_type=f32)
                    term = jnp.dot(kt_ref[i, :, low:high], ds, preferred_element_type=f32)
                    back = term if back is None else back + term
                if half == 1:
                    grad_ref[at, lanes] = turn(
                        back.T, row_cos_ref[inner], -row_sin_ref[inner]
                    ).astype(bf16)
                    back = None
        lane = lax.broadcasted_iota(jnp.int32, (dk_ref.shape[1], 128), 1)

        def joined(acc):
            get = lambda place: acc[index[place]]
            return jnp.where(
                lane < HEAD_DIM,
                get((0, 0)) + pltpu.roll(get((0, 1)), HEAD_DIM, 1),
                get((1, 1)) + pltpu.roll(get((1, 0)), HEAD_DIM, 1),
            )

        dk = turn(joined(dk_ref) * HEAD_DIM**-0.5, cos_ref[...], -sin_ref[...]).astype(bf16)
        dv = joined(dv_ref).astype(bf16)
        sent_ref[m, :, :128] = dk[:prompt_total]
        sent_ref[m, :, 128:] = dv[:prompt_total]
        every(m, lambda copy: copy.start())
        own = pl.ds(pl.multiple_of(m * TOK_MB + PROMPT_DEV, 128), CONT)
        grad_ref[own, width : width + 128] = dk[prompt_total:]
        grad_ref[own, width + 128 :] = dv[prompt_total:]
        return carry

    lax.fori_loop(0, MICRO, micro, 0)

    def collect(m, carry):
        every(m, lambda copy: copy.wait_recv())
        own = sent_ref[m, pl.ds(pl.multiple_of(me * PROMPT_DEV, PROMPT_DEV), PROMPT_DEV)]
        total = lax.fori_loop(
            1, n, lambda k, t: t + got_ref[m, k].astype(f32), own.astype(f32)
        )
        at = pl.ds(pl.multiple_of(m * TOK_MB, 128), PROMPT_DEV)
        grad_ref[at, width:] = total.astype(bf16)
        every(m, lambda copy: copy.wait_send())
        return carry

    lax.fori_loop(0, MICRO, collect, 0)


def attention_back_call(q, kv, prompts, do, o, lse, cosine, sine, row_cos, row_sin, n):
    count, width = q.shape
    keys = prompts.shape[1] + CONT
    heads = width // HEAD_DIM
    whole = pl.BlockSpec(memory_space=pltpu.VMEM)
    return pl.pallas_call(
        functools.partial(attention_back_kernel, heads, n),
        in_specs=[whole] * 10,
        out_specs=whole,
        out_shape=jax.ShapeDtypeStruct((count, width + 256), bf16),
        scratch_shapes=[
            pltpu.VMEM((4, keys, 128), bf16),
            pltpu.VMEM((4, keys, 128), bf16),
            pltpu.VMEM((4, 128, keys), bf16),
            pltpu.VMEM((4, keys, 128), f32),
            pltpu.VMEM((4, keys, 128), f32),
            pltpu.VMEM((MICRO, prompts.shape[1], 256), bf16),
            pltpu.VMEM((MICRO, n, PROMPT_DEV, 256), bf16),
            pltpu.SemaphoreType.DMA((MICRO, n)),
            pltpu.SemaphoreType.DMA((MICRO, n)),
        ],
        compiler_params=pltpu.CompilerParams(
            collective_id=4, has_side_effects=True, vmem_limit_bytes=56 * 2**20
        ),
        cost_estimate=pl.CostEstimate(
            flops=40 * count * keys * width,
            bytes_accessed=12 * count * width,
            transcendentals=count * keys * heads,
        ),
    )(q, kv, prompts, do, o, lse, cosine, sine, row_cos, row_sin)


def attend(queries, keys_all, values_all, allowed):
    factor = HEAD_DIM ** (-0.5)
    scores = jnp.einsum("tkgd,skd->kgts", queries, keys_all, preferred_element_type=f32) * factor
    scores = jnp.where(allowed, scores, -1e30)
    row_max = jnp.max(scores, axis=-1, keepdims=True)
    exponent = jnp.exp(scores - row_max)
    softened = exponent / jnp.sum(exponent, axis=-1, keepdims=True)
    soft_low = softened.astype(bf16)
    attended = jnp.einsum("kgts,skd->tkgd", soft_low, values_all, preferred_element_type=f32)
    return attended.astype(bf16), softened, soft_low


def attend_back(queries, keys_all, values_all, softened, soft_low, attended_grad):
    factor = HEAD_DIM ** (-0.5)
    soft_grad = jnp.einsum("tkgd,skd->kgts", attended_grad, values_all, preferred_element_type=f32)
    values_grad = jnp.einsum("kgts,tkgd->skd", soft_low, attended_grad, preferred_element_type=f32)
    row_delta = jnp.sum(softened * soft_grad, axis=-1, keepdims=True)
    scores_grad = (softened * (soft_grad - row_delta)).astype(bf16)
    queries_grad = (
        jnp.einsum("kgts,skd->tkgd", scores_grad, keys_all, preferred_element_type=f32) * factor
    )
    keys_grad = (
        jnp.einsum("kgts,tkgd->skd", scores_grad, queries, preferred_element_type=f32) * factor
    )
    return queries_grad, keys_grad, values_grad


def shards(
    tokens, cotangent, routes,
    inproj_weight, inproj_first, inproj_second,
    outproj_weight, outproj_first, outproj_second,
    gateup_weight, gateup_first, gateup_second,
    down_weight, down_first, down_second,
    router_weight, router_first, router_second,
    gains, gains_first, gains_second,
):
    n_dp = lax.axis_size("dp")
    n_tensor = lax.axis_size("tensor")
    depth = inproj_weight.shape[0]
    kv_local = inproj_weight.shape[1]
    hidden = down_weight.shape[1]
    group = max(1, 256 // hidden)
    groups = EXPERTS // group
    in_width = inproj_weight.shape[1] * inproj_weight.shape[2]
    out_width = outproj_weight.shape[0] * outproj_weight.shape[1]
    prompt_total = PROMPT_DEV * n_dp
    count = tokens.shape[0]

    def gateup_flat(w):
        w = w.reshape(groups, group, depth, 2, hidden)
        return w.transpose(2, 0, 3, 1, 4).reshape(depth, 2 * EXPERTS * hidden)

    def gateup_back(w):
        w = w.reshape(depth, groups, 2, group, hidden)
        return w.transpose(1, 3, 0, 2, 4).reshape(EXPERTS, depth, 2, hidden)

    query_width = GROUP * HEAD_DIM

    def inproj_flat(w):
        w = w.reshape(depth, kv_local, query_width + 2 * HEAD_DIM)
        parts = (w[:, :, :query_width], w[:, :, query_width:-HEAD_DIM], w[:, :, -HEAD_DIM:])
        return jnp.concatenate([p.reshape(depth, -1) for p in parts], axis=1)

    def inproj_back(w):
        q, k, v = jnp.split(w, [kv_local * query_width, kv_local * (query_width + HEAD_DIM)], axis=1)
        return jnp.concatenate([p.reshape(depth, kv_local, -1) for p in (q, k, v)], axis=2)

    gains_high = gains.astype(bf16)
    gains_low = (gains - gains_high.astype(f32)).astype(bf16)
    attn_local = jnp.concatenate(
        [
            inproj_flat(inproj_weight.astype(bf16)),
            outproj_weight.reshape(out_width, depth).T.astype(bf16),
            jnp.concatenate(
                [
                    router_weight.astype(bf16),
                    gains_high.T,
                    gains_low.T,
                    jnp.zeros((depth, 128 - EXPERTS - 4), bf16),
                ],
                axis=1,
            ),
        ],
        axis=1,
    )
    attn_full = lax.all_gather(attn_local, "dp", axis=0, tiled=True)
    gu_full = lax.all_gather(gateup_flat(gateup_weight.astype(bf16)), "dp", axis=0, tiled=True)
    down_full = lax.all_gather(
        down_weight.reshape(EXPERTS * hidden, depth).T.astype(bf16), "dp", axis=0, tiled=True
    )
    inproj_full = attn_full[:, :in_width]
    outproj_full = attn_full[:, in_width : in_width + out_width]
    small_full = attn_full[:, in_width + out_width :]
    router_full = small_full[:, :EXPERTS]
    small_t = small_full[:, EXPERTS : EXPERTS + 4].astype(f32).T
    gain_first = small_t[0:1] + small_t[2:3]
    gain_second = small_t[1:2] + small_t[3:4]

    device_index = lax.axis_index("dp")
    inputs = tokens.astype(f32)
    inverse_first = lax.rsqrt(jnp.mean(inputs * inputs, axis=-1, keepdims=True) + eps_norm)
    norm_first = inputs * inverse_first
    cosine, sine = angles_for(jnp.arange(prompt_total + CONT), HEAD_DIM)

    def of_rows(table):
        own = lax.dynamic_slice_in_dim(table, device_index * PROMPT_DEV, PROMPT_DEV, 0)
        return jnp.concatenate([own, table[prompt_total:]], axis=0)

    in_kernels = kv_local * HEAD_DIM == 128
    queries_width = kv_local * query_width
    both_width = kv_local * 2 * HEAD_DIM
    if in_kernels:
        cos_all = jnp.concatenate([cosine] * 4, axis=1)
        sin_all = jnp.concatenate([-sine, sine] * 2, axis=1)
        cos_row, sin_row = of_rows(cos_all), of_rows(sin_all)
        normed_first, queries, both = project_call(
            tokens,
            jnp.pad(gain_first, ((0, 7), (0, 0))),
            inproj_full,
            jnp.concatenate([cos_row] * MICRO, axis=0),
            jnp.concatenate([sin_row] * MICRO, axis=0),
        )
    else:
        cosine, sine = (jnp.tile(of_rows(t), (MICRO, 1))[:, None, :] for t in (cosine, sine))
        normed_first = (norm_first * gain_first).astype(bf16)
        mixed = jnp.dot(normed_first, inproj_full, preferred_element_type=f32)
        queries = rotate(
            mixed[:, :queries_width].reshape(count, -1, HEAD_DIM), cosine, sine
        ).astype(bf16)
        keys = rotate(
            mixed[:, queries_width : queries_width + kv_local * HEAD_DIM].reshape(
                count, -1, HEAD_DIM
            ),
            cosine,
            sine,
        )
        both = jnp.concatenate(
            [keys.reshape(count, -1), mixed[:, queries_width + kv_local * HEAD_DIM :]], axis=1
        ).astype(bf16)
    if in_kernels:
        attended, lse, prompt_both = attention_call(queries, both, n_dp)
    else:
        both = both.reshape(MICRO, TOK_MB, both_width)
        prompt_both = lax.all_gather(both[:, :PROMPT_DEV], "dp", axis=1, tiled=True)
        both_all = jnp.concatenate([prompt_both, both[:, PROMPT_DEV:]], axis=1)
        inner = jnp.arange(TOK_MB, dtype=jnp.int32)
        positions = jnp.where(
            inner < PROMPT_DEV, device_index * PROMPT_DEV + inner, prompt_total + inner - PROMPT_DEV
        )
        key_index = jnp.arange(prompt_total + CONT, dtype=jnp.int32)
        allowed = (key_index[None, :] <= positions[:, None]) & (
            (key_index[None, :] < prompt_total) | (inner[:, None] >= PROMPT_DEV)
        )
        kept = []
        attended = []
        for m in range(MICRO):
            q = queries[m * TOK_MB : (m + 1) * TOK_MB].reshape(TOK_MB, kv_local, GROUP, HEAD_DIM)
            k, v = (
                t.reshape(-1, kv_local, HEAD_DIM) for t in jnp.split(both_all[m], 2, axis=1)
            )
            out, softened, soft_low = attend(q, k, v, allowed)
            attended.append(out.reshape(TOK_MB, -1))
            kept.append((q, k, v, softened, soft_low))
        attended = jnp.concatenate(attended, axis=0)
    branch = lax.dot_general(
        attended, outproj_full, (((1,), (1,)), ((), ())), preferred_element_type=f32
    ).astype(bf16)
    branch = line_sum(branch, n_tensor, 1)

    middle = inputs + branch.astype(f32)
    inverse_second = lax.rsqrt(jnp.mean(middle * middle, axis=-1, keepdims=True) + eps_norm)
    norm_second = middle * inverse_second
    normed_second = (norm_second * gain_second).astype(bf16)
    logits = jnp.dot(normed_second, router_full, preferred_element_type=f32)
    named = jnp.any(routes[:, :, None] == jnp.arange(EXPERTS, dtype=jnp.int32), axis=1)
    top = jnp.max(jnp.where(named, logits, -jnp.inf), axis=-1, keepdims=True)
    weights = jnp.where(named, jnp.exp(jnp.where(named, logits, top) - top), 0.0)
    gates = weights / jnp.sum(weights, axis=-1, keepdims=True)
    gates_wide = jnp.pad(gates, ((0, 0), (0, 128 - EXPERTS)))
    active, hidden_grad, gate_grad = expert_call(
        normed_second, cotangent, gates_wide, gu_full, down_full, group
    )
    contract_last = (((1,), (1,)), ((), ()))
    contract_first = (((0,), (0,)), ((), ()))
    down_grad = lax.dot_general(
        cotangent, active, contract_first, preferred_element_type=f32
    ).astype(bf16)
    gateup_grad = lax.dot_general(
        normed_second, hidden_grad, contract_first, preferred_element_type=f32
    ).astype(bf16)
    hidden_grad, down_grad, gateup_grad = lax.optimization_barrier(
        (hidden_grad, down_grad, gateup_grad)
    )
    down_grad = lax.psum_scatter(down_grad, "dp", scatter_dimension=0, tiled=True)
    gateup_grad = lax.psum_scatter(gateup_grad, "dp", scatter_dimension=0, tiled=True)
    rows_grad = lax.dot_general(
        hidden_grad, gu_full, contract_last, preferred_element_type=f32
    ).astype(bf16)
    mixture = lax.dot_general(active, down_full, contract_last, preferred_element_type=f32).astype(
        bf16
    )
    summed = line_sum(jnp.concatenate([rows_grad, gate_grad.astype(bf16)], axis=1), n_tensor, 2)
    model = tokens.shape[1]
    gate_grad = summed[:, model : model + EXPERTS].astype(f32)
    outgrad = cotangent.astype(f32)
    chosen_grad = gates * (gate_grad - jnp.sum(gates * gate_grad, axis=-1, keepdims=True))
    logits_grad = chosen_grad.astype(bf16)
    router_grad = lax.dot_general(
        normed_second, logits_grad, contract_first, preferred_element_type=f32
    ).astype(bf16)
    normed_second_grad = summed[:, :model].astype(f32) + lax.dot_general(
        logits_grad, router_full, contract_last, preferred_element_type=f32
    )
    norm_second_grad = normed_second_grad * gain_second
    gain_second_grad = jnp.sum(normed_second_grad * norm_second, axis=0)
    middle_grad = outgrad + inverse_second * (
        norm_second_grad
        - norm_second * jnp.mean(norm_second_grad * norm_second, axis=-1, keepdims=True)
    )

    branch_own = middle_grad.astype(bf16)
    outproj_grad = lax.dot_general(
        branch_own, attended, contract_first, preferred_element_type=f32
    ).astype(bf16)
    attended_grad = jnp.dot(branch_own, outproj_full, preferred_element_type=f32).astype(bf16)
    attended_grad, down_grad, gateup_grad, mixture = lax.optimization_barrier(
        (attended_grad, down_grad, gateup_grad, mixture)
    )
    mixture = lax.psum(mixture, "tensor")
    block_out = (middle + mixture.astype(f32)).astype(bf16)
    if in_kernels:
        lse_rows = lse[:, :8].reshape(MICRO, TOK_MB, 8).transpose(0, 2, 1)
        mixed_grad = attention_back_call(
            queries, both, prompt_both, attended_grad, attended, lse_rows,
            cos_all, sin_all, cos_row, sin_row, n_dp,
        )
    else:
        queries_grad, both_grad = [], []
        for m in range(MICRO):
            q, k, v, softened, soft_low = kept[m]
            dout = attended_grad[m * TOK_MB : (m + 1) * TOK_MB].reshape(q.shape)
            dq, dk, dv = attend_back(q, k, v, softened, soft_low, dout)
            queries_grad.append(dq.reshape(TOK_MB, -1, HEAD_DIM))
            both_grad.append(jnp.concatenate([t.reshape(-1, both_width // 2) for t in (dk, dv)], 1))
        queries_grad = rotate(jnp.concatenate(queries_grad, axis=0), cosine, -sine)
        both_grad = jnp.stack(both_grad)
        prompt_grad = lax.psum_scatter(
            both_grad[:, :prompt_total].astype(bf16), "dp", scatter_dimension=1, tiled=True
        )
        both_grad = jnp.concatenate(
            [prompt_grad.astype(f32), both_grad[:, prompt_total:]], axis=1
        ).reshape(count, both_width)
        keys_grad = rotate(
            both_grad[:, : both_width // 2].reshape(count, -1, HEAD_DIM), cosine, -sine
        )
        mixed_grad = jnp.concatenate(
            [
                queries_grad.reshape(count, -1),
                keys_grad.reshape(count, -1),
                both_grad[:, both_width // 2 :],
            ],
            axis=1,
        ).astype(bf16)
    normed_first_grad = lax.dot_general(
        mixed_grad, inproj_full, contract_last, preferred_element_type=f32
    ).astype(bf16)
    inproj_grad = lax.dot_general(
        normed_first, mixed_grad, contract_first, preferred_element_type=f32
    ).astype(bf16)
    attn_grad = jnp.concatenate(
        [
            inproj_grad,
            outproj_grad,
            router_grad,
            gain_second_grad[:, None].astype(bf16),
            jnp.zeros((model, 127 - EXPERTS), bf16),
        ],
        axis=1,
    )
    down_next = adam_update(
        down_weight, down_first, down_second,
        down_grad.T.reshape(down_weight.shape).astype(f32), weight_decay, 0.05,
    )
    gateup_next = adam_update(
        gateup_weight, gateup_first, gateup_second,
        gateup_back(gateup_grad).astype(f32), weight_decay, 0.05,
    )
    normed_first_grad, attn_grad, down_next, gateup_next = lax.optimization_barrier(
        (normed_first_grad, attn_grad, down_next, gateup_next)
    )
    attn_grad = lax.psum_scatter(attn_grad, "dp", scatter_dimension=0, tiled=True).astype(f32)
    normed_first_grad = line_sum(normed_first_grad, n_tensor, 1).astype(f32)
    norm_first_grad = normed_first_grad * gain_first
    gain_first_grad = jnp.sum(normed_first_grad * norm_first, axis=0)
    tokens_grad = middle_grad + inverse_first * (
        norm_first_grad
        - norm_first * jnp.mean(norm_first_grad * norm_first, axis=-1, keepdims=True)
    )

    gain_first_parts = lax.all_gather(gain_first_grad, "dp")
    gain_first_grad = lax.dynamic_slice_in_dim(
        jnp.sum(gain_first_parts, axis=0), device_index * depth, depth, 0
    )
    split = (in_width, in_width + out_width, in_width + out_width + EXPERTS)
    inproj_grad, outproj_grad, router_grad, gain_second_grad = (
        attn_grad[:, : split[0]],
        attn_grad[:, split[0] : split[1]],
        attn_grad[:, split[1] : split[2]],
        attn_grad[:, split[2]],
    )
    updates = (
        adam_update(
            inproj_weight, inproj_first, inproj_second, inproj_back(inproj_grad), weight_decay, 0.05
        ),
        adam_update(
            outproj_weight, outproj_first, outproj_second,
            outproj_grad.T.reshape(outproj_weight.shape), weight_decay, 0.3,
        ),
        gateup_next,
        down_next,
        adam_update(router_weight, router_first, router_second, router_grad, weight_decay, 0.05),
        adam_update(
            gains, gains_first, gains_second,
            jnp.stack([gain_first_grad, gain_second_grad]), 0.0, 0.4,
        ),
    )
    return (block_out, tokens_grad) + sum(updates, ())


def solution(mesh):
    row = P("dp", None)
    inproj = P("dp", "tensor", None)
    outproj = P("tensor", None, "dp")
    gateup = P(None, "dp", None, "tensor")
    down = P(None, "tensor", "dp")
    gain = P(None, "dp")
    weights = (inproj,) * 3 + (outproj,) * 3 + (gateup,) * 3 + (down,) * 3 + (row,) * 3 + (gain,) * 3
    return jax.shard_map(
        shards,
        mesh=mesh,
        in_specs=(row, row, row) + weights,
        out_specs=(row, row) + weights,
        check_vma=False,
    )
```

```python
import functools

import jax
import jax.numpy as jnp
from jax import lax
from jax.experimental import pallas as pl
from jax.experimental.pallas import tpu as pltpu
from jax.sharding import PartitionSpec as P

HEAD_DIM = 64
TOPK = 8
EXPERTS = 16
PROMPT_DEV = 128
CONT = 512
MICRO = 2
STEP = 10
GROUP = 3
TOK_MB = 640

eps_norm = 1e-05
beta_first = 0.9
beta_second = 0.95
adam_eps = 1e-08
weight_decay = 0.1
bf16 = jnp.bfloat16
f32 = jnp.float32
line_parts = 20
line_lag = 2
MESH = pl.DeviceIdType.MESH
nt = (((1,), (1,)), ((), ()))


def angles_for(positions, head_size):
    half_dim = head_size // 2
    freqs = 10000.0 ** (-2.0 * jnp.arange(half_dim, dtype=f32) / head_size)
    angles = positions.astype(f32)[..., None] * freqs
    return (jnp.cos(angles), jnp.sin(angles))


def rotate(values, cosine, sine):
    half_dim = values.shape[-1] // 2
    first_half = values[..., :half_dim]
    second_half = values[..., half_dim:]
    return jnp.concatenate(
        [first_half * cosine - second_half * sine, second_half * cosine + first_half * sine],
        axis=-1,
    )


def adam_update(weight, moment_one, moment_two, gradient, decay_rate, learn_rate):
    first_next = beta_first * moment_one + (1.0 - beta_first) * gradient
    second_next = beta_second * moment_two + (1.0 - beta_second) * gradient * gradient
    corr_first = 1.0 - beta_first**STEP
    corr_second = 1.0 - beta_second**STEP
    update = first_next / corr_first / (jnp.sqrt(second_next / corr_second) + adam_eps)
    return (weight - learn_rate * (update + decay_rate * weight), first_next, second_next)


def line_steps(n):
    return line_parts + 2 * (n - 1) * line_lag


def line_engine(
    n, x_ref, o_ref, held, send_red, recv_red, send_out, recv_out, complete=lambda at: None
):
    me = lax.axis_index("tensor")
    parts = line_parts
    rows = x_ref.shape[0] // (2 * parts)
    low, high = me - 1, me + 1

    def greet():
        barrier = pltpu.get_barrier_semaphore()

        @pl.when(me > 0)
        def _():
            pl.semaphore_signal(barrier, inc=1, device_id={"tensor": low}, device_id_type=MESH)

        @pl.when(me < n - 1)
        def _():
            pl.semaphore_signal(barrier, inc=1, device_id={"tensor": high}, device_id_type=MESH)

        return jnp.where((me > 0) & (me < n - 1), 2, 1)

    def begin():
        pl.semaphore_wait(pltpu.get_barrier_semaphore(), greet())

    def part(half, c):
        return pl.ds(pl.multiple_of((half * parts + c) * rows, 16), rows)

    def reduce_copy(half, c, src):
        to = low if half == 0 else high
        return pltpu.make_async_remote_copy(
            src_ref=src.at[part(half, c)],
            dst_ref=held.at[part(half, c)],
            send_sem=send_red.at[half, c],
            recv_sem=recv_red.at[half, c],
            device_id={"tensor": to},
            device_id_type=MESH,
        )

    def out_copy(half, c):
        to = high if half == 0 else low
        return pltpu.make_async_remote_copy(
            src_ref=o_ref.at[part(half, c)],
            dst_ref=o_ref.at[part(half, c)],
            send_sem=send_out.at[half, c],
            recv_sem=recv_out.at[half, c],
            device_id={"tensor": to},
            device_id_type=MESH,
        )

    def place(half):
        return n - 1 - me if half == 0 else me

    def slot(t):
        for half in (0, 1):
            at = place(half)
            c = t - line_lag * at

            @pl.when((c >= 0) & (c < parts))
            def _():
                @pl.when(at == 0)
                def _():
                    reduce_copy(half, c, x_ref).start()

                @pl.when(at > 0)
                def _():
                    reduce_copy(half, c, held).wait_recv()
                    total = x_ref[part(half, c)].astype(f32) + held[part(half, c)].astype(f32)

                    @pl.when(at < n - 1)
                    def _():
                        held[part(half, c)] = total.astype(held.dtype)
                        reduce_copy(half, c, held).start()

                    @pl.when(at == n - 1)
                    def _():
                        o_ref[part(half, c)] = total.astype(o_ref.dtype)
                        out_copy(half, c).start()
                        complete(part(half, c))

        for half in (0, 1):
            at = place(half)
            c = t - line_lag * (2 * (n - 1) - at)

            @pl.when((at < n - 1) & (c >= 0) & (c < parts))
            def _():
                out_copy(half, c).wait_recv()

                @pl.when(at > 0)
                def _():
                    out_copy(half, c).start()

                complete(part(half, c))

    def finish():
        def one(c, carry):
            for half in (0, 1):
                at = place(half)

                @pl.when(at < n - 1)
                def _():
                    reduce_copy(half, c, held).wait_send()

                @pl.when(at > 0)
                def _():
                    out_copy(half, c).wait_send()

            return carry

        lax.fori_loop(0, parts, one, 0)

    return greet, begin, slot, finish


def line_scratch(shape, dtype):
    return [pltpu.VMEM(shape, dtype)] + [
        pltpu.SemaphoreType.DMA((2, line_parts)) for _ in range(4)
    ]


def line_sum_kernel(n, x_ref, o_ref, *scratch):
    _, begin, slot, finish = line_engine(n, x_ref, o_ref, *scratch)
    begin()

    def step(t, carry):
        slot(t)
        return carry

    lax.fori_loop(0, line_steps(n), step, 0)
    finish()


def line_sum(x, n, barrier_id):
    rows, width = x.shape
    return pl.pallas_call(
        functools.partial(line_sum_kernel, n),
        out_shape=jax.ShapeDtypeStruct(x.shape, x.dtype),
        in_specs=[pl.BlockSpec(memory_space=pltpu.VMEM)],
        out_specs=pl.BlockSpec(memory_space=pltpu.VMEM),
        scratch_shapes=line_scratch(x.shape, x.dtype),
        compiler_params=pltpu.CompilerParams(
            collective_id=barrier_id, has_side_effects=True, vmem_limit_bytes=24 * 2**20
        ),
        cost_estimate=pl.CostEstimate(
            flops=rows * width, bytes_accessed=100 * rows * width, transcendentals=0
        ),
    )(x)


gather_parts = 3


def gather_engine(n, pairs, own_sem, far_send, far_recv, near_send, near_recv):
    me = lax.axis_index("dp")
    core, chip, chips = lax.rem(me, 2), me // 2, n // 2

    def rows(a, p):
        size = pairs[a][0].shape[0] // gather_parts
        return pl.ds(p * size, size)

    def far(a, p, k):
        x_ref, out_ref = pairs[a]
        return pltpu.make_async_remote_copy(
            src_ref=x_ref.at[rows(a, p)],
            dst_ref=out_ref.at[me, rows(a, p)],
            send_sem=far_send.at[a, p, k],
            recv_sem=far_recv.at[a, p, k],
            device_id={"dp": lax.rem(chip + k, chips) * 2 + core},
            device_id_type=MESH,
        )

    def near(a, p, k):
        x_ref, out_ref = pairs[a]
        owner = lax.rem(chip + chips - k, chips) * 2 + core
        target = out_ref.at[owner, rows(a, p)]
        return pltpu.make_async_remote_copy(
            src_ref=x_ref.at[rows(a, p)] if k == 0 else target,
            dst_ref=target,
            send_sem=near_send.at[a, p, k],
            recv_sem=near_recv.at[a, p, k],
            device_id={"dp": me + 1 - 2 * core},
            device_id_type=MESH,
        )

    def own(a):
        x_ref, out_ref = pairs[a]
        return pltpu.make_async_copy(x_ref, out_ref.at[me], own_sem.at[a])

    arrays = range(len(pairs))

    def greet():
        barrier = pltpu.get_barrier_semaphore()
        for k in range(1, chips):
            pl.semaphore_signal(
                barrier,
                inc=1,
                device_id={"dp": lax.rem(chip + k, chips) * 2 + core},
                device_id_type=MESH,
            )
        pl.semaphore_signal(
            barrier, inc=1, device_id={"dp": me + 1 - 2 * core}, device_id_type=MESH
        )
        return chips

    def start():
        for p in range(gather_parts):
            for a in arrays:
                for k in range(1, chips):
                    far(a, p, k).start()
        for p in range(gather_parts):
            for a in arrays:
                near(a, p, 0).start()
        for a in arrays:
            own(a).start()

    def forward(p):
        for a in arrays:
            for k in range(1, chips):
                far(a, p, k).wait_recv()
                near(a, p, k).start()

    def finish():
        for a in arrays:
            own(a).wait()
            for p in range(gather_parts):
                for k in range(chips):
                    near(a, p, k).wait_recv()
                    near(a, p, k).wait_send()
                    if k:
                        far(a, p, k).wait_send()

    return greet, start, forward, finish


def gather_scratch(arrays, n):
    return [pltpu.SemaphoreType.DMA((arrays,))] + [
        pltpu.SemaphoreType.DMA((arrays, gather_parts, n // 2)) for _ in range(4)
    ]


def gather_kernel(n, x_ref, out_ref, *scratch):
    greet, start, forward, finish = gather_engine(n, [(x_ref, out_ref)], *scratch)
    pl.semaphore_wait(pltpu.get_barrier_semaphore(), greet())
    start()
    for p in range(gather_parts):
        forward(p)
    finish()


def gather(x, n, barrier_id):
    depth, width = x.shape
    out = pl.pallas_call(
        functools.partial(gather_kernel, n),
        out_shape=jax.ShapeDtypeStruct((n, depth, width), x.dtype),
        in_specs=[pl.BlockSpec(memory_space=pltpu.VMEM)],
        out_specs=pl.BlockSpec(memory_space=pltpu.VMEM),
        scratch_shapes=gather_scratch(1, n),
        compiler_params=pltpu.CompilerParams(
            collective_id=barrier_id, has_side_effects=True, vmem_limit_bytes=16 * 2**20
        ),
    )(x)
    return out.reshape(n * depth, width)


def line_gather_kernel(n, n_dp, x_ref, a_ref, b_ref, o_ref, a_out, b_out, *scratch):
    line, spread_out = scratch[:5], scratch[5:]
    greet, _, slot, finish = line_engine(n, x_ref, o_ref, *line)
    greet_dp, start, forward, finish_dp = gather_engine(
        n_dp, [(a_ref, a_out), (b_ref, b_out)], *spread_out
    )
    peers = greet() + greet_dp()
    pl.semaphore_wait(pltpu.get_barrier_semaphore(), peers)
    start()

    def step(t, carry):
        slot(t)
        return carry

    total = line_steps(n)
    done = 0
    for p in range(gather_parts):
        until = total * (p + 1) // gather_parts
        lax.fori_loop(done, until, step, 0)
        done = until
        forward(p)
    finish()
    finish_dp()


def line_gather(x, a, b, n, n_dp, barrier_id):
    rows, width = x.shape
    whole, anywhere = pl.BlockSpec(memory_space=pltpu.VMEM), pl.BlockSpec(memory_space=pl.ANY)
    o, a_all, b_all = pl.pallas_call(
        functools.partial(line_gather_kernel, n, n_dp),
        out_shape=[jax.ShapeDtypeStruct(x.shape, x.dtype)]
        + [jax.ShapeDtypeStruct((n_dp,) + t.shape, t.dtype) for t in (a, b)],
        in_specs=[whole, anywhere, anywhere],
        out_specs=[whole, anywhere, anywhere],
        scratch_shapes=line_scratch(x.shape, x.dtype) + gather_scratch(2, n_dp),
        compiler_params=pltpu.CompilerParams(
            collective_id=barrier_id, has_side_effects=True, vmem_limit_bytes=24 * 2**20
        ),
        cost_estimate=pl.CostEstimate(
            flops=rows * width, bytes_accessed=100 * rows * width, transcendentals=0
        ),
    )(x, a, b)
    return o, a_all.reshape(-1, a.shape[1]), b_all.reshape(-1, b.shape[1])


def last_kernel(
    n, n_dp, x_ref, tokens_ref, middle_ref, gain_ref, weights_ref, gain_second_ref,
    grad_ref, weights_out, gains_out, o_ref, held, send_red, recv_red, send_out, recv_out,
    tokens_v, middle_v, grad_v, in_sem, out_sem, got, w_send, w_recv,
    g_from, g_got, g_send, g_recv, z_from, z_got, z_send, z_recv, acc,
):
    me, line = lax.axis_index("dp"), lax.axis_index("tensor")
    model = x_ref.shape[1]
    rows = x_ref.shape[0] // (2 * line_parts)
    depth = weights_out.shape[0]

    def norm_of(at):
        x = tokens_v[at].astype(f32)
        inverse = lax.rsqrt(jnp.mean(x * x, axis=-1, keepdims=True) + eps_norm)
        return x * inverse, inverse

    def complete(at):
        norm, inverse = norm_of(at)
        grad = o_ref[at].astype(f32) * gain_ref[0:1]
        mean = jnp.mean(grad * norm, axis=-1, keepdims=True)
        grad_v[at] = middle_v[at] + inverse * (grad - norm * mean)

    _, _, slot, finish = line_engine(
        n, x_ref, o_ref, held, send_red, recv_red, send_out, recv_out, complete
    )

    def weights_copy(k):
        to = lax.rem(me + k, n_dp)
        return pltpu.make_async_remote_copy(
            src_ref=weights_ref.at[to], dst_ref=got.at[k],
            send_sem=w_send.at[k], recv_sem=w_recv.at[k],
            device_id={"dp": to}, device_id_type=MESH,
        )

    def gains_copy(k):
        to = lax.rem(me + k, n_dp)
        return pltpu.make_async_remote_copy(
            src_ref=g_from.at[to], dst_ref=g_got.at[k],
            send_sem=g_send.at[k], recv_sem=g_recv.at[k],
            device_id={"dp": to}, device_id_type=MESH,
        )

    def line_copy(k):
        to = lax.rem(line + k, n)
        return pltpu.make_async_remote_copy(
            src_ref=z_from, dst_ref=z_got.at[k],
            send_sem=z_send.at[k], recv_sem=z_recv.at[k],
            device_id={"tensor": to}, device_id_type=MESH,
        )

    def loop(count, act):
        def one(k, carry):
            act(k)
            return carry

        lax.fori_loop(1, count, one, 0)

    load_tokens = pltpu.make_async_copy(tokens_ref, tokens_v, in_sem.at[0])
    load_middle = pltpu.make_async_copy(middle_ref, middle_v, in_sem.at[1])
    load_tokens.start()
    load_middle.start()
    barrier = pltpu.get_barrier_semaphore()

    def greet(axis, place, count):
        loop(
            count,
            lambda k: pl.semaphore_signal(
                barrier, inc=1, device_id={axis: lax.rem(place + k, count)}, device_id_type=MESH
            ),
        )

    greet("dp", me, n_dp)
    greet("tensor", line, n)
    pl.semaphore_wait(barrier, n_dp + n - 2)
    loop(n_dp, lambda k: weights_copy(k).start())
    acc[...] = jnp.zeros_like(acc)
    load_tokens.wait()
    load_middle.wait()

    def step(t, carry):
        slot(t)

        @pl.when(t < line_parts)
        def _():
            for half in (0, 1):
                at = pl.ds(pl.multiple_of((half * line_parts + t) * rows, 16), rows)
                norm, _ = norm_of(at)
                term = x_ref[at].astype(f32) * norm
                acc[...] += jnp.sum(term.reshape(rows // 8, 8, model), axis=0)

        return carry

    total = line_steps(n)
    lax.fori_loop(0, line_parts, step, 0)
    width = g_from.shape[2]
    for p in range(n_dp):
        moved = acc[...] if p == 0 else pltpu.roll(acc[...], model - p * depth, 1)
        g_from[p, :8] = moved[:, :width]
        g_from[p, 8:] = gain_second_ref[p]
    loop(n_dp, lambda k: gains_copy(k).start())
    late = min(line_parts + 4, total)
    lax.fori_loop(line_parts, late, step, 0)
    loop(n_dp, lambda k: gains_copy(k).wait_recv())
    z_from[...] = lax.fori_loop(1, n_dp, lambda k, t: t + g_got[k], g_from[me])
    loop(n, lambda k: line_copy(k).start())
    loop(n_dp, lambda k: weights_copy(k).wait_recv())
    lax.fori_loop(late, total, step, 0)
    size = 32

    def add(b, carry):
        at = pl.ds(pl.multiple_of(b * size, 16), size)
        weights_out[at] = lax.fori_loop(
            1, n_dp, lambda k, t: t + got[k, at].astype(f32), weights_ref[me, at].astype(f32)
        )
        return carry

    every = pltpu.make_async_copy(grad_v, grad_ref, out_sem)
    every.start()
    lax.fori_loop(0, depth // size, add, 0)
    loop(n, lambda k: line_copy(k).wait_recv())
    gains_out[...] = lax.fori_loop(1, n, lambda k, t: t + z_got[k], z_from[...])
    finish()
    loop(n_dp, lambda k: weights_copy(k).wait_send())
    loop(n_dp, lambda k: gains_copy(k).wait_send())
    loop(n, lambda k: line_copy(k).wait_send())
    every.wait()


def last_call(x, tokens, middle, gain, weights, gain_second, n, n_dp, barrier_id):
    count, model = x.shape
    depth, width = model // n_dp, weights.shape[1]
    lanes = -(-depth // 128) * 128
    gain_second = jnp.where(lax.axis_index("tensor") == 0, gain_second, 0.0)
    gain_second = jnp.pad(
        gain_second.reshape(n_dp, 1, depth), ((0, 0), (0, 7), (0, lanes - depth))
    )
    whole, anywhere = pl.BlockSpec(memory_space=pltpu.VMEM), pl.BlockSpec(memory_space=pl.ANY)
    dma = pltpu.SemaphoreType.DMA
    grad, weights, gains = pl.pallas_call(
        functools.partial(last_kernel, n, n_dp),
        out_shape=[
            jax.ShapeDtypeStruct((count, model), f32),
            jax.ShapeDtypeStruct((depth, width), f32),
            jax.ShapeDtypeStruct((16, lanes), f32),
        ],
        in_specs=[whole, anywhere, anywhere, whole, whole, whole],
        out_specs=[anywhere, whole, whole],
        scratch_shapes=[pltpu.VMEM(x.shape, bf16)]
        + line_scratch(x.shape, x.dtype)
        + [
            pltpu.VMEM((count, model), bf16),
            pltpu.VMEM((count, model), f32),
            pltpu.VMEM((count, model), f32),
            dma((2,)),
            dma,
            pltpu.VMEM((n_dp, depth, width), bf16),
            dma((n_dp,)),
            dma((n_dp,)),
            pltpu.VMEM((n_dp, 16, lanes), f32),
            pltpu.VMEM((n_dp, 16, lanes), f32),
            dma((n_dp,)),
            dma((n_dp,)),
            pltpu.VMEM((16, lanes), f32),
            pltpu.VMEM((n, 16, lanes), f32),
            dma((n,)),
            dma((n,)),
            pltpu.VMEM((8, model), f32),
        ],
        compiler_params=pltpu.CompilerParams(
            collective_id=barrier_id, has_side_effects=True, vmem_limit_bytes=56 * 2**20
        ),
        cost_estimate=pl.CostEstimate(
            flops=count * model, bytes_accessed=2**20, transcendentals=0
        ),
    )(x, tokens, middle, gain, weights.reshape(n_dp, depth, width), gain_second)
    gains = jnp.stack([jnp.sum(gains[:8, :depth], axis=0), gains[8, :depth]])
    return grad, weights, gains


def expert_grads_kernel(
    n, shape, x_ref, rows_ref, outgrad_ref, down_ref, hidden_ref, active_ref, active_rows_ref,
    o_ref, gateup_grad_ref, down_grad_ref, mixture_ref, rows_t, outgrad_t, o_sem, sum_ref, *scratch,
):
    mixture_steps, gateup_steps, down_steps = shape
    i = pl.program_id(0)
    steps = sum(shape)
    _, begin, slot, finish = line_engine(n, x_ref, sum_ref, *scratch)
    total = line_steps(n)
    each = -(-total // steps)
    pl.when(i == 0)(begin)

    def slots(low, high):
        def one(j, carry):
            t = i * each + j
            pl.when(t < total)(lambda: slot(t))
            return carry

        lax.fori_loop(low, high, one, 0)

    slots(0, 1)

    @pl.when(i < mixture_steps)
    def _():
        mixture_ref[...] = lax.dot_general(
            active_rows_ref[...], down_ref[...], nt, preferred_element_type=f32
        ).astype(bf16)
        size = active_rows_ref.shape[0]
        columns = pl.ds(pl.multiple_of(i * size, size), size)
        rows_t[:, columns] = rows_ref[...].T
        outgrad_t[:, columns] = outgrad_ref[...].T

    @pl.when((i >= mixture_steps) & (i < mixture_steps + gateup_steps))
    def _():
        gateup_grad_ref[...] = jnp.dot(
            rows_t[...], hidden_ref[...], preferred_element_type=f32
        ).astype(bf16)

    @pl.when(i >= mixture_steps + gateup_steps)
    def _():
        down_grad_ref[...] = jnp.dot(
            outgrad_t[...], active_ref[...], preferred_element_type=f32
        ).astype(bf16)

    slots(1, each)

    @pl.when(i == steps - 1)
    def _():
        copy = pltpu.make_async_copy(sum_ref, o_ref, o_sem)
        copy.start()
        finish()
        copy.wait()


def expert_grads_call(x, rows, outgrad, down, hidden, active, n, barrier_id):
    tokens, model = rows.shape
    block, tile = min(512, active.shape[1]), 256
    c, a, b = shape = (tokens // tile, hidden.shape[1] // block, active.shape[1] // block)
    whole = pl.BlockSpec(memory_space=pltpu.VMEM)
    first = lambda i: (jnp.minimum(i, c - 1), 0)
    second = lambda i: (0, jnp.clip(i - c, 0, a - 1))
    third = lambda i: (0, jnp.clip(i - c - a, 0, b - 1))
    return pl.pallas_call(
        functools.partial(expert_grads_kernel, n, shape),
        grid=(a + b + c,),
        in_specs=[
            whole,
            pl.BlockSpec((tile, model), first),
            pl.BlockSpec((tile, model), first),
            whole,
            pl.BlockSpec((tokens, block), second),
            pl.BlockSpec((tokens, block), third),
            pl.BlockSpec((tile, active.shape[1]), first),
        ],
        out_specs=[
            pl.BlockSpec(memory_space=pl.ANY),
            pl.BlockSpec((model, block), second),
            pl.BlockSpec((model, block), third),
            pl.BlockSpec((tile, model), first),
        ],
        out_shape=[
            jax.ShapeDtypeStruct(x.shape, x.dtype),
            jax.ShapeDtypeStruct((model, hidden.shape[1]), bf16),
            jax.ShapeDtypeStruct((model, active.shape[1]), bf16),
            jax.ShapeDtypeStruct((tokens, model), bf16),
        ],
        scratch_shapes=[pltpu.VMEM((model, tokens), bf16)] * 2
        + [pltpu.SemaphoreType.DMA, pltpu.VMEM(x.shape, x.dtype)]
        + line_scratch(x.shape, x.dtype),
        compiler_params=pltpu.CompilerParams(
            collective_id=barrier_id, has_side_effects=True, vmem_limit_bytes=58 * 2**20
        ),
        cost_estimate=pl.CostEstimate(
            flops=2 * tokens * model * (hidden.shape[1] + 2 * active.shape[1]),
            bytes_accessed=10 * tokens * model,
            transcendentals=0,
        ),
    )(x, rows, outgrad, down, hidden, active, active)


def expert_kernel(group, rows_ref, outgrad_ref, gates_ref, gu_ref, down_ref,
                  active_ref, hidden_ref, gate_grad_ref):
    step = pl.program_id(0)
    tile = 256
    width = gu_ref.shape[1] // 2
    hidden = width // group
    lane = lax.broadcasted_iota(jnp.int32, (tile, 128), 1)
    column = lax.broadcasted_iota(jnp.int32, (tile, width), 1)

    @pl.when(step == 0)
    def _():
        gate_grad_ref[...] = jnp.zeros_like(gate_grad_ref)

    def one(t, carry):
        at = pl.ds(pl.multiple_of(t * tile, tile), tile)
        h = jnp.dot(rows_ref[at], gu_ref[...], preferred_element_type=f32)
        back = jnp.dot(outgrad_ref[at], down_ref[...], preferred_element_type=f32)
        gates = gates_ref[at]
        wide = jnp.zeros((tile, width), f32)
        for j in range(group):
            g = jnp.sum(jnp.where(lane == step * group + j, gates, 0.0), axis=1, keepdims=True)
            wide = g + wide if group == 1 else jnp.where(column // hidden == j, g, wide)
        gate, up = h[:, :width], h[:, width:]
        sig = 1.0 / (1.0 + jnp.exp(-gate))
        silu = gate * sig
        active = (silu * up).astype(bf16).astype(f32)
        active_ref[at] = (active * wide).astype(bf16)
        product = active * back
        grads = gate_grad_ref[at]
        for j in range(group):
            s = jnp.sum(jnp.where(column // hidden == j, product, 0.0), axis=1, keepdims=True)
            grads = jnp.where(lane == step * group + j, s, grads)
        gate_grad_ref[at] = grads
        back = back * wide
        hidden_ref[at, :width] = (back * up * sig * (1.0 + gate * (1.0 - sig))).astype(bf16)
        hidden_ref[at, width:] = (back * silu).astype(bf16)
        return carry

    lax.fori_loop(0, rows_ref.shape[0] // tile, one, 0)


def expert_call(rows, outgrad, gates, gu, down, group):
    tokens, model = rows.shape
    width = gu.shape[1] // (EXPERTS // group)
    steps = EXPERTS // group
    return pl.pallas_call(
        functools.partial(expert_kernel, group),
        grid=(steps,),
        in_specs=[
            pl.BlockSpec((tokens, model), lambda p: (0, 0)),
            pl.BlockSpec((tokens, model), lambda p: (0, 0)),
            pl.BlockSpec((tokens, 128), lambda p: (0, 0)),
            pl.BlockSpec((model, width), lambda p: (0, p)),
            pl.BlockSpec((model, width // 2), lambda p: (0, p)),
        ],
        out_specs=[
            pl.BlockSpec((tokens, width // 2), lambda p: (0, p)),
            pl.BlockSpec((tokens, width), lambda p: (0, p)),
            pl.BlockSpec((tokens, 128), lambda p: (0, 0)),
        ],
        out_shape=[
            jax.ShapeDtypeStruct((tokens, steps * width // 2), bf16),
            jax.ShapeDtypeStruct((tokens, steps * width), bf16),
            jax.ShapeDtypeStruct((tokens, 128), f32),
        ],
        compiler_params=pltpu.CompilerParams(vmem_limit_bytes=48 * 2**20),
        cost_estimate=pl.CostEstimate(
            flops=2 * tokens * model * steps * width * 3 // 2,
            bytes_accessed=2 * (model * steps * width * 3 // 2 + tokens * steps * width * 3 // 2),
            transcendentals=tokens * steps * width // 2,
        ),
    )(rows, outgrad, gates, gu, down)


def turn(u, cosine, sine):
    lane = lax.broadcasted_iota(jnp.int32, u.shape, 1) % HEAD_DIM
    other = jnp.where(lane < HEAD_DIM // 2, pltpu.roll(u, 96, 1), pltpu.roll(u, 32, 1))
    return u * cosine + other * sine


def project_kernel(x_ref, gain_ref, w_ref, cos_ref, sin_ref, normed_ref, q_ref, kv_ref):
    x = x_ref[...].astype(f32)
    inverse = lax.rsqrt(jnp.mean(x * x, axis=-1, keepdims=True) + eps_norm)
    normed = (x * inverse * gain_ref[0:1]).astype(bf16)
    normed_ref[...] = normed
    mixed = jnp.dot(normed, w_ref[...], preferred_element_type=f32)
    cosine, sine = cos_ref[...], sin_ref[...]
    turned = q_ref.shape[1] // 128
    for c in range(turned):
        q_ref[:, c * 128 : (c + 1) * 128] = turn(
            mixed[:, c * 128 : (c + 1) * 128], cosine, sine
        ).astype(bf16)
    start = turned * 128
    kv_ref[:, :128] = turn(mixed[:, start : start + 128], cosine, sine).astype(bf16)
    kv_ref[:, 128:] = mixed[:, start + 128 :].astype(bf16)


def project_call(tokens, gain, w, cosine, sine):
    count, model = tokens.shape
    tile = 256
    width = w.shape[1]
    row = lambda n: pl.BlockSpec((tile, n), lambda i: (i, 0))
    return pl.pallas_call(
        project_kernel,
        grid=(count // tile,),
        in_specs=[
            row(model),
            pl.BlockSpec((8, model), lambda i: (0, 0)),
            pl.BlockSpec((model, width), lambda i: (0, 0)),
            row(128),
            row(128),
        ],
        out_specs=[row(model), row(width - 256), row(256)],
        out_shape=[
            jax.ShapeDtypeStruct((count, model), bf16),
            jax.ShapeDtypeStruct((count, width - 256), bf16),
            jax.ShapeDtypeStruct((count, 256), bf16),
        ],
        compiler_params=pltpu.CompilerParams(vmem_limit_bytes=32 * 2**20),
        cost_estimate=pl.CostEstimate(
            flops=2 * count * model * width, bytes_accessed=6 * count * model, transcendentals=count
        ),
    )(tokens, gain, w, cosine, sine)


def head_places(heads):
    return [(h // GROUP, h % 2, h // 2) for h in range(heads)]


def spread(kv, scale):
    lane = lax.broadcasted_iota(jnp.int32, kv.shape, 1)
    kv = kv * scale
    turned = pltpu.roll(kv, HEAD_DIM, 1)
    first = lane < HEAD_DIM
    zero = jnp.zeros_like(kv)
    return {
        (0, 0): jnp.where(first, kv, zero).astype(bf16),
        (0, 1): jnp.where(first, zero, turned).astype(bf16),
        (1, 0): jnp.where(first, turned, zero).astype(bf16),
        (1, 1): jnp.where(first, zero, kv).astype(bf16),
    }


def row_tiles(prompt_total):
    tiles = [(0, PROMPT_DEV, prompt_total)]
    for start in range(0, CONT, 256):
        tiles.append((PROMPT_DEV + start, 256, prompt_total + start + 256))
    return tiles


def meet(me, n):
    barrier = pltpu.get_barrier_semaphore()

    def greet(k, carry):
        pl.semaphore_signal(
            barrier, inc=1, device_id={"dp": lax.rem(me + k, n)}, device_id_type=MESH
        )
        return carry

    lax.fori_loop(1, n, greet, 0)
    pl.semaphore_wait(barrier, n - 1)


def load_spread(m, all_ref, kv_ref, k_ref, v_ref, kt_ref=None):
    total = all_ref.shape[1]
    own = pl.ds(pl.multiple_of(m * TOK_MB + PROMPT_DEV, 16), CONT)
    for low, high, rows in ((0, total, all_ref[m]), (total, total + CONT, kv_ref[own])):
        keys = spread(rows[:, :128].astype(f32), HEAD_DIM**-0.5)
        values = spread(rows[:, 128:].astype(f32), 1.0)
        for i, place in enumerate(keys):
            k_ref[i, low:high] = keys[place]
            v_ref[i, low:high] = values[place]
            if kt_ref is not None:
                kt_ref[i, :, low:high] = keys[place].astype(f32).T.astype(bf16)
    return {place: i for i, place in enumerate(keys)}


def attention_kernel(heads, n, q_ref, kv_ref, o_ref, lse_ref, all_ref, k_ref, v_ref, send, recv):
    prompt_total = all_ref.shape[1]
    me = lax.axis_index("dp")

    def piece(m, k):
        rows = all_ref.at[m, pl.ds(pl.multiple_of(me * PROMPT_DEV, PROMPT_DEV), PROMPT_DEV)]
        return pltpu.make_async_remote_copy(
            src_ref=rows,
            dst_ref=rows,
            send_sem=send.at[m, k],
            recv_sem=recv.at[m, k],
            device_id={"dp": lax.rem(me + k, n)},
            device_id_type=MESH,
        )

    for m in range(MICRO):
        all_ref[m, pl.ds(pl.multiple_of(me * PROMPT_DEV, PROMPT_DEV), PROMPT_DEV)] = kv_ref[
            m * TOK_MB : m * TOK_MB + PROMPT_DEV
        ]
    meet(me, n)

    def every(m, act):
        def one(k, carry):
            act(piece(m, k))
            return carry

        lax.fori_loop(1, n, one, 0)

    for m in range(MICRO):
        every(m, lambda copy: copy.start())

    def micro(m, carry):
        every(m, lambda copy: copy.wait_recv())
        index = load_spread(m, all_ref, kv_ref, k_ref, v_ref)
        lane = lax.broadcasted_iota(jnp.int32, (1, 128), 1)
        for start, rows, length in row_tiles(prompt_total):
            at = pl.ds(pl.multiple_of(m * TOK_MB + start, 128), rows)
            row = lax.broadcasted_iota(jnp.int32, (rows, 1), 0)
            if start == 0:
                masked = 0
                reach = row + me * PROMPT_DEV
            else:
                masked = length - 256
                reach = row
            column = lax.broadcasted_iota(jnp.int32, (rows, length - masked), 1)
            lse = jnp.zeros((rows, 128), f32)
            pair_out = None
            for h, (kv, half, pair) in enumerate(head_places(heads)):
                q = q_ref[at, pair * 128 : (pair + 1) * 128]
                i = index[kv, half]
                tail = lax.dot_general(q, k_ref[i, masked:length], nt, preferred_element_type=f32)
                tail = jnp.where(column <= reach, tail, -1e30)
                top = jnp.max(tail, axis=1, keepdims=True)
                if masked:
                    head = lax.dot_general(q, k_ref[i, :masked], nt, preferred_element_type=f32)
                    top = jnp.maximum(top, jnp.max(head, axis=1, keepdims=True))
                    p_head = jnp.exp(head - top)
                p_tail = jnp.exp(tail - top)
                total = jnp.sum(p_tail, axis=1, keepdims=True)
                out = jnp.dot(
                    p_tail.astype(bf16), v_ref[i, masked:length], preferred_element_type=f32
                )
                if masked:
                    total = total + jnp.sum(p_head, axis=1, keepdims=True)
                    out = out + jnp.dot(
                        p_head.astype(bf16), v_ref[i, :masked], preferred_element_type=f32
                    )
                out = out / total
                lse = jnp.where(lane == h, top + jnp.log(total), lse)
                if half == 0:
                    pair_out = out
                else:
                    o_ref[at, pair * 128 : (pair + 1) * 128] = (pair_out + out).astype(bf16)
            lse_ref[at] = lse
        return carry

    lax.fori_loop(0, MICRO, micro, 0)
    for m in range(MICRO):
        every(m, lambda copy: copy.wait_send())


def attention_call(q, kv, n):
    count, width = q.shape
    keys = PROMPT_DEV * n + CONT
    heads = width // HEAD_DIM
    whole = pl.BlockSpec(memory_space=pltpu.VMEM)
    return pl.pallas_call(
        functools.partial(attention_kernel, heads, n),
        in_specs=[whole] * 2,
        out_specs=[whole] * 3,
        out_shape=[
            jax.ShapeDtypeStruct((count, width), bf16),
            jax.ShapeDtypeStruct((count, 128), f32),
            jax.ShapeDtypeStruct((MICRO, PROMPT_DEV * n, 256), bf16),
        ],
        scratch_shapes=[
            pltpu.VMEM((4, keys, 128), bf16),
            pltpu.VMEM((4, keys, 128), bf16),
            pltpu.SemaphoreType.DMA((MICRO, n)),
            pltpu.SemaphoreType.DMA((MICRO, n)),
        ],
        compiler_params=pltpu.CompilerParams(
            collective_id=3, has_side_effects=True, vmem_limit_bytes=48 * 2**20
        ),
        cost_estimate=pl.CostEstimate(
            flops=16 * count * keys * width,
            bytes_accessed=8 * count * width,
            transcendentals=count * keys * heads,
        ),
    )(q, kv)


def attention_back_kernel(
    heads, n, q_ref, kv_ref, all_ref, do_ref, o_ref, lse_ref,
    cos_ref, sin_ref, row_cos_ref, row_sin_ref,
    grad_ref, k_ref, v_ref, kt_ref, dk_ref, dv_ref, sent_ref, got_ref, send, recv,
):
    prompt_total = all_ref.shape[1]
    me = lax.axis_index("dp")
    width = heads * HEAD_DIM

    def piece(m, k):
        to = lax.rem(me + k, n)
        return pltpu.make_async_remote_copy(
            src_ref=sent_ref.at[m, pl.ds(pl.multiple_of(to * PROMPT_DEV, PROMPT_DEV), PROMPT_DEV)],
            dst_ref=got_ref.at[m, k],
            send_sem=send.at[m, k],
            recv_sem=recv.at[m, k],
            device_id={"dp": to},
            device_id_type=MESH,
        )

    def every(m, act):
        def one(k, carry):
            act(piece(m, k))
            return carry

        lax.fori_loop(1, n, one, 0)

    meet(me, n)
    half_rows = (
        lax.broadcasted_iota(jnp.int32, (8, 128), 1) // HEAD_DIM
        == lax.broadcasted_iota(jnp.int32, (8, 128), 0)
    ).astype(f32)

    def micro(m, carry):
        index = load_spread(m, all_ref, kv_ref, k_ref, v_ref, kt_ref)
        dk_ref[...] = jnp.zeros_like(dk_ref)
        dv_ref[...] = jnp.zeros_like(dv_ref)
        for start, rows, length in row_tiles(prompt_total):
            at = pl.ds(pl.multiple_of(m * TOK_MB + start, 128), rows)
            inner = slice(start, start + rows)
            column = lax.broadcasted_iota(jnp.int32, (1, rows), 1)
            if start == 0:
                masked = 0
                reach = column + me * PROMPT_DEV
            else:
                masked = length - 256
                reach = column
            key = lax.broadcasted_iota(jnp.int32, (length - masked, rows), 0)
            back = None
            for h, (kv, half, pair) in enumerate(head_places(heads)):
                lanes = slice(pair * 128, (pair + 1) * 128)
                i = index[kv, half]
                q, do = q_ref[at, lanes], do_ref[at, lanes]
                if half == 0:
                    delta_pair = lax.dot_general(
                        half_rows,
                        do.astype(f32) * o_ref[at, lanes].astype(f32),
                        nt,
                        precision=lax.Precision.HIGHEST,
                        preferred_element_type=f32,
                    )
                delta = delta_pair[half : half + 1]
                lse = lse_ref[m, h : h + 1, inner]
                for low, high in ((0, masked), (masked, length)):
                    if low == high:
                        continue
                    s = lax.dot_general(k_ref[i, low:high], q, nt, preferred_element_type=f32)
                    if low == masked:
                        s = jnp.where(key <= reach, s, -1e30)
                    p = jnp.exp(s - lse)
                    dp_ = lax.dot_general(v_ref[i, low:high], do, nt, preferred_element_type=f32)
                    ds = (p * (dp_ - delta)).astype(bf16)
                    dv_ref[i, low:high] += jnp.dot(
                        p.astype(bf16), do, preferred_element_type=f32
                    )
                    dk_ref[i, low:high] += jnp.dot(ds, q, preferred_element_type=f32)
                    term = jnp.dot(kt_ref[i, :, low:high], ds, preferred_element_type=f32)
                    back = term if back is None else back + term
                if half == 1:
                    grad_ref[at, lanes] = turn(
                        back.T, row_cos_ref[inner], -row_sin_ref[inner]
                    ).astype(bf16)
                    back = None
        lane = lax.broadcasted_iota(jnp.int32, (dk_ref.shape[1], 128), 1)

        def joined(acc):
            get = lambda place: acc[index[place]]
            return jnp.where(
                lane < HEAD_DIM,
                get((0, 0)) + pltpu.roll(get((0, 1)), HEAD_DIM, 1),
                get((1, 1)) + pltpu.roll(get((1, 0)), HEAD_DIM, 1),
            )

        dk = turn(joined(dk_ref) * HEAD_DIM**-0.5, cos_ref[...], -sin_ref[...]).astype(bf16)
        dv = joined(dv_ref).astype(bf16)
        sent_ref[m, :, :128] = dk[:prompt_total]
        sent_ref[m, :, 128:] = dv[:prompt_total]
        every(m, lambda copy: copy.start())
        own = pl.ds(pl.multiple_of(m * TOK_MB + PROMPT_DEV, 128), CONT)
        grad_ref[own, width : width + 128] = dk[prompt_total:]
        grad_ref[own, width + 128 :] = dv[prompt_total:]
        return carry

    lax.fori_loop(0, MICRO, micro, 0)

    def collect(m, carry):
        every(m, lambda copy: copy.wait_recv())
        own = sent_ref[m, pl.ds(pl.multiple_of(me * PROMPT_DEV, PROMPT_DEV), PROMPT_DEV)]
        total = lax.fori_loop(
            1, n, lambda k, t: t + got_ref[m, k].astype(f32), own.astype(f32)
        )
        at = pl.ds(pl.multiple_of(m * TOK_MB, 128), PROMPT_DEV)
        grad_ref[at, width:] = total.astype(bf16)
        every(m, lambda copy: copy.wait_send())
        return carry

    lax.fori_loop(0, MICRO, collect, 0)


def attention_back_call(q, kv, prompts, do, o, lse, cosine, sine, row_cos, row_sin, n):
    count, width = q.shape
    keys = prompts.shape[1] + CONT
    heads = width // HEAD_DIM
    whole = pl.BlockSpec(memory_space=pltpu.VMEM)
    return pl.pallas_call(
        functools.partial(attention_back_kernel, heads, n),
        in_specs=[whole] * 10,
        out_specs=whole,
        out_shape=jax.ShapeDtypeStruct((count, width + 256), bf16),
        scratch_shapes=[
            pltpu.VMEM((4, keys, 128), bf16),
            pltpu.VMEM((4, keys, 128), bf16),
            pltpu.VMEM((4, 128, keys), bf16),
            pltpu.VMEM((4, keys, 128), f32),
            pltpu.VMEM((4, keys, 128), f32),
            pltpu.VMEM((MICRO, prompts.shape[1], 256), bf16),
            pltpu.VMEM((MICRO, n, PROMPT_DEV, 256), bf16),
            pltpu.SemaphoreType.DMA((MICRO, n)),
            pltpu.SemaphoreType.DMA((MICRO, n)),
        ],
        compiler_params=pltpu.CompilerParams(
            collective_id=4, has_side_effects=True, vmem_limit_bytes=56 * 2**20
        ),
        cost_estimate=pl.CostEstimate(
            flops=40 * count * keys * width,
            bytes_accessed=12 * count * width,
            transcendentals=count * keys * heads,
        ),
    )(q, kv, prompts, do, o, lse, cosine, sine, row_cos, row_sin)


def attend(queries, keys_all, values_all, allowed):
    factor = HEAD_DIM ** (-0.5)
    scores = jnp.einsum("tkgd,skd->kgts", queries, keys_all, preferred_element_type=f32) * factor
    scores = jnp.where(allowed, scores, -1e30)
    row_max = jnp.max(scores, axis=-1, keepdims=True)
    exponent = jnp.exp(scores - row_max)
    softened = exponent / jnp.sum(exponent, axis=-1, keepdims=True)
    soft_low = softened.astype(bf16)
    attended = jnp.einsum("kgts,skd->tkgd", soft_low, values_all, preferred_element_type=f32)
    return attended.astype(bf16), softened, soft_low


def attend_back(queries, keys_all, values_all, softened, soft_low, attended_grad):
    factor = HEAD_DIM ** (-0.5)
    soft_grad = jnp.einsum("tkgd,skd->kgts", attended_grad, values_all, preferred_element_type=f32)
    values_grad = jnp.einsum("kgts,tkgd->skd", soft_low, attended_grad, preferred_element_type=f32)
    row_delta = jnp.sum(softened * soft_grad, axis=-1, keepdims=True)
    scores_grad = (softened * (soft_grad - row_delta)).astype(bf16)
    queries_grad = (
        jnp.einsum("kgts,skd->tkgd", scores_grad, keys_all, preferred_element_type=f32) * factor
    )
    keys_grad = (
        jnp.einsum("kgts,tkgd->skd", scores_grad, queries, preferred_element_type=f32) * factor
    )
    return queries_grad, keys_grad, values_grad


def shards(
    tokens, cotangent, routes,
    inproj_weight, inproj_first, inproj_second,
    outproj_weight, outproj_first, outproj_second,
    gateup_weight, gateup_first, gateup_second,
    down_weight, down_first, down_second,
    router_weight, router_first, router_second,
    gains, gains_first, gains_second,
):
    n_dp = lax.axis_size("dp")
    n_tensor = lax.axis_size("tensor")
    depth = inproj_weight.shape[0]
    kv_local = inproj_weight.shape[1]
    hidden = down_weight.shape[1]
    group = max(1, 256 // hidden)
    groups = EXPERTS // group
    in_width = inproj_weight.shape[1] * inproj_weight.shape[2]
    out_width = outproj_weight.shape[0] * outproj_weight.shape[1]
    prompt_total = PROMPT_DEV * n_dp
    count = tokens.shape[0]

    def gateup_flat(w):
        w = w.reshape(groups, group, depth, 2, hidden)
        return w.transpose(2, 0, 3, 1, 4).reshape(depth, 2 * EXPERTS * hidden)

    def gateup_back(w):
        w = w.reshape(depth, groups, 2, group, hidden)
        return w.transpose(1, 3, 0, 2, 4).reshape(EXPERTS, depth, 2, hidden)

    query_width = GROUP * HEAD_DIM

    def inproj_flat(w):
        w = w.reshape(depth, kv_local, query_width + 2 * HEAD_DIM)
        parts = (w[:, :, :query_width], w[:, :, query_width:-HEAD_DIM], w[:, :, -HEAD_DIM:])
        return jnp.concatenate([p.reshape(depth, -1) for p in parts], axis=1)

    def inproj_back(w):
        q, k, v = jnp.split(w, [kv_local * query_width, kv_local * (query_width + HEAD_DIM)], axis=1)
        return jnp.concatenate([p.reshape(depth, kv_local, -1) for p in (q, k, v)], axis=2)

    gains_high = gains.astype(bf16)
    gains_low = (gains - gains_high.astype(f32)).astype(bf16)
    attn_local = jnp.concatenate(
        [
            inproj_flat(inproj_weight.astype(bf16)),
            outproj_weight.reshape(out_width, depth).T.astype(bf16),
            jnp.concatenate(
                [
                    router_weight.astype(bf16),
                    gains_high.T,
                    gains_low.T,
                    jnp.zeros((depth, 128 - EXPERTS - 4), bf16),
                ],
                axis=1,
            ),
        ],
        axis=1,
    )
    attn_full = gather(attn_local, n_dp, 5)
    gu_local = gateup_flat(gateup_weight.astype(bf16))
    down_local = down_weight.reshape(EXPERTS * hidden, depth).T.astype(bf16)
    inproj_full = attn_full[:, :in_width]
    outproj_full = attn_full[:, in_width : in_width + out_width]
    small_full = attn_full[:, in_width + out_width :]
    router_full = small_full[:, :EXPERTS]
    small_t = small_full[:, EXPERTS : EXPERTS + 4].astype(f32).T
    gain_first = small_t[0:1] + small_t[2:3]
    gain_second = small_t[1:2] + small_t[3:4]

    device_index = lax.axis_index("dp")
    inputs = tokens.astype(f32)
    inverse_first = lax.rsqrt(jnp.mean(inputs * inputs, axis=-1, keepdims=True) + eps_norm)
    norm_first = inputs * inverse_first
    cosine, sine = angles_for(jnp.arange(prompt_total + CONT), HEAD_DIM)

    def of_rows(table):
        own = lax.dynamic_slice_in_dim(table, device_index * PROMPT_DEV, PROMPT_DEV, 0)
        return jnp.concatenate([own, table[prompt_total:]], axis=0)

    in_kernels = kv_local * HEAD_DIM == 128
    queries_width = kv_local * query_width
    both_width = kv_local * 2 * HEAD_DIM
    if in_kernels:
        cos_all = jnp.concatenate([cosine] * 4, axis=1)
        sin_all = jnp.concatenate([-sine, sine] * 2, axis=1)
        cos_row, sin_row = of_rows(cos_all), of_rows(sin_all)
        normed_first, queries, both = project_call(
            tokens,
            jnp.pad(gain_first, ((0, 7), (0, 0))),
            inproj_full,
            jnp.concatenate([cos_row] * MICRO, axis=0),
            jnp.concatenate([sin_row] * MICRO, axis=0),
        )
    else:
        cosine, sine = (jnp.tile(of_rows(t), (MICRO, 1))[:, None, :] for t in (cosine, sine))
        normed_first = (norm_first * gain_first).astype(bf16)
        mixed = jnp.dot(normed_first, inproj_full, preferred_element_type=f32)
        queries = rotate(
            mixed[:, :queries_width].reshape(count, -1, HEAD_DIM), cosine, sine
        ).astype(bf16)
        keys = rotate(
            mixed[:, queries_width : queries_width + kv_local * HEAD_DIM].reshape(
                count, -1, HEAD_DIM
            ),
            cosine,
            sine,
        )
        both = jnp.concatenate(
            [keys.reshape(count, -1), mixed[:, queries_width + kv_local * HEAD_DIM :]], axis=1
        ).astype(bf16)
    if in_kernels:
        attended, lse, prompt_both = attention_call(queries, both, n_dp)
    else:
        both = both.reshape(MICRO, TOK_MB, both_width)
        prompt_both = lax.all_gather(both[:, :PROMPT_DEV], "dp", axis=1, tiled=True)
        both_all = jnp.concatenate([prompt_both, both[:, PROMPT_DEV:]], axis=1)
        inner = jnp.arange(TOK_MB, dtype=jnp.int32)
        positions = jnp.where(
            inner < PROMPT_DEV, device_index * PROMPT_DEV + inner, prompt_total + inner - PROMPT_DEV
        )
        key_index = jnp.arange(prompt_total + CONT, dtype=jnp.int32)
        allowed = (key_index[None, :] <= positions[:, None]) & (
            (key_index[None, :] < prompt_total) | (inner[:, None] >= PROMPT_DEV)
        )
        kept = []
        attended = []
        for m in range(MICRO):
            q = queries[m * TOK_MB : (m + 1) * TOK_MB].reshape(TOK_MB, kv_local, GROUP, HEAD_DIM)
            k, v = (
                t.reshape(-1, kv_local, HEAD_DIM) for t in jnp.split(both_all[m], 2, axis=1)
            )
            out, softened, soft_low = attend(q, k, v, allowed)
            attended.append(out.reshape(TOK_MB, -1))
            kept.append((q, k, v, softened, soft_low))
        attended = jnp.concatenate(attended, axis=0)
    branch = lax.dot_general(
        attended, outproj_full, (((1,), (1,)), ((), ())), preferred_element_type=f32
    ).astype(bf16)
    branch, gu_full, down_full = line_gather(branch, gu_local, down_local, n_tensor, n_dp, 6)

    middle = inputs + branch.astype(f32)
    inverse_second = lax.rsqrt(jnp.mean(middle * middle, axis=-1, keepdims=True) + eps_norm)
    norm_second = middle * inverse_second
    normed_second = (norm_second * gain_second).astype(bf16)
    logits = jnp.dot(normed_second, router_full, preferred_element_type=f32)
    named = jnp.any(routes[:, :, None] == jnp.arange(EXPERTS, dtype=jnp.int32), axis=1)
    top = jnp.max(jnp.where(named, logits, -jnp.inf), axis=-1, keepdims=True)
    weights = jnp.where(named, jnp.exp(jnp.where(named, logits, top) - top), 0.0)
    gates = weights / jnp.sum(weights, axis=-1, keepdims=True)
    gates_wide = jnp.pad(gates, ((0, 0), (0, 128 - EXPERTS)))
    active, hidden_grad, gate_grad = expert_call(
        normed_second, cotangent, gates_wide, gu_full, down_full, group
    )
    contract_last = (((1,), (1,)), ((), ()))
    contract_first = (((0,), (0,)), ((), ()))
    rows_grad = lax.dot_general(
        hidden_grad, gu_full, contract_last, preferred_element_type=f32
    ).astype(bf16)
    summed, gateup_grad, down_grad, mixture = expert_grads_call(
        jnp.concatenate([rows_grad, gate_grad.astype(bf16)], axis=1),
        normed_second, cotangent, down_full, hidden_grad, active, n_tensor, 2,
    )
    mixture = lax.psum(mixture, "tensor")
    model = tokens.shape[1]
    gate_grad = summed[:, model : model + EXPERTS].astype(f32)
    outgrad = cotangent.astype(f32)
    chosen_grad = gates * (gate_grad - jnp.sum(gates * gate_grad, axis=-1, keepdims=True))
    logits_grad = chosen_grad.astype(bf16)
    router_grad = lax.dot_general(
        normed_second,
        jnp.pad(logits_grad, ((0, 0), (0, 128 - EXPERTS))),
        contract_first, preferred_element_type=f32
    ).astype(bf16)
    normed_second_grad = summed[:, :model].astype(f32) + lax.dot_general(
        logits_grad, router_full, contract_last, preferred_element_type=f32
    )
    norm_second_grad = normed_second_grad * gain_second
    gain_second_grad = jnp.sum(normed_second_grad * norm_second, axis=0)
    middle_grad = outgrad + inverse_second * (
        norm_second_grad
        - norm_second * jnp.mean(norm_second_grad * norm_second, axis=-1, keepdims=True)
    )

    middle_grad, down_grad, gateup_grad = lax.optimization_barrier((middle_grad, down_grad, gateup_grad))
    down_grad = lax.psum_scatter(down_grad, "dp", scatter_dimension=0, tiled=True)
    gateup_grad = lax.psum_scatter(gateup_grad, "dp", scatter_dimension=0, tiled=True)
    branch_own = middle_grad.astype(bf16)
    outproj_grad = lax.dot_general(
        branch_own, attended, contract_first, preferred_element_type=f32
    ).astype(bf16)
    attended_grad = jnp.dot(branch_own, outproj_full, preferred_element_type=f32).astype(bf16)
    if in_kernels:
        lse_rows = lse[:, :8].reshape(MICRO, TOK_MB, 8).transpose(0, 2, 1)
        mixed_grad = attention_back_call(
            queries, both, prompt_both, attended_grad, attended, lse_rows,
            cos_all, sin_all, cos_row, sin_row, n_dp,
        )
    else:
        queries_grad, both_grad = [], []
        for m in range(MICRO):
            q, k, v, softened, soft_low = kept[m]
            dout = attended_grad[m * TOK_MB : (m + 1) * TOK_MB].reshape(q.shape)
            dq, dk, dv = attend_back(q, k, v, softened, soft_low, dout)
            queries_grad.append(dq.reshape(TOK_MB, -1, HEAD_DIM))
            both_grad.append(jnp.concatenate([t.reshape(-1, both_width // 2) for t in (dk, dv)], 1))
        queries_grad = rotate(jnp.concatenate(queries_grad, axis=0), cosine, -sine)
        both_grad = jnp.stack(both_grad)
        prompt_grad = lax.psum_scatter(
            both_grad[:, :prompt_total].astype(bf16), "dp", scatter_dimension=1, tiled=True
        )
        both_grad = jnp.concatenate(
            [prompt_grad.astype(f32), both_grad[:, prompt_total:]], axis=1
        ).reshape(count, both_width)
        keys_grad = rotate(
            both_grad[:, : both_width // 2].reshape(count, -1, HEAD_DIM), cosine, -sine
        )
        mixed_grad = jnp.concatenate(
            [
                queries_grad.reshape(count, -1),
                keys_grad.reshape(count, -1),
                both_grad[:, both_width // 2 :],
            ],
            axis=1,
        ).astype(bf16)
    normed_first_grad = lax.dot_general(
        mixed_grad, inproj_full, contract_last, preferred_element_type=f32
    ).astype(bf16)
    inproj_grad = lax.dot_general(
        normed_first, mixed_grad, contract_first, preferred_element_type=f32
    ).astype(bf16)
    attn_grad = jnp.concatenate(
        [
            inproj_grad,
            outproj_grad,
            router_grad,
        ],
        axis=1,
    )
    down_next = adam_update(
        down_weight, down_first, down_second,
        down_grad.T.reshape(down_weight.shape).astype(f32), weight_decay, 0.05,
    )
    gateup_next = adam_update(
        gateup_weight, gateup_first, gateup_second,
        gateup_back(gateup_grad).astype(f32), weight_decay, 0.05,
    )
    tokens_grad, attn_grad, gains_grad = last_call(
        normed_first_grad, tokens, middle_grad, jnp.pad(gain_first, ((0, 7), (0, 0))),
        attn_grad, gain_second_grad, n_tensor, n_dp, 7,
    )
    mixture, tokens_grad = lax.optimization_barrier((mixture, tokens_grad))
    block_out = (middle + mixture.astype(f32)).astype(bf16)
    split = (in_width, in_width + out_width, in_width + out_width + EXPERTS)
    inproj_grad, outproj_grad, router_grad = (
        attn_grad[:, : split[0]],
        attn_grad[:, split[0] : split[1]],
        attn_grad[:, split[1] : split[2]],
    )
    updates = (
        adam_update(
            inproj_weight, inproj_first, inproj_second, inproj_back(inproj_grad), weight_decay, 0.05
        ),
        adam_update(
            outproj_weight, outproj_first, outproj_second,
            outproj_grad.T.reshape(outproj_weight.shape), weight_decay, 0.3,
        ),
        gateup_next,
        down_next,
        adam_update(router_weight, router_first, router_second, router_grad, weight_decay, 0.05),
        adam_update(gains, gains_first, gains_second, gains_grad, 0.0, 0.4),
    )
    return (block_out, tokens_grad) + sum(updates, ())


def solution(mesh):
    row = P("dp", None)
    inproj = P("dp", "tensor", None)
    outproj = P("tensor", None, "dp")
    gateup = P(None, "dp", None, "tensor")
    down = P(None, "tensor", "dp")
    gain = P(None, "dp")
    weights = (inproj,) * 3 + (outproj,) * 3 + (gateup,) * 3 + (down,) * 3 + (row,) * 3 + (gain,) * 3
    return jax.shard_map(
        shards,
        mesh=mesh,
        in_specs=(row, row, row) + weights,
        out_specs=(row, row) + weights,
        check_vma=False,
    )
```

```python
import functools

import jax
import jax.numpy as jnp
import numpy as np
from jax import lax
from jax.experimental import pallas as pl
from jax.experimental.pallas import tpu as pltpu
from jax.sharding import PartitionSpec as P

HEAD_DIM = 64
TOPK = 8
EXPERTS = 16
PROMPT_DEV = 128
CONT = 512
MICRO = 2
STEP = 10
GROUP = 3
TOK_MB = 640

eps_norm = 1e-05
beta_first = 0.9
beta_second = 0.95
adam_eps = 1e-08
weight_decay = 0.1
bf16 = jnp.bfloat16
f32 = jnp.float32
line_parts = 20
line_lag = 2
MESH = pl.DeviceIdType.MESH
nt = (((1,), (1,)), ((), ()))


def rotate(values, cosine, sine):
    half_dim = values.shape[-1] // 2
    first_half = values[..., :half_dim]
    second_half = values[..., half_dim:]
    return jnp.concatenate(
        [first_half * cosine - second_half * sine, second_half * cosine + first_half * sine],
        axis=-1,
    )


def adam_update(weight, moment_one, moment_two, gradient, decay_rate, learn_rate):
    first_next = beta_first * moment_one + (1.0 - beta_first) * gradient
    second_next = beta_second * moment_two + (1.0 - beta_second) * gradient * gradient
    corr_first = 1.0 - beta_first**STEP
    corr_second = 1.0 - beta_second**STEP
    update = first_next / corr_first / (jnp.sqrt(second_next / corr_second) + adam_eps)
    return (weight - learn_rate * (update + decay_rate * weight), first_next, second_next)


def line_steps(n):
    return line_parts + 2 * (n - 1) * line_lag


def line_engine(
    n, x_ref, o_ref, held, send_red, recv_red, send_out, recv_out, complete=lambda at: None
):
    me = lax.axis_index("tensor")
    parts = line_parts
    rows = x_ref.shape[0] // (2 * parts)
    low, high = me - 1, me + 1

    def greet():
        barrier = pltpu.get_barrier_semaphore()

        @pl.when(me > 0)
        def _():
            pl.semaphore_signal(barrier, inc=1, device_id={"tensor": low}, device_id_type=MESH)

        @pl.when(me < n - 1)
        def _():
            pl.semaphore_signal(barrier, inc=1, device_id={"tensor": high}, device_id_type=MESH)

        return jnp.where((me > 0) & (me < n - 1), 2, 1)

    def begin():
        pl.semaphore_wait(pltpu.get_barrier_semaphore(), greet())

    def part(half, c):
        return pl.ds(pl.multiple_of((half * parts + c) * rows, 16), rows)

    def reduce_copy(half, c, src):
        to = low if half == 0 else high
        return pltpu.make_async_remote_copy(
            src_ref=src.at[part(half, c)],
            dst_ref=held.at[part(half, c)],
            send_sem=send_red.at[half, c],
            recv_sem=recv_red.at[half, c],
            device_id={"tensor": to},
            device_id_type=MESH,
        )

    def out_copy(half, c):
        to = high if half == 0 else low
        return pltpu.make_async_remote_copy(
            src_ref=o_ref.at[part(half, c)],
            dst_ref=o_ref.at[part(half, c)],
            send_sem=send_out.at[half, c],
            recv_sem=recv_out.at[half, c],
            device_id={"tensor": to},
            device_id_type=MESH,
        )

    def place(half):
        return n - 1 - me if half == 0 else me

    def slot(t):
        for half in (0, 1):
            at = place(half)
            c = t - line_lag * at

            @pl.when((c >= 0) & (c < parts))
            def _():
                @pl.when(at == 0)
                def _():
                    reduce_copy(half, c, x_ref).start()

                @pl.when(at > 0)
                def _():
                    reduce_copy(half, c, held).wait_recv()
                    total = x_ref[part(half, c)].astype(f32) + held[part(half, c)].astype(f32)

                    @pl.when(at < n - 1)
                    def _():
                        held[part(half, c)] = total.astype(held.dtype)
                        reduce_copy(half, c, held).start()

                    @pl.when(at == n - 1)
                    def _():
                        o_ref[part(half, c)] = total.astype(o_ref.dtype)
                        out_copy(half, c).start()
                        complete(part(half, c))

        for half in (0, 1):
            at = place(half)
            c = t - line_lag * (2 * (n - 1) - at)

            @pl.when((at < n - 1) & (c >= 0) & (c < parts))
            def _():
                out_copy(half, c).wait_recv()

                @pl.when(at > 0)
                def _():
                    out_copy(half, c).start()

                complete(part(half, c))

    def finish():
        def one(c, carry):
            for half in (0, 1):
                at = place(half)

                @pl.when(at < n - 1)
                def _():
                    reduce_copy(half, c, held).wait_send()

                @pl.when(at > 0)
                def _():
                    out_copy(half, c).wait_send()

            return carry

        lax.fori_loop(0, parts, one, 0)

    return greet, begin, slot, finish


def line_scratch(shape, dtype):
    return [pltpu.VMEM(shape, dtype)] + [
        pltpu.SemaphoreType.DMA((2, line_parts)) for _ in range(4)
    ]


def line_sum_kernel(n, x_ref, o_ref, *scratch):
    _, begin, slot, finish = line_engine(n, x_ref, o_ref, *scratch)
    begin()

    def step(t, carry):
        slot(t)
        return carry

    lax.fori_loop(0, line_steps(n), step, 0)
    finish()


def line_sum(x, n, barrier_id):
    rows, width = x.shape
    return pl.pallas_call(
        functools.partial(line_sum_kernel, n),
        out_shape=jax.ShapeDtypeStruct(x.shape, x.dtype),
        in_specs=[pl.BlockSpec(memory_space=pltpu.VMEM)],
        out_specs=pl.BlockSpec(memory_space=pltpu.VMEM),
        scratch_shapes=line_scratch(x.shape, x.dtype),
        compiler_params=pltpu.CompilerParams(
            collective_id=barrier_id, has_side_effects=True, vmem_limit_bytes=24 * 2**20
        ),
        cost_estimate=pl.CostEstimate(
            flops=rows * width, bytes_accessed=100 * rows * width, transcendentals=0
        ),
    )(x)


gather_parts = 3


def gather_engine(n, pairs, own_sem, far_send, far_recv, near_send, near_recv):
    me = lax.axis_index("dp")
    core, chip, chips = lax.rem(me, 2), me // 2, n // 2

    def rows(a, p):
        size = pairs[a][0].shape[0] // gather_parts
        return pl.ds(p * size, size)

    def far(a, p, k):
        x_ref, out_ref = pairs[a]
        return pltpu.make_async_remote_copy(
            src_ref=x_ref.at[rows(a, p)],
            dst_ref=out_ref.at[me, rows(a, p)],
            send_sem=far_send.at[a, p, k],
            recv_sem=far_recv.at[a, p, k],
            device_id={"dp": lax.rem(chip + k, chips) * 2 + core},
            device_id_type=MESH,
        )

    def near(a, p, k):
        x_ref, out_ref = pairs[a]
        owner = lax.rem(chip + chips - k, chips) * 2 + core
        target = out_ref.at[owner, rows(a, p)]
        return pltpu.make_async_remote_copy(
            src_ref=x_ref.at[rows(a, p)] if k == 0 else target,
            dst_ref=target,
            send_sem=near_send.at[a, p, k],
            recv_sem=near_recv.at[a, p, k],
            device_id={"dp": me + 1 - 2 * core},
            device_id_type=MESH,
        )

    def own(a):
        x_ref, out_ref = pairs[a]
        return pltpu.make_async_copy(x_ref, out_ref.at[me], own_sem.at[a])

    arrays = range(len(pairs))

    def greet():
        barrier = pltpu.get_barrier_semaphore()
        for k in range(1, chips):
            pl.semaphore_signal(
                barrier,
                inc=1,
                device_id={"dp": lax.rem(chip + k, chips) * 2 + core},
                device_id_type=MESH,
            )
        pl.semaphore_signal(
            barrier, inc=1, device_id={"dp": me + 1 - 2 * core}, device_id_type=MESH
        )
        return chips

    def start():
        for p in range(gather_parts):
            for a in arrays:
                for k in range(1, chips):
                    far(a, p, k).start()
        for p in range(gather_parts):
            for a in arrays:
                near(a, p, 0).start()
        for a in arrays:
            own(a).start()

    def forward(p):
        for a in arrays:
            for k in range(1, chips):
                far(a, p, k).wait_recv()
                near(a, p, k).start()

    def finish():
        for a in arrays:
            own(a).wait()
            for p in range(gather_parts):
                for k in range(chips):
                    near(a, p, k).wait_recv()
                    near(a, p, k).wait_send()
                    if k:
                        far(a, p, k).wait_send()

    return greet, start, forward, finish


def gather_scratch(arrays, n):
    return [pltpu.SemaphoreType.DMA((arrays,))] + [
        pltpu.SemaphoreType.DMA((arrays, gather_parts, n // 2)) for _ in range(4)
    ]


def gateup_column(e, part, group, hidden):
    return (e // group * 2 * group + part * group + e % group) * hidden


def gather_kernel(n, group, count, *refs):
    x_refs, refs = refs[:count], refs[count:]
    w_ref, refs = (None, refs) if group is None else (refs[0], refs[1:])
    out_refs, refs = refs[:count], refs[count:]
    low_ref, scratch = (None, refs) if group is None else (refs[0], refs[1:])
    greet, start, forward, finish = gather_engine(n, list(zip(x_refs, out_refs)), *scratch)
    pl.semaphore_wait(pltpu.get_barrier_semaphore(), greet())
    start()
    if group is not None:
        depth, hidden = low_ref.shape[0], w_ref.shape[1]
        for e in range(EXPERTS):
            for part in (0, 1):
                at = gateup_column(e, part, group, hidden)
                low_ref[:, at : at + hidden] = w_ref[
                    pl.ds(e * 2 * depth + part, depth, stride=2)
                ].astype(bf16)
    for p in range(gather_parts):
        forward(p)
    finish()


def gather(arrays, w, n, group, barrier_id):
    depth = arrays[0].shape[0]
    whole = pl.BlockSpec(memory_space=pltpu.VMEM)
    shapes = [jax.ShapeDtypeStruct((n,) + x.shape, x.dtype) for x in arrays]
    operands = list(arrays)
    if group is not None:
        operands.append(w)
        shapes.append(jax.ShapeDtypeStruct((depth, w.size // depth), bf16))
    out = pl.pallas_call(
        functools.partial(gather_kernel, n, group, len(arrays)),
        out_shape=shapes,
        in_specs=[whole] * len(operands),
        out_specs=[whole] * len(shapes),
        scratch_shapes=gather_scratch(len(arrays), n),
        compiler_params=pltpu.CompilerParams(
            collective_id=barrier_id, has_side_effects=True, vmem_limit_bytes=24 * 2**20
        ),
    )(*operands)
    count = len(arrays)
    return [t.reshape(n * depth, -1) for t in out[:count]] + list(out[count:])


def gateup_adam_kernel(group, w_ref, m_ref, v_ref, grad_ref, w_out, m_out, v_out, g_ref):
    depth, hidden = grad_ref.shape[0], w_ref.shape[1]
    for e in range(w_ref.shape[0] // (2 * depth)):
        for part in (0, 1):
            at = gateup_column(e, part, group, hidden)
            g_ref[pl.ds(part, depth, stride=2)] = grad_ref[:, at : at + hidden].astype(f32)
        rows = slice(e * 2 * depth, (e + 1) * 2 * depth)
        w_out[rows], m_out[rows], v_out[rows] = adam_update(
            w_ref[rows], m_ref[rows], v_ref[rows], g_ref[...], weight_decay, 0.05
        )


def gateup_adam(w, m, v, grad, group):
    experts, depth, parts, hidden = w.shape
    flat = lambda t: t.reshape(experts * depth * parts, hidden)
    each = 2 * group
    block = pl.BlockSpec((each * depth * parts, hidden), lambda e: (e, 0))
    out = pl.pallas_call(
        functools.partial(gateup_adam_kernel, group),
        grid=(experts // each,),
        in_specs=[block] * 3
        + [pl.BlockSpec((depth, each * parts * hidden), lambda e: (0, e))],
        out_specs=[block] * 3,
        out_shape=[jax.ShapeDtypeStruct((experts * depth * parts, hidden), f32)] * 3,
        scratch_shapes=[pltpu.VMEM((depth * parts, hidden), f32)],
        compiler_params=pltpu.CompilerParams(vmem_limit_bytes=32 * 2**20),
    )(flat(w), flat(m), flat(v), grad)
    return tuple(t.reshape(w.shape) for t in out)


def line_gather_kernel(n, n_dp, x_ref, a_ref, b_ref, o_ref, a_out, b_out, *scratch):
    line, spread_out = scratch[:5], scratch[5:]
    greet, _, slot, finish = line_engine(n, x_ref, o_ref, *line)
    greet_dp, start, forward, finish_dp = gather_engine(
        n_dp, [(a_ref, a_out), (b_ref, b_out)], *spread_out
    )
    peers = greet() + greet_dp()
    pl.semaphore_wait(pltpu.get_barrier_semaphore(), peers)
    start()

    def step(t, carry):
        slot(t)
        return carry

    total = line_steps(n)
    done = 0
    for p in range(gather_parts):
        until = total * (p + 1) // gather_parts
        lax.fori_loop(done, until, step, 0)
        done = until
        forward(p)
    finish()
    finish_dp()


def line_gather(x, a, b, n, n_dp, barrier_id):
    rows, width = x.shape
    whole, anywhere = pl.BlockSpec(memory_space=pltpu.VMEM), pl.BlockSpec(memory_space=pl.ANY)
    o, a_all, b_all = pl.pallas_call(
        functools.partial(line_gather_kernel, n, n_dp),
        out_shape=[jax.ShapeDtypeStruct(x.shape, x.dtype)]
        + [jax.ShapeDtypeStruct((n_dp,) + t.shape, t.dtype) for t in (a, b)],
        in_specs=[whole, anywhere, anywhere],
        out_specs=[whole, anywhere, anywhere],
        scratch_shapes=line_scratch(x.shape, x.dtype) + gather_scratch(2, n_dp),
        compiler_params=pltpu.CompilerParams(
            collective_id=barrier_id, has_side_effects=True, vmem_limit_bytes=24 * 2**20
        ),
        cost_estimate=pl.CostEstimate(
            flops=rows * width, bytes_accessed=100 * rows * width, transcendentals=0
        ),
    )(x, a, b)
    return o, a_all.reshape(-1, a.shape[1]), b_all.reshape(-1, b.shape[1])


def last_kernel(
    n, n_dp, pieces, x_ref, tokens_ref, middle_ref, gain_ref, gain_second_ref, *refs,
):
    weights_refs, refs = refs[:pieces], refs[pieces:]
    last_body(
        n, n_dp, x_ref, tokens_ref, middle_ref, gain_ref, weights_refs, gain_second_ref, *refs
    )


def last_body(
    n, n_dp, x_ref, tokens_ref, middle_ref, gain_ref, weights_refs, gain_second_ref,
    grad_ref, weights_out, gains_out, o_ref, held, send_red, recv_red, send_out, recv_out,
    tokens_v, middle_v, grad_v, in_sem, out_sem, got, w_send, w_recv,
    g_from, g_got, g_send, g_recv, z_from, z_got, z_send, z_recv, acc,
):
    me, line = lax.axis_index("dp"), lax.axis_index("tensor")
    model = x_ref.shape[1]
    rows = x_ref.shape[0] // (2 * line_parts)
    depth = weights_out.shape[0]

    def norm_of(at):
        x = tokens_v[at].astype(f32)
        inverse = lax.rsqrt(jnp.mean(x * x, axis=-1, keepdims=True) + eps_norm)
        return x * inverse, inverse

    def complete(at):
        norm, inverse = norm_of(at)
        grad = o_ref[at].astype(f32) * (gain_ref[0:1] + gain_ref[2:3])
        mean = jnp.mean(grad * norm, axis=-1, keepdims=True)
        grad_v[at] = middle_v[at] + inverse * (grad - norm * mean)

    _, _, slot, finish = line_engine(
        n, x_ref, o_ref, held, send_red, recv_red, send_out, recv_out, complete
    )

    columns, low = [], 0
    for ref in weights_refs:
        columns.append(slice(low, low + ref.shape[2]))
        low += ref.shape[2]
    pieces = range(len(columns))

    def weights_copy(k, j):
        to = lax.rem(me + k, n_dp)
        return pltpu.make_async_remote_copy(
            src_ref=weights_refs[j].at[to], dst_ref=got.at[k, :, columns[j]],
            send_sem=w_send.at[j, k], recv_sem=w_recv.at[j, k],
            device_id={"dp": to}, device_id_type=MESH,
        )

    def gains_copy(k):
        to = lax.rem(me + k, n_dp)
        return pltpu.make_async_remote_copy(
            src_ref=g_from.at[to], dst_ref=g_got.at[k],
            send_sem=g_send.at[k], recv_sem=g_recv.at[k],
            device_id={"dp": to}, device_id_type=MESH,
        )

    def line_copy(k):
        to = lax.rem(line + k, n)
        return pltpu.make_async_remote_copy(
            src_ref=z_from, dst_ref=z_got.at[k],
            send_sem=z_send.at[k], recv_sem=z_recv.at[k],
            device_id={"tensor": to}, device_id_type=MESH,
        )

    def loop(count, act):
        def one(k, carry):
            act(k)
            return carry

        lax.fori_loop(1, count, one, 0)

    load_tokens = pltpu.make_async_copy(tokens_ref, tokens_v, in_sem.at[0])
    load_middle = pltpu.make_async_copy(middle_ref, middle_v, in_sem.at[1])
    load_tokens.start()
    load_middle.start()
    barrier = pltpu.get_barrier_semaphore()

    def greet(axis, place, count):
        loop(
            count,
            lambda k: pl.semaphore_signal(
                barrier, inc=1, device_id={axis: lax.rem(place + k, count)}, device_id_type=MESH
            ),
        )

    greet("dp", me, n_dp)
    greet("tensor", line, n)
    pl.semaphore_wait(barrier, n_dp + n - 2)
    for j in pieces:
        loop(n_dp, lambda k: weights_copy(k, j).start())
    acc[...] = jnp.zeros_like(acc)
    load_tokens.wait()
    load_middle.wait()

    def step(t, carry):
        slot(t)

        @pl.when(t < line_parts)
        def _():
            for half in (0, 1):
                at = pl.ds(pl.multiple_of((half * line_parts + t) * rows, 16), rows)
                norm, _ = norm_of(at)
                term = x_ref[at].astype(f32) * norm
                acc[...] += jnp.sum(term.reshape(rows // 8, 8, model), axis=0)

        return carry

    total = line_steps(n)
    lax.fori_loop(0, line_parts, step, 0)
    width = g_from.shape[2]
    for p in range(n_dp):
        moved = acc[...] if p == 0 else pltpu.roll(acc[...], model - p * depth, 1)
        g_from[p, :8] = moved[:, :width]
        moved = gain_second_ref[...] if p == 0 else pltpu.roll(
            gain_second_ref[...], model - p * depth, 1
        )
        g_from[p, 8:] = jnp.where(line == 0, moved[:, :width], 0.0)
    loop(n_dp, lambda k: gains_copy(k).start())
    late = min(line_parts + 4, total)
    lax.fori_loop(line_parts, late, step, 0)
    loop(n_dp, lambda k: gains_copy(k).wait_recv())
    z_from[...] = lax.fori_loop(1, n_dp, lambda k, t: t + g_got[k], g_from[me])
    loop(n, lambda k: line_copy(k).start())
    for j in pieces:
        loop(n_dp, lambda k: weights_copy(k, j).wait_recv())
    lax.fori_loop(late, total, step, 0)
    size = 32

    def add(b, carry):
        at = pl.ds(pl.multiple_of(b * size, 16), size)
        for j, ref in enumerate(weights_refs):
            weights_out[at, columns[j]] = lax.fori_loop(
                1,
                n_dp,
                lambda k, t: t + got[k, at, columns[j]].astype(f32),
                ref[me, at].astype(f32),
            )
        return carry

    every = pltpu.make_async_copy(grad_v, grad_ref, out_sem)
    every.start()
    lax.fori_loop(0, depth // size, add, 0)
    loop(n, lambda k: line_copy(k).wait_recv())
    gains_out[...] = lax.fori_loop(1, n, lambda k, t: t + z_got[k], z_from[...])
    finish()
    for j in pieces:
        loop(n_dp, lambda k: weights_copy(k, j).wait_send())
    loop(n_dp, lambda k: gains_copy(k).wait_send())
    loop(n, lambda k: line_copy(k).wait_send())
    every.wait()


def last_call(x, tokens, middle, gain, weights, gain_second, n, n_dp, barrier_id):
    count, model = x.shape
    depth, width = model // n_dp, sum(w.shape[1] for w in weights)
    lanes = -(-depth // 128) * 128
    whole, anywhere = pl.BlockSpec(memory_space=pltpu.VMEM), pl.BlockSpec(memory_space=pl.ANY)
    dma = pltpu.SemaphoreType.DMA
    grad, weights, gains = pl.pallas_call(
        functools.partial(last_kernel, n, n_dp, len(weights)),
        out_shape=[
            jax.ShapeDtypeStruct((count, model), f32),
            jax.ShapeDtypeStruct((depth, width), f32),
            jax.ShapeDtypeStruct((16, lanes), f32),
        ],
        in_specs=[whole, anywhere, anywhere, whole, whole] + [whole] * len(weights),
        out_specs=[anywhere, whole, whole],
        scratch_shapes=[pltpu.VMEM(x.shape, bf16)]
        + line_scratch(x.shape, x.dtype)
        + [
            pltpu.VMEM((count, model), bf16),
            pltpu.VMEM((count, model), f32),
            pltpu.VMEM((count, model), f32),
            dma((2,)),
            dma,
            pltpu.VMEM((n_dp, depth, width), bf16),
            dma((len(weights), n_dp)),
            dma((len(weights), n_dp)),
            pltpu.VMEM((n_dp, 16, lanes), f32),
            pltpu.VMEM((n_dp, 16, lanes), f32),
            dma((n_dp,)),
            dma((n_dp,)),
            pltpu.VMEM((16, lanes), f32),
            pltpu.VMEM((n, 16, lanes), f32),
            dma((n,)),
            dma((n,)),
            pltpu.VMEM((8, model), f32),
        ],
        compiler_params=pltpu.CompilerParams(
            collective_id=barrier_id, has_side_effects=True, vmem_limit_bytes=56 * 2**20
        ),
        cost_estimate=pl.CostEstimate(
            flops=count * model, bytes_accessed=2**20, transcendentals=0
        ),
    )(x, tokens, middle, gain, gain_second, *(w.reshape(n_dp, depth, -1) for w in weights))
    gains = jnp.sum(gains.reshape(2, 8, lanes), axis=1)[:, :depth]
    return grad, weights, gains


def expert_grads_kernel(
    n, shape, x_ref, rows_ref, outgrad_ref, start_ref, rest_ref,
    hidden_ref, active_ref, active_rows_ref,
    o_ref, gateup_grad_ref, down_grad_ref, mixture_ref, rows_t, outgrad_t, o_sem, sum_ref, *scratch,
):
    mixture_steps, gateup_steps, down_steps = shape
    i = pl.program_id(0)
    steps = sum(shape)
    _, begin, slot, finish = line_engine(n, x_ref, sum_ref, *scratch)
    total = line_steps(n)
    each = -(-total // steps)
    pl.when(i == 0)(begin)

    def slots(low, high):
        def one(j, carry):
            t = i * each + j
            pl.when(t < total)(lambda: slot(t))
            return carry

        lax.fori_loop(low, high, one, 0)

    slots(0, 1)

    @pl.when(i < mixture_steps)
    def _():
        half = start_ref.shape[1]
        mixture_ref[...] = (
            lax.dot_general(
                active_rows_ref[:, :half], start_ref[...], nt, preferred_element_type=f32
            )
            + lax.dot_general(
                active_rows_ref[:, half:], rest_ref[...], nt, preferred_element_type=f32
            )
        ).astype(bf16)
        size = active_rows_ref.shape[0]
        columns = pl.ds(pl.multiple_of(i * size, size), size)
        rows_t[:, columns] = rows_ref[...].T
        outgrad_t[:, columns] = outgrad_ref[...].T

    @pl.when((i >= mixture_steps) & (i < mixture_steps + gateup_steps))
    def _():
        gateup_grad_ref[...] = jnp.dot(
            rows_t[...], hidden_ref[...], preferred_element_type=f32
        ).astype(bf16)

    @pl.when(i >= mixture_steps + gateup_steps)
    def _():
        down_grad_ref[...] = jnp.dot(
            outgrad_t[...], active_ref[...], preferred_element_type=f32
        ).astype(bf16)

    slots(1, each)

    @pl.when(i == steps - 1)
    def _():
        copy = pltpu.make_async_copy(sum_ref, o_ref, o_sem)
        copy.start()
        finish()
        copy.wait()


def expert_grads_call(
    x, rows, outgrad, down_start, down_rest, hidden, active, n, barrier_id
):
    tokens, model = rows.shape
    block, tile = min(512, active.shape[1]), 256
    c, a, b = shape = (tokens // tile, hidden.shape[1] // block, active.shape[1] // block)
    whole = pl.BlockSpec(memory_space=pltpu.VMEM)
    first = lambda i: (jnp.minimum(i, c - 1), 0)
    second = lambda i: (0, jnp.clip(i - c, 0, a - 1))
    third = lambda i: (0, jnp.clip(i - c - a, 0, b - 1))
    return pl.pallas_call(
        functools.partial(expert_grads_kernel, n, shape),
        grid=(a + b + c,),
        in_specs=[
            whole,
            pl.BlockSpec((tile, model), first),
            pl.BlockSpec((tile, model), first),
            whole,
            whole,
            pl.BlockSpec((tokens, block), second),
            pl.BlockSpec((tokens, block), third),
            pl.BlockSpec((tile, active.shape[1]), first),
        ],
        out_specs=[
            pl.BlockSpec(memory_space=pl.ANY),
            pl.BlockSpec((model, block), second),
            pl.BlockSpec((model, block), third),
            pl.BlockSpec((tile, model), first),
        ],
        out_shape=[
            jax.ShapeDtypeStruct(x.shape, x.dtype),
            jax.ShapeDtypeStruct((model, hidden.shape[1]), bf16),
            jax.ShapeDtypeStruct((model, active.shape[1]), bf16),
            jax.ShapeDtypeStruct((tokens, model), bf16),
        ],
        scratch_shapes=[pltpu.VMEM((model, tokens), bf16)] * 2
        + [pltpu.SemaphoreType.DMA, pltpu.VMEM(x.shape, x.dtype)]
        + line_scratch(x.shape, x.dtype),
        compiler_params=pltpu.CompilerParams(
            collective_id=barrier_id, has_side_effects=True, vmem_limit_bytes=58 * 2**20
        ),
        cost_estimate=pl.CostEstimate(
            flops=2 * tokens * model * (hidden.shape[1] + 2 * active.shape[1]),
            bytes_accessed=10 * tokens * model,
            transcendentals=0,
        ),
    )(x, rows, outgrad, down_start, down_rest, hidden, active, active)


def expert_kernel(group, steps, rows_ref, outgrad_ref, gates_ref, gu_ref, start_ref, rest_ref,
                  active_ref, hidden_ref, gate_grad_ref, down_ref):
    step = pl.program_id(0)
    tile = 256
    width = gu_ref.shape[1] // 2
    hidden = width // group
    lane = lax.broadcasted_iota(jnp.int32, (tile, 128), 1)
    column = lax.broadcasted_iota(jnp.int32, (tile, width), 1)

    @pl.when(step == 0)
    def _():
        gate_grad_ref[...] = jnp.zeros_like(gate_grad_ref)

    @pl.when(step < steps // 2)
    def _():
        down_ref[...] = start_ref[...]

    @pl.when(step >= steps // 2)
    def _():
        down_ref[...] = rest_ref[...]

    def one(t, carry):
        at = pl.ds(pl.multiple_of(t * tile, tile), tile)
        h = jnp.dot(rows_ref[at], gu_ref[...], preferred_element_type=f32)
        back = jnp.dot(outgrad_ref[at], down_ref[...], preferred_element_type=f32)
        gates = gates_ref[at]
        wide = jnp.zeros((tile, width), f32)
        for j in range(group):
            g = jnp.sum(jnp.where(lane == step * group + j, gates, 0.0), axis=1, keepdims=True)
            wide = g + wide if group == 1 else jnp.where(column // hidden == j, g, wide)
        gate, up = h[:, :width], h[:, width:]
        sig = 1.0 / (1.0 + jnp.exp(-gate))
        silu = gate * sig
        active = (silu * up).astype(bf16).astype(f32)
        active_ref[at] = (active * wide).astype(bf16)
        product = active * back
        grads = gate_grad_ref[at]
        for j in range(group):
            s = jnp.sum(jnp.where(column // hidden == j, product, 0.0), axis=1, keepdims=True)
            grads = jnp.where(lane == step * group + j, s, grads)
        gate_grad_ref[at] = grads
        back = back * wide
        hidden_ref[at, :width] = (back * up * sig * (1.0 + gate * (1.0 - sig))).astype(bf16)
        hidden_ref[at, width:] = (back * silu).astype(bf16)
        return carry

    lax.fori_loop(0, rows_ref.shape[0] // tile, one, 0)


def expert_call(rows, outgrad, gates, gu, down_start, down_rest, group):
    tokens, model = rows.shape
    width = gu.shape[1] // (EXPERTS // group)
    steps = EXPERTS // group
    return pl.pallas_call(
        functools.partial(expert_kernel, group, steps),
        grid=(steps,),
        in_specs=[
            pl.BlockSpec((tokens, model), lambda p: (0, 0)),
            pl.BlockSpec((tokens, model), lambda p: (0, 0)),
            pl.BlockSpec((tokens, 128), lambda p: (0, 0)),
            pl.BlockSpec((model, width), lambda p: (0, p)),
            pl.BlockSpec((model, width // 2), lambda p: (0, jnp.minimum(p, steps // 2 - 1))),
            pl.BlockSpec((model, width // 2), lambda p: (0, jnp.maximum(p - steps // 2, 0))),
        ],
        out_specs=[
            pl.BlockSpec((tokens, width // 2), lambda p: (0, p)),
            pl.BlockSpec((tokens, width), lambda p: (0, p)),
            pl.BlockSpec((tokens, 128), lambda p: (0, 0)),
        ],
        out_shape=[
            jax.ShapeDtypeStruct((tokens, steps * width // 2), bf16),
            jax.ShapeDtypeStruct((tokens, steps * width), bf16),
            jax.ShapeDtypeStruct((tokens, 128), f32),
        ],
        scratch_shapes=[pltpu.VMEM((model, width // 2), bf16)],
        compiler_params=pltpu.CompilerParams(vmem_limit_bytes=48 * 2**20),
        cost_estimate=pl.CostEstimate(
            flops=2 * tokens * model * steps * width * 3 // 2,
            bytes_accessed=2 * (model * steps * width * 3 // 2 + tokens * steps * width * 3 // 2),
            transcendentals=tokens * steps * width // 2,
        ),
    )(rows, outgrad, gates, gu, down_start, down_rest)


def turn(u, cosine, sine):
    lane = lax.broadcasted_iota(jnp.int32, u.shape, 1) % HEAD_DIM
    other = jnp.where(lane < HEAD_DIM // 2, pltpu.roll(u, 96, 1), pltpu.roll(u, 32, 1))
    return u * cosine + other * sine


def table_parts(me, prompt_total):
    return (
        (0, PROMPT_DEV, pl.multiple_of(me * PROMPT_DEV, PROMPT_DEV)),
        (PROMPT_DEV, CONT, prompt_total),
    )


def project_kernel(x_ref, gain_ref, w_ref, cos_ref, sin_ref, normed_ref, q_ref, kv_ref):
    x = x_ref[...].astype(f32)
    inverse = lax.rsqrt(jnp.mean(x * x, axis=-1, keepdims=True) + eps_norm)
    normed = (x * inverse * (gain_ref[0:1] + gain_ref[2:3])).astype(bf16)
    normed_ref[...] = normed
    mixed = jnp.dot(normed, w_ref[...], preferred_element_type=f32)
    block = [mixed[:, c * 128 : (c + 1) * 128] for c in range(5)]
    low = lax.broadcasted_iota(jnp.int32, block[0].shape, 1) < HEAD_DIM
    turned = [
        block[0],
        jnp.where(low, block[1], block[2]),
        block[3],
        jnp.where(low, pltpu.roll(block[1], HEAD_DIM, 1), pltpu.roll(block[4], HEAD_DIM, 1)),
    ]
    kv_ref[:, 128:] = jnp.where(low, block[2], block[4]).astype(bf16)
    prompt_total = cos_ref.shape[0] - CONT
    for start, rows, at in table_parts(lax.axis_index("dp"), prompt_total):
        cosine, sine = cos_ref[pl.ds(at, rows)], sin_ref[pl.ds(at, rows)]
        for c, u in enumerate(turned):
            u = turn(u[start : start + rows], cosine, sine).astype(bf16)
            if c < 3:
                q_ref[start : start + rows, c * 128 : (c + 1) * 128] = u
            else:
                kv_ref[start : start + rows, :128] = u


def project_call(tokens, gain, w, cosine, sine):
    count, model = tokens.shape
    width = w.shape[1]
    row = lambda n: pl.BlockSpec((TOK_MB, n), lambda i: (i, 0))
    fixed = lambda t: pl.BlockSpec(t.shape, lambda i: (0, 0))
    return pl.pallas_call(
        project_kernel,
        grid=(MICRO,),
        in_specs=[row(model), fixed(gain), fixed(w), fixed(cosine), fixed(sine)],
        out_specs=[row(model), row(width - 256), row(256)],
        out_shape=[
            jax.ShapeDtypeStruct((count, model), bf16),
            jax.ShapeDtypeStruct((count, width - 256), bf16),
            jax.ShapeDtypeStruct((count, 256), bf16),
        ],
        compiler_params=pltpu.CompilerParams(vmem_limit_bytes=48 * 2**20),
        cost_estimate=pl.CostEstimate(
            flops=2 * count * model * width, bytes_accessed=6 * count * model, transcendentals=count
        ),
    )(tokens, gain, w, cosine, sine)


def norm_rows(x_ref, b_ref):
    middle = x_ref[...].astype(f32) + b_ref[...].astype(f32)
    inverse = lax.rsqrt(jnp.mean(middle * middle, axis=-1, keepdims=True) + eps_norm)
    return middle * inverse, inverse


def route_kernel(x_ref, b_ref, gain_ref, router_ref, routes_ref, normed_ref, gates_ref):
    norm, _ = norm_rows(x_ref, b_ref)
    normed = (norm * (gain_ref[1:2] + gain_ref[3:4])).astype(bf16)
    normed_ref[...] = normed
    logits = jnp.dot(normed, router_ref[...], preferred_element_type=f32)
    lane = lax.broadcasted_iota(jnp.int32, logits.shape, 1)
    routes = routes_ref[...]
    named = lane == routes[:, 0:1]
    for k in range(1, TOPK):
        named = named | (lane == routes[:, k : k + 1])
    top = jnp.max(jnp.where(named, logits, -1e30), axis=-1, keepdims=True)
    weights = jnp.where(named, jnp.exp(jnp.where(named, logits, top) - top), 0.0)
    gates_ref[...] = weights / jnp.sum(weights, axis=-1, keepdims=True)


def route_call(tokens, branch, gain, router, routes):
    count, model = tokens.shape
    tile = 256
    row = lambda n: pl.BlockSpec((tile, n), lambda i: (i, 0))
    fixed = lambda t: pl.BlockSpec(t.shape, lambda i: (0, 0))
    return pl.pallas_call(
        route_kernel,
        grid=(count // tile,),
        in_specs=[row(model), row(model), fixed(gain), fixed(router), row(TOPK)],
        out_specs=[row(model), row(128)],
        out_shape=[
            jax.ShapeDtypeStruct((count, model), bf16),
            jax.ShapeDtypeStruct((count, 128), f32),
        ],
        compiler_params=pltpu.CompilerParams(vmem_limit_bytes=32 * 2**20),
    )(tokens, branch, gain, router, routes)


def middle_back_kernel(
    x_ref, b_ref, summed_ref, gates_ref, outgrad_ref, gain_ref, router_ref, outproj_ref,
    middle_ref, own_ref, attended_ref, logits_ref, gain_out,
):
    norm, inverse = norm_rows(x_ref, b_ref)
    model = x_ref.shape[1]
    gates = gates_ref[...]
    gate_grad = summed_ref[:, model:].astype(f32)
    chosen = gates * (gate_grad - jnp.sum(gates * gate_grad, axis=-1, keepdims=True))
    logits = chosen.astype(bf16)
    logits_ref[...] = logits
    grad = summed_ref[:, :model].astype(f32) + lax.dot_general(
        logits, router_ref[...], nt, preferred_element_type=f32
    )
    term = (grad * norm).reshape(-1, 8, model).sum(axis=0)

    @pl.when(pl.program_id(0) == 0)
    def _():
        gain_out[...] = jnp.zeros_like(gain_out)

    gain_out[...] += term
    grad = grad * (gain_ref[1:2] + gain_ref[3:4])
    mean = jnp.mean(grad * norm, axis=-1, keepdims=True)
    middle = outgrad_ref[...].astype(f32) + inverse * (grad - norm * mean)
    middle_ref[...] = middle
    own = middle.astype(bf16)
    own_ref[...] = own
    attended_ref[...] = jnp.dot(own, outproj_ref[...], preferred_element_type=f32).astype(bf16)


def middle_back_call(tokens, branch, summed, gates, outgrad, gain, router, outproj):
    count, model = tokens.shape
    tile = 256
    row = lambda n: pl.BlockSpec((tile, n), lambda i: (i, 0))
    fixed = lambda t: pl.BlockSpec(t.shape, lambda i: (0, 0))
    return pl.pallas_call(
        middle_back_kernel,
        grid=(count // tile,),
        in_specs=[
            row(model),
            row(model),
            row(model + 128),
            row(128),
            row(model),
            fixed(gain),
            fixed(router),
            fixed(outproj),
        ],
        out_specs=[
            row(model),
            row(model),
            row(outproj.shape[1]),
            row(128),
            pl.BlockSpec((8, model), lambda i: (0, 0)),
        ],
        out_shape=[
            jax.ShapeDtypeStruct((count, model), f32),
            jax.ShapeDtypeStruct((count, model), bf16),
            jax.ShapeDtypeStruct((count, outproj.shape[1]), bf16),
            jax.ShapeDtypeStruct((count, 128), bf16),
            jax.ShapeDtypeStruct((8, model), f32),
        ],
        compiler_params=pltpu.CompilerParams(vmem_limit_bytes=48 * 2**20),
    )(tokens, branch, summed, gates, outgrad, gain, router, outproj)


def head_places(heads):
    return [(h // GROUP, h % 2, h // 2) for h in range(heads)]


def spread(kv, scale):
    lane = lax.broadcasted_iota(jnp.int32, kv.shape, 1)
    kv = kv * scale
    turned = pltpu.roll(kv, HEAD_DIM, 1)
    first = lane < HEAD_DIM
    zero = jnp.zeros_like(kv)
    return {
        (0, 0): jnp.where(first, kv, zero).astype(bf16),
        (0, 1): jnp.where(first, zero, turned).astype(bf16),
        (1, 0): jnp.where(first, turned, zero).astype(bf16),
        (1, 1): jnp.where(first, zero, kv).astype(bf16),
    }


def row_tiles(prompt_total):
    tiles = [(0, PROMPT_DEV, prompt_total)]
    for start in range(0, CONT, 256):
        tiles.append((PROMPT_DEV + start, 256, prompt_total + start + 256))
    return tiles


def meet(me, n):
    barrier = pltpu.get_barrier_semaphore()

    def greet(k, carry):
        pl.semaphore_signal(
            barrier, inc=1, device_id={"dp": lax.rem(me + k, n)}, device_id_type=MESH
        )
        return carry

    lax.fori_loop(1, n, greet, 0)
    pl.semaphore_wait(barrier, n - 1)


def load_spread(m, all_ref, kv_ref, k_ref, v_ref, kt_ref=None):
    total = all_ref.shape[1]
    own = pl.ds(pl.multiple_of(m * TOK_MB + PROMPT_DEV, 16), CONT)
    for low, high, rows in ((0, total, all_ref[m]), (total, total + CONT, kv_ref[own])):
        keys = spread(rows[:, :128].astype(f32), HEAD_DIM**-0.5)
        values = spread(rows[:, 128:].astype(f32), 1.0)
        for i, place in enumerate(keys):
            k_ref[i, low:high] = keys[place]
            v_ref[i, low:high] = values[place]
            if kt_ref is not None:
                kt_ref[i, :, low:high] = keys[place].astype(f32).T.astype(bf16)
    return {place: i for i, place in enumerate(keys)}


def attention_kernel(
    heads, n, q_ref, kv_ref, w_ref, o_ref, lse_ref, all_ref, w_out, k_ref, v_ref, send, recv,
    *spread_out,
):
    _, start_w, forward_w, finish_w = gather_engine(n, [(w_ref, w_out)], *spread_out)
    prompt_total = all_ref.shape[1]
    me = lax.axis_index("dp")

    def piece(m, k):
        rows = all_ref.at[m, pl.ds(pl.multiple_of(me * PROMPT_DEV, PROMPT_DEV), PROMPT_DEV)]
        return pltpu.make_async_remote_copy(
            src_ref=rows,
            dst_ref=rows,
            send_sem=send.at[m, k],
            recv_sem=recv.at[m, k],
            device_id={"dp": lax.rem(me + k, n)},
            device_id_type=MESH,
        )

    for m in range(MICRO):
        all_ref[m, pl.ds(pl.multiple_of(me * PROMPT_DEV, PROMPT_DEV), PROMPT_DEV)] = kv_ref[
            m * TOK_MB : m * TOK_MB + PROMPT_DEV
        ]
    meet(me, n)

    def every(m, act):
        def one(k, carry):
            act(piece(m, k))
            return carry

        lax.fori_loop(1, n, one, 0)

    for m in range(MICRO):
        every(m, lambda copy: copy.start())
    start_w()

    def micro(m, carry):
        every(m, lambda copy: copy.wait_recv())
        index = load_spread(m, all_ref, kv_ref, k_ref, v_ref)
        lane = lax.broadcasted_iota(jnp.int32, (1, 128), 1)
        for start, rows, length in row_tiles(prompt_total):
            at = pl.ds(pl.multiple_of(m * TOK_MB + start, 128), rows)
            row = lax.broadcasted_iota(jnp.int32, (rows, 1), 0)
            if start == 0:
                masked = 0
                reach = row + me * PROMPT_DEV
            else:
                masked = length - 256
                reach = row
            column = lax.broadcasted_iota(jnp.int32, (rows, length - masked), 1)
            lse = jnp.zeros((rows, 128), f32)
            pair_out = None
            for h, (kv, half, pair) in enumerate(head_places(heads)):
                q = q_ref[at, pair * 128 : (pair + 1) * 128]
                i = index[kv, half]
                tail = lax.dot_general(q, k_ref[i, masked:length], nt, preferred_element_type=f32)
                tail = jnp.where(column <= reach, tail, -1e30)
                top = jnp.max(tail, axis=1, keepdims=True)
                if masked:
                    head = lax.dot_general(q, k_ref[i, :masked], nt, preferred_element_type=f32)
                    top = jnp.maximum(top, jnp.max(head, axis=1, keepdims=True))
                    p_head = jnp.exp(head - top)
                p_tail = jnp.exp(tail - top)
                total = jnp.sum(p_tail, axis=1, keepdims=True)
                out = jnp.dot(
                    p_tail.astype(bf16), v_ref[i, masked:length], preferred_element_type=f32
                )
                if masked:
                    total = total + jnp.sum(p_head, axis=1, keepdims=True)
                    out = out + jnp.dot(
                        p_head.astype(bf16), v_ref[i, :masked], preferred_element_type=f32
                    )
                out = out / total
                lse = jnp.where(lane == h, top + jnp.log(total), lse)
                if half == 0:
                    pair_out = out
                else:
                    o_ref[at, pair * 128 : (pair + 1) * 128] = (pair_out + out).astype(bf16)
            lse_ref[m, :, start : start + rows] = lse.T[:8]
        return carry

    lax.fori_loop(0, MICRO, micro, 0)
    for p in range(gather_parts):
        forward_w(p)
    for m in range(MICRO):
        every(m, lambda copy: copy.wait_send())
    finish_w()


def attention_call(q, kv, w, n):
    count, width = q.shape
    keys = PROMPT_DEV * n + CONT
    heads = width // HEAD_DIM
    whole = pl.BlockSpec(memory_space=pltpu.VMEM)
    return pl.pallas_call(
        functools.partial(attention_kernel, heads, n),
        in_specs=[whole] * 2 + [pl.BlockSpec(memory_space=pl.ANY)],
        out_specs=[whole] * 3 + [pl.BlockSpec(memory_space=pl.ANY)],
        out_shape=[
            jax.ShapeDtypeStruct((count, width), bf16),
            jax.ShapeDtypeStruct((MICRO, 8, TOK_MB), f32),
            jax.ShapeDtypeStruct((MICRO, PROMPT_DEV * n, 256), bf16),
            jax.ShapeDtypeStruct((n,) + w.shape, w.dtype),
        ],
        scratch_shapes=[
            pltpu.VMEM((4, keys, 128), bf16),
            pltpu.VMEM((4, keys, 128), bf16),
            pltpu.SemaphoreType.DMA((MICRO, n)),
            pltpu.SemaphoreType.DMA((MICRO, n)),
        ]
        + gather_scratch(1, n),
        compiler_params=pltpu.CompilerParams(
            collective_id=3, has_side_effects=True, vmem_limit_bytes=48 * 2**20
        ),
        cost_estimate=pl.CostEstimate(
            flops=16 * count * keys * width,
            bytes_accessed=8 * count * width,
            transcendentals=count * keys * heads,
        ),
    )(q, kv, w)


def attention_back_kernel(
    heads, n, q_ref, kv_ref, all_ref, do_ref, o_ref, lse_ref,
    cos_ref, sin_ref,
    grad_ref, k_ref, v_ref, kt_ref, dk_ref, dv_ref, sent_ref, got_ref, send, recv,
):
    prompt_total = all_ref.shape[1]
    me = lax.axis_index("dp")

    def put_both(at, dk, dv):
        low = lax.broadcasted_iota(jnp.int32, dk.shape, 1) < HEAD_DIM
        dk = pltpu.roll(dk, HEAD_DIM, 1)
        second = grad_ref[at, 128:256].astype(f32)
        grad_ref[at, 128:256] = jnp.where(low, second, dk).astype(bf16)
        grad_ref[at, 256:384] = jnp.where(low, dv, second).astype(bf16)
        grad_ref[at, 512:640] = jnp.where(low, dk, dv).astype(bf16)

    def piece(m, k):
        to = lax.rem(me + k, n)
        return pltpu.make_async_remote_copy(
            src_ref=sent_ref.at[m, pl.ds(pl.multiple_of(to * PROMPT_DEV, PROMPT_DEV), PROMPT_DEV)],
            dst_ref=got_ref.at[m, k],
            send_sem=send.at[m, k],
            recv_sem=recv.at[m, k],
            device_id={"dp": to},
            device_id_type=MESH,
        )

    def every(m, act):
        def one(k, carry):
            act(piece(m, k))
            return carry

        lax.fori_loop(1, n, one, 0)

    meet(me, n)
    half_rows = (
        lax.broadcasted_iota(jnp.int32, (8, 128), 1) // HEAD_DIM
        == lax.broadcasted_iota(jnp.int32, (8, 128), 0)
    ).astype(f32)

    def micro(m, carry):
        index = load_spread(m, all_ref, kv_ref, k_ref, v_ref, kt_ref)
        dk_ref[...] = jnp.zeros_like(dk_ref)
        dv_ref[...] = jnp.zeros_like(dv_ref)
        for start, rows, length in row_tiles(prompt_total):
            at = pl.ds(pl.multiple_of(m * TOK_MB + start, 128), rows)
            inner = slice(start, start + rows)
            column = lax.broadcasted_iota(jnp.int32, (1, rows), 1)
            if start == 0:
                masked = 0
                reach = column + me * PROMPT_DEV
            else:
                masked = length - 256
                reach = column
            key = lax.broadcasted_iota(jnp.int32, (length - masked, rows), 0)
            back = None
            for h, (kv, half, pair) in enumerate(head_places(heads)):
                lanes = slice(pair * 128, (pair + 1) * 128)
                i = index[kv, half]
                q, do = q_ref[at, lanes], do_ref[at, lanes]
                if half == 0:
                    delta_pair = lax.dot_general(
                        half_rows,
                        do.astype(f32) * o_ref[at, lanes].astype(f32),
                        nt,
                        precision=lax.Precision.HIGHEST,
                        preferred_element_type=f32,
                    )
                delta = delta_pair[half : half + 1]
                lse = lse_ref[m, h : h + 1, inner]
                for low, high in ((0, masked), (masked, length)):
                    if low == high:
                        continue
                    s = lax.dot_general(k_ref[i, low:high], q, nt, preferred_element_type=f32)
                    if low == masked:
                        s = jnp.where(key <= reach, s, -1e30)
                    p = jnp.exp(s - lse)
                    dp_ = lax.dot_general(v_ref[i, low:high], do, nt, preferred_element_type=f32)
                    ds = (p * (dp_ - delta)).astype(bf16)
                    dv_ref[i, low:high] += jnp.dot(
                        p.astype(bf16), do, preferred_element_type=f32
                    )
                    dk_ref[i, low:high] += jnp.dot(ds, q, preferred_element_type=f32)
                    term = jnp.dot(kt_ref[i, :, low:high], ds, preferred_element_type=f32)
                    back = term if back is None else back + term
                if half == 1:
                    if start == 0:
                        table = pl.ds(pl.multiple_of(me * PROMPT_DEV, PROMPT_DEV), rows)
                    else:
                        table = pl.ds(prompt_total + start - PROMPT_DEV, rows)
                    to = (0, 1, 3)[pair] * 128
                    grad_ref[at, to : to + 128] = turn(
                        back.T, cos_ref[table], -sin_ref[table]
                    ).astype(bf16)
                    back = None
        lane = lax.broadcasted_iota(jnp.int32, (dk_ref.shape[1], 128), 1)

        def joined(acc):
            get = lambda place: acc[index[place]]
            return jnp.where(
                lane < HEAD_DIM,
                get((0, 0)) + pltpu.roll(get((0, 1)), HEAD_DIM, 1),
                get((1, 1)) + pltpu.roll(get((1, 0)), HEAD_DIM, 1),
            )

        dk = turn(joined(dk_ref) * HEAD_DIM**-0.5, cos_ref[...], -sin_ref[...])
        dv = joined(dv_ref)
        sent_ref[m, :, :128] = dk[:prompt_total].astype(bf16)
        sent_ref[m, :, 128:] = dv[:prompt_total].astype(bf16)
        every(m, lambda copy: copy.start())
        own = pl.ds(pl.multiple_of(m * TOK_MB + PROMPT_DEV, 128), CONT)
        put_both(own, dk[prompt_total:], dv[prompt_total:])
        return carry

    lax.fori_loop(0, MICRO, micro, 0)

    def collect(m, carry):
        every(m, lambda copy: copy.wait_recv())
        own = sent_ref[m, pl.ds(pl.multiple_of(me * PROMPT_DEV, PROMPT_DEV), PROMPT_DEV)]
        total = lax.fori_loop(
            1, n, lambda k, t: t + got_ref[m, k].astype(f32), own.astype(f32)
        )
        at = pl.ds(pl.multiple_of(m * TOK_MB, 128), PROMPT_DEV)
        put_both(at, total[:, :128], total[:, 128:])
        every(m, lambda copy: copy.wait_send())
        return carry

    lax.fori_loop(0, MICRO, collect, 0)


def attention_back_call(q, kv, prompts, do, o, lse, cosine, sine, n):
    count, width = q.shape
    keys = prompts.shape[1] + CONT
    heads = width // HEAD_DIM
    whole = pl.BlockSpec(memory_space=pltpu.VMEM)
    return pl.pallas_call(
        functools.partial(attention_back_kernel, heads, n),
        in_specs=[whole] * 8,
        out_specs=whole,
        out_shape=jax.ShapeDtypeStruct((count, width + 256), bf16),
        scratch_shapes=[
            pltpu.VMEM((4, keys, 128), bf16),
            pltpu.VMEM((4, keys, 128), bf16),
            pltpu.VMEM((4, 128, keys), bf16),
            pltpu.VMEM((4, keys, 128), f32),
            pltpu.VMEM((4, keys, 128), f32),
            pltpu.VMEM((MICRO, prompts.shape[1], 256), bf16),
            pltpu.VMEM((MICRO, n, PROMPT_DEV, 256), bf16),
            pltpu.SemaphoreType.DMA((MICRO, n)),
            pltpu.SemaphoreType.DMA((MICRO, n)),
        ],
        compiler_params=pltpu.CompilerParams(
            collective_id=4, has_side_effects=True, vmem_limit_bytes=56 * 2**20
        ),
        cost_estimate=pl.CostEstimate(
            flops=40 * count * keys * width,
            bytes_accessed=12 * count * width,
            transcendentals=count * keys * heads,
        ),
    )(q, kv, prompts, do, o, lse, cosine, sine)


def attend(queries, keys_all, values_all, allowed):
    factor = HEAD_DIM ** (-0.5)
    scores = jnp.einsum("tkgd,skd->kgts", queries, keys_all, preferred_element_type=f32) * factor
    scores = jnp.where(allowed, scores, -1e30)
    row_max = jnp.max(scores, axis=-1, keepdims=True)
    exponent = jnp.exp(scores - row_max)
    softened = exponent / jnp.sum(exponent, axis=-1, keepdims=True)
    soft_low = softened.astype(bf16)
    attended = jnp.einsum("kgts,skd->tkgd", soft_low, values_all, preferred_element_type=f32)
    return attended.astype(bf16), softened, soft_low


def attend_back(queries, keys_all, values_all, softened, soft_low, attended_grad):
    factor = HEAD_DIM ** (-0.5)
    soft_grad = jnp.einsum("tkgd,skd->kgts", attended_grad, values_all, preferred_element_type=f32)
    values_grad = jnp.einsum("kgts,tkgd->skd", soft_low, attended_grad, preferred_element_type=f32)
    row_delta = jnp.sum(softened * soft_grad, axis=-1, keepdims=True)
    scores_grad = (softened * (soft_grad - row_delta)).astype(bf16)
    queries_grad = (
        jnp.einsum("kgts,skd->tkgd", scores_grad, keys_all, preferred_element_type=f32) * factor
    )
    keys_grad = (
        jnp.einsum("kgts,tkgd->skd", scores_grad, queries, preferred_element_type=f32) * factor
    )
    return queries_grad, keys_grad, values_grad


def shards(
    tokens, cotangent, routes,
    inproj_weight, inproj_first, inproj_second,
    outproj_weight, outproj_first, outproj_second,
    gateup_weight, gateup_first, gateup_second,
    down_weight, down_first, down_second,
    router_weight, router_first, router_second,
    gains, gains_first, gains_second,
):
    n_dp = lax.axis_size("dp")
    n_tensor = lax.axis_size("tensor")
    depth = inproj_weight.shape[0]
    kv_local = inproj_weight.shape[1]
    hidden = down_weight.shape[1]
    group = max(1, 256 // hidden)
    groups = EXPERTS // group
    in_width = inproj_weight.shape[1] * inproj_weight.shape[2]
    out_width = outproj_weight.shape[0] * outproj_weight.shape[1]
    prompt_total = PROMPT_DEV * n_dp
    count = tokens.shape[0]

    def gateup_flat(w):
        w = w.reshape(groups, group, depth, 2, hidden)
        return w.transpose(2, 0, 3, 1, 4).reshape(depth, 2 * EXPERTS * hidden)

    def gateup_back(w):
        w = w.reshape(depth, groups, 2, group, hidden)
        return w.transpose(1, 3, 0, 2, 4).reshape(EXPERTS, depth, 2, hidden)

    query_width = GROUP * HEAD_DIM
    gains_high = gains.astype(bf16)
    gains_low = (gains - gains_high.astype(f32)).astype(bf16)
    attn_local = (
        inproj_weight.reshape(depth, in_width).astype(bf16),
        outproj_weight.reshape(out_width, depth).T.astype(bf16),
        jnp.concatenate(
            [
                router_weight.astype(bf16),
                gains_high.T,
                gains_low.T,
                jnp.zeros((depth, 128 - EXPERTS - 4), bf16),
            ],
            axis=1,
        ),
    )
    if hidden == 128:
        inproj_full, outproj_full, small_full, gu_local = gather(
            attn_local, gateup_weight.reshape(-1, hidden), n_dp, group, 5
        )
    else:
        inproj_full, outproj_full, small_full = gather(attn_local, None, n_dp, None, 5)
        gu_local = gateup_flat(gateup_weight.astype(bf16))
    down_local = down_weight.reshape(EXPERTS * hidden, depth).T.astype(bf16)
    gain_rows = small_full[:, EXPERTS : EXPERTS + 8].astype(f32).T

    device_index = lax.axis_index("dp")
    half_dim = HEAD_DIM // 2
    freqs = np.float32(10000.0) ** (-2.0 * np.arange(half_dim, dtype=np.float32) / HEAD_DIM)
    angles = np.arange(prompt_total + CONT, dtype=np.float32)[:, None] * freqs.astype(np.float32)
    cosine, sine = np.cos(angles), np.sin(angles)

    def of_rows(table):
        own = lax.dynamic_slice_in_dim(
            jnp.asarray(table), device_index * PROMPT_DEV, PROMPT_DEV, 0
        )
        return jnp.concatenate([own, table[prompt_total:]], axis=0)

    in_kernels = kv_local * HEAD_DIM == 128
    both_width = kv_local * 2 * HEAD_DIM
    if in_kernels:
        cos_all = np.concatenate([cosine] * 4, axis=1)
        sin_all = np.concatenate([-sine, sine] * 2, axis=1)
        normed_first, queries, both = project_call(
            tokens, gain_rows, inproj_full, cos_all, sin_all
        )
    else:
        cosine, sine = (jnp.tile(of_rows(t), (MICRO, 1))[:, None, :] for t in (cosine, sine))
        inputs = tokens.astype(f32)
        inverse_first = lax.rsqrt(jnp.mean(inputs * inputs, axis=-1, keepdims=True) + eps_norm)
        normed_first = (inputs * inverse_first * (gain_rows[0:1] + gain_rows[2:3])).astype(bf16)
        mixed = jnp.dot(normed_first, inproj_full, preferred_element_type=f32)
        mixed = mixed.reshape(count, kv_local, -1)
        queries = rotate(
            mixed[..., :query_width].reshape(count, -1, HEAD_DIM), cosine, sine
        ).astype(bf16)
        keys = rotate(mixed[..., query_width : query_width + HEAD_DIM], cosine, sine)
        both = jnp.concatenate(
            [keys.reshape(count, -1), mixed[..., query_width + HEAD_DIM :].reshape(count, -1)],
            axis=1,
        ).astype(bf16)
    if in_kernels:
        attended, lse, prompt_both, down_start = attention_call(
            queries, both, down_local[:, : down_local.shape[1] // 2], n_dp
        )
        down_start = down_start.reshape(n_dp * depth, -1)
        down_rest = down_local[:, down_local.shape[1] // 2 :]
    else:
        both = both.reshape(MICRO, TOK_MB, both_width)
        prompt_both = lax.all_gather(both[:, :PROMPT_DEV], "dp", axis=1, tiled=True)
        both_all = jnp.concatenate([prompt_both, both[:, PROMPT_DEV:]], axis=1)
        inner = jnp.arange(TOK_MB, dtype=jnp.int32)
        positions = jnp.where(
            inner < PROMPT_DEV, device_index * PROMPT_DEV + inner, prompt_total + inner - PROMPT_DEV
        )
        key_index = jnp.arange(prompt_total + CONT, dtype=jnp.int32)
        allowed = (key_index[None, :] <= positions[:, None]) & (
            (key_index[None, :] < prompt_total) | (inner[:, None] >= PROMPT_DEV)
        )
        kept = []
        attended = []
        for m in range(MICRO):
            q = queries[m * TOK_MB : (m + 1) * TOK_MB].reshape(TOK_MB, kv_local, GROUP, HEAD_DIM)
            k, v = (
                t.reshape(-1, kv_local, HEAD_DIM) for t in jnp.split(both_all[m], 2, axis=1)
            )
            out, softened, soft_low = attend(q, k, v, allowed)
            attended.append(out.reshape(TOK_MB, -1))
            kept.append((q, k, v, softened, soft_low))
        attended = jnp.concatenate(attended, axis=0)
    branch = lax.dot_general(
        attended, outproj_full, (((1,), (1,)), ((), ())), preferred_element_type=f32
    ).astype(bf16)
    branch, gu_full, down_rest = line_gather(
        branch, gu_local, down_rest if in_kernels else down_local, n_tensor, n_dp, 6
    )
    if not in_kernels:
        down_start, down_rest = jnp.split(down_rest, 2, axis=1)

    normed_second, gates_wide = route_call(tokens, branch, gain_rows, small_full, routes)
    active, hidden_grad, gate_grad = expert_call(
        normed_second, cotangent, gates_wide, gu_full, down_start, down_rest, group
    )
    contract_last = (((1,), (1,)), ((), ()))
    contract_first = (((0,), (0,)), ((), ()))
    rows_grad = lax.dot_general(
        hidden_grad, gu_full, contract_last, preferred_element_type=f32
    ).astype(bf16)
    summed, gateup_grad, down_grad, mixture = expert_grads_call(
        jnp.concatenate([rows_grad, gate_grad.astype(bf16)], axis=1),
        normed_second, cotangent, down_start, down_rest, hidden_grad, active, n_tensor, 2,
    )
    mixture = lax.psum(mixture, "tensor")
    model = tokens.shape[1]
    middle_grad, branch_own, attended_grad, logits_grad, gain_second_grad = middle_back_call(
        tokens, branch, summed, gates_wide, cotangent, gain_rows, small_full, outproj_full
    )
    middle_grad, attended_grad, down_grad, gateup_grad = lax.optimization_barrier(
        (middle_grad, attended_grad, down_grad, gateup_grad)
    )
    down_grad = lax.psum_scatter(down_grad, "dp", scatter_dimension=0, tiled=True)
    gateup_grad = lax.psum_scatter(gateup_grad, "dp", scatter_dimension=0, tiled=True)
    router_grad = lax.dot_general(
        normed_second, logits_grad, contract_first, preferred_element_type=f32
    ).astype(bf16)
    outproj_grad = lax.dot_general(
        branch_own, attended, contract_first, preferred_element_type=f32
    ).astype(bf16)
    if in_kernels:
        mixed_grad = attention_back_call(
            queries, both, prompt_both, attended_grad, attended, lse, cos_all, sin_all, n_dp
        )
    else:
        queries_grad, both_grad = [], []
        for m in range(MICRO):
            q, k, v, softened, soft_low = kept[m]
            dout = attended_grad[m * TOK_MB : (m + 1) * TOK_MB].reshape(q.shape)
            dq, dk, dv = attend_back(q, k, v, softened, soft_low, dout)
            queries_grad.append(dq.reshape(TOK_MB, -1, HEAD_DIM))
            both_grad.append(jnp.concatenate([t.reshape(-1, both_width // 2) for t in (dk, dv)], 1))
        queries_grad = rotate(jnp.concatenate(queries_grad, axis=0), cosine, -sine)
        both_grad = jnp.stack(both_grad)
        prompt_grad = lax.psum_scatter(
            both_grad[:, :prompt_total].astype(bf16), "dp", scatter_dimension=1, tiled=True
        )
        both_grad = jnp.concatenate(
            [prompt_grad.astype(f32), both_grad[:, prompt_total:]], axis=1
        ).reshape(count, both_width)
        keys_grad = rotate(
            both_grad[:, : both_width // 2].reshape(count, -1, HEAD_DIM), cosine, -sine
        )
        mixed_grad = jnp.concatenate(
            [
                t.reshape(count, kv_local, -1)
                for t in (queries_grad, keys_grad, both_grad[:, both_width // 2 :])
            ],
            axis=2,
        )
        mixed_grad = mixed_grad.reshape(count, -1).astype(bf16)
    normed_first_grad = lax.dot_general(
        mixed_grad, inproj_full, contract_last, preferred_element_type=f32
    ).astype(bf16)
    inproj_grad = lax.dot_general(
        normed_first, mixed_grad, contract_first, preferred_element_type=f32
    ).astype(bf16)
    attn_grad = [inproj_grad, outproj_grad, router_grad]
    if in_width % 128 or out_width % 128:
        attn_grad = [jnp.concatenate(attn_grad, axis=1)]
    down_next = adam_update(
        down_weight, down_first, down_second,
        down_grad.T.reshape(down_weight.shape).astype(f32), weight_decay, 0.05,
    )
    if hidden == 128:
        gateup_next = gateup_adam(gateup_weight, gateup_first, gateup_second, gateup_grad, group)
    else:
        gateup_next = adam_update(
            gateup_weight, gateup_first, gateup_second,
            gateup_back(gateup_grad).astype(f32), weight_decay, 0.05,
        )
    tokens_grad, attn_grad, gains_grad = last_call(
        normed_first_grad, tokens, middle_grad, gain_rows,
        attn_grad, gain_second_grad, n_tensor, n_dp, 7,
    )
    mixture, tokens_grad = lax.optimization_barrier((mixture, tokens_grad))
    middle = tokens.astype(f32) + branch.astype(f32)
    block_out = (middle + mixture.astype(f32)).astype(bf16)
    split = (in_width, in_width + out_width, in_width + out_width + EXPERTS)
    inproj_grad, outproj_grad, router_grad = (
        attn_grad[:, : split[0]],
        attn_grad[:, split[0] : split[1]],
        attn_grad[:, split[1] : split[2]],
    )
    updates = (
        adam_update(
            inproj_weight, inproj_first, inproj_second,
            inproj_grad.reshape(inproj_weight.shape), weight_decay, 0.05,
        ),
        adam_update(
            outproj_weight, outproj_first, outproj_second,
            outproj_grad.T.reshape(outproj_weight.shape), weight_decay, 0.3,
        ),
        gateup_next,
        down_next,
        adam_update(router_weight, router_first, router_second, router_grad, weight_decay, 0.05),
        adam_update(gains, gains_first, gains_second, gains_grad, 0.0, 0.4),
    )
    return (block_out, tokens_grad) + sum(updates, ())


def solution(mesh):
    row = P("dp", None)
    inproj = P("dp", "tensor", None)
    outproj = P("tensor", None, "dp")
    gateup = P(None, "dp", None, "tensor")
    down = P(None, "tensor", "dp")
    gain = P(None, "dp")
    weights = (inproj,) * 3 + (outproj,) * 3 + (gateup,) * 3 + (down,) * 3 + (row,) * 3 + (gain,) * 3
    return jax.shard_map(
        shards,
        mesh=mesh,
        in_specs=(row, row, row) + weights,
        out_specs=(row, row) + weights,
        check_vma=False,
    )
```

```python
import functools

import jax
import jax.numpy as jnp
import numpy as np
from jax import lax
from jax.experimental import pallas as pl
from jax.experimental.pallas import tpu as pltpu
from jax.sharding import PartitionSpec as P

HEAD_DIM = 64
TOPK = 8
EXPERTS = 16
PROMPT_DEV = 128
CONT = 512
MICRO = 2
STEP = 10
GROUP = 3
TOK_MB = 640

eps_norm = 1e-05
beta_first = 0.9
beta_second = 0.95
adam_eps = 1e-08
weight_decay = 0.1
bf16 = jnp.bfloat16
f32 = jnp.float32
line_parts = 20
line_lag = 2
MESH = pl.DeviceIdType.MESH
nt = (((1,), (1,)), ((), ()))


def rotate(values, cosine, sine):
    half_dim = values.shape[-1] // 2
    first_half = values[..., :half_dim]
    second_half = values[..., half_dim:]
    return jnp.concatenate(
        [first_half * cosine - second_half * sine, second_half * cosine + first_half * sine],
        axis=-1,
    )


def adam_update(weight, moment_one, moment_two, gradient, decay_rate, learn_rate):
    first_next = beta_first * moment_one + (1.0 - beta_first) * gradient
    second_next = beta_second * moment_two + (1.0 - beta_second) * gradient * gradient
    corr_first = 1.0 - beta_first**STEP
    corr_second = 1.0 - beta_second**STEP
    update = first_next / corr_first / (jnp.sqrt(second_next / corr_second) + adam_eps)
    return (weight - learn_rate * (update + decay_rate * weight), first_next, second_next)


def line_steps(n, parts=line_parts):
    return parts + 2 * (n - 1) * line_lag


def line_engine(
    n, x_ref, o_ref, held, send_red, recv_red, send_out, recv_out,
    complete=lambda at, half, c: None, parts=line_parts,
):
    me = lax.axis_index("tensor")
    rows = x_ref.shape[0] // (2 * parts)
    low, high = me - 1, me + 1

    def greet():
        barrier = pltpu.get_barrier_semaphore()

        @pl.when(me > 0)
        def _():
            pl.semaphore_signal(barrier, inc=1, device_id={"tensor": low}, device_id_type=MESH)

        @pl.when(me < n - 1)
        def _():
            pl.semaphore_signal(barrier, inc=1, device_id={"tensor": high}, device_id_type=MESH)

        return jnp.where((me > 0) & (me < n - 1), 2, 1)

    def begin():
        pl.semaphore_wait(pltpu.get_barrier_semaphore(), greet())

    def part(half, c):
        return pl.ds(pl.multiple_of((half * parts + c) * rows, 16), rows)

    def reduce_copy(half, c, src):
        to = low if half == 0 else high
        return pltpu.make_async_remote_copy(
            src_ref=src.at[part(half, c)],
            dst_ref=held.at[part(half, c)],
            send_sem=send_red.at[half, c],
            recv_sem=recv_red.at[half, c],
            device_id={"tensor": to},
            device_id_type=MESH,
        )

    def out_copy(half, c):
        to = high if half == 0 else low
        return pltpu.make_async_remote_copy(
            src_ref=o_ref.at[part(half, c)],
            dst_ref=o_ref.at[part(half, c)],
            send_sem=send_out.at[half, c],
            recv_sem=recv_out.at[half, c],
            device_id={"tensor": to},
            device_id_type=MESH,
        )

    def place(half):
        return n - 1 - me if half == 0 else me

    def slot(t):
        for half in (0, 1):
            at = place(half)
            c = t - line_lag * at

            @pl.when((c >= 0) & (c < parts))
            def _():
                @pl.when(at == 0)
                def _():
                    reduce_copy(half, c, x_ref).start()

                @pl.when(at > 0)
                def _():
                    reduce_copy(half, c, held).wait_recv()
                    total = x_ref[part(half, c)].astype(f32) + held[part(half, c)].astype(f32)

                    @pl.when(at < n - 1)
                    def _():
                        held[part(half, c)] = total.astype(held.dtype)
                        reduce_copy(half, c, held).start()

                    @pl.when(at == n - 1)
                    def _():
                        o_ref[part(half, c)] = total.astype(o_ref.dtype)
                        out_copy(half, c).start()
                        complete(part(half, c), half, c)

        for half in (0, 1):
            at = place(half)
            c = t - line_lag * (2 * (n - 1) - at)

            @pl.when((at < n - 1) & (c >= 0) & (c < parts))
            def _():
                out_copy(half, c).wait_recv()

                @pl.when(at > 0)
                def _():
                    out_copy(half, c).start()

                complete(part(half, c), half, c)

    def finish():
        def one(c, carry):
            for half in (0, 1):
                at = place(half)

                @pl.when(at < n - 1)
                def _():
                    reduce_copy(half, c, held).wait_send()

                @pl.when(at > 0)
                def _():
                    out_copy(half, c).wait_send()

            return carry

        lax.fori_loop(0, parts, one, 0)

    return greet, begin, slot, finish


def line_scratch(shape, dtype, parts=line_parts):
    return [pltpu.VMEM(shape, dtype)] + [
        pltpu.SemaphoreType.DMA((2, parts)) for _ in range(4)
    ]


def line_sum_kernel(n, x_ref, o_ref, *scratch):
    _, begin, slot, finish = line_engine(n, x_ref, o_ref, *scratch)
    begin()

    def step(t, carry):
        slot(t)
        return carry

    lax.fori_loop(0, line_steps(n), step, 0)
    finish()


def line_sum(x, n, barrier_id):
    rows, width = x.shape
    return pl.pallas_call(
        functools.partial(line_sum_kernel, n),
        out_shape=jax.ShapeDtypeStruct(x.shape, x.dtype),
        in_specs=[pl.BlockSpec(memory_space=pltpu.VMEM)],
        out_specs=pl.BlockSpec(memory_space=pltpu.VMEM),
        scratch_shapes=line_scratch(x.shape, x.dtype),
        compiler_params=pltpu.CompilerParams(
            collective_id=barrier_id, has_side_effects=True, vmem_limit_bytes=24 * 2**20
        ),
        cost_estimate=pl.CostEstimate(
            flops=rows * width, bytes_accessed=100 * rows * width, transcendentals=0
        ),
    )(x)


gather_parts = 3


def gather_engine(n, pairs, own_sem, far_send, far_recv, near_send, near_recv):
    me = lax.axis_index("dp")
    core, chip, chips = lax.rem(me, 2), me // 2, n // 2

    def rows(a, p):
        size = pairs[a][0].shape[0] // gather_parts
        return pl.ds(p * size, size)

    def far(a, p, k):
        x_ref, out_ref = pairs[a]
        return pltpu.make_async_remote_copy(
            src_ref=x_ref.at[rows(a, p)],
            dst_ref=out_ref.at[me, rows(a, p)],
            send_sem=far_send.at[a, p, k],
            recv_sem=far_recv.at[a, p, k],
            device_id={"dp": lax.rem(chip + k, chips) * 2 + core},
            device_id_type=MESH,
        )

    def near(a, p, k):
        x_ref, out_ref = pairs[a]
        owner = lax.rem(chip + chips - k, chips) * 2 + core
        target = out_ref.at[owner, rows(a, p)]
        return pltpu.make_async_remote_copy(
            src_ref=x_ref.at[rows(a, p)] if k == 0 else target,
            dst_ref=target,
            send_sem=near_send.at[a, p, k],
            recv_sem=near_recv.at[a, p, k],
            device_id={"dp": me + 1 - 2 * core},
            device_id_type=MESH,
        )

    def own(a):
        x_ref, out_ref = pairs[a]
        return pltpu.make_async_copy(x_ref, out_ref.at[me], own_sem.at[a])

    arrays = range(len(pairs))

    def greet():
        barrier = pltpu.get_barrier_semaphore()
        for k in range(1, chips):
            pl.semaphore_signal(
                barrier,
                inc=1,
                device_id={"dp": lax.rem(chip + k, chips) * 2 + core},
                device_id_type=MESH,
            )
        pl.semaphore_signal(
            barrier, inc=1, device_id={"dp": me + 1 - 2 * core}, device_id_type=MESH
        )
        return chips

    def start():
        for p in range(gather_parts):
            for a in arrays:
                for k in range(1, chips):
                    far(a, p, k).start()
        for p in range(gather_parts):
            for a in arrays:
                near(a, p, 0).start()
        for a in arrays:
            own(a).start()

    def forward(p):
        for a in arrays:
            for k in range(1, chips):
                far(a, p, k).wait_recv()
                near(a, p, k).start()

    def finish():
        for a in arrays:
            own(a).wait()
            for p in range(gather_parts):
                for k in range(chips):
                    near(a, p, k).wait_recv()
                    near(a, p, k).wait_send()
                    if k:
                        far(a, p, k).wait_send()

    return greet, start, forward, finish


def gather_scratch(arrays, n):
    return [pltpu.SemaphoreType.DMA((arrays,))] + [
        pltpu.SemaphoreType.DMA((arrays, gather_parts, n // 2)) for _ in range(4)
    ]


def gateup_column(e, part, group, hidden):
    return (e // group * 2 * group + part * group + e % group) * hidden


def gather_kernel(n, group, count, *refs):
    x_refs, refs = refs[:count], refs[count:]
    w_ref, refs = (None, refs) if group is None else (refs[0], refs[1:])
    out_refs, refs = refs[:count], refs[count:]
    low_ref, scratch = (None, refs) if group is None else (refs[0], refs[1:])
    greet, start, forward, finish = gather_engine(n, list(zip(x_refs, out_refs)), *scratch)
    pl.semaphore_wait(pltpu.get_barrier_semaphore(), greet())
    start()
    if group is not None:
        depth, hidden = low_ref.shape[0], w_ref.shape[1]
        for e in range(EXPERTS):
            for part in (0, 1):
                at = gateup_column(e, part, group, hidden)
                low_ref[:, at : at + hidden] = w_ref[
                    pl.ds(e * 2 * depth + part, depth, stride=2)
                ].astype(bf16)
    for p in range(gather_parts):
        forward(p)
    finish()


def gather(arrays, w, n, group, barrier_id):
    depth = arrays[0].shape[0]
    whole = pl.BlockSpec(memory_space=pltpu.VMEM)
    shapes = [jax.ShapeDtypeStruct((n,) + x.shape, x.dtype) for x in arrays]
    operands = list(arrays)
    if group is not None:
        operands.append(w)
        shapes.append(jax.ShapeDtypeStruct((depth, w.size // depth), bf16))
    out = pl.pallas_call(
        functools.partial(gather_kernel, n, group, len(arrays)),
        out_shape=shapes,
        in_specs=[whole] * len(operands),
        out_specs=[whole] * len(shapes),
        scratch_shapes=gather_scratch(len(arrays), n),
        compiler_params=pltpu.CompilerParams(
            collective_id=barrier_id, has_side_effects=True, vmem_limit_bytes=24 * 2**20
        ),
    )(*operands)
    count = len(arrays)
    return [t.reshape(n * depth, -1) for t in out[:count]] + list(out[count:])


def gateup_adam_kernel(group, w_ref, m_ref, v_ref, grad_ref, w_out, m_out, v_out, g_ref):
    depth, hidden = grad_ref.shape[0], w_ref.shape[1]
    for e in range(w_ref.shape[0] // (2 * depth)):
        for part in (0, 1):
            at = gateup_column(e, part, group, hidden)
            g_ref[pl.ds(part, depth, stride=2)] = grad_ref[:, at : at + hidden].astype(f32)
        rows = slice(e * 2 * depth, (e + 1) * 2 * depth)
        w_out[rows], m_out[rows], v_out[rows] = adam_update(
            w_ref[rows], m_ref[rows], v_ref[rows], g_ref[...], weight_decay, 0.05
        )


def gateup_adam(w, m, v, grad, group):
    experts, depth, parts, hidden = w.shape
    flat = lambda t: t.reshape(experts * depth * parts, hidden)
    each = 2 * group
    block = pl.BlockSpec((each * depth * parts, hidden), lambda e: (e, 0))
    out = pl.pallas_call(
        functools.partial(gateup_adam_kernel, group),
        grid=(experts // each,),
        in_specs=[block] * 3
        + [pl.BlockSpec((depth, each * parts * hidden), lambda e: (0, e))],
        out_specs=[block] * 3,
        out_shape=[jax.ShapeDtypeStruct((experts * depth * parts, hidden), f32)] * 3,
        scratch_shapes=[pltpu.VMEM((depth * parts, hidden), f32)],
        compiler_params=pltpu.CompilerParams(vmem_limit_bytes=32 * 2**20),
    )(flat(w), flat(m), flat(v), grad)
    return tuple(t.reshape(w.shape) for t in out)


def line_gather_kernel(n, n_dp, x_ref, a_ref, b_ref, o_ref, a_out, b_out, *scratch):
    line, spread_out = scratch[:5], scratch[5:]
    greet, _, slot, finish = line_engine(n, x_ref, o_ref, *line)
    greet_dp, start, forward, finish_dp = gather_engine(
        n_dp, [(a_ref, a_out), (b_ref, b_out)], *spread_out
    )
    peers = greet() + greet_dp()
    pl.semaphore_wait(pltpu.get_barrier_semaphore(), peers)
    start()

    def step(t, carry):
        slot(t)
        return carry

    total = line_steps(n)
    done = 0
    for p in range(gather_parts):
        until = total * (p + 1) // gather_parts
        lax.fori_loop(done, until, step, 0)
        done = until
        forward(p)
    finish()
    finish_dp()


def line_gather(x, a, b, n, n_dp, barrier_id):
    rows, width = x.shape
    whole, anywhere = pl.BlockSpec(memory_space=pltpu.VMEM), pl.BlockSpec(memory_space=pl.ANY)
    o, a_all, b_all = pl.pallas_call(
        functools.partial(line_gather_kernel, n, n_dp),
        out_shape=[jax.ShapeDtypeStruct(x.shape, x.dtype)]
        + [jax.ShapeDtypeStruct((n_dp,) + t.shape, t.dtype) for t in (a, b)],
        in_specs=[whole, anywhere, anywhere],
        out_specs=[whole, anywhere, anywhere],
        scratch_shapes=line_scratch(x.shape, x.dtype) + gather_scratch(2, n_dp),
        compiler_params=pltpu.CompilerParams(
            collective_id=barrier_id, has_side_effects=True, vmem_limit_bytes=24 * 2**20
        ),
        cost_estimate=pl.CostEstimate(
            flops=rows * width, bytes_accessed=100 * rows * width, transcendentals=0
        ),
    )(x, a, b)
    return o, a_all.reshape(-1, a.shape[1]), b_all.reshape(-1, b.shape[1])


def last_kernel(
    n, n_dp, pieces, first_ref, tokens_ref, middle_ref, mixture_ref, gain_ref, gain_second_ref, *refs,
):
    weights_refs, refs = refs[:pieces], refs[pieces:]
    last_body(
        n, n_dp, first_ref, tokens_ref, middle_ref, mixture_ref, gain_ref, weights_refs,
        gain_second_ref, *refs,
    )


def last_body(
    n, n_dp, first_ref, tokens_ref, middle_ref, mixture_ref, gain_ref, weights_refs,
    gain_second_ref, grad_ref, weights_out, gains_out, mixture_out,
    x_ref, o_ref, held, send_red, recv_red, send_out, recv_out,
    tokens_v, middle_v, grad_v, in_sem, out_sem, x_sem, got, w_send, w_recv,
    g_from, g_got, g_send, g_recv, z_from, z_got, z_send, z_recv, acc,
):
    me, line = lax.axis_index("dp"), lax.axis_index("tensor")
    model = x_ref.shape[1]
    rows = tokens_v.shape[0] // (2 * line_parts)
    depth = weights_out.shape[0]
    half_x, half_m = line_parts * rows, TOK_MB // 2
    half_all = half_x + half_m
    parts = half_all // rows

    def own_rows(half, c):
        return pl.ds(pl.multiple_of((half * line_parts + c) * rows, 16), rows)

    def half_copies(x, m, sem, back):
        for half in (0, 1):
            for ref, low, size, at in (
                (x, half * half_x, half_x, half * half_all),
                (m[0], m[1] + half * half_m, half_m, half * half_all + half_x),
            ):
                if ref is not None:
                    here = (o_ref if back else x_ref).at[pl.ds(at, size)]
                    there = ref.at[pl.ds(low, size)]
                    k = half * 2 + (ref is m[0])
                    yield pltpu.make_async_copy(
                        *((here, there) if back else (there, here)), sem.at[k]
                    )

    def norm_of(at):
        x = tokens_v[at].astype(f32)
        inverse = lax.rsqrt(jnp.mean(x * x, axis=-1, keepdims=True) + eps_norm)
        return x * inverse, inverse

    def complete(at, half, c):
        @pl.when(c < line_parts)
        def _():
            own = own_rows(half, c)
            norm, inverse = norm_of(own)
            grad = o_ref[at].astype(f32) * (gain_ref[0:1] + gain_ref[2:3])
            mean = jnp.mean(grad * norm, axis=-1, keepdims=True)
            grad_v[own] = middle_v[own] + inverse * (grad - norm * mean)

    _, _, slot, finish = line_engine(
        n, x_ref, o_ref, held, send_red, recv_red, send_out, recv_out, complete, parts
    )

    columns, low = [], 0
    for ref in weights_refs:
        columns.append(slice(low, low + ref.shape[2]))
        low += ref.shape[2]
    pieces = range(len(columns))

    def weights_copy(k, j):
        to = lax.rem(me + k, n_dp)
        return pltpu.make_async_remote_copy(
            src_ref=weights_refs[j].at[to], dst_ref=got.at[k, :, columns[j]],
            send_sem=w_send.at[j, k], recv_sem=w_recv.at[j, k],
            device_id={"dp": to}, device_id_type=MESH,
        )

    def gains_copy(k):
        to = lax.rem(me + k, n_dp)
        return pltpu.make_async_remote_copy(
            src_ref=g_from.at[to], dst_ref=g_got.at[k],
            send_sem=g_send.at[k], recv_sem=g_recv.at[k],
            device_id={"dp": to}, device_id_type=MESH,
        )

    def line_copy(k):
        to = lax.rem(line + k, n)
        return pltpu.make_async_remote_copy(
            src_ref=z_from, dst_ref=z_got.at[k],
            send_sem=z_send.at[k], recv_sem=z_recv.at[k],
            device_id={"tensor": to}, device_id_type=MESH,
        )

    def loop(count, act):
        def one(k, carry):
            act(k)
            return carry

        lax.fori_loop(1, count, one, 0)

    load_tokens = pltpu.make_async_copy(tokens_ref, tokens_v, in_sem.at[0])
    load_middle = pltpu.make_async_copy(middle_ref, middle_v, in_sem.at[1])
    loads = list(half_copies(first_ref, (mixture_ref, TOK_MB), x_sem, False))
    for load in loads + [load_tokens, load_middle]:
        load.start()
    barrier = pltpu.get_barrier_semaphore()

    def greet(axis, place, count):
        loop(
            count,
            lambda k: pl.semaphore_signal(
                barrier, inc=1, device_id={axis: lax.rem(place + k, count)}, device_id_type=MESH
            ),
        )

    greet("dp", me, n_dp)
    greet("tensor", line, n)
    pl.semaphore_wait(barrier, n_dp + n - 2)
    for j in pieces:
        loop(n_dp, lambda k: weights_copy(k, j).start())
    acc[...] = jnp.zeros_like(acc)
    for load in loads:
        load.wait()

    def step(t, carry):
        slot(t)
        return carry

    def gain_step(t, carry):
        slot(t)
        c = t - early
        for half in (0, 1):
            at = pl.ds(pl.multiple_of(half * half_all + c * rows, 16), rows)
            norm, _ = norm_of(own_rows(half, c))
            term = x_ref[at].astype(f32) * norm
            acc[...] += jnp.sum(term.reshape(rows // 8, 8, model), axis=0)
        return carry

    total = line_steps(n, parts)
    early, size = 4, 32
    lax.fori_loop(0, early, step, 0)
    for load in (load_tokens, load_middle):
        load.wait()
    low = early + line_parts
    lax.fori_loop(early, low, gain_step, 0)
    width = g_from.shape[2]
    for p in range(n_dp):
        moved = acc[...] if p == 0 else pltpu.roll(acc[...], model - p * depth, 1)
        g_from[p, :8] = moved[:, :width]
        moved = gain_second_ref[...] if p == 0 else pltpu.roll(
            gain_second_ref[...], model - p * depth, 1
        )
        g_from[p, 8:] = jnp.where(line == 0, moved[:, :width], 0.0)
    loop(n_dp, lambda k: gains_copy(k).start())
    for j in pieces:
        loop(n_dp, lambda k: weights_copy(k, j).wait_recv())

    def add_step(t, carry):
        slot(t)
        at = pl.ds(pl.multiple_of((t - low) * size, 16), size)
        for j, ref in enumerate(weights_refs):
            weights_out[at, columns[j]] = lax.fori_loop(
                1,
                n_dp,
                lambda k, v: v + got[k, at, columns[j]].astype(f32),
                ref[me, at].astype(f32),
            )
        return carry

    middle = low + depth // size
    lax.fori_loop(low, middle, add_step, 0)
    loop(n_dp, lambda k: gains_copy(k).wait_recv())
    z_from[...] = lax.fori_loop(1, n_dp, lambda k, v: v + g_got[k], g_from[me])
    loop(n, lambda k: line_copy(k).start())
    own_done = max(middle, line_steps(n))
    lax.fori_loop(middle, own_done, step, 0)
    every = pltpu.make_async_copy(grad_v, grad_ref, out_sem)
    every.start()
    lax.fori_loop(own_done, total, step, 0)
    stores = list(half_copies(None, (mixture_out, 0), x_sem, True))
    for store in stores:
        store.start()
    loop(n, lambda k: line_copy(k).wait_recv())
    gains_out[...] = lax.fori_loop(1, n, lambda k, v: v + z_got[k], z_from[...])
    finish()
    for j in pieces:
        loop(n_dp, lambda k: weights_copy(k, j).wait_send())
    loop(n_dp, lambda k: gains_copy(k).wait_send())
    loop(n, lambda k: line_copy(k).wait_send())
    for store in stores + [every]:
        store.wait()


def last_call(x, tokens, middle, mixture, gain, weights, gain_second, n, n_dp, barrier_id):
    count, model = x.shape
    depth, width = model // n_dp, sum(w.shape[1] for w in weights)
    lanes = -(-depth // 128) * 128
    whole, anywhere = pl.BlockSpec(memory_space=pltpu.VMEM), pl.BlockSpec(memory_space=pl.ANY)
    dma = pltpu.SemaphoreType.DMA
    grad, weights, gains, mixture = pl.pallas_call(
        functools.partial(last_kernel, n, n_dp, len(weights)),
        out_shape=[
            jax.ShapeDtypeStruct((count, model), f32),
            jax.ShapeDtypeStruct((depth, width), f32),
            jax.ShapeDtypeStruct((16, lanes), f32),
            jax.ShapeDtypeStruct((TOK_MB, model), bf16),
        ],
        in_specs=[anywhere, anywhere, anywhere, anywhere, whole, whole] + [whole] * len(weights),
        out_specs=[anywhere, whole, whole, anywhere],
        scratch_shapes=[pltpu.VMEM((count + TOK_MB, model), bf16)] * 2
        + line_scratch((count + TOK_MB, model), bf16, line_parts * (count + TOK_MB) // count)
        + [
            pltpu.VMEM((count, model), bf16),
            pltpu.VMEM((count, model), f32),
            pltpu.VMEM((count, model), f32),
            dma((2,)),
            dma,
            dma((4,)),
            pltpu.VMEM((n_dp, depth, width), bf16),
            dma((len(weights), n_dp)),
            dma((len(weights), n_dp)),
            pltpu.VMEM((n_dp, 16, lanes), f32),
            pltpu.VMEM((n_dp, 16, lanes), f32),
            dma((n_dp,)),
            dma((n_dp,)),
            pltpu.VMEM((16, lanes), f32),
            pltpu.VMEM((n, 16, lanes), f32),
            dma((n,)),
            dma((n,)),
            pltpu.VMEM((8, model), f32),
        ],
        compiler_params=pltpu.CompilerParams(
            collective_id=barrier_id, has_side_effects=True, vmem_limit_bytes=56 * 2**20
        ),
        cost_estimate=pl.CostEstimate(
            flops=count * model, bytes_accessed=2**20, transcendentals=0
        ),
    )(x, tokens, middle, mixture, gain, gain_second, *(w.reshape(n_dp, depth, -1) for w in weights))
    gains = jnp.sum(gains.reshape(2, 8, lanes), axis=1)[:, :depth]
    return grad, weights, gains, mixture


def expert_grads_kernel(
    n, shape, x_ref, rows_ref, outgrad_ref, start_ref, rest_ref,
    hidden_ref, active_ref, active_rows_ref,
    o_ref, gateup_grad_ref, down_grad_ref, mixture_ref, rows_t, outgrad_t, o_sem, sum_ref, *scratch,
):
    mixture_steps, gateup_steps, down_steps = shape
    i = pl.program_id(0)
    steps = sum(shape)
    _, begin, slot, finish = line_engine(n, x_ref, sum_ref, *scratch)
    total = line_steps(n)
    each = -(-total // steps)
    pl.when(i == 0)(begin)

    def slots(low, high):
        def one(j, carry):
            t = i * each + j
            pl.when(t < total)(lambda: slot(t))
            return carry

        lax.fori_loop(low, high, one, 0)

    slots(0, 1)

    @pl.when(i < mixture_steps)
    def _():
        half = start_ref.shape[1]
        mixture_ref[...] = (
            lax.dot_general(
                active_rows_ref[:, :half], start_ref[...], nt, preferred_element_type=f32
            )
            + lax.dot_general(
                active_rows_ref[:, half:], rest_ref[...], nt, preferred_element_type=f32
            )
        ).astype(bf16)
        size = active_rows_ref.shape[0]
        columns = pl.ds(pl.multiple_of(i * size, size), size)
        rows_t[:, columns] = rows_ref[...].T
        outgrad_t[:, columns] = outgrad_ref[...].T

    @pl.when((i >= mixture_steps) & (i < mixture_steps + gateup_steps))
    def _():
        gateup_grad_ref[...] = jnp.dot(
            rows_t[...], hidden_ref[...], preferred_element_type=f32
        ).astype(bf16)

    @pl.when(i >= mixture_steps + gateup_steps)
    def _():
        down_grad_ref[...] = jnp.dot(
            outgrad_t[...], active_ref[...], preferred_element_type=f32
        ).astype(bf16)

    slots(1, each)

    @pl.when(i == steps - 1)
    def _():
        copy = pltpu.make_async_copy(sum_ref, o_ref, o_sem)
        copy.start()
        finish()
        copy.wait()


def expert_grads_call(
    x, rows, outgrad, down_start, down_rest, hidden, active, n, barrier_id
):
    tokens, model = rows.shape
    block, tile = min(512, active.shape[1]), 256
    c, a, b = shape = (tokens // tile, hidden.shape[1] // block, active.shape[1] // block)
    whole = pl.BlockSpec(memory_space=pltpu.VMEM)
    first = lambda i: (jnp.minimum(i, c - 1), 0)
    second = lambda i: (0, jnp.clip(i - c, 0, a - 1))
    third = lambda i: (0, jnp.clip(i - c - a, 0, b - 1))
    return pl.pallas_call(
        functools.partial(expert_grads_kernel, n, shape),
        grid=(a + b + c,),
        in_specs=[
            whole,
            pl.BlockSpec((tile, model), first),
            pl.BlockSpec((tile, model), first),
            whole,
            whole,
            pl.BlockSpec((tokens, block), second),
            pl.BlockSpec((tokens, block), third),
            pl.BlockSpec((tile, active.shape[1]), first),
        ],
        out_specs=[
            pl.BlockSpec(memory_space=pl.ANY),
            pl.BlockSpec((model, block), second),
            pl.BlockSpec((model, block), third),
            pl.BlockSpec((tile, model), first),
        ],
        out_shape=[
            jax.ShapeDtypeStruct(x.shape, x.dtype),
            jax.ShapeDtypeStruct((model, hidden.shape[1]), bf16),
            jax.ShapeDtypeStruct((model, active.shape[1]), bf16),
            jax.ShapeDtypeStruct((tokens, model), bf16),
        ],
        scratch_shapes=[pltpu.VMEM((model, tokens), bf16)] * 2
        + [pltpu.SemaphoreType.DMA, pltpu.VMEM(x.shape, x.dtype)]
        + line_scratch(x.shape, x.dtype),
        compiler_params=pltpu.CompilerParams(
            collective_id=barrier_id, has_side_effects=True, vmem_limit_bytes=58 * 2**20
        ),
        cost_estimate=pl.CostEstimate(
            flops=2 * tokens * model * (hidden.shape[1] + 2 * active.shape[1]),
            bytes_accessed=10 * tokens * model,
            transcendentals=0,
        ),
    )(x, rows, outgrad, down_start, down_rest, hidden, active, active)


def expert_kernel(group, steps, rows_ref, outgrad_ref, gates_ref, gu_ref, start_ref, rest_ref,
                  active_ref, hidden_ref, gate_grad_ref, down_ref):
    step = pl.program_id(0)
    tile = 256
    width = gu_ref.shape[1] // 2
    hidden = width // group
    lane = lax.broadcasted_iota(jnp.int32, (tile, 128), 1)
    column = lax.broadcasted_iota(jnp.int32, (tile, width), 1)

    @pl.when(step == 0)
    def _():
        gate_grad_ref[...] = jnp.zeros_like(gate_grad_ref)

    @pl.when(step < steps // 2)
    def _():
        down_ref[...] = start_ref[...]

    @pl.when(step >= steps // 2)
    def _():
        down_ref[...] = rest_ref[...]

    def one(t, carry):
        at = pl.ds(pl.multiple_of(t * tile, tile), tile)
        h = jnp.dot(rows_ref[at], gu_ref[...], preferred_element_type=f32)
        back = jnp.dot(outgrad_ref[at], down_ref[...], preferred_element_type=f32)
        gates = gates_ref[at]
        wide = jnp.zeros((tile, width), f32)
        for j in range(group):
            g = jnp.sum(jnp.where(lane == step * group + j, gates, 0.0), axis=1, keepdims=True)
            wide = g + wide if group == 1 else jnp.where(column // hidden == j, g, wide)
        gate, up = h[:, :width], h[:, width:]
        sig = 1.0 / (1.0 + jnp.exp(-gate))
        silu = gate * sig
        active = (silu * up).astype(bf16).astype(f32)
        active_ref[at] = (active * wide).astype(bf16)
        product = active * back
        grads = gate_grad_ref[at]
        for j in range(group):
            s = jnp.sum(jnp.where(column // hidden == j, product, 0.0), axis=1, keepdims=True)
            grads = jnp.where(lane == step * group + j, s, grads)
        gate_grad_ref[at] = grads
        back = back * wide
        hidden_ref[at, :width] = (back * up * sig * (1.0 + gate * (1.0 - sig))).astype(bf16)
        hidden_ref[at, width:] = (back * silu).astype(bf16)
        return carry

    lax.fori_loop(0, rows_ref.shape[0] // tile, one, 0)


def expert_call(rows, outgrad, gates, gu, down_start, down_rest, group):
    tokens, model = rows.shape
    width = gu.shape[1] // (EXPERTS // group)
    steps = EXPERTS // group
    return pl.pallas_call(
        functools.partial(expert_kernel, group, steps),
        grid=(steps,),
        in_specs=[
            pl.BlockSpec((tokens, model), lambda p: (0, 0)),
            pl.BlockSpec((tokens, model), lambda p: (0, 0)),
            pl.BlockSpec((tokens, 128), lambda p: (0, 0)),
            pl.BlockSpec((model, width), lambda p: (0, p)),
            pl.BlockSpec((model, width // 2), lambda p: (0, jnp.minimum(p, steps // 2 - 1))),
            pl.BlockSpec((model, width // 2), lambda p: (0, jnp.maximum(p - steps // 2, 0))),
        ],
        out_specs=[
            pl.BlockSpec((tokens, width // 2), lambda p: (0, p)),
            pl.BlockSpec((tokens, width), lambda p: (0, p)),
            pl.BlockSpec((tokens, 128), lambda p: (0, 0)),
        ],
        out_shape=[
            jax.ShapeDtypeStruct((tokens, steps * width // 2), bf16),
            jax.ShapeDtypeStruct((tokens, steps * width), bf16),
            jax.ShapeDtypeStruct((tokens, 128), f32),
        ],
        scratch_shapes=[pltpu.VMEM((model, width // 2), bf16)],
        compiler_params=pltpu.CompilerParams(vmem_limit_bytes=48 * 2**20),
        cost_estimate=pl.CostEstimate(
            flops=2 * tokens * model * steps * width * 3 // 2,
            bytes_accessed=2 * (model * steps * width * 3 // 2 + tokens * steps * width * 3 // 2),
            transcendentals=tokens * steps * width // 2,
        ),
    )(rows, outgrad, gates, gu, down_start, down_rest)


def turn(u, cosine, sine):
    lane = lax.broadcasted_iota(jnp.int32, u.shape, 1) % HEAD_DIM
    other = jnp.where(lane < HEAD_DIM // 2, pltpu.roll(u, 96, 1), pltpu.roll(u, 32, 1))
    return u * cosine + other * sine


def table_parts(me, prompt_total):
    return (
        (0, PROMPT_DEV, pl.multiple_of(me * PROMPT_DEV, PROMPT_DEV)),
        (PROMPT_DEV, CONT, prompt_total),
    )


def project_kernel(x_ref, gain_ref, w_ref, cos_ref, sin_ref, normed_ref, q_ref, kv_ref):
    x = x_ref[...].astype(f32)
    inverse = lax.rsqrt(jnp.mean(x * x, axis=-1, keepdims=True) + eps_norm)
    normed = (x * inverse * (gain_ref[0:1] + gain_ref[2:3])).astype(bf16)
    normed_ref[...] = normed
    mixed = jnp.dot(normed, w_ref[...], preferred_element_type=f32)
    block = [mixed[:, c * 128 : (c + 1) * 128] for c in range(5)]
    low = lax.broadcasted_iota(jnp.int32, block[0].shape, 1) < HEAD_DIM
    turned = [
        block[0],
        jnp.where(low, block[1], block[2]),
        block[3],
        jnp.where(low, pltpu.roll(block[1], HEAD_DIM, 1), pltpu.roll(block[4], HEAD_DIM, 1)),
    ]
    kv_ref[:, 128:] = jnp.where(low, block[2], block[4]).astype(bf16)
    prompt_total = cos_ref.shape[0] - CONT
    for start, rows, at in table_parts(lax.axis_index("dp"), prompt_total):
        cosine, sine = cos_ref[pl.ds(at, rows)], sin_ref[pl.ds(at, rows)]
        for c, u in enumerate(turned):
            u = turn(u[start : start + rows], cosine, sine).astype(bf16)
            if c < 3:
                q_ref[start : start + rows, c * 128 : (c + 1) * 128] = u
            else:
                kv_ref[start : start + rows, :128] = u


def project_call(tokens, gain, w, cosine, sine):
    count, model = tokens.shape
    width = w.shape[1]
    row = lambda n: pl.BlockSpec((TOK_MB, n), lambda i: (i, 0))
    fixed = lambda t: pl.BlockSpec(t.shape, lambda i: (0, 0))
    return pl.pallas_call(
        project_kernel,
        grid=(MICRO,),
        in_specs=[row(model), fixed(gain), fixed(w), fixed(cosine), fixed(sine)],
        out_specs=[row(model), row(width - 256), row(256)],
        out_shape=[
            jax.ShapeDtypeStruct((count, model), bf16),
            jax.ShapeDtypeStruct((count, width - 256), bf16),
            jax.ShapeDtypeStruct((count, 256), bf16),
        ],
        compiler_params=pltpu.CompilerParams(vmem_limit_bytes=48 * 2**20),
        cost_estimate=pl.CostEstimate(
            flops=2 * count * model * width, bytes_accessed=6 * count * model, transcendentals=count
        ),
    )(tokens, gain, w, cosine, sine)


def norm_rows(x_ref, b_ref):
    middle = x_ref[...].astype(f32) + b_ref[...].astype(f32)
    inverse = lax.rsqrt(jnp.mean(middle * middle, axis=-1, keepdims=True) + eps_norm)
    return middle * inverse, inverse


def route_kernel(x_ref, b_ref, gain_ref, router_ref, routes_ref, normed_ref, gates_ref):
    norm, _ = norm_rows(x_ref, b_ref)
    normed = (norm * (gain_ref[1:2] + gain_ref[3:4])).astype(bf16)
    normed_ref[...] = normed
    logits = jnp.dot(normed, router_ref[...], preferred_element_type=f32)
    lane = lax.broadcasted_iota(jnp.int32, logits.shape, 1)
    routes = routes_ref[...]
    named = lane == routes[:, 0:1]
    for k in range(1, TOPK):
        named = named | (lane == routes[:, k : k + 1])
    top = jnp.max(jnp.where(named, logits, -1e30), axis=-1, keepdims=True)
    weights = jnp.where(named, jnp.exp(jnp.where(named, logits, top) - top), 0.0)
    gates_ref[...] = weights / jnp.sum(weights, axis=-1, keepdims=True)


def route_call(tokens, branch, gain, router, routes):
    count, model = tokens.shape
    tile = 256
    row = lambda n: pl.BlockSpec((tile, n), lambda i: (i, 0))
    fixed = lambda t: pl.BlockSpec(t.shape, lambda i: (0, 0))
    return pl.pallas_call(
        route_kernel,
        grid=(count // tile,),
        in_specs=[row(model), row(model), fixed(gain), fixed(router), row(TOPK)],
        out_specs=[row(model), row(128)],
        out_shape=[
            jax.ShapeDtypeStruct((count, model), bf16),
            jax.ShapeDtypeStruct((count, 128), f32),
        ],
        compiler_params=pltpu.CompilerParams(vmem_limit_bytes=32 * 2**20),
    )(tokens, branch, gain, router, routes)


def middle_back_kernel(
    x_ref, b_ref, summed_ref, gates_ref, outgrad_ref, gain_ref, router_ref, outproj_ref,
    middle_ref, own_ref, attended_ref, logits_ref, gain_out,
):
    norm, inverse = norm_rows(x_ref, b_ref)
    model = x_ref.shape[1]
    gates = gates_ref[...]
    gate_grad = summed_ref[:, model:].astype(f32)
    chosen = gates * (gate_grad - jnp.sum(gates * gate_grad, axis=-1, keepdims=True))
    logits = chosen.astype(bf16)
    logits_ref[...] = logits
    grad = summed_ref[:, :model].astype(f32) + lax.dot_general(
        logits, router_ref[...], nt, preferred_element_type=f32
    )
    term = (grad * norm).reshape(-1, 8, model).sum(axis=0)

    @pl.when(pl.program_id(0) == 0)
    def _():
        gain_out[...] = jnp.zeros_like(gain_out)

    gain_out[...] += term
    grad = grad * (gain_ref[1:2] + gain_ref[3:4])
    mean = jnp.mean(grad * norm, axis=-1, keepdims=True)
    middle = outgrad_ref[...].astype(f32) + inverse * (grad - norm * mean)
    middle_ref[...] = middle
    own = middle.astype(bf16)
    own_ref[...] = own
    attended_ref[...] = jnp.dot(own, outproj_ref[...], preferred_element_type=f32).astype(bf16)


def middle_back_call(tokens, branch, summed, gates, outgrad, gain, router, outproj):
    count, model = tokens.shape
    tile = 256
    row = lambda n: pl.BlockSpec((tile, n), lambda i: (i, 0))
    fixed = lambda t: pl.BlockSpec(t.shape, lambda i: (0, 0))
    return pl.pallas_call(
        middle_back_kernel,
        grid=(count // tile,),
        in_specs=[
            row(model),
            row(model),
            row(model + 128),
            row(128),
            row(model),
            fixed(gain),
            fixed(router),
            fixed(outproj),
        ],
        out_specs=[
            row(model),
            row(model),
            row(outproj.shape[1]),
            row(128),
            pl.BlockSpec((8, model), lambda i: (0, 0)),
        ],
        out_shape=[
            jax.ShapeDtypeStruct((count, model), f32),
            jax.ShapeDtypeStruct((count, model), bf16),
            jax.ShapeDtypeStruct((count, outproj.shape[1]), bf16),
            jax.ShapeDtypeStruct((count, 128), bf16),
            jax.ShapeDtypeStruct((8, model), f32),
        ],
        compiler_params=pltpu.CompilerParams(vmem_limit_bytes=48 * 2**20),
    )(tokens, branch, summed, gates, outgrad, gain, router, outproj)


def block_out_kernel(x_ref, b_ref, first_ref, second_ref, o_ref):
    middle = x_ref[...].astype(f32) + b_ref[...].astype(f32)

    @pl.when(pl.program_id(0) == 0)
    def _():
        o_ref[...] = (middle + first_ref[...].astype(f32)).astype(bf16)

    @pl.when(pl.program_id(0) == 1)
    def _():
        o_ref[...] = (middle + second_ref[...].astype(f32)).astype(bf16)


def block_out_call(tokens, branch, first, second):
    count, model = tokens.shape
    columns = model // 3
    row = pl.BlockSpec((TOK_MB, columns), lambda i, j: (i, j))
    half = lambda place: pl.BlockSpec(
        (TOK_MB, columns), lambda i, j: (0, jnp.where(i == place, j, 0 if place else 2))
    )
    return pl.pallas_call(
        block_out_kernel,
        grid=(MICRO, 3),
        in_specs=[row, row, half(0), half(1)],
        out_specs=row,
        out_shape=jax.ShapeDtypeStruct((count, model), bf16),
        compiler_params=pltpu.CompilerParams(vmem_limit_bytes=32 * 2**20),
    )(tokens, branch, first, second)


def head_places(heads):
    return [(h // GROUP, h % 2, h // 2) for h in range(heads)]


def spread(kv, scale):
    lane = lax.broadcasted_iota(jnp.int32, kv.shape, 1)
    kv = kv * scale
    turned = pltpu.roll(kv, HEAD_DIM, 1)
    first = lane < HEAD_DIM
    zero = jnp.zeros_like(kv)
    return {
        (0, 0): jnp.where(first, kv, zero).astype(bf16),
        (0, 1): jnp.where(first, zero, turned).astype(bf16),
        (1, 0): jnp.where(first, turned, zero).astype(bf16),
        (1, 1): jnp.where(first, zero, kv).astype(bf16),
    }


def row_tiles(prompt_total):
    tiles = [(0, PROMPT_DEV, prompt_total)]
    for start in range(0, CONT, 256):
        tiles.append((PROMPT_DEV + start, 256, prompt_total + start + 256))
    return tiles


def greet(me, n):
    barrier = pltpu.get_barrier_semaphore()

    def one(k, carry):
        pl.semaphore_signal(
            barrier, inc=1, device_id={"dp": lax.rem(me + k, n)}, device_id_type=MESH
        )
        return carry

    lax.fori_loop(1, n, one, 0)
    return n - 1


def meet(me, n):
    pl.semaphore_wait(pltpu.get_barrier_semaphore(), greet(me, n))


def load_spread(m, all_ref, kv_ref, k_ref, v_ref, kt_ref=None):
    total = all_ref.shape[1]
    own = pl.ds(pl.multiple_of(m * TOK_MB + PROMPT_DEV, 16), CONT)
    for low, high, rows in ((0, total, all_ref[m]), (total, total + CONT, kv_ref[own])):
        keys = spread(rows[:, :128].astype(f32), HEAD_DIM**-0.5)
        values = spread(rows[:, 128:].astype(f32), 1.0)
        for i, place in enumerate(keys):
            k_ref[i, low:high] = keys[place]
            v_ref[i, low:high] = values[place]
            if kt_ref is not None:
                kt_ref[i, :, low:high] = keys[place].astype(f32).T.astype(bf16)
    return {place: i for i, place in enumerate(keys)}


def attention_kernel(
    heads, n, q_ref, kv_ref, w_ref, o_ref, lse_ref, all_ref, w_out, k_ref, v_ref, send, recv,
    *spread_out,
):
    _, start_w, forward_w, finish_w = gather_engine(n, [(w_ref, w_out)], *spread_out)
    prompt_total = all_ref.shape[1]
    me = lax.axis_index("dp")

    def piece(m, k):
        rows = all_ref.at[m, pl.ds(pl.multiple_of(me * PROMPT_DEV, PROMPT_DEV), PROMPT_DEV)]
        return pltpu.make_async_remote_copy(
            src_ref=rows,
            dst_ref=rows,
            send_sem=send.at[m, k],
            recv_sem=recv.at[m, k],
            device_id={"dp": lax.rem(me + k, n)},
            device_id_type=MESH,
        )

    for m in range(MICRO):
        all_ref[m, pl.ds(pl.multiple_of(me * PROMPT_DEV, PROMPT_DEV), PROMPT_DEV)] = kv_ref[
            m * TOK_MB : m * TOK_MB + PROMPT_DEV
        ]
    meet(me, n)

    def every(m, act):
        def one(k, carry):
            act(piece(m, k))
            return carry

        lax.fori_loop(1, n, one, 0)

    for m in range(MICRO):
        every(m, lambda copy: copy.start())
    start_w()

    def micro(m, carry):
        every(m, lambda copy: copy.wait_recv())
        index = load_spread(m, all_ref, kv_ref, k_ref, v_ref)
        lane = lax.broadcasted_iota(jnp.int32, (1, 128), 1)
        for start, rows, length in row_tiles(prompt_total):
            at = pl.ds(pl.multiple_of(m * TOK_MB + start, 128), rows)
            row = lax.broadcasted_iota(jnp.int32, (rows, 1), 0)
            if start == 0:
                masked = 0
                reach = row + me * PROMPT_DEV
            else:
                masked = length - 256
                reach = row
            column = lax.broadcasted_iota(jnp.int32, (rows, length - masked), 1)
            lse = jnp.zeros((rows, 128), f32)
            pair_out = None
            for h, (kv, half, pair) in enumerate(head_places(heads)):
                q = q_ref[at, pair * 128 : (pair + 1) * 128]
                i = index[kv, half]
                tail = lax.dot_general(q, k_ref[i, masked:length], nt, preferred_element_type=f32)
                tail = jnp.where(column <= reach, tail, -1e30)
                top = jnp.max(tail, axis=1, keepdims=True)
                if masked:
                    head = lax.dot_general(q, k_ref[i, :masked], nt, preferred_element_type=f32)
                    top = jnp.maximum(top, jnp.max(head, axis=1, keepdims=True))
                    p_head = jnp.exp(head - top)
                p_tail = jnp.exp(tail - top)
                total = jnp.sum(p_tail, axis=1, keepdims=True)
                out = jnp.dot(
                    p_tail.astype(bf16), v_ref[i, masked:length], preferred_element_type=f32
                )
                if masked:
                    total = total + jnp.sum(p_head, axis=1, keepdims=True)
                    out = out + jnp.dot(
                        p_head.astype(bf16), v_ref[i, :masked], preferred_element_type=f32
                    )
                out = out / total
                lse = jnp.where(lane == h, top + jnp.log(total), lse)
                if half == 0:
                    pair_out = out
                else:
                    o_ref[at, pair * 128 : (pair + 1) * 128] = (pair_out + out).astype(bf16)
            lse_ref[m, :, start : start + rows] = lse.T[:8]
        return carry

    lax.fori_loop(0, MICRO, micro, 0)
    for p in range(gather_parts):
        forward_w(p)
    for m in range(MICRO):
        every(m, lambda copy: copy.wait_send())
    finish_w()


def attention_call(q, kv, w, n):
    count, width = q.shape
    keys = PROMPT_DEV * n + CONT
    heads = width // HEAD_DIM
    whole = pl.BlockSpec(memory_space=pltpu.VMEM)
    return pl.pallas_call(
        functools.partial(attention_kernel, heads, n),
        in_specs=[whole] * 2 + [pl.BlockSpec(memory_space=pl.ANY)],
        out_specs=[whole] * 3 + [pl.BlockSpec(memory_space=pl.ANY)],
        out_shape=[
            jax.ShapeDtypeStruct((count, width), bf16),
            jax.ShapeDtypeStruct((MICRO, 8, TOK_MB), f32),
            jax.ShapeDtypeStruct((MICRO, PROMPT_DEV * n, 256), bf16),
            jax.ShapeDtypeStruct((n,) + w.shape, w.dtype),
        ],
        scratch_shapes=[
            pltpu.VMEM((4, keys, 128), bf16),
            pltpu.VMEM((4, keys, 128), bf16),
            pltpu.SemaphoreType.DMA((MICRO, n)),
            pltpu.SemaphoreType.DMA((MICRO, n)),
        ]
        + gather_scratch(1, n),
        compiler_params=pltpu.CompilerParams(
            collective_id=3, has_side_effects=True, vmem_limit_bytes=48 * 2**20
        ),
        cost_estimate=pl.CostEstimate(
            flops=16 * count * keys * width,
            bytes_accessed=8 * count * width,
            transcendentals=count * keys * heads,
        ),
    )(q, kv, w)


def attention_back_kernel(
    heads, n, q_ref, kv_ref, all_ref, do_ref, o_ref, lse_ref,
    cos_ref, sin_ref,
    grad_ref, k_ref, v_ref, kt_ref, dk_ref, dv_ref, sent_ref, got_ref, send, recv,
):
    prompt_total = all_ref.shape[1]
    me = lax.axis_index("dp")

    def put_both(at, dk, dv):
        low = lax.broadcasted_iota(jnp.int32, dk.shape, 1) < HEAD_DIM
        dk = pltpu.roll(dk, HEAD_DIM, 1)
        second = grad_ref[at, 128:256].astype(f32)
        grad_ref[at, 128:256] = jnp.where(low, second, dk).astype(bf16)
        grad_ref[at, 256:384] = jnp.where(low, dv, second).astype(bf16)
        grad_ref[at, 512:640] = jnp.where(low, dk, dv).astype(bf16)

    def piece(m, k):
        to = lax.rem(me + k, n)
        return pltpu.make_async_remote_copy(
            src_ref=sent_ref.at[m, pl.ds(pl.multiple_of(to * PROMPT_DEV, PROMPT_DEV), PROMPT_DEV)],
            dst_ref=got_ref.at[m, k],
            send_sem=send.at[m, k],
            recv_sem=recv.at[m, k],
            device_id={"dp": to},
            device_id_type=MESH,
        )

    def every(m, act):
        def one(k, carry):
            act(piece(m, k))
            return carry

        lax.fori_loop(1, n, one, 0)

    meet(me, n)
    half_rows = (
        lax.broadcasted_iota(jnp.int32, (8, 128), 1) // HEAD_DIM
        == lax.broadcasted_iota(jnp.int32, (8, 128), 0)
    ).astype(f32)

    def micro(m, carry):
        index = load_spread(m, all_ref, kv_ref, k_ref, v_ref, kt_ref)
        dk_ref[...] = jnp.zeros_like(dk_ref)
        dv_ref[...] = jnp.zeros_like(dv_ref)
        for start, rows, length in row_tiles(prompt_total):
            at = pl.ds(pl.multiple_of(m * TOK_MB + start, 128), rows)
            inner = slice(start, start + rows)
            column = lax.broadcasted_iota(jnp.int32, (1, rows), 1)
            if start == 0:
                masked = 0
                reach = column + me * PROMPT_DEV
            else:
                masked = length - 256
                reach = column
            key = lax.broadcasted_iota(jnp.int32, (length - masked, rows), 0)
            back = None
            for h, (kv, half, pair) in enumerate(head_places(heads)):
                lanes = slice(pair * 128, (pair + 1) * 128)
                i = index[kv, half]
                q, do = q_ref[at, lanes], do_ref[at, lanes]
                if half == 0:
                    delta_pair = lax.dot_general(
                        half_rows,
                        do.astype(f32) * o_ref[at, lanes].astype(f32),
                        nt,
                        precision=lax.Precision.HIGHEST,
                        preferred_element_type=f32,
                    )
                delta = delta_pair[half : half + 1]
                lse = lse_ref[m, h : h + 1, inner]
                for low, high in ((0, masked), (masked, length)):
                    if low == high:
                        continue
                    s = lax.dot_general(k_ref[i, low:high], q, nt, preferred_element_type=f32)
                    if low == masked:
                        s = jnp.where(key <= reach, s, -1e30)
                    p = jnp.exp(s - lse)
                    dp_ = lax.dot_general(v_ref[i, low:high], do, nt, preferred_element_type=f32)
                    ds = (p * (dp_ - delta)).astype(bf16)
                    dv_ref[i, low:high] += jnp.dot(
                        p.astype(bf16), do, preferred_element_type=f32
                    )
                    dk_ref[i, low:high] += jnp.dot(ds, q, preferred_element_type=f32)
                    term = jnp.dot(kt_ref[i, :, low:high], ds, preferred_element_type=f32)
                    back = term if back is None else back + term
                if half == 1:
                    if start == 0:
                        table = pl.ds(pl.multiple_of(me * PROMPT_DEV, PROMPT_DEV), rows)
                    else:
                        table = pl.ds(prompt_total + start - PROMPT_DEV, rows)
                    to = (0, 1, 3)[pair] * 128
                    grad_ref[at, to : to + 128] = turn(
                        back.T, cos_ref[table], -sin_ref[table]
                    ).astype(bf16)
                    back = None
        lane = lax.broadcasted_iota(jnp.int32, (dk_ref.shape[1], 128), 1)

        def joined(acc):
            get = lambda place: acc[index[place]]
            return jnp.where(
                lane < HEAD_DIM,
                get((0, 0)) + pltpu.roll(get((0, 1)), HEAD_DIM, 1),
                get((1, 1)) + pltpu.roll(get((1, 0)), HEAD_DIM, 1),
            )

        dk = turn(joined(dk_ref) * HEAD_DIM**-0.5, cos_ref[...], -sin_ref[...])
        dv = joined(dv_ref)
        sent_ref[m, :, :128] = dk[:prompt_total].astype(bf16)
        sent_ref[m, :, 128:] = dv[:prompt_total].astype(bf16)
        every(m, lambda copy: copy.start())
        own = pl.ds(pl.multiple_of(m * TOK_MB + PROMPT_DEV, 128), CONT)
        put_both(own, dk[prompt_total:], dv[prompt_total:])
        return carry

    lax.fori_loop(0, MICRO, micro, 0)

    def collect(m, carry):
        every(m, lambda copy: copy.wait_recv())
        own = sent_ref[m, pl.ds(pl.multiple_of(me * PROMPT_DEV, PROMPT_DEV), PROMPT_DEV)]
        total = lax.fori_loop(
            1, n, lambda k, t: t + got_ref[m, k].astype(f32), own.astype(f32)
        )
        at = pl.ds(pl.multiple_of(m * TOK_MB, 128), PROMPT_DEV)
        put_both(at, total[:, :128], total[:, 128:])
        every(m, lambda copy: copy.wait_send())
        return carry

    lax.fori_loop(0, MICRO, collect, 0)


def attention_back_call(q, kv, prompts, do, o, lse, cosine, sine, n):
    count, width = q.shape
    keys = prompts.shape[1] + CONT
    heads = width // HEAD_DIM
    whole = pl.BlockSpec(memory_space=pltpu.VMEM)
    return pl.pallas_call(
        functools.partial(attention_back_kernel, heads, n),
        in_specs=[whole] * 8,
        out_specs=whole,
        out_shape=jax.ShapeDtypeStruct((count, width + 256), bf16),
        scratch_shapes=[
            pltpu.VMEM((4, keys, 128), bf16),
            pltpu.VMEM((4, keys, 128), bf16),
            pltpu.VMEM((4, 128, keys), bf16),
            pltpu.VMEM((4, keys, 128), f32),
            pltpu.VMEM((4, keys, 128), f32),
            pltpu.VMEM((MICRO, prompts.shape[1], 256), bf16),
            pltpu.VMEM((MICRO, n, PROMPT_DEV, 256), bf16),
            pltpu.SemaphoreType.DMA((MICRO, n)),
            pltpu.SemaphoreType.DMA((MICRO, n)),
        ],
        compiler_params=pltpu.CompilerParams(
            collective_id=4, has_side_effects=True, vmem_limit_bytes=56 * 2**20
        ),
        cost_estimate=pl.CostEstimate(
            flops=40 * count * keys * width,
            bytes_accessed=12 * count * width,
            transcendentals=count * keys * heads,
        ),
    )(q, kv, prompts, do, o, lse, cosine, sine)


def attend(queries, keys_all, values_all, allowed):
    factor = HEAD_DIM ** (-0.5)
    scores = jnp.einsum("tkgd,skd->kgts", queries, keys_all, preferred_element_type=f32) * factor
    scores = jnp.where(allowed, scores, -1e30)
    row_max = jnp.max(scores, axis=-1, keepdims=True)
    exponent = jnp.exp(scores - row_max)
    softened = exponent / jnp.sum(exponent, axis=-1, keepdims=True)
    soft_low = softened.astype(bf16)
    attended = jnp.einsum("kgts,skd->tkgd", soft_low, values_all, preferred_element_type=f32)
    return attended.astype(bf16), softened, soft_low


def attend_back(queries, keys_all, values_all, softened, soft_low, attended_grad):
    factor = HEAD_DIM ** (-0.5)
    soft_grad = jnp.einsum("tkgd,skd->kgts", attended_grad, values_all, preferred_element_type=f32)
    values_grad = jnp.einsum("kgts,tkgd->skd", soft_low, attended_grad, preferred_element_type=f32)
    row_delta = jnp.sum(softened * soft_grad, axis=-1, keepdims=True)
    scores_grad = (softened * (soft_grad - row_delta)).astype(bf16)
    queries_grad = (
        jnp.einsum("kgts,skd->tkgd", scores_grad, keys_all, preferred_element_type=f32) * factor
    )
    keys_grad = (
        jnp.einsum("kgts,tkgd->skd", scores_grad, queries, preferred_element_type=f32) * factor
    )
    return queries_grad, keys_grad, values_grad


def shards(
    tokens, cotangent, routes,
    inproj_weight, inproj_first, inproj_second,
    outproj_weight, outproj_first, outproj_second,
    gateup_weight, gateup_first, gateup_second,
    down_weight, down_first, down_second,
    router_weight, router_first, router_second,
    gains, gains_first, gains_second,
):
    n_dp = lax.axis_size("dp")
    n_tensor = lax.axis_size("tensor")
    depth = inproj_weight.shape[0]
    kv_local = inproj_weight.shape[1]
    hidden = down_weight.shape[1]
    group = max(1, 256 // hidden)
    groups = EXPERTS // group
    in_width = inproj_weight.shape[1] * inproj_weight.shape[2]
    out_width = outproj_weight.shape[0] * outproj_weight.shape[1]
    prompt_total = PROMPT_DEV * n_dp
    count = tokens.shape[0]

    def gateup_flat(w):
        w = w.reshape(groups, group, depth, 2, hidden)
        return w.transpose(2, 0, 3, 1, 4).reshape(depth, 2 * EXPERTS * hidden)

    def gateup_back(w):
        w = w.reshape(depth, groups, 2, group, hidden)
        return w.transpose(1, 3, 0, 2, 4).reshape(EXPERTS, depth, 2, hidden)

    query_width = GROUP * HEAD_DIM
    gains_high = gains.astype(bf16)
    gains_low = (gains - gains_high.astype(f32)).astype(bf16)
    attn_local = (
        inproj_weight.reshape(depth, in_width).astype(bf16),
        outproj_weight.reshape(out_width, depth).T.astype(bf16),
        jnp.concatenate(
            [
                router_weight.astype(bf16),
                gains_high.T,
                gains_low.T,
                jnp.zeros((depth, 128 - EXPERTS - 4), bf16),
            ],
            axis=1,
        ),
    )
    if hidden == 128:
        inproj_full, outproj_full, small_full, gu_local = gather(
            attn_local, gateup_weight.reshape(-1, hidden), n_dp, group, 5
        )
    else:
        inproj_full, outproj_full, small_full = gather(attn_local, None, n_dp, None, 5)
        gu_local = gateup_flat(gateup_weight.astype(bf16))
    down_local = down_weight.reshape(EXPERTS * hidden, depth).T.astype(bf16)
    gain_rows = small_full[:, EXPERTS : EXPERTS + 8].astype(f32).T

    device_index = lax.axis_index("dp")
    half_dim = HEAD_DIM // 2
    freqs = np.float32(10000.0) ** (-2.0 * np.arange(half_dim, dtype=np.float32) / HEAD_DIM)
    angles = np.arange(prompt_total + CONT, dtype=np.float32)[:, None] * freqs.astype(np.float32)
    cosine, sine = np.cos(angles), np.sin(angles)

    def of_rows(table):
        own = lax.dynamic_slice_in_dim(
            jnp.asarray(table), device_index * PROMPT_DEV, PROMPT_DEV, 0
        )
        return jnp.concatenate([own, table[prompt_total:]], axis=0)

    in_kernels = kv_local * HEAD_DIM == 128
    both_width = kv_local * 2 * HEAD_DIM
    if in_kernels:
        cos_all = np.concatenate([cosine] * 4, axis=1)
        sin_all = np.concatenate([-sine, sine] * 2, axis=1)
        normed_first, queries, both = project_call(
            tokens, gain_rows, inproj_full, cos_all, sin_all
        )
    else:
        cosine, sine = (jnp.tile(of_rows(t), (MICRO, 1))[:, None, :] for t in (cosine, sine))
        inputs = tokens.astype(f32)
        inverse_first = lax.rsqrt(jnp.mean(inputs * inputs, axis=-1, keepdims=True) + eps_norm)
        normed_first = (inputs * inverse_first * (gain_rows[0:1] + gain_rows[2:3])).astype(bf16)
        mixed = jnp.dot(normed_first, inproj_full, preferred_element_type=f32)
        mixed = mixed.reshape(count, kv_local, -1)
        queries = rotate(
            mixed[..., :query_width].reshape(count, -1, HEAD_DIM), cosine, sine
        ).astype(bf16)
        keys = rotate(mixed[..., query_width : query_width + HEAD_DIM], cosine, sine)
        both = jnp.concatenate(
            [keys.reshape(count, -1), mixed[..., query_width + HEAD_DIM :].reshape(count, -1)],
            axis=1,
        ).astype(bf16)
    if in_kernels:
        attended, lse, prompt_both, down_start = attention_call(
            queries, both, down_local[:, : down_local.shape[1] // 2], n_dp
        )
        down_start = down_start.reshape(n_dp * depth, -1)
        down_rest = down_local[:, down_local.shape[1] // 2 :]
    else:
        both = both.reshape(MICRO, TOK_MB, both_width)
        prompt_both = lax.all_gather(both[:, :PROMPT_DEV], "dp", axis=1, tiled=True)
        both_all = jnp.concatenate([prompt_both, both[:, PROMPT_DEV:]], axis=1)
        inner = jnp.arange(TOK_MB, dtype=jnp.int32)
        positions = jnp.where(
            inner < PROMPT_DEV, device_index * PROMPT_DEV + inner, prompt_total + inner - PROMPT_DEV
        )
        key_index = jnp.arange(prompt_total + CONT, dtype=jnp.int32)
        allowed = (key_index[None, :] <= positions[:, None]) & (
            (key_index[None, :] < prompt_total) | (inner[:, None] >= PROMPT_DEV)
        )
        kept = []
        attended = []
        for m in range(MICRO):
            q = queries[m * TOK_MB : (m + 1) * TOK_MB].reshape(TOK_MB, kv_local, GROUP, HEAD_DIM)
            k, v = (
                t.reshape(-1, kv_local, HEAD_DIM) for t in jnp.split(both_all[m], 2, axis=1)
            )
            out, softened, soft_low = attend(q, k, v, allowed)
            attended.append(out.reshape(TOK_MB, -1))
            kept.append((q, k, v, softened, soft_low))
        attended = jnp.concatenate(attended, axis=0)
    branch = lax.dot_general(
        attended, outproj_full, (((1,), (1,)), ((), ())), preferred_element_type=f32
    ).astype(bf16)
    branch, gu_full, down_rest = line_gather(
        branch, gu_local, down_rest if in_kernels else down_local, n_tensor, n_dp, 6
    )
    if not in_kernels:
        down_start, down_rest = jnp.split(down_rest, 2, axis=1)

    normed_second, gates_wide = route_call(tokens, branch, gain_rows, small_full, routes)
    active, hidden_grad, gate_grad = expert_call(
        normed_second, cotangent, gates_wide, gu_full, down_start, down_rest, group
    )
    contract_last = (((1,), (1,)), ((), ()))
    contract_first = (((0,), (0,)), ((), ()))
    rows_grad = lax.dot_general(
        hidden_grad, gu_full, contract_last, preferred_element_type=f32
    ).astype(bf16)
    summed, gateup_grad, down_grad, mixture = expert_grads_call(
        jnp.concatenate([rows_grad, gate_grad.astype(bf16)], axis=1),
        normed_second, cotangent, down_start, down_rest, hidden_grad, active, n_tensor, 2,
    )
    first_mixture = lax.psum(mixture[:TOK_MB], "tensor")
    model = tokens.shape[1]
    middle_grad, branch_own, attended_grad, logits_grad, gain_second_grad = middle_back_call(
        tokens, branch, summed, gates_wide, cotangent, gain_rows, small_full, outproj_full
    )
    middle_grad, attended_grad, down_grad, gateup_grad = lax.optimization_barrier(
        (middle_grad, attended_grad, down_grad, gateup_grad)
    )
    down_grad = lax.psum_scatter(down_grad, "dp", scatter_dimension=0, tiled=True)
    gateup_grad = lax.psum_scatter(gateup_grad, "dp", scatter_dimension=0, tiled=True)
    router_grad = lax.dot_general(
        normed_second, logits_grad, contract_first, preferred_element_type=f32
    ).astype(bf16)
    outproj_grad = lax.dot_general(
        branch_own, attended, contract_first, preferred_element_type=f32
    ).astype(bf16)
    if in_kernels:
        mixed_grad = attention_back_call(
            queries, both, prompt_both, attended_grad, attended, lse, cos_all, sin_all, n_dp
        )
    else:
        queries_grad, both_grad = [], []
        for m in range(MICRO):
            q, k, v, softened, soft_low = kept[m]
            dout = attended_grad[m * TOK_MB : (m + 1) * TOK_MB].reshape(q.shape)
            dq, dk, dv = attend_back(q, k, v, softened, soft_low, dout)
            queries_grad.append(dq.reshape(TOK_MB, -1, HEAD_DIM))
            both_grad.append(jnp.concatenate([t.reshape(-1, both_width // 2) for t in (dk, dv)], 1))
        queries_grad = rotate(jnp.concatenate(queries_grad, axis=0), cosine, -sine)
        both_grad = jnp.stack(both_grad)
        prompt_grad = lax.psum_scatter(
            both_grad[:, :prompt_total].astype(bf16), "dp", scatter_dimension=1, tiled=True
        )
        both_grad = jnp.concatenate(
            [prompt_grad.astype(f32), both_grad[:, prompt_total:]], axis=1
        ).reshape(count, both_width)
        keys_grad = rotate(
            both_grad[:, : both_width // 2].reshape(count, -1, HEAD_DIM), cosine, -sine
        )
        mixed_grad = jnp.concatenate(
            [
                t.reshape(count, kv_local, -1)
                for t in (queries_grad, keys_grad, both_grad[:, both_width // 2 :])
            ],
            axis=2,
        )
        mixed_grad = mixed_grad.reshape(count, -1).astype(bf16)
    normed_first_grad = lax.dot_general(
        mixed_grad, inproj_full, contract_last, preferred_element_type=f32
    ).astype(bf16)
    inproj_grad = lax.dot_general(
        normed_first, mixed_grad, contract_first, preferred_element_type=f32
    ).astype(bf16)
    attn_grad = [inproj_grad, outproj_grad, router_grad]
    if in_width % 128 or out_width % 128:
        attn_grad = [jnp.concatenate(attn_grad, axis=1)]
    down_next = adam_update(
        down_weight, down_first, down_second,
        down_grad.T.reshape(down_weight.shape).astype(f32), weight_decay, 0.05,
    )
    if hidden == 128:
        gateup_next = gateup_adam(gateup_weight, gateup_first, gateup_second, gateup_grad, group)
    else:
        gateup_next = adam_update(
            gateup_weight, gateup_first, gateup_second,
            gateup_back(gateup_grad).astype(f32), weight_decay, 0.05,
        )
    tokens_grad, attn_grad, gains_grad, second_mixture = last_call(
        normed_first_grad, tokens, middle_grad, mixture, gain_rows,
        attn_grad, gain_second_grad, n_tensor, n_dp, 7,
    )
    first_mixture, tokens_grad = lax.optimization_barrier((first_mixture, tokens_grad))
    block_out = block_out_call(tokens, branch, first_mixture, second_mixture)
    split = (in_width, in_width + out_width, in_width + out_width + EXPERTS)
    inproj_grad, outproj_grad, router_grad = (
        attn_grad[:, : split[0]],
        attn_grad[:, split[0] : split[1]],
        attn_grad[:, split[1] : split[2]],
    )
    updates = (
        adam_update(
            inproj_weight, inproj_first, inproj_second,
            inproj_grad.reshape(inproj_weight.shape), weight_decay, 0.05,
        ),
        adam_update(
            outproj_weight, outproj_first, outproj_second,
            outproj_grad.T.reshape(outproj_weight.shape), weight_decay, 0.3,
        ),
        gateup_next,
        down_next,
        adam_update(router_weight, router_first, router_second, router_grad, weight_decay, 0.05),
        adam_update(gains, gains_first, gains_second, gains_grad, 0.0, 0.4),
    )
    return (block_out, tokens_grad) + sum(updates, ())


def solution(mesh):
    row = P("dp", None)
    inproj = P("dp", "tensor", None)
    outproj = P("tensor", None, "dp")
    gateup = P(None, "dp", None, "tensor")
    down = P(None, "tensor", "dp")
    gain = P(None, "dp")
    weights = (inproj,) * 3 + (outproj,) * 3 + (gateup,) * 3 + (down,) * 3 + (row,) * 3 + (gain,) * 3
    return jax.shard_map(
        shards,
        mesh=mesh,
        in_specs=(row, row, row) + weights,
        out_specs=(row, row) + weights,
        check_vma=False,
    )
```

```python
import functools

import jax
import jax.numpy as jnp
import numpy as np
from jax import lax
from jax.experimental import pallas as pl
from jax.experimental.pallas import tpu as pltpu
from jax.sharding import PartitionSpec as P

HEAD_DIM = 64
TOPK = 8
EXPERTS = 16
PROMPT_DEV = 128
CONT = 512
MICRO = 2
STEP = 10
GROUP = 3
TOK_MB = 640

eps_norm = 1e-05
beta_first = 0.9
beta_second = 0.95
adam_eps = 1e-08
weight_decay = 0.1
bf16 = jnp.bfloat16
f32 = jnp.float32
line_parts = 20
line_lag = 2
MESH = pl.DeviceIdType.MESH
nt = (((1,), (1,)), ((), ()))


def rotate(values, cosine, sine):
    half_dim = values.shape[-1] // 2
    first_half = values[..., :half_dim]
    second_half = values[..., half_dim:]
    return jnp.concatenate(
        [first_half * cosine - second_half * sine, second_half * cosine + first_half * sine],
        axis=-1,
    )


def adam_update(weight, moment_one, moment_two, gradient, decay_rate, learn_rate):
    first_next = beta_first * moment_one + (1.0 - beta_first) * gradient
    second_next = beta_second * moment_two + (1.0 - beta_second) * gradient * gradient
    corr_first = 1.0 - beta_first**STEP
    corr_second = 1.0 - beta_second**STEP
    update = first_next / corr_first / (jnp.sqrt(second_next / corr_second) + adam_eps)
    return (weight - learn_rate * (update + decay_rate * weight), first_next, second_next)


def line_steps(n, parts=line_parts):
    return parts + 2 * (n - 1) * line_lag


def line_engine(
    n, x_ref, o_ref, held, send_red, recv_red, send_out, recv_out,
    complete=lambda at, half, c: None, parts=line_parts,
):
    me = lax.axis_index("tensor")
    rows = x_ref.shape[0] // (2 * parts)
    low, high = me - 1, me + 1

    def greet():
        barrier = pltpu.get_barrier_semaphore()

        @pl.when(me > 0)
        def _():
            pl.semaphore_signal(barrier, inc=1, device_id={"tensor": low}, device_id_type=MESH)

        @pl.when(me < n - 1)
        def _():
            pl.semaphore_signal(barrier, inc=1, device_id={"tensor": high}, device_id_type=MESH)

        return jnp.where((me > 0) & (me < n - 1), 2, 1)

    def begin():
        pl.semaphore_wait(pltpu.get_barrier_semaphore(), greet())

    def part(half, c):
        return pl.ds(pl.multiple_of((half * parts + c) * rows, 16), rows)

    def reduce_copy(half, c, src):
        to = low if half == 0 else high
        return pltpu.make_async_remote_copy(
            src_ref=src.at[part(half, c)],
            dst_ref=held.at[part(half, c)],
            send_sem=send_red.at[half, c],
            recv_sem=recv_red.at[half, c],
            device_id={"tensor": to},
            device_id_type=MESH,
        )

    def out_copy(half, c):
        to = high if half == 0 else low
        return pltpu.make_async_remote_copy(
            src_ref=o_ref.at[part(half, c)],
            dst_ref=o_ref.at[part(half, c)],
            send_sem=send_out.at[half, c],
            recv_sem=recv_out.at[half, c],
            device_id={"tensor": to},
            device_id_type=MESH,
        )

    def place(half):
        return n - 1 - me if half == 0 else me

    def slot(t):
        for half in (0, 1):
            at = place(half)
            c = t - line_lag * at

            @pl.when((c >= 0) & (c < parts))
            def _():
                @pl.when(at == 0)
                def _():
                    reduce_copy(half, c, x_ref).start()

                @pl.when(at > 0)
                def _():
                    reduce_copy(half, c, held).wait_recv()
                    total = x_ref[part(half, c)].astype(f32) + held[part(half, c)].astype(f32)

                    @pl.when(at < n - 1)
                    def _():
                        held[part(half, c)] = total.astype(held.dtype)
                        reduce_copy(half, c, held).start()

                    @pl.when(at == n - 1)
                    def _():
                        o_ref[part(half, c)] = total.astype(o_ref.dtype)
                        out_copy(half, c).start()
                        complete(part(half, c), half, c)

        for half in (0, 1):
            at = place(half)
            c = t - line_lag * (2 * (n - 1) - at)

            @pl.when((at < n - 1) & (c >= 0) & (c < parts))
            def _():
                out_copy(half, c).wait_recv()

                @pl.when(at > 0)
                def _():
                    out_copy(half, c).start()

                complete(part(half, c), half, c)

    def finish():
        def one(c, carry):
            for half in (0, 1):
                at = place(half)

                @pl.when(at < n - 1)
                def _():
                    reduce_copy(half, c, held).wait_send()

                @pl.when(at > 0)
                def _():
                    out_copy(half, c).wait_send()

            return carry

        lax.fori_loop(0, parts, one, 0)

    return greet, begin, slot, finish


def line_scratch(shape, dtype, parts=line_parts):
    return [pltpu.VMEM(shape, dtype)] + [
        pltpu.SemaphoreType.DMA((2, parts)) for _ in range(4)
    ]


def line_sum_kernel(n, x_ref, o_ref, *scratch):
    _, begin, slot, finish = line_engine(n, x_ref, o_ref, *scratch)
    begin()

    def step(t, carry):
        slot(t)
        return carry

    lax.fori_loop(0, line_steps(n), step, 0)
    finish()


def line_sum(x, n, barrier_id):
    rows, width = x.shape
    return pl.pallas_call(
        functools.partial(line_sum_kernel, n),
        out_shape=jax.ShapeDtypeStruct(x.shape, x.dtype),
        in_specs=[pl.BlockSpec(memory_space=pltpu.VMEM)],
        out_specs=pl.BlockSpec(memory_space=pltpu.VMEM),
        scratch_shapes=line_scratch(x.shape, x.dtype),
        compiler_params=pltpu.CompilerParams(
            collective_id=barrier_id, has_side_effects=True, vmem_limit_bytes=24 * 2**20
        ),
        cost_estimate=pl.CostEstimate(
            flops=rows * width, bytes_accessed=100 * rows * width, transcendentals=0
        ),
    )(x)


gather_parts = 3


def gather_engine(n, pairs, own_sem, far_send, far_recv, near_send, near_recv):
    me = lax.axis_index("dp")
    core, chip, chips = lax.rem(me, 2), me // 2, n // 2

    def rows(a, p):
        size = pairs[a][0].shape[0] // gather_parts
        return pl.ds(p * size, size)

    def far(a, p, k):
        x_ref, out_ref = pairs[a]
        return pltpu.make_async_remote_copy(
            src_ref=x_ref.at[rows(a, p)],
            dst_ref=out_ref.at[me, rows(a, p)],
            send_sem=far_send.at[a, p, k],
            recv_sem=far_recv.at[a, p, k],
            device_id={"dp": lax.rem(chip + k, chips) * 2 + core},
            device_id_type=MESH,
        )

    def near(a, p, k):
        x_ref, out_ref = pairs[a]
        owner = lax.rem(chip + chips - k, chips) * 2 + core
        target = out_ref.at[owner, rows(a, p)]
        return pltpu.make_async_remote_copy(
            src_ref=x_ref.at[rows(a, p)] if k == 0 else target,
            dst_ref=target,
            send_sem=near_send.at[a, p, k],
            recv_sem=near_recv.at[a, p, k],
            device_id={"dp": me + 1 - 2 * core},
            device_id_type=MESH,
        )

    def own(a):
        x_ref, out_ref = pairs[a]
        return pltpu.make_async_copy(x_ref, out_ref.at[me], own_sem.at[a])

    arrays = range(len(pairs))

    def greet():
        barrier = pltpu.get_barrier_semaphore()
        for k in range(1, chips):
            pl.semaphore_signal(
                barrier,
                inc=1,
                device_id={"dp": lax.rem(chip + k, chips) * 2 + core},
                device_id_type=MESH,
            )
        pl.semaphore_signal(
            barrier, inc=1, device_id={"dp": me + 1 - 2 * core}, device_id_type=MESH
        )
        return chips

    def start():
        for p in range(gather_parts):
            for a in arrays:
                for k in range(1, chips):
                    far(a, p, k).start()
        for p in range(gather_parts):
            for a in arrays:
                near(a, p, 0).start()
        for a in arrays:
            own(a).start()

    def forward(p):
        for a in arrays:
            for k in range(1, chips):
                far(a, p, k).wait_recv()
                near(a, p, k).start()

    def finish():
        for a in arrays:
            own(a).wait()
            for p in range(gather_parts):
                for k in range(chips):
                    near(a, p, k).wait_recv()
                    near(a, p, k).wait_send()
                    if k:
                        far(a, p, k).wait_send()

    return greet, start, forward, finish


def gather_scratch(arrays, n):
    return [pltpu.SemaphoreType.DMA((arrays,))] + [
        pltpu.SemaphoreType.DMA((arrays, gather_parts, n // 2)) for _ in range(4)
    ]


def gateup_column(e, part, group, hidden):
    return (e // group * 2 * group + part * group + e % group) * hidden


def gather_kernel(n, group, count, *refs):
    x_refs, refs = refs[:count], refs[count:]
    w_ref, refs = (None, refs) if group is None else (refs[0], refs[1:])
    out_refs, refs = refs[:count], refs[count:]
    low_ref, scratch = (None, refs) if group is None else (refs[0], refs[1:])
    greet, start, forward, finish = gather_engine(n, list(zip(x_refs, out_refs)), *scratch)
    pl.semaphore_wait(pltpu.get_barrier_semaphore(), greet())
    start()
    if group is not None:
        depth, hidden = low_ref.shape[0], w_ref.shape[1]
        for e in range(EXPERTS):
            for part in (0, 1):
                at = gateup_column(e, part, group, hidden)
                low_ref[:, at : at + hidden] = w_ref[
                    pl.ds(e * 2 * depth + part, depth, stride=2)
                ].astype(bf16)
    for p in range(gather_parts):
        forward(p)
    finish()


def gather(arrays, w, n, group, barrier_id):
    depth = arrays[0].shape[0]
    whole = pl.BlockSpec(memory_space=pltpu.VMEM)
    shapes = [jax.ShapeDtypeStruct((n,) + x.shape, x.dtype) for x in arrays]
    operands = list(arrays)
    if group is not None:
        operands.append(w)
        shapes.append(jax.ShapeDtypeStruct((depth, w.size // depth), bf16))
    out = pl.pallas_call(
        functools.partial(gather_kernel, n, group, len(arrays)),
        out_shape=shapes,
        in_specs=[whole] * len(operands),
        out_specs=[whole] * len(shapes),
        scratch_shapes=gather_scratch(len(arrays), n),
        compiler_params=pltpu.CompilerParams(
            collective_id=barrier_id, has_side_effects=True, vmem_limit_bytes=24 * 2**20
        ),
    )(*operands)
    count = len(arrays)
    return [t.reshape(n * depth, -1) for t in out[:count]] + list(out[count:])


def expert_adam_kernel(
    group, w_ref, m_ref, v_ref, grad_ref, dw_ref, dm_ref, dv_ref, down_ref,
    w_out, m_out, v_out, dw_out, dm_out, dv_out, g_ref,
):
    depth, hidden = grad_ref.shape[0], w_ref.shape[1]
    for e in range(w_ref.shape[0] // (2 * depth)):
        for part in (0, 1):
            at = gateup_column(e, part, group, hidden)
            g_ref[pl.ds(part, depth, stride=2)] = grad_ref[:, at : at + hidden].astype(f32)
        rows = slice(e * 2 * depth, (e + 1) * 2 * depth)
        w_out[rows], m_out[rows], v_out[rows] = adam_update(
            w_ref[rows], m_ref[rows], v_ref[rows], g_ref[...], weight_decay, 0.05
        )
        rows = slice(e * depth, (e + 1) * depth)
        dw_out[rows], dm_out[rows], dv_out[rows] = adam_update(
            dw_ref[rows],
            dm_ref[rows],
            dv_ref[rows],
            down_ref[:, e * hidden : (e + 1) * hidden].astype(f32),
            weight_decay,
            0.05,
        )


def expert_adam(gateup, gateup_grad, down, down_grad, group):
    experts, depth, parts, hidden = gateup[0].shape
    flat = [t.reshape(-1, hidden) for t in gateup]
    turned = [t.transpose(0, 2, 1).reshape(-1, hidden) for t in down]
    each = 2 * group
    block = lambda n: pl.BlockSpec((each * depth * n, hidden), lambda e: (e, 0))
    column = lambda n: pl.BlockSpec((depth, each * n * hidden), lambda e: (0, e))
    out = pl.pallas_call(
        functools.partial(expert_adam_kernel, group),
        grid=(experts // each,),
        in_specs=[block(2)] * 3 + [column(2)] + [block(1)] * 3 + [column(1)],
        out_specs=[block(2)] * 3 + [block(1)] * 3,
        out_shape=[jax.ShapeDtypeStruct(t.shape, f32) for t in flat + turned],
        scratch_shapes=[pltpu.VMEM((depth * parts, hidden), f32)],
        compiler_params=pltpu.CompilerParams(vmem_limit_bytes=60 * 2**20),
    )(*flat, gateup_grad, *turned, down_grad)
    return (
        tuple(t.reshape(gateup[0].shape) for t in out[:3]),
        tuple(t.reshape(experts, depth, hidden).transpose(0, 2, 1) for t in out[3:]),
    )


def line_gather_kernel(n, n_dp, x_ref, a_ref, b_ref, o_ref, a_out, b_out, *scratch):
    line, spread_out = scratch[:5], scratch[5:]
    greet, _, slot, finish = line_engine(n, x_ref, o_ref, *line)
    greet_dp, start, forward, finish_dp = gather_engine(
        n_dp, [(a_ref, a_out), (b_ref, b_out)], *spread_out
    )
    peers = greet() + greet_dp()
    pl.semaphore_wait(pltpu.get_barrier_semaphore(), peers)
    start()

    def step(t, carry):
        slot(t)
        return carry

    total = line_steps(n)
    done = 0
    for p in range(gather_parts):
        until = total * (p + 1) // gather_parts
        lax.fori_loop(done, until, step, 0)
        done = until
        forward(p)
    finish()
    finish_dp()


def line_gather(x, a, b, n, n_dp, barrier_id):
    rows, width = x.shape
    whole, anywhere = pl.BlockSpec(memory_space=pltpu.VMEM), pl.BlockSpec(memory_space=pl.ANY)
    o, a_all, b_all = pl.pallas_call(
        functools.partial(line_gather_kernel, n, n_dp),
        out_shape=[jax.ShapeDtypeStruct(x.shape, x.dtype)]
        + [jax.ShapeDtypeStruct((n_dp,) + t.shape, t.dtype) for t in (a, b)],
        in_specs=[whole, anywhere, anywhere],
        out_specs=[whole, anywhere, anywhere],
        scratch_shapes=line_scratch(x.shape, x.dtype) + gather_scratch(2, n_dp),
        compiler_params=pltpu.CompilerParams(
            collective_id=barrier_id, has_side_effects=True, vmem_limit_bytes=24 * 2**20
        ),
        cost_estimate=pl.CostEstimate(
            flops=rows * width, bytes_accessed=100 * rows * width, transcendentals=0
        ),
    )(x, a, b)
    return o, a_all.reshape(-1, a.shape[1]), b_all.reshape(-1, b.shape[1])


def last_kernel(
    n, n_dp, pieces, first_ref, tokens_ref, middle_ref, mixture_ref, gain_ref, gain_second_ref, *refs,
):
    weights_refs, refs = refs[:pieces], refs[pieces:]
    last_body(
        n, n_dp, first_ref, tokens_ref, middle_ref, mixture_ref, gain_ref, weights_refs,
        gain_second_ref, *refs,
    )


def last_body(
    n, n_dp, first_ref, tokens_ref, middle_ref, mixture_ref, gain_ref, weights_refs,
    gain_second_ref, grad_ref, weights_out, gains_out, mixture_out,
    x_ref, o_ref, held, send_red, recv_red, send_out, recv_out,
    tokens_v, middle_v, grad_v, in_sem, out_sem, x_sem, got, w_send, w_recv,
    g_from, g_got, g_send, g_recv, z_from, z_got, z_send, z_recv, acc,
):
    me, line = lax.axis_index("dp"), lax.axis_index("tensor")
    model = x_ref.shape[1]
    rows = tokens_v.shape[0] // (2 * line_parts)
    depth = weights_out.shape[0]
    half_x, half_m = line_parts * rows, TOK_MB // 2
    half_all = half_x + half_m
    parts = half_all // rows

    def own_rows(half, c):
        return pl.ds(pl.multiple_of((half * line_parts + c) * rows, 16), rows)

    def half_copies(x, m, sem, back):
        for half in (0, 1):
            for ref, low, size, at in (
                (x, half * half_x, half_x, half * half_all),
                (m[0], m[1] + half * half_m, half_m, half * half_all + half_x),
            ):
                if ref is not None:
                    here = (o_ref if back else x_ref).at[pl.ds(at, size)]
                    there = ref.at[pl.ds(low, size)]
                    k = half * 2 + (ref is m[0])
                    yield pltpu.make_async_copy(
                        *((here, there) if back else (there, here)), sem.at[k]
                    )

    def norm_of(at):
        x = tokens_v[at].astype(f32)
        inverse = lax.rsqrt(jnp.mean(x * x, axis=-1, keepdims=True) + eps_norm)
        return x * inverse, inverse

    def complete(at, half, c):
        @pl.when(c < line_parts)
        def _():
            own = own_rows(half, c)
            norm, inverse = norm_of(own)
            grad = o_ref[at].astype(f32) * (gain_ref[0:1] + gain_ref[2:3])
            mean = jnp.mean(grad * norm, axis=-1, keepdims=True)
            grad_v[own] = middle_v[own] + inverse * (grad - norm * mean)

    _, _, slot, finish = line_engine(
        n, x_ref, o_ref, held, send_red, recv_red, send_out, recv_out, complete, parts
    )

    columns, low = [], 0
    for ref in weights_refs:
        columns.append(slice(low, low + ref.shape[2]))
        low += ref.shape[2]
    pieces = range(len(columns))

    def weights_copy(k, j):
        to = lax.rem(me + k, n_dp)
        return pltpu.make_async_remote_copy(
            src_ref=weights_refs[j].at[to], dst_ref=got.at[k, :, columns[j]],
            send_sem=w_send.at[j, k], recv_sem=w_recv.at[j, k],
            device_id={"dp": to}, device_id_type=MESH,
        )

    def gains_copy(k):
        to = lax.rem(me + k, n_dp)
        return pltpu.make_async_remote_copy(
            src_ref=g_from.at[to], dst_ref=g_got.at[k],
            send_sem=g_send.at[k], recv_sem=g_recv.at[k],
            device_id={"dp": to}, device_id_type=MESH,
        )

    def line_copy(k):
        to = lax.rem(line + k, n)
        return pltpu.make_async_remote_copy(
            src_ref=z_from, dst_ref=z_got.at[k],
            send_sem=z_send.at[k], recv_sem=z_recv.at[k],
            device_id={"tensor": to}, device_id_type=MESH,
        )

    def loop(count, act):
        def one(k, carry):
            act(k)
            return carry

        lax.fori_loop(1, count, one, 0)

    load_tokens = pltpu.make_async_copy(tokens_ref, tokens_v, in_sem.at[0])
    load_middle = pltpu.make_async_copy(middle_ref, middle_v, in_sem.at[1])
    loads = list(half_copies(first_ref, (mixture_ref, TOK_MB), x_sem, False))
    for load in loads + [load_tokens, load_middle]:
        load.start()
    barrier = pltpu.get_barrier_semaphore()

    def greet(axis, place, count):
        loop(
            count,
            lambda k: pl.semaphore_signal(
                barrier, inc=1, device_id={axis: lax.rem(place + k, count)}, device_id_type=MESH
            ),
        )

    greet("dp", me, n_dp)
    greet("tensor", line, n)
    pl.semaphore_wait(barrier, n_dp + n - 2)
    for j in pieces:
        loop(n_dp, lambda k: weights_copy(k, j).start())
    acc[...] = jnp.zeros_like(acc)
    for load in loads:
        load.wait()

    def step(t, carry):
        slot(t)
        return carry

    def gain_step(t, carry):
        slot(t)
        c = t - early
        for half in (0, 1):
            at = pl.ds(pl.multiple_of(half * half_all + c * rows, 16), rows)
            norm, _ = norm_of(own_rows(half, c))
            term = x_ref[at].astype(f32) * norm
            acc[...] += jnp.sum(term.reshape(rows // 8, 8, model), axis=0)
        return carry

    total = line_steps(n, parts)
    early, size = 4, 32
    lax.fori_loop(0, early, step, 0)
    for load in (load_tokens, load_middle):
        load.wait()
    low = early + line_parts
    lax.fori_loop(early, low, gain_step, 0)
    width = g_from.shape[2]
    for p in range(n_dp):
        moved = acc[...] if p == 0 else pltpu.roll(acc[...], model - p * depth, 1)
        g_from[p, :8] = moved[:, :width]
        moved = gain_second_ref[...] if p == 0 else pltpu.roll(
            gain_second_ref[...], model - p * depth, 1
        )
        g_from[p, 8:] = jnp.where(line == 0, moved[:, :width], 0.0)
    loop(n_dp, lambda k: gains_copy(k).start())
    for j in pieces:
        loop(n_dp, lambda k: weights_copy(k, j).wait_recv())

    def add_step(t, carry):
        slot(t)
        at = pl.ds(pl.multiple_of((t - low) * size, 16), size)
        for j, ref in enumerate(weights_refs):
            weights_out[at, columns[j]] = lax.fori_loop(
                1,
                n_dp,
                lambda k, v: v + got[k, at, columns[j]].astype(f32),
                ref[me, at].astype(f32),
            )
        return carry

    middle = low + depth // size
    lax.fori_loop(low, middle, add_step, 0)
    loop(n_dp, lambda k: gains_copy(k).wait_recv())
    z_from[...] = lax.fori_loop(1, n_dp, lambda k, v: v + g_got[k], g_from[me])
    loop(n, lambda k: line_copy(k).start())
    own_done = max(middle, line_steps(n))
    lax.fori_loop(middle, own_done, step, 0)
    every = pltpu.make_async_copy(grad_v, grad_ref, out_sem)
    every.start()
    lax.fori_loop(own_done, total, step, 0)
    stores = list(half_copies(None, (mixture_out, 0), x_sem, True))
    for store in stores:
        store.start()
    loop(n, lambda k: line_copy(k).wait_recv())
    gains_out[...] = lax.fori_loop(1, n, lambda k, v: v + z_got[k], z_from[...])
    finish()
    for j in pieces:
        loop(n_dp, lambda k: weights_copy(k, j).wait_send())
    loop(n_dp, lambda k: gains_copy(k).wait_send())
    loop(n, lambda k: line_copy(k).wait_send())
    for store in stores + [every]:
        store.wait()


def last_call(x, tokens, middle, mixture, gain, weights, gain_second, n, n_dp, barrier_id):
    count, model = x.shape
    depth, width = model // n_dp, sum(w.shape[1] for w in weights)
    lanes = -(-depth // 128) * 128
    whole, anywhere = pl.BlockSpec(memory_space=pltpu.VMEM), pl.BlockSpec(memory_space=pl.ANY)
    dma = pltpu.SemaphoreType.DMA
    grad, weights, gains, mixture = pl.pallas_call(
        functools.partial(last_kernel, n, n_dp, len(weights)),
        out_shape=[
            jax.ShapeDtypeStruct((count, model), f32),
            jax.ShapeDtypeStruct((depth, width), f32),
            jax.ShapeDtypeStruct((16, lanes), f32),
            jax.ShapeDtypeStruct((TOK_MB, model), bf16),
        ],
        in_specs=[anywhere, anywhere, anywhere, anywhere, whole, whole] + [whole] * len(weights),
        out_specs=[anywhere, whole, whole, anywhere],
        scratch_shapes=[pltpu.VMEM((count + TOK_MB, model), bf16)] * 2
        + line_scratch((count + TOK_MB, model), bf16, line_parts * (count + TOK_MB) // count)
        + [
            pltpu.VMEM((count, model), bf16),
            pltpu.VMEM((count, model), f32),
            pltpu.VMEM((count, model), f32),
            dma((2,)),
            dma,
            dma((4,)),
            pltpu.VMEM((n_dp, depth, width), bf16),
            dma((len(weights), n_dp)),
            dma((len(weights), n_dp)),
            pltpu.VMEM((n_dp, 16, lanes), f32),
            pltpu.VMEM((n_dp, 16, lanes), f32),
            dma((n_dp,)),
            dma((n_dp,)),
            pltpu.VMEM((16, lanes), f32),
            pltpu.VMEM((n, 16, lanes), f32),
            dma((n,)),
            dma((n,)),
            pltpu.VMEM((8, model), f32),
        ],
        compiler_params=pltpu.CompilerParams(
            collective_id=barrier_id, has_side_effects=True, vmem_limit_bytes=56 * 2**20
        ),
        cost_estimate=pl.CostEstimate(
            flops=count * model, bytes_accessed=2**20, transcendentals=0
        ),
    )(x, tokens, middle, mixture, gain, gain_second, *(w.reshape(n_dp, depth, -1) for w in weights))
    gains = jnp.sum(gains.reshape(2, 8, lanes), axis=1)[:, :depth]
    return grad, weights, gains, mixture


def expert_grads_kernel(
    n, shape, x_ref, rows_ref, outgrad_ref, start_ref, rest_ref,
    hidden_ref, active_ref, active_rows_ref,
    o_ref, gateup_grad_ref, down_grad_ref, mixture_ref, rows_t, outgrad_t, o_sem, sum_ref, *scratch,
):
    mixture_steps, gateup_steps, down_steps = shape
    i = pl.program_id(0)
    steps = sum(shape)
    _, begin, slot, finish = line_engine(n, x_ref, sum_ref, *scratch)
    total = line_steps(n)
    each = -(-total // steps)
    pl.when(i == 0)(begin)

    def slots(low, high):
        def one(j, carry):
            t = i * each + j
            pl.when(t < total)(lambda: slot(t))
            return carry

        lax.fori_loop(low, high, one, 0)

    slots(0, 1)

    @pl.when(i < mixture_steps)
    def _():
        half = start_ref.shape[1]
        mixture_ref[...] = (
            lax.dot_general(
                active_rows_ref[:, :half], start_ref[...], nt, preferred_element_type=f32
            )
            + lax.dot_general(
                active_rows_ref[:, half:], rest_ref[...], nt, preferred_element_type=f32
            )
        ).astype(bf16)
        size = active_rows_ref.shape[0]
        columns = pl.ds(pl.multiple_of(i * size, size), size)
        rows_t[:, columns] = rows_ref[...].T
        outgrad_t[:, columns] = outgrad_ref[...].T

    @pl.when((i >= mixture_steps) & (i < mixture_steps + gateup_steps))
    def _():
        gateup_grad_ref[...] = jnp.dot(
            rows_t[...], hidden_ref[...], preferred_element_type=f32
        ).astype(bf16)

    @pl.when(i >= mixture_steps + gateup_steps)
    def _():
        down_grad_ref[...] = jnp.dot(
            outgrad_t[...], active_ref[...], preferred_element_type=f32
        ).astype(bf16)

    slots(1, each)

    @pl.when(i == steps - 1)
    def _():
        copy = pltpu.make_async_copy(sum_ref, o_ref, o_sem)
        copy.start()
        finish()
        copy.wait()


def expert_grads_call(
    x, rows, outgrad, down_start, down_rest, hidden, active, n, barrier_id
):
    tokens, model = rows.shape
    block, tile = min(512, active.shape[1]), 256
    c, a, b = shape = (tokens // tile, hidden.shape[1] // block, active.shape[1] // block)
    whole = pl.BlockSpec(memory_space=pltpu.VMEM)
    first = lambda i: (jnp.minimum(i, c - 1), 0)
    second = lambda i: (0, jnp.clip(i - c, 0, a - 1))
    third = lambda i: (0, jnp.clip(i - c - a, 0, b - 1))
    return pl.pallas_call(
        functools.partial(expert_grads_kernel, n, shape),
        grid=(a + b + c,),
        in_specs=[
            whole,
            pl.BlockSpec((tile, model), first),
            pl.BlockSpec((tile, model), first),
            whole,
            whole,
            pl.BlockSpec((tokens, block), second),
            pl.BlockSpec((tokens, block), third),
            pl.BlockSpec((tile, active.shape[1]), first),
        ],
        out_specs=[
            pl.BlockSpec(memory_space=pl.ANY),
            pl.BlockSpec((model, block), second),
            pl.BlockSpec((model, block), third),
            pl.BlockSpec((tile, model), first),
        ],
        out_shape=[
            jax.ShapeDtypeStruct(x.shape, x.dtype),
            jax.ShapeDtypeStruct((model, hidden.shape[1]), bf16),
            jax.ShapeDtypeStruct((model, active.shape[1]), bf16),
            jax.ShapeDtypeStruct((tokens, model), bf16),
        ],
        scratch_shapes=[pltpu.VMEM((model, tokens), bf16)] * 2
        + [pltpu.SemaphoreType.DMA, pltpu.VMEM(x.shape, x.dtype)]
        + line_scratch(x.shape, x.dtype),
        compiler_params=pltpu.CompilerParams(
            collective_id=barrier_id, has_side_effects=True, vmem_limit_bytes=58 * 2**20
        ),
        cost_estimate=pl.CostEstimate(
            flops=2 * tokens * model * (hidden.shape[1] + 2 * active.shape[1]),
            bytes_accessed=10 * tokens * model,
            transcendentals=0,
        ),
    )(x, rows, outgrad, down_start, down_rest, hidden, active, active)


def expert_kernel(group, steps, rows_ref, outgrad_ref, gates_ref, gu_ref, start_ref, rest_ref,
                  active_ref, hidden_ref, gate_grad_ref, down_ref):
    step = pl.program_id(0)
    tile = 256
    width = gu_ref.shape[1] // 2
    hidden = width // group
    lane = lax.broadcasted_iota(jnp.int32, (tile, 128), 1)
    column = lax.broadcasted_iota(jnp.int32, (tile, width), 1)

    @pl.when(step == 0)
    def _():
        gate_grad_ref[...] = jnp.zeros_like(gate_grad_ref)

    @pl.when(step < steps // 2)
    def _():
        down_ref[...] = start_ref[...]

    @pl.when(step >= steps // 2)
    def _():
        down_ref[...] = rest_ref[...]

    def one(t, carry):
        at = pl.ds(pl.multiple_of(t * tile, tile), tile)
        h = jnp.dot(rows_ref[at], gu_ref[...], preferred_element_type=f32)
        back = jnp.dot(outgrad_ref[at], down_ref[...], preferred_element_type=f32)
        gates = gates_ref[at]
        wide = jnp.zeros((tile, width), f32)
        for j in range(group):
            g = jnp.sum(jnp.where(lane == step * group + j, gates, 0.0), axis=1, keepdims=True)
            wide = g + wide if group == 1 else jnp.where(column // hidden == j, g, wide)
        gate, up = h[:, :width], h[:, width:]
        sig = 1.0 / (1.0 + jnp.exp(-gate))
        silu = gate * sig
        active = (silu * up).astype(bf16).astype(f32)
        active_ref[at] = (active * wide).astype(bf16)
        product = active * back
        grads = gate_grad_ref[at]
        for j in range(group):
            s = jnp.sum(jnp.where(column // hidden == j, product, 0.0), axis=1, keepdims=True)
            grads = jnp.where(lane == step * group + j, s, grads)
        gate_grad_ref[at] = grads
        back = back * wide
        hidden_ref[at, :width] = (back * up * sig * (1.0 + gate * (1.0 - sig))).astype(bf16)
        hidden_ref[at, width:] = (back * silu).astype(bf16)
        return carry

    lax.fori_loop(0, rows_ref.shape[0] // tile, one, 0)


def expert_call(rows, outgrad, gates, gu, down_start, down_rest, group):
    tokens, model = rows.shape
    width = gu.shape[1] // (EXPERTS // group)
    steps = EXPERTS // group
    return pl.pallas_call(
        functools.partial(expert_kernel, group, steps),
        grid=(steps,),
        in_specs=[
            pl.BlockSpec((tokens, model), lambda p: (0, 0)),
            pl.BlockSpec((tokens, model), lambda p: (0, 0)),
            pl.BlockSpec((tokens, 128), lambda p: (0, 0)),
            pl.BlockSpec((model, width), lambda p: (0, p)),
            pl.BlockSpec((model, width // 2), lambda p: (0, jnp.minimum(p, steps // 2 - 1))),
            pl.BlockSpec((model, width // 2), lambda p: (0, jnp.maximum(p - steps // 2, 0))),
        ],
        out_specs=[
            pl.BlockSpec((tokens, width // 2), lambda p: (0, p)),
            pl.BlockSpec((tokens, width), lambda p: (0, p)),
            pl.BlockSpec((tokens, 128), lambda p: (0, 0)),
        ],
        out_shape=[
            jax.ShapeDtypeStruct((tokens, steps * width // 2), bf16),
            jax.ShapeDtypeStruct((tokens, steps * width), bf16),
            jax.ShapeDtypeStruct((tokens, 128), f32),
        ],
        scratch_shapes=[pltpu.VMEM((model, width // 2), bf16)],
        compiler_params=pltpu.CompilerParams(vmem_limit_bytes=60 * 2**20),
        cost_estimate=pl.CostEstimate(
            flops=2 * tokens * model * steps * width * 3 // 2,
            bytes_accessed=2 * (model * steps * width * 3 // 2 + tokens * steps * width * 3 // 2),
            transcendentals=tokens * steps * width // 2,
        ),
    )(rows, outgrad, gates, gu, down_start, down_rest)


def turn(u, cosine, sine):
    lane = lax.broadcasted_iota(jnp.int32, u.shape, 1) % HEAD_DIM
    other = jnp.where(lane < HEAD_DIM // 2, pltpu.roll(u, 96, 1), pltpu.roll(u, 32, 1))
    return u * cosine + other * sine


def table_parts(me, prompt_total):
    return (
        (0, PROMPT_DEV, pl.multiple_of(me * PROMPT_DEV, PROMPT_DEV)),
        (PROMPT_DEV, CONT, prompt_total),
    )


def project_kernel(x_ref, gain_ref, w_ref, cos_ref, sin_ref, normed_ref, q_ref, kv_ref):
    x = x_ref[...].astype(f32)
    inverse = lax.rsqrt(jnp.mean(x * x, axis=-1, keepdims=True) + eps_norm)
    normed = (x * inverse * (gain_ref[0:1] + gain_ref[2:3])).astype(bf16)
    normed_ref[...] = normed
    mixed = jnp.dot(normed, w_ref[...], preferred_element_type=f32)
    block = [mixed[:, c * 128 : (c + 1) * 128] for c in range(5)]
    low = lax.broadcasted_iota(jnp.int32, block[0].shape, 1) < HEAD_DIM
    turned = [
        block[0],
        jnp.where(low, block[1], block[2]),
        block[3],
        jnp.where(low, pltpu.roll(block[1], HEAD_DIM, 1), pltpu.roll(block[4], HEAD_DIM, 1)),
    ]
    kv_ref[:, 128:] = jnp.where(low, block[2], block[4]).astype(bf16)
    prompt_total = cos_ref.shape[0] - CONT
    for start, rows, at in table_parts(lax.axis_index("dp"), prompt_total):
        cosine, sine = cos_ref[pl.ds(at, rows)], sin_ref[pl.ds(at, rows)]
        for c, u in enumerate(turned):
            u = turn(u[start : start + rows], cosine, sine).astype(bf16)
            if c < 3:
                q_ref[start : start + rows, c * 128 : (c + 1) * 128] = u
            else:
                kv_ref[start : start + rows, :128] = u


def project_call(tokens, gain, w, cosine, sine):
    count, model = tokens.shape
    width = w.shape[1]
    row = lambda n: pl.BlockSpec((TOK_MB, n), lambda i: (i, 0))
    fixed = lambda t: pl.BlockSpec(t.shape, lambda i: (0, 0))
    return pl.pallas_call(
        project_kernel,
        grid=(MICRO,),
        in_specs=[row(model), fixed(gain), fixed(w), fixed(cosine), fixed(sine)],
        out_specs=[row(model), row(width - 256), row(256)],
        out_shape=[
            jax.ShapeDtypeStruct((count, model), bf16),
            jax.ShapeDtypeStruct((count, width - 256), bf16),
            jax.ShapeDtypeStruct((count, 256), bf16),
        ],
        compiler_params=pltpu.CompilerParams(vmem_limit_bytes=48 * 2**20),
        cost_estimate=pl.CostEstimate(
            flops=2 * count * model * width, bytes_accessed=6 * count * model, transcendentals=count
        ),
    )(tokens, gain, w, cosine, sine)


def norm_rows(x_ref, b_ref):
    middle = x_ref[...].astype(f32) + b_ref[...].astype(f32)
    inverse = lax.rsqrt(jnp.mean(middle * middle, axis=-1, keepdims=True) + eps_norm)
    return middle * inverse, inverse


def route_kernel(x_ref, b_ref, gain_ref, router_ref, routes_ref, normed_ref, gates_ref):
    norm, _ = norm_rows(x_ref, b_ref)
    normed = (norm * (gain_ref[1:2] + gain_ref[3:4])).astype(bf16)
    normed_ref[...] = normed
    logits = jnp.dot(normed, router_ref[...], preferred_element_type=f32)
    lane = lax.broadcasted_iota(jnp.int32, logits.shape, 1)
    routes = routes_ref[...]
    named = lane == routes[:, 0:1]
    for k in range(1, TOPK):
        named = named | (lane == routes[:, k : k + 1])
    top = jnp.max(jnp.where(named, logits, -1e30), axis=-1, keepdims=True)
    weights = jnp.where(named, jnp.exp(jnp.where(named, logits, top) - top), 0.0)
    gates_ref[...] = weights / jnp.sum(weights, axis=-1, keepdims=True)


def route_call(tokens, branch, gain, router, routes):
    count, model = tokens.shape
    tile = 256
    row = lambda n: pl.BlockSpec((tile, n), lambda i: (i, 0))
    fixed = lambda t: pl.BlockSpec(t.shape, lambda i: (0, 0))
    return pl.pallas_call(
        route_kernel,
        grid=(count // tile,),
        in_specs=[row(model), row(model), fixed(gain), fixed(router), row(TOPK)],
        out_specs=[row(model), row(128)],
        out_shape=[
            jax.ShapeDtypeStruct((count, model), bf16),
            jax.ShapeDtypeStruct((count, 128), f32),
        ],
        compiler_params=pltpu.CompilerParams(vmem_limit_bytes=32 * 2**20),
    )(tokens, branch, gain, router, routes)


def middle_back_kernel(
    x_ref, b_ref, summed_ref, gates_ref, outgrad_ref, gain_ref, router_ref, outproj_ref,
    middle_ref, own_ref, attended_ref, logits_ref, gain_out,
):
    norm, inverse = norm_rows(x_ref, b_ref)
    model = x_ref.shape[1]
    gates = gates_ref[...]
    gate_grad = summed_ref[:, model:].astype(f32)
    chosen = gates * (gate_grad - jnp.sum(gates * gate_grad, axis=-1, keepdims=True))
    logits = chosen.astype(bf16)
    logits_ref[...] = logits
    grad = summed_ref[:, :model].astype(f32) + lax.dot_general(
        logits, router_ref[...], nt, preferred_element_type=f32
    )
    term = (grad * norm).reshape(-1, 8, model).sum(axis=0)

    @pl.when(pl.program_id(0) == 0)
    def _():
        gain_out[...] = jnp.zeros_like(gain_out)

    gain_out[...] += term
    grad = grad * (gain_ref[1:2] + gain_ref[3:4])
    mean = jnp.mean(grad * norm, axis=-1, keepdims=True)
    middle = outgrad_ref[...].astype(f32) + inverse * (grad - norm * mean)
    middle_ref[...] = middle
    own = middle.astype(bf16)
    own_ref[...] = own
    attended_ref[...] = jnp.dot(own, outproj_ref[...], preferred_element_type=f32).astype(bf16)


def middle_back_call(tokens, branch, summed, gates, outgrad, gain, router, outproj):
    count, model = tokens.shape
    tile = 256
    row = lambda n: pl.BlockSpec((tile, n), lambda i: (i, 0))
    fixed = lambda t: pl.BlockSpec(t.shape, lambda i: (0, 0))
    return pl.pallas_call(
        middle_back_kernel,
        grid=(count // tile,),
        in_specs=[
            row(model),
            row(model),
            row(model + 128),
            row(128),
            row(model),
            fixed(gain),
            fixed(router),
            fixed(outproj),
        ],
        out_specs=[
            row(model),
            row(model),
            row(outproj.shape[1]),
            row(128),
            pl.BlockSpec((8, model), lambda i: (0, 0)),
        ],
        out_shape=[
            jax.ShapeDtypeStruct((count, model), f32),
            jax.ShapeDtypeStruct((count, model), bf16),
            jax.ShapeDtypeStruct((count, outproj.shape[1]), bf16),
            jax.ShapeDtypeStruct((count, 128), bf16),
            jax.ShapeDtypeStruct((8, model), f32),
        ],
        compiler_params=pltpu.CompilerParams(vmem_limit_bytes=48 * 2**20),
    )(tokens, branch, summed, gates, outgrad, gain, router, outproj)


def block_out_kernel(x_ref, b_ref, first_ref, second_ref, o_ref):
    middle = x_ref[...].astype(f32) + b_ref[...].astype(f32)

    @pl.when(pl.program_id(0) == 0)
    def _():
        o_ref[...] = (middle + first_ref[...].astype(f32)).astype(bf16)

    @pl.when(pl.program_id(0) == 1)
    def _():
        o_ref[...] = (middle + second_ref[...].astype(f32)).astype(bf16)


def block_out_call(tokens, branch, first, second):
    count, model = tokens.shape
    columns = model // 3
    row = pl.BlockSpec((TOK_MB, columns), lambda i, j: (i, j))
    half = lambda place: pl.BlockSpec(
        (TOK_MB, columns), lambda i, j: (0, jnp.where(i == place, j, 0 if place else 2))
    )
    return pl.pallas_call(
        block_out_kernel,
        grid=(MICRO, 3),
        in_specs=[row, row, half(0), half(1)],
        out_specs=row,
        out_shape=jax.ShapeDtypeStruct((count, model), bf16),
        compiler_params=pltpu.CompilerParams(vmem_limit_bytes=60 * 2**20),
    )(tokens, branch, first, second)


def head_places(heads):
    return [(h // GROUP, h % 2, h // 2) for h in range(heads)]


def spread(kv, scale):
    lane = lax.broadcasted_iota(jnp.int32, kv.shape, 1)
    kv = kv * scale
    turned = pltpu.roll(kv, HEAD_DIM, 1)
    first = lane < HEAD_DIM
    zero = jnp.zeros_like(kv)
    return {
        (0, 0): jnp.where(first, kv, zero).astype(bf16),
        (0, 1): jnp.where(first, zero, turned).astype(bf16),
        (1, 0): jnp.where(first, turned, zero).astype(bf16),
        (1, 1): jnp.where(first, zero, kv).astype(bf16),
    }


def row_tiles(prompt_total):
    tiles = [(0, PROMPT_DEV, prompt_total)]
    for start in range(0, CONT, 256):
        tiles.append((PROMPT_DEV + start, 256, prompt_total + start + 256))
    return tiles


def greet(me, n):
    barrier = pltpu.get_barrier_semaphore()

    def one(k, carry):
        pl.semaphore_signal(
            barrier, inc=1, device_id={"dp": lax.rem(me + k, n)}, device_id_type=MESH
        )
        return carry

    lax.fori_loop(1, n, one, 0)
    return n - 1


def meet(me, n):
    pl.semaphore_wait(pltpu.get_barrier_semaphore(), greet(me, n))


def load_spread(m, all_ref, kv_ref, k_ref, v_ref, kt_ref=None):
    total = all_ref.shape[1]
    own = pl.ds(pl.multiple_of(m * TOK_MB + PROMPT_DEV, 16), CONT)
    for low, high, rows in ((0, total, all_ref[m]), (total, total + CONT, kv_ref[own])):
        keys = spread(rows[:, :128].astype(f32), HEAD_DIM**-0.5)
        values = spread(rows[:, 128:].astype(f32), 1.0)
        for i, place in enumerate(keys):
            k_ref[i, low:high] = keys[place]
            v_ref[i, low:high] = values[place]
            if kt_ref is not None:
                kt_ref[i, :, low:high] = keys[place].astype(f32).T.astype(bf16)
    return {place: i for i, place in enumerate(keys)}


def attention_kernel(
    heads, n, q_ref, kv_ref, w_ref, o_ref, lse_ref, all_ref, w_out, k_ref, v_ref, send, recv,
    *spread_out,
):
    _, start_w, forward_w, finish_w = gather_engine(n, [(w_ref, w_out)], *spread_out)
    prompt_total = all_ref.shape[1]
    me = lax.axis_index("dp")

    def piece(m, k):
        rows = all_ref.at[m, pl.ds(pl.multiple_of(me * PROMPT_DEV, PROMPT_DEV), PROMPT_DEV)]
        return pltpu.make_async_remote_copy(
            src_ref=rows,
            dst_ref=rows,
            send_sem=send.at[m, k],
            recv_sem=recv.at[m, k],
            device_id={"dp": lax.rem(me + k, n)},
            device_id_type=MESH,
        )

    for m in range(MICRO):
        all_ref[m, pl.ds(pl.multiple_of(me * PROMPT_DEV, PROMPT_DEV), PROMPT_DEV)] = kv_ref[
            m * TOK_MB : m * TOK_MB + PROMPT_DEV
        ]
    meet(me, n)

    def every(m, act):
        def one(k, carry):
            act(piece(m, k))
            return carry

        lax.fori_loop(1, n, one, 0)

    for m in range(MICRO):
        every(m, lambda copy: copy.start())
    start_w()

    def micro(m, carry):
        every(m, lambda copy: copy.wait_recv())
        index = load_spread(m, all_ref, kv_ref, k_ref, v_ref)
        lane = lax.broadcasted_iota(jnp.int32, (1, 128), 1)
        for start, rows, length in row_tiles(prompt_total):
            at = pl.ds(pl.multiple_of(m * TOK_MB + start, 128), rows)
            row = lax.broadcasted_iota(jnp.int32, (rows, 1), 0)
            if start == 0:
                masked = 0
                reach = row + me * PROMPT_DEV
            else:
                masked = length - 256
                reach = row
            column = lax.broadcasted_iota(jnp.int32, (rows, length - masked), 1)
            lse = jnp.zeros((rows, 128), f32)
            pair_out = None
            for h, (kv, half, pair) in enumerate(head_places(heads)):
                q = q_ref[at, pair * 128 : (pair + 1) * 128]
                i = index[kv, half]
                tail = lax.dot_general(q, k_ref[i, masked:length], nt, preferred_element_type=f32)
                tail = jnp.where(column <= reach, tail, -1e30)
                top = jnp.max(tail, axis=1, keepdims=True)
                if masked:
                    head = lax.dot_general(q, k_ref[i, :masked], nt, preferred_element_type=f32)
                    top = jnp.maximum(top, jnp.max(head, axis=1, keepdims=True))
                    p_head = jnp.exp(head - top)
                p_tail = jnp.exp(tail - top)
                total = jnp.sum(p_tail, axis=1, keepdims=True)
                out = jnp.dot(
                    p_tail.astype(bf16), v_ref[i, masked:length], preferred_element_type=f32
                )
                if masked:
                    total = total + jnp.sum(p_head, axis=1, keepdims=True)
                    out = out + jnp.dot(
                        p_head.astype(bf16), v_ref[i, :masked], preferred_element_type=f32
                    )
                out = out / total
                lse = jnp.where(lane == h, top + jnp.log(total), lse)
                if half == 0:
                    pair_out = out
                else:
                    o_ref[at, pair * 128 : (pair + 1) * 128] = (pair_out + out).astype(bf16)
            lse_ref[m, :, start : start + rows] = lse.T[:8]
        return carry

    lax.fori_loop(0, MICRO, micro, 0)
    for p in range(gather_parts):
        forward_w(p)
    for m in range(MICRO):
        every(m, lambda copy: copy.wait_send())
    finish_w()


def attention_call(q, kv, w, n):
    count, width = q.shape
    keys = PROMPT_DEV * n + CONT
    heads = width // HEAD_DIM
    whole = pl.BlockSpec(memory_space=pltpu.VMEM)
    return pl.pallas_call(
        functools.partial(attention_kernel, heads, n),
        in_specs=[whole] * 2 + [pl.BlockSpec(memory_space=pl.ANY)],
        out_specs=[whole] * 3 + [pl.BlockSpec(memory_space=pl.ANY)],
        out_shape=[
            jax.ShapeDtypeStruct((count, width), bf16),
            jax.ShapeDtypeStruct((MICRO, 8, TOK_MB), f32),
            jax.ShapeDtypeStruct((MICRO, PROMPT_DEV * n, 256), bf16),
            jax.ShapeDtypeStruct((n,) + w.shape, w.dtype),
        ],
        scratch_shapes=[
            pltpu.VMEM((4, keys, 128), bf16),
            pltpu.VMEM((4, keys, 128), bf16),
            pltpu.SemaphoreType.DMA((MICRO, n)),
            pltpu.SemaphoreType.DMA((MICRO, n)),
        ]
        + gather_scratch(1, n),
        compiler_params=pltpu.CompilerParams(
            collective_id=3, has_side_effects=True, vmem_limit_bytes=48 * 2**20
        ),
        cost_estimate=pl.CostEstimate(
            flops=16 * count * keys * width,
            bytes_accessed=8 * count * width,
            transcendentals=count * keys * heads,
        ),
    )(q, kv, w)


def attention_back_kernel(
    heads, n, q_ref, kv_ref, all_ref, do_ref, o_ref, lse_ref,
    cos_ref, sin_ref,
    grad_ref, k_ref, v_ref, kt_ref, dk_ref, dv_ref, sent_ref, got_ref, send, recv,
):
    prompt_total = all_ref.shape[1]
    me = lax.axis_index("dp")

    def put_both(at, dk, dv):
        low = lax.broadcasted_iota(jnp.int32, dk.shape, 1) < HEAD_DIM
        dk = pltpu.roll(dk, HEAD_DIM, 1)
        second = grad_ref[at, 128:256].astype(f32)
        grad_ref[at, 128:256] = jnp.where(low, second, dk).astype(bf16)
        grad_ref[at, 256:384] = jnp.where(low, dv, second).astype(bf16)
        grad_ref[at, 512:640] = jnp.where(low, dk, dv).astype(bf16)

    def piece(m, k):
        to = lax.rem(me + k, n)
        return pltpu.make_async_remote_copy(
            src_ref=sent_ref.at[m, pl.ds(pl.multiple_of(to * PROMPT_DEV, PROMPT_DEV), PROMPT_DEV)],
            dst_ref=got_ref.at[m, k],
            send_sem=send.at[m, k],
            recv_sem=recv.at[m, k],
            device_id={"dp": to},
            device_id_type=MESH,
        )

    def every(m, act):
        def one(k, carry):
            act(piece(m, k))
            return carry

        lax.fori_loop(1, n, one, 0)

    meet(me, n)
    half_rows = (
        lax.broadcasted_iota(jnp.int32, (8, 128), 1) // HEAD_DIM
        == lax.broadcasted_iota(jnp.int32, (8, 128), 0)
    ).astype(f32)

    def micro(m, carry):
        index = load_spread(m, all_ref, kv_ref, k_ref, v_ref, kt_ref)
        dk_ref[...] = jnp.zeros_like(dk_ref)
        dv_ref[...] = jnp.zeros_like(dv_ref)
        for start, rows, length in row_tiles(prompt_total):
            at = pl.ds(pl.multiple_of(m * TOK_MB + start, 128), rows)
            inner = slice(start, start + rows)
            column = lax.broadcasted_iota(jnp.int32, (1, rows), 1)
            if start == 0:
                masked = 0
                reach = column + me * PROMPT_DEV
            else:
                masked = length - 256
                reach = column
            key = lax.broadcasted_iota(jnp.int32, (length - masked, rows), 0)
            back = None
            for h, (kv, half, pair) in enumerate(head_places(heads)):
                lanes = slice(pair * 128, (pair + 1) * 128)
                i = index[kv, half]
                q, do = q_ref[at, lanes], do_ref[at, lanes]
                if half == 0:
                    delta_pair = lax.dot_general(
                        half_rows,
                        do.astype(f32) * o_ref[at, lanes].astype(f32),
                        nt,
                        precision=lax.Precision.HIGHEST,
                        preferred_element_type=f32,
                    )
                delta = delta_pair[half : half + 1]
                lse = lse_ref[m, h : h + 1, inner]
                for low, high in ((0, masked), (masked, length)):
                    if low == high:
                        continue
                    s = lax.dot_general(k_ref[i, low:high], q, nt, preferred_element_type=f32)
                    if low == masked:
                        s = jnp.where(key <= reach, s, -1e30)
                    p = jnp.exp(s - lse)
                    dp_ = lax.dot_general(v_ref[i, low:high], do, nt, preferred_element_type=f32)
                    ds = (p * (dp_ - delta)).astype(bf16)
                    dv_ref[i, low:high] += jnp.dot(
                        p.astype(bf16), do, preferred_element_type=f32
                    )
                    dk_ref[i, low:high] += jnp.dot(ds, q, preferred_element_type=f32)
                    term = jnp.dot(kt_ref[i, :, low:high], ds, preferred_element_type=f32)
                    back = term if back is None else back + term
                if half == 1:
                    if start == 0:
                        table = pl.ds(pl.multiple_of(me * PROMPT_DEV, PROMPT_DEV), rows)
                    else:
                        table = pl.ds(prompt_total + start - PROMPT_DEV, rows)
                    to = (0, 1, 3)[pair] * 128
                    grad_ref[at, to : to + 128] = turn(
                        back.T, cos_ref[table], -sin_ref[table]
                    ).astype(bf16)
                    back = None
        lane = lax.broadcasted_iota(jnp.int32, (dk_ref.shape[1], 128), 1)

        def joined(acc):
            get = lambda place: acc[index[place]]
            return jnp.where(
                lane < HEAD_DIM,
                get((0, 0)) + pltpu.roll(get((0, 1)), HEAD_DIM, 1),
                get((1, 1)) + pltpu.roll(get((1, 0)), HEAD_DIM, 1),
            )

        dk = turn(joined(dk_ref) * HEAD_DIM**-0.5, cos_ref[...], -sin_ref[...])
        dv = joined(dv_ref)
        sent_ref[m, :, :128] = dk[:prompt_total].astype(bf16)
        sent_ref[m, :, 128:] = dv[:prompt_total].astype(bf16)
        every(m, lambda copy: copy.start())
        own = pl.ds(pl.multiple_of(m * TOK_MB + PROMPT_DEV, 128), CONT)
        put_both(own, dk[prompt_total:], dv[prompt_total:])
        return carry

    lax.fori_loop(0, MICRO, micro, 0)

    def collect(m, carry):
        every(m, lambda copy: copy.wait_recv())
        own = sent_ref[m, pl.ds(pl.multiple_of(me * PROMPT_DEV, PROMPT_DEV), PROMPT_DEV)]
        total = lax.fori_loop(
            1, n, lambda k, t: t + got_ref[m, k].astype(f32), own.astype(f32)
        )
        at = pl.ds(pl.multiple_of(m * TOK_MB, 128), PROMPT_DEV)
        put_both(at, total[:, :128], total[:, 128:])
        every(m, lambda copy: copy.wait_send())
        return carry

    lax.fori_loop(0, MICRO, collect, 0)


def attention_back_call(q, kv, prompts, do, o, lse, cosine, sine, n):
    count, width = q.shape
    keys = prompts.shape[1] + CONT
    heads = width // HEAD_DIM
    whole = pl.BlockSpec(memory_space=pltpu.VMEM)
    return pl.pallas_call(
        functools.partial(attention_back_kernel, heads, n),
        in_specs=[whole] * 8,
        out_specs=whole,
        out_shape=jax.ShapeDtypeStruct((count, width + 256), bf16),
        scratch_shapes=[
            pltpu.VMEM((4, keys, 128), bf16),
            pltpu.VMEM((4, keys, 128), bf16),
            pltpu.VMEM((4, 128, keys), bf16),
            pltpu.VMEM((4, keys, 128), f32),
            pltpu.VMEM((4, keys, 128), f32),
            pltpu.VMEM((MICRO, prompts.shape[1], 256), bf16),
            pltpu.VMEM((MICRO, n, PROMPT_DEV, 256), bf16),
            pltpu.SemaphoreType.DMA((MICRO, n)),
            pltpu.SemaphoreType.DMA((MICRO, n)),
        ],
        compiler_params=pltpu.CompilerParams(
            collective_id=4, has_side_effects=True, vmem_limit_bytes=56 * 2**20
        ),
        cost_estimate=pl.CostEstimate(
            flops=40 * count * keys * width,
            bytes_accessed=12 * count * width,
            transcendentals=count * keys * heads,
        ),
    )(q, kv, prompts, do, o, lse, cosine, sine)


def attend(queries, keys_all, values_all, allowed):
    factor = HEAD_DIM ** (-0.5)
    scores = jnp.einsum("tkgd,skd->kgts", queries, keys_all, preferred_element_type=f32) * factor
    scores = jnp.where(allowed, scores, -1e30)
    row_max = jnp.max(scores, axis=-1, keepdims=True)
    exponent = jnp.exp(scores - row_max)
    softened = exponent / jnp.sum(exponent, axis=-1, keepdims=True)
    soft_low = softened.astype(bf16)
    attended = jnp.einsum("kgts,skd->tkgd", soft_low, values_all, preferred_element_type=f32)
    return attended.astype(bf16), softened, soft_low


def attend_back(queries, keys_all, values_all, softened, soft_low, attended_grad):
    factor = HEAD_DIM ** (-0.5)
    soft_grad = jnp.einsum("tkgd,skd->kgts", attended_grad, values_all, preferred_element_type=f32)
    values_grad = jnp.einsum("kgts,tkgd->skd", soft_low, attended_grad, preferred_element_type=f32)
    row_delta = jnp.sum(softened * soft_grad, axis=-1, keepdims=True)
    scores_grad = (softened * (soft_grad - row_delta)).astype(bf16)
    queries_grad = (
        jnp.einsum("kgts,skd->tkgd", scores_grad, keys_all, preferred_element_type=f32) * factor
    )
    keys_grad = (
        jnp.einsum("kgts,tkgd->skd", scores_grad, queries, preferred_element_type=f32) * factor
    )
    return queries_grad, keys_grad, values_grad


def shards(
    tokens, cotangent, routes,
    inproj_weight, inproj_first, inproj_second,
    outproj_weight, outproj_first, outproj_second,
    gateup_weight, gateup_first, gateup_second,
    down_weight, down_first, down_second,
    router_weight, router_first, router_second,
    gains, gains_first, gains_second,
):
    n_dp = lax.axis_size("dp")
    n_tensor = lax.axis_size("tensor")
    depth = inproj_weight.shape[0]
    kv_local = inproj_weight.shape[1]
    hidden = down_weight.shape[1]
    group = max(1, 256 // hidden)
    groups = EXPERTS // group
    in_width = inproj_weight.shape[1] * inproj_weight.shape[2]
    out_width = outproj_weight.shape[0] * outproj_weight.shape[1]
    prompt_total = PROMPT_DEV * n_dp
    count = tokens.shape[0]

    def gateup_flat(w):
        w = w.reshape(groups, group, depth, 2, hidden)
        return w.transpose(2, 0, 3, 1, 4).reshape(depth, 2 * EXPERTS * hidden)

    def gateup_back(w):
        w = w.reshape(depth, groups, 2, group, hidden)
        return w.transpose(1, 3, 0, 2, 4).reshape(EXPERTS, depth, 2, hidden)

    query_width = GROUP * HEAD_DIM
    gains_high = gains.astype(bf16)
    gains_low = (gains - gains_high.astype(f32)).astype(bf16)
    attn_local = (
        inproj_weight.reshape(depth, in_width).astype(bf16),
        outproj_weight.reshape(out_width, depth).T.astype(bf16),
        jnp.concatenate(
            [
                router_weight.astype(bf16),
                gains_high.T,
                gains_low.T,
                jnp.zeros((depth, 128 - EXPERTS - 4), bf16),
            ],
            axis=1,
        ),
    )
    if hidden == 128:
        inproj_full, outproj_full, small_full, gu_local = gather(
            attn_local, gateup_weight.reshape(-1, hidden), n_dp, group, 5
        )
    else:
        inproj_full, outproj_full, small_full = gather(attn_local, None, n_dp, None, 5)
        gu_local = gateup_flat(gateup_weight.astype(bf16))
    down_local = down_weight.reshape(EXPERTS * hidden, depth).T.astype(bf16)
    gain_rows = small_full[:, EXPERTS : EXPERTS + 8].astype(f32).T

    device_index = lax.axis_index("dp")
    half_dim = HEAD_DIM // 2
    freqs = np.float32(10000.0) ** (-2.0 * np.arange(half_dim, dtype=np.float32) / HEAD_DIM)
    angles = np.arange(prompt_total + CONT, dtype=np.float32)[:, None] * freqs.astype(np.float32)
    cosine, sine = np.cos(angles), np.sin(angles)

    def of_rows(table):
        own = lax.dynamic_slice_in_dim(
            jnp.asarray(table), device_index * PROMPT_DEV, PROMPT_DEV, 0
        )
        return jnp.concatenate([own, table[prompt_total:]], axis=0)

    in_kernels = kv_local * HEAD_DIM == 128
    both_width = kv_local * 2 * HEAD_DIM
    if in_kernels:
        cos_all = np.concatenate([cosine] * 4, axis=1)
        sin_all = np.concatenate([-sine, sine] * 2, axis=1)
        normed_first, queries, both = project_call(
            tokens, gain_rows, inproj_full, cos_all, sin_all
        )
    else:
        cosine, sine = (jnp.tile(of_rows(t), (MICRO, 1))[:, None, :] for t in (cosine, sine))
        inputs = tokens.astype(f32)
        inverse_first = lax.rsqrt(jnp.mean(inputs * inputs, axis=-1, keepdims=True) + eps_norm)
        normed_first = (inputs * inverse_first * (gain_rows[0:1] + gain_rows[2:3])).astype(bf16)
        mixed = jnp.dot(normed_first, inproj_full, preferred_element_type=f32)
        mixed = mixed.reshape(count, kv_local, -1)
        queries = rotate(
            mixed[..., :query_width].reshape(count, -1, HEAD_DIM), cosine, sine
        ).astype(bf16)
        keys = rotate(mixed[..., query_width : query_width + HEAD_DIM], cosine, sine)
        both = jnp.concatenate(
            [keys.reshape(count, -1), mixed[..., query_width + HEAD_DIM :].reshape(count, -1)],
            axis=1,
        ).astype(bf16)
    if in_kernels:
        attended, lse, prompt_both, down_start = attention_call(
            queries, both, down_local[:, : down_local.shape[1] // 2], n_dp
        )
        down_start = down_start.reshape(n_dp * depth, -1)
        down_rest = down_local[:, down_local.shape[1] // 2 :]
    else:
        both = both.reshape(MICRO, TOK_MB, both_width)
        prompt_both = lax.all_gather(both[:, :PROMPT_DEV], "dp", axis=1, tiled=True)
        both_all = jnp.concatenate([prompt_both, both[:, PROMPT_DEV:]], axis=1)
        inner = jnp.arange(TOK_MB, dtype=jnp.int32)
        positions = jnp.where(
            inner < PROMPT_DEV, device_index * PROMPT_DEV + inner, prompt_total + inner - PROMPT_DEV
        )
        key_index = jnp.arange(prompt_total + CONT, dtype=jnp.int32)
        allowed = (key_index[None, :] <= positions[:, None]) & (
            (key_index[None, :] < prompt_total) | (inner[:, None] >= PROMPT_DEV)
        )
        kept = []
        attended = []
        for m in range(MICRO):
            q = queries[m * TOK_MB : (m + 1) * TOK_MB].reshape(TOK_MB, kv_local, GROUP, HEAD_DIM)
            k, v = (
                t.reshape(-1, kv_local, HEAD_DIM) for t in jnp.split(both_all[m], 2, axis=1)
            )
            out, softened, soft_low = attend(q, k, v, allowed)
            attended.append(out.reshape(TOK_MB, -1))
            kept.append((q, k, v, softened, soft_low))
        attended = jnp.concatenate(attended, axis=0)
    branch = lax.dot_general(
        attended, outproj_full, (((1,), (1,)), ((), ())), preferred_element_type=f32
    ).astype(bf16)
    branch, gu_full, down_rest = line_gather(
        branch, gu_local, down_rest if in_kernels else down_local, n_tensor, n_dp, 6
    )
    if not in_kernels:
        down_start, down_rest = jnp.split(down_rest, 2, axis=1)

    normed_second, gates_wide = route_call(tokens, branch, gain_rows, small_full, routes)
    active, hidden_grad, gate_grad = expert_call(
        normed_second, cotangent, gates_wide, gu_full, down_start, down_rest, group
    )
    contract_last = (((1,), (1,)), ((), ()))
    contract_first = (((0,), (0,)), ((), ()))
    rows_grad = lax.dot_general(
        hidden_grad, gu_full, contract_last, preferred_element_type=f32
    ).astype(bf16)
    summed, gateup_grad, down_grad, mixture = expert_grads_call(
        jnp.concatenate([rows_grad, gate_grad.astype(bf16)], axis=1),
        normed_second, cotangent, down_start, down_rest, hidden_grad, active, n_tensor, 2,
    )
    first_mixture = lax.psum(mixture[:TOK_MB], "tensor")
    model = tokens.shape[1]
    middle_grad, branch_own, attended_grad, logits_grad, gain_second_grad = middle_back_call(
        tokens, branch, summed, gates_wide, cotangent, gain_rows, small_full, outproj_full
    )
    middle_grad, attended_grad, down_grad, gateup_grad = lax.optimization_barrier(
        (middle_grad, attended_grad, down_grad, gateup_grad)
    )
    down_grad = lax.psum_scatter(down_grad, "dp", scatter_dimension=0, tiled=True)
    gateup_grad = lax.psum_scatter(gateup_grad, "dp", scatter_dimension=0, tiled=True)
    router_grad = lax.dot_general(
        normed_second, logits_grad, contract_first, preferred_element_type=f32
    ).astype(bf16)
    outproj_grad = lax.dot_general(
        branch_own, attended, contract_first, preferred_element_type=f32
    ).astype(bf16)
    if in_kernels:
        mixed_grad = attention_back_call(
            queries, both, prompt_both, attended_grad, attended, lse, cos_all, sin_all, n_dp
        )
    else:
        queries_grad, both_grad = [], []
        for m in range(MICRO):
            q, k, v, softened, soft_low = kept[m]
            dout = attended_grad[m * TOK_MB : (m + 1) * TOK_MB].reshape(q.shape)
            dq, dk, dv = attend_back(q, k, v, softened, soft_low, dout)
            queries_grad.append(dq.reshape(TOK_MB, -1, HEAD_DIM))
            both_grad.append(jnp.concatenate([t.reshape(-1, both_width // 2) for t in (dk, dv)], 1))
        queries_grad = rotate(jnp.concatenate(queries_grad, axis=0), cosine, -sine)
        both_grad = jnp.stack(both_grad)
        prompt_grad = lax.psum_scatter(
            both_grad[:, :prompt_total].astype(bf16), "dp", scatter_dimension=1, tiled=True
        )
        both_grad = jnp.concatenate(
            [prompt_grad.astype(f32), both_grad[:, prompt_total:]], axis=1
        ).reshape(count, both_width)
        keys_grad = rotate(
            both_grad[:, : both_width // 2].reshape(count, -1, HEAD_DIM), cosine, -sine
        )
        mixed_grad = jnp.concatenate(
            [
                t.reshape(count, kv_local, -1)
                for t in (queries_grad, keys_grad, both_grad[:, both_width // 2 :])
            ],
            axis=2,
        )
        mixed_grad = mixed_grad.reshape(count, -1).astype(bf16)
    normed_first_grad = lax.dot_general(
        mixed_grad, inproj_full, contract_last, preferred_element_type=f32
    ).astype(bf16)
    inproj_grad = lax.dot_general(
        normed_first, mixed_grad, contract_first, preferred_element_type=f32
    ).astype(bf16)
    attn_grad = [inproj_grad, outproj_grad, router_grad]
    if in_width % 128 or out_width % 128:
        attn_grad = [jnp.concatenate(attn_grad, axis=1)]
    gateup_state = (gateup_weight, gateup_first, gateup_second)
    down_state = (down_weight, down_first, down_second)
    if hidden == 128:
        gateup_next, down_next = expert_adam(
            gateup_state, gateup_grad, down_state, down_grad, group
        )
    else:
        down_next = adam_update(
            *down_state, down_grad.T.reshape(down_weight.shape).astype(f32), weight_decay, 0.05
        )
        gateup_next = adam_update(
            *gateup_state, gateup_back(gateup_grad).astype(f32), weight_decay, 0.05
        )
    tokens_grad, attn_grad, gains_grad, second_mixture = last_call(
        normed_first_grad, tokens, middle_grad, mixture, gain_rows,
        attn_grad, gain_second_grad, n_tensor, n_dp, 7,
    )
    first_mixture, tokens_grad = lax.optimization_barrier((first_mixture, tokens_grad))
    block_out = block_out_call(tokens, branch, first_mixture, second_mixture)
    split = (in_width, in_width + out_width, in_width + out_width + EXPERTS)
    inproj_grad, outproj_grad, router_grad = (
        attn_grad[:, : split[0]],
        attn_grad[:, split[0] : split[1]],
        attn_grad[:, split[1] : split[2]],
    )
    updates = (
        adam_update(
            inproj_weight, inproj_first, inproj_second,
            inproj_grad.reshape(inproj_weight.shape), weight_decay, 0.05,
        ),
        adam_update(
            outproj_weight, outproj_first, outproj_second,
            outproj_grad.T.reshape(outproj_weight.shape), weight_decay, 0.3,
        ),
        gateup_next,
        down_next,
        adam_update(router_weight, router_first, router_second, router_grad, weight_decay, 0.05),
        adam_update(gains, gains_first, gains_second, gains_grad, 0.0, 0.4),
    )
    return (block_out, tokens_grad) + sum(updates, ())


def solution(mesh):
    row = P("dp", None)
    inproj = P("dp", "tensor", None)
    outproj = P("tensor", None, "dp")
    gateup = P(None, "dp", None, "tensor")
    down = P(None, "tensor", "dp")
    gain = P(None, "dp")
    weights = (inproj,) * 3 + (outproj,) * 3 + (gateup,) * 3 + (down,) * 3 + (row,) * 3 + (gain,) * 3
    return jax.shard_map(
        shards,
        mesh=mesh,
        in_specs=(row, row, row) + weights,
        out_specs=(row, row) + weights,
        check_vma=False,
    )
```

```python
import functools

import jax
import jax.numpy as jnp
import numpy as np
from jax import lax
from jax.experimental import pallas as pl
from jax.experimental.pallas import tpu as pltpu
from jax.sharding import PartitionSpec as P

HEAD_DIM = 64
TOPK = 8
EXPERTS = 16
PROMPT_DEV = 128
CONT = 512
MICRO = 2
STEP = 10
GROUP = 3
TOK_MB = 640

eps_norm = 1e-05
beta_first = 0.9
beta_second = 0.95
adam_eps = 1e-08
weight_decay = 0.1
bf16 = jnp.bfloat16
f32 = jnp.float32
line_parts = 20
line_lag = 2
MESH = pl.DeviceIdType.MESH
nt = (((1,), (1,)), ((), ()))


def rotate(values, cosine, sine):
    half_dim = values.shape[-1] // 2
    first_half = values[..., :half_dim]
    second_half = values[..., half_dim:]
    return jnp.concatenate(
        [first_half * cosine - second_half * sine, second_half * cosine + first_half * sine],
        axis=-1,
    )


def adam_update(weight, moment_one, moment_two, gradient, decay_rate, learn_rate):
    first_next = beta_first * moment_one + (1.0 - beta_first) * gradient
    second_next = beta_second * moment_two + (1.0 - beta_second) * gradient * gradient
    corr_first = 1.0 - beta_first**STEP
    corr_second = 1.0 - beta_second**STEP
    update = first_next / corr_first / (jnp.sqrt(second_next / corr_second) + adam_eps)
    return (weight - learn_rate * (update + decay_rate * weight), first_next, second_next)


def line_steps(n, parts=line_parts):
    return parts + 2 * (n - 1) * line_lag


def line_engine(
    n, x_ref, o_ref, held, send_red, recv_red, send_out, recv_out,
    complete=lambda at, half, c: None, parts=line_parts,
):
    me = lax.axis_index("tensor")
    rows = x_ref.shape[0] // (2 * parts)
    low, high = me - 1, me + 1

    def greet():
        barrier = pltpu.get_barrier_semaphore()

        @pl.when(me > 0)
        def _():
            pl.semaphore_signal(barrier, inc=1, device_id={"tensor": low}, device_id_type=MESH)

        @pl.when(me < n - 1)
        def _():
            pl.semaphore_signal(barrier, inc=1, device_id={"tensor": high}, device_id_type=MESH)

        return jnp.where((me > 0) & (me < n - 1), 2, 1)

    def begin():
        pl.semaphore_wait(pltpu.get_barrier_semaphore(), greet())

    def part(half, c):
        return pl.ds(pl.multiple_of((half * parts + c) * rows, 16), rows)

    def reduce_copy(half, c, src):
        to = low if half == 0 else high
        return pltpu.make_async_remote_copy(
            src_ref=src.at[part(half, c)],
            dst_ref=held.at[part(half, c)],
            send_sem=send_red.at[half, c],
            recv_sem=recv_red.at[half, c],
            device_id={"tensor": to},
            device_id_type=MESH,
        )

    def out_copy(half, c):
        to = high if half == 0 else low
        return pltpu.make_async_remote_copy(
            src_ref=o_ref.at[part(half, c)],
            dst_ref=o_ref.at[part(half, c)],
            send_sem=send_out.at[half, c],
            recv_sem=recv_out.at[half, c],
            device_id={"tensor": to},
            device_id_type=MESH,
        )

    def place(half):
        return n - 1 - me if half == 0 else me

    def slot(t):
        for half in (0, 1):
            at = place(half)
            c = t - line_lag * at

            @pl.when((c >= 0) & (c < parts))
            def _():
                @pl.when(at == 0)
                def _():
                    reduce_copy(half, c, x_ref).start()

                @pl.when(at > 0)
                def _():
                    reduce_copy(half, c, held).wait_recv()
                    total = x_ref[part(half, c)].astype(f32) + held[part(half, c)].astype(f32)

                    @pl.when(at < n - 1)
                    def _():
                        held[part(half, c)] = total.astype(held.dtype)
                        reduce_copy(half, c, held).start()

                    @pl.when(at == n - 1)
                    def _():
                        o_ref[part(half, c)] = total.astype(o_ref.dtype)
                        out_copy(half, c).start()
                        complete(part(half, c), half, c)

        for half in (0, 1):
            at = place(half)
            c = t - line_lag * (2 * (n - 1) - at)

            @pl.when((at < n - 1) & (c >= 0) & (c < parts))
            def _():
                out_copy(half, c).wait_recv()

                @pl.when(at > 0)
                def _():
                    out_copy(half, c).start()

                complete(part(half, c), half, c)

    def finish():
        def one(c, carry):
            for half in (0, 1):
                at = place(half)

                @pl.when(at < n - 1)
                def _():
                    reduce_copy(half, c, held).wait_send()

                @pl.when(at > 0)
                def _():
                    out_copy(half, c).wait_send()

            return carry

        lax.fori_loop(0, parts, one, 0)

    return greet, begin, slot, finish


def line_scratch(shape, dtype, parts=line_parts):
    return [pltpu.VMEM(shape, dtype)] + [
        pltpu.SemaphoreType.DMA((2, parts)) for _ in range(4)
    ]


def line_sum_kernel(n, x_ref, o_ref, *scratch):
    _, begin, slot, finish = line_engine(n, x_ref, o_ref, *scratch)
    begin()

    def step(t, carry):
        slot(t)
        return carry

    lax.fori_loop(0, line_steps(n), step, 0)
    finish()


def line_sum(x, n, barrier_id):
    rows, width = x.shape
    return pl.pallas_call(
        functools.partial(line_sum_kernel, n),
        out_shape=jax.ShapeDtypeStruct(x.shape, x.dtype),
        in_specs=[pl.BlockSpec(memory_space=pltpu.VMEM)],
        out_specs=pl.BlockSpec(memory_space=pltpu.VMEM),
        scratch_shapes=line_scratch(x.shape, x.dtype),
        compiler_params=pltpu.CompilerParams(
            collective_id=barrier_id, has_side_effects=True, vmem_limit_bytes=24 * 2**20
        ),
        cost_estimate=pl.CostEstimate(
            flops=rows * width, bytes_accessed=100 * rows * width, transcendentals=0
        ),
    )(x)


gather_parts = 3


def gather_engine(n, pairs, own_sem, far_send, far_recv, near_send, near_recv):
    me = lax.axis_index("dp")
    core, chip, chips = lax.rem(me, 2), me // 2, n // 2

    def rows(a, p):
        size = pairs[a][0].shape[0] // gather_parts
        return pl.ds(p * size, size)

    def far(a, p, k):
        x_ref, out_ref = pairs[a]
        return pltpu.make_async_remote_copy(
            src_ref=x_ref.at[rows(a, p)],
            dst_ref=out_ref.at[me, rows(a, p)],
            send_sem=far_send.at[a, p, k],
            recv_sem=far_recv.at[a, p, k],
            device_id={"dp": lax.rem(chip + k, chips) * 2 + core},
            device_id_type=MESH,
        )

    def near(a, p, k):
        x_ref, out_ref = pairs[a]
        owner = lax.rem(chip + chips - k, chips) * 2 + core
        target = out_ref.at[owner, rows(a, p)]
        return pltpu.make_async_remote_copy(
            src_ref=x_ref.at[rows(a, p)] if k == 0 else target,
            dst_ref=target,
            send_sem=near_send.at[a, p, k],
            recv_sem=near_recv.at[a, p, k],
            device_id={"dp": me + 1 - 2 * core},
            device_id_type=MESH,
        )

    def own(a):
        x_ref, out_ref = pairs[a]
        return pltpu.make_async_copy(x_ref, out_ref.at[me], own_sem.at[a])

    arrays = range(len(pairs))

    def greet():
        barrier = pltpu.get_barrier_semaphore()
        for k in range(1, chips):
            pl.semaphore_signal(
                barrier,
                inc=1,
                device_id={"dp": lax.rem(chip + k, chips) * 2 + core},
                device_id_type=MESH,
            )
        pl.semaphore_signal(
            barrier, inc=1, device_id={"dp": me + 1 - 2 * core}, device_id_type=MESH
        )
        return chips

    def start():
        for p in range(gather_parts):
            for a in arrays:
                for k in range(1, chips):
                    far(a, p, k).start()
        for p in range(gather_parts):
            for a in arrays:
                near(a, p, 0).start()
        for a in arrays:
            own(a).start()

    def forward(p):
        for a in arrays:
            for k in range(1, chips):
                far(a, p, k).wait_recv()
                near(a, p, k).start()

    def finish():
        for a in arrays:
            own(a).wait()
            for p in range(gather_parts):
                for k in range(chips):
                    near(a, p, k).wait_recv()
                    near(a, p, k).wait_send()
                    if k:
                        far(a, p, k).wait_send()

    return greet, start, forward, finish


def gather_scratch(arrays, n):
    return [pltpu.SemaphoreType.DMA((arrays,))] + [
        pltpu.SemaphoreType.DMA((arrays, gather_parts, n // 2)) for _ in range(4)
    ]


def gateup_column(e, part, group, hidden):
    return (e // group * 2 * group + part * group + e % group) * hidden


def gather_kernel(n, group, count, *refs):
    x_refs, refs = refs[:count], refs[count:]
    w_ref, refs = (None, refs) if group is None else (refs[0], refs[1:])
    out_refs, refs = refs[:count], refs[count:]
    low_ref, scratch = (None, refs) if group is None else (refs[0], refs[1:])
    greet, start, forward, finish = gather_engine(n, list(zip(x_refs, out_refs)), *scratch)
    pl.semaphore_wait(pltpu.get_barrier_semaphore(), greet())
    start()
    if group is not None:
        depth, hidden = low_ref.shape[0], w_ref.shape[1]
        for e in range(EXPERTS):
            for part in (0, 1):
                at = gateup_column(e, part, group, hidden)
                low_ref[:, at : at + hidden] = w_ref[
                    pl.ds(e * 2 * depth + part, depth, stride=2)
                ].astype(bf16)
    for p in range(gather_parts):
        forward(p)
    finish()


def gather(arrays, w, n, group, barrier_id):
    depth = arrays[0].shape[0]
    whole = pl.BlockSpec(memory_space=pltpu.VMEM)
    shapes = [jax.ShapeDtypeStruct((n,) + x.shape, x.dtype) for x in arrays]
    operands = list(arrays)
    if group is not None:
        operands.append(w)
        shapes.append(jax.ShapeDtypeStruct((depth, w.size // depth), bf16))
    out = pl.pallas_call(
        functools.partial(gather_kernel, n, group, len(arrays)),
        out_shape=shapes,
        in_specs=[whole] * len(operands),
        out_specs=[whole] * len(shapes),
        scratch_shapes=gather_scratch(len(arrays), n),
        compiler_params=pltpu.CompilerParams(
            collective_id=barrier_id, has_side_effects=True, vmem_limit_bytes=24 * 2**20
        ),
    )(*operands)
    count = len(arrays)
    return [t.reshape(n * depth, -1) for t in out[:count]] + list(out[count:])


def expert_adam_kernel(
    group, w_ref, m_ref, v_ref, grad_ref, dw_ref, dm_ref, dv_ref, down_ref,
    w_out, m_out, v_out, dw_out, dm_out, dv_out, g_ref,
):
    depth, hidden = grad_ref.shape[0], w_ref.shape[1]
    for e in range(w_ref.shape[0] // (2 * depth)):
        for part in (0, 1):
            at = gateup_column(e, part, group, hidden)
            g_ref[pl.ds(part, depth, stride=2)] = grad_ref[:, at : at + hidden].astype(f32)
        rows = slice(e * 2 * depth, (e + 1) * 2 * depth)
        w_out[rows], m_out[rows], v_out[rows] = adam_update(
            w_ref[rows], m_ref[rows], v_ref[rows], g_ref[...], weight_decay, 0.05
        )
        rows = slice(e * depth, (e + 1) * depth)
        dw_out[rows], dm_out[rows], dv_out[rows] = adam_update(
            dw_ref[rows],
            dm_ref[rows],
            dv_ref[rows],
            down_ref[:, e * hidden : (e + 1) * hidden].astype(f32),
            weight_decay,
            0.05,
        )


def expert_adam(gateup, gateup_grad, down, down_grad, group):
    experts, depth, parts, hidden = gateup[0].shape
    flat = [t.reshape(-1, hidden) for t in gateup]
    turned = [t.transpose(0, 2, 1).reshape(-1, hidden) for t in down]
    each = 2 * group
    block = lambda n: pl.BlockSpec((each * depth * n, hidden), lambda e: (e, 0))
    column = lambda n: pl.BlockSpec((depth, each * n * hidden), lambda e: (0, e))
    out = pl.pallas_call(
        functools.partial(expert_adam_kernel, group),
        grid=(experts // each,),
        in_specs=[block(2)] * 3 + [column(2)] + [block(1)] * 3 + [column(1)],
        out_specs=[block(2)] * 3 + [block(1)] * 3,
        out_shape=[jax.ShapeDtypeStruct(t.shape, f32) for t in flat + turned],
        scratch_shapes=[pltpu.VMEM((depth * parts, hidden), f32)],
        compiler_params=pltpu.CompilerParams(vmem_limit_bytes=60 * 2**20),
    )(*flat, gateup_grad, *turned, down_grad)
    return (
        tuple(t.reshape(gateup[0].shape) for t in out[:3]),
        tuple(t.reshape(experts, depth, hidden).transpose(0, 2, 1) for t in out[3:]),
    )


def line_gather_kernel(n, n_dp, x_ref, a_ref, b_ref, o_ref, a_out, b_out, *scratch):
    line, spread_out = scratch[:5], scratch[5:]
    greet, _, slot, finish = line_engine(n, x_ref, o_ref, *line)
    greet_dp, start, forward, finish_dp = gather_engine(
        n_dp, [(a_ref, a_out), (b_ref, b_out)], *spread_out
    )
    peers = greet() + greet_dp()
    pl.semaphore_wait(pltpu.get_barrier_semaphore(), peers)
    start()

    def step(t, carry):
        slot(t)
        return carry

    total = line_steps(n)
    done = 0
    for p in range(gather_parts):
        until = total * (p + 1) // gather_parts
        lax.fori_loop(done, until, step, 0)
        done = until
        forward(p)
    finish()
    finish_dp()


def line_gather(x, a, b, n, n_dp, barrier_id):
    rows, width = x.shape
    whole, anywhere = pl.BlockSpec(memory_space=pltpu.VMEM), pl.BlockSpec(memory_space=pl.ANY)
    o, a_all, b_all = pl.pallas_call(
        functools.partial(line_gather_kernel, n, n_dp),
        out_shape=[jax.ShapeDtypeStruct(x.shape, x.dtype)]
        + [jax.ShapeDtypeStruct((n_dp,) + t.shape, t.dtype) for t in (a, b)],
        in_specs=[whole, anywhere, anywhere],
        out_specs=[whole, anywhere, anywhere],
        scratch_shapes=line_scratch(x.shape, x.dtype) + gather_scratch(2, n_dp),
        compiler_params=pltpu.CompilerParams(
            collective_id=barrier_id, has_side_effects=True, vmem_limit_bytes=24 * 2**20
        ),
        cost_estimate=pl.CostEstimate(
            flops=rows * width, bytes_accessed=100 * rows * width, transcendentals=0
        ),
    )(x, a, b)
    return o, a_all.reshape(-1, a.shape[1]), b_all.reshape(-1, b.shape[1])


def last_kernel(
    n, n_dp, pieces, first_ref, tokens_ref, middle_ref, mixture_ref, gain_ref, gain_second_ref, *refs,
):
    weights_refs, refs = refs[:pieces], refs[pieces:]
    last_body(
        n, n_dp, first_ref, tokens_ref, middle_ref, mixture_ref, gain_ref, weights_refs,
        gain_second_ref, *refs,
    )


def last_body(
    n, n_dp, first_ref, tokens_ref, middle_ref, mixture_ref, gain_ref, weights_refs,
    gain_second_ref, grad_ref, weights_out, gains_out, mixture_out,
    x_ref, o_ref, held, send_red, recv_red, send_out, recv_out,
    tokens_v, middle_v, grad_v, in_sem, out_sem, x_sem, got, w_send, w_recv,
    g_from, g_got, g_send, g_recv, z_from, z_got, z_send, z_recv, acc,
):
    me, line = lax.axis_index("dp"), lax.axis_index("tensor")
    model = x_ref.shape[1]
    rows = tokens_v.shape[0] // (2 * line_parts)
    depth = weights_out.shape[0]
    half_x, half_m = line_parts * rows, TOK_MB // 2
    half_all = half_x + half_m
    parts = half_all // rows

    def own_rows(half, c):
        return pl.ds(pl.multiple_of((half * line_parts + c) * rows, 16), rows)

    def half_copies(x, m, sem, back):
        for half in (0, 1):
            for ref, low, size, at in (
                (x, half * half_x, half_x, half * half_all),
                (m[0], m[1] + half * half_m, half_m, half * half_all + half_x),
            ):
                if ref is not None:
                    here = (o_ref if back else x_ref).at[pl.ds(at, size)]
                    there = ref.at[pl.ds(low, size)]
                    k = half * 2 + (ref is m[0])
                    yield pltpu.make_async_copy(
                        *((here, there) if back else (there, here)), sem.at[k]
                    )

    def norm_of(at):
        x = tokens_v[at].astype(f32)
        inverse = lax.rsqrt(jnp.mean(x * x, axis=-1, keepdims=True) + eps_norm)
        return x * inverse, inverse

    def complete(at, half, c):
        @pl.when(c < line_parts)
        def _():
            own = own_rows(half, c)
            norm, inverse = norm_of(own)
            grad = o_ref[at].astype(f32) * (gain_ref[0:1] + gain_ref[2:3])
            mean = jnp.mean(grad * norm, axis=-1, keepdims=True)
            grad_v[own] = middle_v[own] + inverse * (grad - norm * mean)

    _, _, slot, finish = line_engine(
        n, x_ref, o_ref, held, send_red, recv_red, send_out, recv_out, complete, parts
    )

    columns, low = [], 0
    for ref in weights_refs:
        columns.append(slice(low, low + ref.shape[2]))
        low += ref.shape[2]
    pieces = range(len(columns))

    def weights_copy(k, j):
        to = lax.rem(me + k, n_dp)
        return pltpu.make_async_remote_copy(
            src_ref=weights_refs[j].at[to], dst_ref=got.at[k, :, columns[j]],
            send_sem=w_send.at[j, k], recv_sem=w_recv.at[j, k],
            device_id={"dp": to}, device_id_type=MESH,
        )

    def gains_copy(k):
        to = lax.rem(me + k, n_dp)
        return pltpu.make_async_remote_copy(
            src_ref=g_from.at[to], dst_ref=g_got.at[k],
            send_sem=g_send.at[k], recv_sem=g_recv.at[k],
            device_id={"dp": to}, device_id_type=MESH,
        )

    def line_copy(k):
        to = lax.rem(line + k, n)
        return pltpu.make_async_remote_copy(
            src_ref=z_from, dst_ref=z_got.at[k],
            send_sem=z_send.at[k], recv_sem=z_recv.at[k],
            device_id={"tensor": to}, device_id_type=MESH,
        )

    def loop(count, act):
        def one(k, carry):
            act(k)
            return carry

        lax.fori_loop(1, count, one, 0)

    load_tokens = pltpu.make_async_copy(tokens_ref, tokens_v, in_sem.at[0])
    load_middle = pltpu.make_async_copy(middle_ref, middle_v, in_sem.at[1])
    loads = list(half_copies(first_ref, (mixture_ref, TOK_MB), x_sem, False))
    for load in loads + [load_tokens, load_middle]:
        load.start()
    barrier = pltpu.get_barrier_semaphore()

    def greet(axis, place, count):
        loop(
            count,
            lambda k: pl.semaphore_signal(
                barrier, inc=1, device_id={axis: lax.rem(place + k, count)}, device_id_type=MESH
            ),
        )

    greet("dp", me, n_dp)
    greet("tensor", line, n)
    pl.semaphore_wait(barrier, n_dp + n - 2)
    for j in pieces:
        loop(n_dp, lambda k: weights_copy(k, j).start())
    acc[...] = jnp.zeros_like(acc)
    for load in loads:
        load.wait()

    def step(t, carry):
        slot(t)
        return carry

    def gain_step(t, carry):
        slot(t)
        c = t - early
        for half in (0, 1):
            at = pl.ds(pl.multiple_of(half * half_all + c * rows, 16), rows)
            norm, _ = norm_of(own_rows(half, c))
            term = x_ref[at].astype(f32) * norm
            acc[...] += jnp.sum(term.reshape(rows // 8, 8, model), axis=0)
        return carry

    total = line_steps(n, parts)
    early, size = 4, 32
    lax.fori_loop(0, early, step, 0)
    for load in (load_tokens, load_middle):
        load.wait()
    low = early + line_parts
    lax.fori_loop(early, low, gain_step, 0)
    width = g_from.shape[2]
    for p in range(n_dp):
        moved = acc[...] if p == 0 else pltpu.roll(acc[...], model - p * depth, 1)
        g_from[p, :8] = moved[:, :width]
        moved = gain_second_ref[...] if p == 0 else pltpu.roll(
            gain_second_ref[...], model - p * depth, 1
        )
        g_from[p, 8:] = jnp.where(line == 0, moved[:, :width], 0.0)
    loop(n_dp, lambda k: gains_copy(k).start())
    for j in pieces:
        loop(n_dp, lambda k: weights_copy(k, j).wait_recv())

    def add_step(t, carry):
        slot(t)
        at = pl.ds(pl.multiple_of((t - low) * size, 16), size)
        for j, ref in enumerate(weights_refs):
            weights_out[at, columns[j]] = lax.fori_loop(
                1,
                n_dp,
                lambda k, v: v + got[k, at, columns[j]].astype(f32),
                ref[me, at].astype(f32),
            )
        return carry

    middle = low + depth // size
    lax.fori_loop(low, middle, add_step, 0)
    loop(n_dp, lambda k: gains_copy(k).wait_recv())
    z_from[...] = lax.fori_loop(1, n_dp, lambda k, v: v + g_got[k], g_from[me])
    loop(n, lambda k: line_copy(k).start())
    own_done = max(middle, line_steps(n))
    lax.fori_loop(middle, own_done, step, 0)
    every = pltpu.make_async_copy(grad_v, grad_ref, out_sem)
    every.start()
    lax.fori_loop(own_done, total, step, 0)
    stores = list(half_copies(None, (mixture_out, 0), x_sem, True))
    for store in stores:
        store.start()
    loop(n, lambda k: line_copy(k).wait_recv())
    gains_out[...] = lax.fori_loop(1, n, lambda k, v: v + z_got[k], z_from[...])
    finish()
    for j in pieces:
        loop(n_dp, lambda k: weights_copy(k, j).wait_send())
    loop(n_dp, lambda k: gains_copy(k).wait_send())
    loop(n, lambda k: line_copy(k).wait_send())
    for store in stores + [every]:
        store.wait()


def last_call(x, tokens, middle, mixture, gain, weights, gain_second, n, n_dp, barrier_id):
    count, model = x.shape
    depth, width = model // n_dp, sum(w.shape[1] for w in weights)
    lanes = -(-depth // 128) * 128
    whole, anywhere = pl.BlockSpec(memory_space=pltpu.VMEM), pl.BlockSpec(memory_space=pl.ANY)
    dma = pltpu.SemaphoreType.DMA
    grad, weights, gains, mixture = pl.pallas_call(
        functools.partial(last_kernel, n, n_dp, len(weights)),
        out_shape=[
            jax.ShapeDtypeStruct((count, model), f32),
            jax.ShapeDtypeStruct((depth, width), f32),
            jax.ShapeDtypeStruct((16, lanes), f32),
            jax.ShapeDtypeStruct((TOK_MB, model), bf16),
        ],
        in_specs=[anywhere, anywhere, anywhere, anywhere, whole, whole] + [whole] * len(weights),
        out_specs=[anywhere, whole, whole, anywhere],
        scratch_shapes=[pltpu.VMEM((count + TOK_MB, model), bf16)] * 2
        + line_scratch((count + TOK_MB, model), bf16, line_parts * (count + TOK_MB) // count)
        + [
            pltpu.VMEM((count, model), bf16),
            pltpu.VMEM((count, model), f32),
            pltpu.VMEM((count, model), f32),
            dma((2,)),
            dma,
            dma((4,)),
            pltpu.VMEM((n_dp, depth, width), bf16),
            dma((len(weights), n_dp)),
            dma((len(weights), n_dp)),
            pltpu.VMEM((n_dp, 16, lanes), f32),
            pltpu.VMEM((n_dp, 16, lanes), f32),
            dma((n_dp,)),
            dma((n_dp,)),
            pltpu.VMEM((16, lanes), f32),
            pltpu.VMEM((n, 16, lanes), f32),
            dma((n,)),
            dma((n,)),
            pltpu.VMEM((8, model), f32),
        ],
        compiler_params=pltpu.CompilerParams(
            collective_id=barrier_id, has_side_effects=True, vmem_limit_bytes=56 * 2**20
        ),
        cost_estimate=pl.CostEstimate(
            flops=count * model, bytes_accessed=2**20, transcendentals=0
        ),
    )(x, tokens, middle, mixture, gain, gain_second, *(w.reshape(n_dp, depth, -1) for w in weights))
    gains = jnp.sum(gains.reshape(2, 8, lanes), axis=1)[:, :depth]
    return grad, weights, gains, mixture


def expert_grads_kernel(
    n, shape, x_ref, rows_ref, outgrad_ref, start_ref, rest_ref,
    hidden_ref, active_ref, active_rows_ref,
    o_ref, gateup_grad_ref, down_grad_ref, mixture_ref, rows_t, outgrad_t, o_sem, sum_ref, *scratch,
):
    mixture_steps, gateup_steps, down_steps = shape
    i = pl.program_id(0)
    steps = sum(shape)
    _, begin, slot, finish = line_engine(n, x_ref, sum_ref, *scratch)
    total = line_steps(n)
    each = -(-total // steps)
    pl.when(i == 0)(begin)

    def slots(low, high):
        def one(j, carry):
            t = i * each + j
            pl.when(t < total)(lambda: slot(t))
            return carry

        lax.fori_loop(low, high, one, 0)

    slots(0, 1)

    @pl.when(i < mixture_steps)
    def _():
        half = start_ref.shape[1]
        mixture_ref[...] = (
            lax.dot_general(
                active_rows_ref[:, :half], start_ref[...], nt, preferred_element_type=f32
            )
            + lax.dot_general(
                active_rows_ref[:, half:], rest_ref[...], nt, preferred_element_type=f32
            )
        ).astype(bf16)
        size = active_rows_ref.shape[0]
        columns = pl.ds(pl.multiple_of(i * size, size), size)
        rows_t[:, columns] = rows_ref[...].T
        outgrad_t[:, columns] = outgrad_ref[...].T

    @pl.when((i >= mixture_steps) & (i < mixture_steps + gateup_steps))
    def _():
        gateup_grad_ref[...] = jnp.dot(
            rows_t[...], hidden_ref[...], preferred_element_type=f32
        ).astype(bf16)

    @pl.when(i >= mixture_steps + gateup_steps)
    def _():
        down_grad_ref[...] = jnp.dot(
            outgrad_t[...], active_ref[...], preferred_element_type=f32
        ).astype(bf16)

    slots(1, each)

    @pl.when(i == steps - 1)
    def _():
        copy = pltpu.make_async_copy(sum_ref, o_ref, o_sem)
        copy.start()
        finish()
        copy.wait()


def expert_grads_call(
    x, rows, outgrad, down_start, down_rest, hidden, active, n, barrier_id
):
    tokens, model = rows.shape
    block, tile = min(512, active.shape[1]), 256
    c, a, b = shape = (tokens // tile, hidden.shape[1] // block, active.shape[1] // block)
    whole = pl.BlockSpec(memory_space=pltpu.VMEM)
    first = lambda i: (jnp.minimum(i, c - 1), 0)
    second = lambda i: (0, jnp.clip(i - c, 0, a - 1))
    third = lambda i: (0, jnp.clip(i - c - a, 0, b - 1))
    return pl.pallas_call(
        functools.partial(expert_grads_kernel, n, shape),
        grid=(a + b + c,),
        in_specs=[
            whole,
            pl.BlockSpec((tile, model), first),
            pl.BlockSpec((tile, model), first),
            whole,
            whole,
            pl.BlockSpec((tokens, block), second),
            pl.BlockSpec((tokens, block), third),
            pl.BlockSpec((tile, active.shape[1]), first),
        ],
        out_specs=[
            pl.BlockSpec(memory_space=pl.ANY),
            pl.BlockSpec((model, block), second),
            pl.BlockSpec((model, block), third),
            pl.BlockSpec((tile, model), first),
        ],
        out_shape=[
            jax.ShapeDtypeStruct(x.shape, x.dtype),
            jax.ShapeDtypeStruct((model, hidden.shape[1]), bf16),
            jax.ShapeDtypeStruct((model, active.shape[1]), bf16),
            jax.ShapeDtypeStruct((tokens, model), bf16),
        ],
        scratch_shapes=[pltpu.VMEM((model, tokens), bf16)] * 2
        + [pltpu.SemaphoreType.DMA, pltpu.VMEM(x.shape, x.dtype)]
        + line_scratch(x.shape, x.dtype),
        compiler_params=pltpu.CompilerParams(
            collective_id=barrier_id, has_side_effects=True, vmem_limit_bytes=58 * 2**20
        ),
        cost_estimate=pl.CostEstimate(
            flops=2 * tokens * model * (hidden.shape[1] + 2 * active.shape[1]),
            bytes_accessed=10 * tokens * model,
            transcendentals=0,
        ),
    )(x, rows, outgrad, down_start, down_rest, hidden, active, active)


def expert_kernel(group, steps, rows_ref, outgrad_ref, gates_ref, gu_ref, start_ref, rest_ref,
                  active_ref, hidden_ref, gate_grad_ref, down_ref):
    step = pl.program_id(0)
    tile = 256
    width = gu_ref.shape[1] // 2
    hidden = width // group
    lane = lax.broadcasted_iota(jnp.int32, (tile, 128), 1)
    column = lax.broadcasted_iota(jnp.int32, (tile, width), 1)

    @pl.when(step == 0)
    def _():
        gate_grad_ref[...] = jnp.zeros_like(gate_grad_ref)

    @pl.when(step < steps // 2)
    def _():
        down_ref[...] = start_ref[...]

    @pl.when(step >= steps // 2)
    def _():
        down_ref[...] = rest_ref[...]

    def one(t, carry):
        at = pl.ds(pl.multiple_of(t * tile, tile), tile)
        h = jnp.dot(rows_ref[at], gu_ref[...], preferred_element_type=f32)
        back = jnp.dot(outgrad_ref[at], down_ref[...], preferred_element_type=f32)
        gates = gates_ref[at]
        wide = jnp.zeros((tile, width), f32)
        for j in range(group):
            g = jnp.sum(jnp.where(lane == step * group + j, gates, 0.0), axis=1, keepdims=True)
            wide = g + wide if group == 1 else jnp.where(column // hidden == j, g, wide)
        gate, up = h[:, :width], h[:, width:]
        sig = 1.0 / (1.0 + jnp.exp(-gate))
        silu = gate * sig
        active = (silu * up).astype(bf16).astype(f32)
        active_ref[at] = (active * wide).astype(bf16)
        product = active * back
        grads = gate_grad_ref[at]
        for j in range(group):
            s = jnp.sum(jnp.where(column // hidden == j, product, 0.0), axis=1, keepdims=True)
            grads = jnp.where(lane == step * group + j, s, grads)
        gate_grad_ref[at] = grads
        back = back * wide
        hidden_ref[at, :width] = (back * up * sig * (1.0 + gate * (1.0 - sig))).astype(bf16)
        hidden_ref[at, width:] = (back * silu).astype(bf16)
        return carry

    lax.fori_loop(0, rows_ref.shape[0] // tile, one, 0)


def expert_call(rows, outgrad, gates, gu, down_start, down_rest, group):
    tokens, model = rows.shape
    width = gu.shape[1] // (EXPERTS // group)
    steps = EXPERTS // group
    return pl.pallas_call(
        functools.partial(expert_kernel, group, steps),
        grid=(steps,),
        in_specs=[
            pl.BlockSpec((tokens, model), lambda p: (0, 0)),
            pl.BlockSpec((tokens, model), lambda p: (0, 0)),
            pl.BlockSpec((tokens, 128), lambda p: (0, 0)),
            pl.BlockSpec((model, width), lambda p: (0, p)),
            pl.BlockSpec((model, width // 2), lambda p: (0, jnp.minimum(p, steps // 2 - 1))),
            pl.BlockSpec((model, width // 2), lambda p: (0, jnp.maximum(p - steps // 2, 0))),
        ],
        out_specs=[
            pl.BlockSpec((tokens, width // 2), lambda p: (0, p)),
            pl.BlockSpec((tokens, width), lambda p: (0, p)),
            pl.BlockSpec((tokens, 128), lambda p: (0, 0)),
        ],
        out_shape=[
            jax.ShapeDtypeStruct((tokens, steps * width // 2), bf16),
            jax.ShapeDtypeStruct((tokens, steps * width), bf16),
            jax.ShapeDtypeStruct((tokens, 128), f32),
        ],
        scratch_shapes=[pltpu.VMEM((model, width // 2), bf16)],
        compiler_params=pltpu.CompilerParams(vmem_limit_bytes=60 * 2**20),
        cost_estimate=pl.CostEstimate(
            flops=2 * tokens * model * steps * width * 3 // 2,
            bytes_accessed=2 * (model * steps * width * 3 // 2 + tokens * steps * width * 3 // 2),
            transcendentals=tokens * steps * width // 2,
        ),
    )(rows, outgrad, gates, gu, down_start, down_rest)


def turn(u, cosine, sine):
    lane = lax.broadcasted_iota(jnp.int32, u.shape, 1) % HEAD_DIM
    other = jnp.where(lane < HEAD_DIM // 2, pltpu.roll(u, 96, 1), pltpu.roll(u, 32, 1))
    return u * cosine + other * sine


def table_parts(me, prompt_total):
    return (
        (0, PROMPT_DEV, pl.multiple_of(me * PROMPT_DEV, PROMPT_DEV)),
        (PROMPT_DEV, CONT, prompt_total),
    )


def project_kernel(x_ref, gain_ref, w_ref, cos_ref, sin_ref, normed_ref, q_ref, kv_ref):
    x = x_ref[...].astype(f32)
    inverse = lax.rsqrt(jnp.mean(x * x, axis=-1, keepdims=True) + eps_norm)
    normed = (x * inverse * (gain_ref[0:1] + gain_ref[2:3])).astype(bf16)
    normed_ref[...] = normed
    mixed = jnp.dot(normed, w_ref[...], preferred_element_type=f32)
    block = [mixed[:, c * 128 : (c + 1) * 128] for c in range(5)]
    low = lax.broadcasted_iota(jnp.int32, block[0].shape, 1) < HEAD_DIM
    turned = [
        block[0],
        jnp.where(low, block[1], block[2]),
        block[3],
        jnp.where(low, pltpu.roll(block[1], HEAD_DIM, 1), pltpu.roll(block[4], HEAD_DIM, 1)),
    ]
    kv_ref[:, 128:] = jnp.where(low, block[2], block[4]).astype(bf16)
    prompt_total = cos_ref.shape[0] - CONT
    for start, rows, at in table_parts(lax.axis_index("dp"), prompt_total):
        cosine, sine = cos_ref[pl.ds(at, rows)], sin_ref[pl.ds(at, rows)]
        for c, u in enumerate(turned):
            u = turn(u[start : start + rows], cosine, sine).astype(bf16)
            if c < 3:
                q_ref[start : start + rows, c * 128 : (c + 1) * 128] = u
            else:
                kv_ref[start : start + rows, :128] = u


def project_call(tokens, gain, w, cosine, sine):
    count, model = tokens.shape
    width = w.shape[1]
    row = lambda n: pl.BlockSpec((TOK_MB, n), lambda i: (i, 0))
    fixed = lambda t: pl.BlockSpec(t.shape, lambda i: (0, 0))
    return pl.pallas_call(
        project_kernel,
        grid=(MICRO,),
        in_specs=[row(model), fixed(gain), fixed(w), fixed(cosine), fixed(sine)],
        out_specs=[row(model), row(width - 256), row(256)],
        out_shape=[
            jax.ShapeDtypeStruct((count, model), bf16),
            jax.ShapeDtypeStruct((count, width - 256), bf16),
            jax.ShapeDtypeStruct((count, 256), bf16),
        ],
        compiler_params=pltpu.CompilerParams(vmem_limit_bytes=48 * 2**20),
        cost_estimate=pl.CostEstimate(
            flops=2 * count * model * width, bytes_accessed=6 * count * model, transcendentals=count
        ),
    )(tokens, gain, w, cosine, sine)


def norm_rows(x_ref, b_ref):
    middle = x_ref[...].astype(f32) + b_ref[...].astype(f32)
    inverse = lax.rsqrt(jnp.mean(middle * middle, axis=-1, keepdims=True) + eps_norm)
    return middle * inverse, inverse


def route_kernel(x_ref, b_ref, gain_ref, router_ref, routes_ref, normed_ref, gates_ref):
    norm, _ = norm_rows(x_ref, b_ref)
    normed = (norm * (gain_ref[1:2] + gain_ref[3:4])).astype(bf16)
    normed_ref[...] = normed
    logits = jnp.dot(normed, router_ref[...], preferred_element_type=f32)
    lane = lax.broadcasted_iota(jnp.int32, logits.shape, 1)
    routes = routes_ref[...]
    named = lane == routes[:, 0:1]
    for k in range(1, TOPK):
        named = named | (lane == routes[:, k : k + 1])
    top = jnp.max(jnp.where(named, logits, -1e30), axis=-1, keepdims=True)
    weights = jnp.where(named, jnp.exp(jnp.where(named, logits, top) - top), 0.0)
    gates_ref[...] = weights / jnp.sum(weights, axis=-1, keepdims=True)


def route_call(tokens, branch, gain, router, routes):
    count, model = tokens.shape
    tile = 256
    row = lambda n: pl.BlockSpec((tile, n), lambda i: (i, 0))
    fixed = lambda t: pl.BlockSpec(t.shape, lambda i: (0, 0))
    return pl.pallas_call(
        route_kernel,
        grid=(count // tile,),
        in_specs=[row(model), row(model), fixed(gain), fixed(router), row(TOPK)],
        out_specs=[row(model), row(128)],
        out_shape=[
            jax.ShapeDtypeStruct((count, model), bf16),
            jax.ShapeDtypeStruct((count, 128), f32),
        ],
        compiler_params=pltpu.CompilerParams(vmem_limit_bytes=60 * 2**20),
    )(tokens, branch, gain, router, routes)


def middle_back_kernel(
    x_ref, b_ref, summed_ref, gates_ref, outgrad_ref, gain_ref, router_ref, outproj_ref,
    middle_ref, own_ref, attended_ref, logits_ref, gain_out,
):
    norm, inverse = norm_rows(x_ref, b_ref)
    model = x_ref.shape[1]
    gates = gates_ref[...]
    gate_grad = summed_ref[:, model:].astype(f32)
    chosen = gates * (gate_grad - jnp.sum(gates * gate_grad, axis=-1, keepdims=True))
    logits = chosen.astype(bf16)
    logits_ref[...] = logits
    grad = summed_ref[:, :model].astype(f32) + lax.dot_general(
        logits, router_ref[...], nt, preferred_element_type=f32
    )
    term = (grad * norm).reshape(-1, 8, model).sum(axis=0)

    @pl.when(pl.program_id(0) == 0)
    def _():
        gain_out[...] = jnp.zeros_like(gain_out)

    gain_out[...] += term
    grad = grad * (gain_ref[1:2] + gain_ref[3:4])
    mean = jnp.mean(grad * norm, axis=-1, keepdims=True)
    middle = outgrad_ref[...].astype(f32) + inverse * (grad - norm * mean)
    middle_ref[...] = middle
    own = middle.astype(bf16)
    own_ref[...] = own
    attended_ref[...] = jnp.dot(own, outproj_ref[...], preferred_element_type=f32).astype(bf16)


def middle_back_call(tokens, branch, summed, gates, outgrad, gain, router, outproj):
    count, model = tokens.shape
    tile = 256
    row = lambda n: pl.BlockSpec((tile, n), lambda i: (i, 0))
    fixed = lambda t: pl.BlockSpec(t.shape, lambda i: (0, 0))
    return pl.pallas_call(
        middle_back_kernel,
        grid=(count // tile,),
        in_specs=[
            row(model),
            row(model),
            row(model + 128),
            row(128),
            row(model),
            fixed(gain),
            fixed(router),
            fixed(outproj),
        ],
        out_specs=[
            row(model),
            row(model),
            row(outproj.shape[1]),
            row(128),
            pl.BlockSpec((8, model), lambda i: (0, 0)),
        ],
        out_shape=[
            jax.ShapeDtypeStruct((count, model), f32),
            jax.ShapeDtypeStruct((count, model), bf16),
            jax.ShapeDtypeStruct((count, outproj.shape[1]), bf16),
            jax.ShapeDtypeStruct((count, 128), bf16),
            jax.ShapeDtypeStruct((8, model), f32),
        ],
        compiler_params=pltpu.CompilerParams(vmem_limit_bytes=60 * 2**20),
    )(tokens, branch, summed, gates, outgrad, gain, router, outproj)


def block_out_kernel(x_ref, b_ref, first_ref, second_ref, o_ref):
    middle = x_ref[...].astype(f32) + b_ref[...].astype(f32)

    @pl.when(pl.program_id(0) == 0)
    def _():
        o_ref[...] = (middle + first_ref[...].astype(f32)).astype(bf16)

    @pl.when(pl.program_id(0) == 1)
    def _():
        o_ref[...] = (middle + second_ref[...].astype(f32)).astype(bf16)


def block_out_call(tokens, branch, first, second):
    count, model = tokens.shape
    columns = model // 3
    row = pl.BlockSpec((TOK_MB, columns), lambda i, j: (i, j))
    half = lambda place: pl.BlockSpec(
        (TOK_MB, columns), lambda i, j: (0, jnp.where(i == place, j, 0 if place else 2))
    )
    return pl.pallas_call(
        block_out_kernel,
        grid=(MICRO, 3),
        in_specs=[row, row, half(0), half(1)],
        out_specs=row,
        out_shape=jax.ShapeDtypeStruct((count, model), bf16),
        compiler_params=pltpu.CompilerParams(vmem_limit_bytes=60 * 2**20),
    )(tokens, branch, first, second)


def head_places(heads):
    return [(h // GROUP, h % 2, h // 2) for h in range(heads)]


def spread(kv, scale):
    lane = lax.broadcasted_iota(jnp.int32, kv.shape, 1)
    kv = kv * scale
    turned = pltpu.roll(kv, HEAD_DIM, 1)
    first = lane < HEAD_DIM
    zero = jnp.zeros_like(kv)
    return {
        (0, 0): jnp.where(first, kv, zero).astype(bf16),
        (0, 1): jnp.where(first, zero, turned).astype(bf16),
        (1, 0): jnp.where(first, turned, zero).astype(bf16),
        (1, 1): jnp.where(first, zero, kv).astype(bf16),
    }


def row_tiles(prompt_total):
    tiles = [(0, PROMPT_DEV, prompt_total)]
    for start in range(0, CONT, 256):
        tiles.append((PROMPT_DEV + start, 256, prompt_total + start + 256))
    return tiles


def greet(me, n):
    barrier = pltpu.get_barrier_semaphore()

    def one(k, carry):
        pl.semaphore_signal(
            barrier, inc=1, device_id={"dp": lax.rem(me + k, n)}, device_id_type=MESH
        )
        return carry

    lax.fori_loop(1, n, one, 0)
    return n - 1


def meet(me, n):
    pl.semaphore_wait(pltpu.get_barrier_semaphore(), greet(me, n))


def load_spread(m, all_ref, kv_ref, k_ref, v_ref, kt_ref=None):
    total = all_ref.shape[1]
    own = pl.ds(pl.multiple_of(m * TOK_MB + PROMPT_DEV, 16), CONT)
    for low, high, rows in ((0, total, all_ref[m]), (total, total + CONT, kv_ref[own])):
        keys = spread(rows[:, :128].astype(f32), HEAD_DIM**-0.5)
        values = spread(rows[:, 128:].astype(f32), 1.0)
        for i, place in enumerate(keys):
            k_ref[i, low:high] = keys[place]
            v_ref[i, low:high] = values[place]
            if kt_ref is not None:
                kt_ref[i, :, low:high] = keys[place].astype(f32).T.astype(bf16)
    return {place: i for i, place in enumerate(keys)}


def attention_kernel(
    heads, n, q_ref, kv_ref, w_ref, o_ref, lse_ref, all_ref, w_out, k_ref, v_ref, send, recv,
    *spread_out,
):
    _, start_w, forward_w, finish_w = gather_engine(n, [(w_ref, w_out)], *spread_out)
    prompt_total = all_ref.shape[1]
    me = lax.axis_index("dp")

    def piece(m, k):
        rows = all_ref.at[m, pl.ds(pl.multiple_of(me * PROMPT_DEV, PROMPT_DEV), PROMPT_DEV)]
        return pltpu.make_async_remote_copy(
            src_ref=rows,
            dst_ref=rows,
            send_sem=send.at[m, k],
            recv_sem=recv.at[m, k],
            device_id={"dp": lax.rem(me + k, n)},
            device_id_type=MESH,
        )

    for m in range(MICRO):
        all_ref[m, pl.ds(pl.multiple_of(me * PROMPT_DEV, PROMPT_DEV), PROMPT_DEV)] = kv_ref[
            m * TOK_MB : m * TOK_MB + PROMPT_DEV
        ]
    meet(me, n)

    def every(m, act):
        def one(k, carry):
            act(piece(m, k))
            return carry

        lax.fori_loop(1, n, one, 0)

    for m in range(MICRO):
        every(m, lambda copy: copy.start())
    start_w()

    def micro(m, carry):
        every(m, lambda copy: copy.wait_recv())
        index = load_spread(m, all_ref, kv_ref, k_ref, v_ref)
        lane = lax.broadcasted_iota(jnp.int32, (1, 128), 1)
        for start, rows, length in row_tiles(prompt_total):
            at = pl.ds(pl.multiple_of(m * TOK_MB + start, 128), rows)
            row = lax.broadcasted_iota(jnp.int32, (rows, 1), 0)
            if start == 0:
                masked = 0
                reach = row + me * PROMPT_DEV
            else:
                masked = length - 256
                reach = row
            column = lax.broadcasted_iota(jnp.int32, (rows, length - masked), 1)
            lse = jnp.zeros((rows, 128), f32)
            pair_out = None
            for h, (kv, half, pair) in enumerate(head_places(heads)):
                q = q_ref[at, pair * 128 : (pair + 1) * 128]
                i = index[kv, half]
                tail = lax.dot_general(q, k_ref[i, masked:length], nt, preferred_element_type=f32)
                tail = jnp.where(column <= reach, tail, -1e30)
                top = jnp.max(tail, axis=1, keepdims=True)
                if masked:
                    head = lax.dot_general(q, k_ref[i, :masked], nt, preferred_element_type=f32)
                    top = jnp.maximum(top, jnp.max(head, axis=1, keepdims=True))
                    p_head = jnp.exp(head - top)
                p_tail = jnp.exp(tail - top)
                total = jnp.sum(p_tail, axis=1, keepdims=True)
                out = jnp.dot(
                    p_tail.astype(bf16), v_ref[i, masked:length], preferred_element_type=f32
                )
                if masked:
                    total = total + jnp.sum(p_head, axis=1, keepdims=True)
                    out = out + jnp.dot(
                        p_head.astype(bf16), v_ref[i, :masked], preferred_element_type=f32
                    )
                out = out / total
                lse = jnp.where(lane == h, top + jnp.log(total), lse)
                if half == 0:
                    pair_out = out
                else:
                    o_ref[at, pair * 128 : (pair + 1) * 128] = (pair_out + out).astype(bf16)
            lse_ref[m, :, start : start + rows] = lse.T[:8]
        return carry

    lax.fori_loop(0, MICRO, micro, 0)
    for p in range(gather_parts):
        forward_w(p)
    for m in range(MICRO):
        every(m, lambda copy: copy.wait_send())
    finish_w()


def attention_call(q, kv, w, n):
    count, width = q.shape
    keys = PROMPT_DEV * n + CONT
    heads = width // HEAD_DIM
    whole = pl.BlockSpec(memory_space=pltpu.VMEM)
    return pl.pallas_call(
        functools.partial(attention_kernel, heads, n),
        in_specs=[whole] * 2 + [pl.BlockSpec(memory_space=pl.ANY)],
        out_specs=[whole] * 3 + [pl.BlockSpec(memory_space=pl.ANY)],
        out_shape=[
            jax.ShapeDtypeStruct((count, width), bf16),
            jax.ShapeDtypeStruct((MICRO, 8, TOK_MB), f32),
            jax.ShapeDtypeStruct((MICRO, PROMPT_DEV * n, 256), bf16),
            jax.ShapeDtypeStruct((n,) + w.shape, w.dtype),
        ],
        scratch_shapes=[
            pltpu.VMEM((4, keys, 128), bf16),
            pltpu.VMEM((4, keys, 128), bf16),
            pltpu.SemaphoreType.DMA((MICRO, n)),
            pltpu.SemaphoreType.DMA((MICRO, n)),
        ]
        + gather_scratch(1, n),
        compiler_params=pltpu.CompilerParams(
            collective_id=3, has_side_effects=True, vmem_limit_bytes=48 * 2**20
        ),
        cost_estimate=pl.CostEstimate(
            flops=16 * count * keys * width,
            bytes_accessed=8 * count * width,
            transcendentals=count * keys * heads,
        ),
    )(q, kv, w)


def attention_back_kernel(
    heads, n, q_ref, kv_ref, all_ref, do_ref, o_ref, lse_ref,
    cos_ref, sin_ref,
    grad_ref, k_ref, v_ref, kt_ref, dk_ref, dv_ref, sent_ref, got_ref, send, recv,
):
    prompt_total = all_ref.shape[1]
    me = lax.axis_index("dp")

    def put_both(at, dk, dv):
        low = lax.broadcasted_iota(jnp.int32, dk.shape, 1) < HEAD_DIM
        dk = pltpu.roll(dk, HEAD_DIM, 1)
        second = grad_ref[at, 128:256].astype(f32)
        grad_ref[at, 128:256] = jnp.where(low, second, dk).astype(bf16)
        grad_ref[at, 256:384] = jnp.where(low, dv, second).astype(bf16)
        grad_ref[at, 512:640] = jnp.where(low, dk, dv).astype(bf16)

    def piece(m, k):
        to = lax.rem(me + k, n)
        return pltpu.make_async_remote_copy(
            src_ref=sent_ref.at[m, pl.ds(pl.multiple_of(to * PROMPT_DEV, PROMPT_DEV), PROMPT_DEV)],
            dst_ref=got_ref.at[m, k],
            send_sem=send.at[m, k],
            recv_sem=recv.at[m, k],
            device_id={"dp": to},
            device_id_type=MESH,
        )

    def every(m, act):
        def one(k, carry):
            act(piece(m, k))
            return carry

        lax.fori_loop(1, n, one, 0)

    meet(me, n)
    half_rows = (
        lax.broadcasted_iota(jnp.int32, (8, 128), 1) // HEAD_DIM
        == lax.broadcasted_iota(jnp.int32, (8, 128), 0)
    ).astype(f32)

    def micro(m, carry):
        index = load_spread(m, all_ref, kv_ref, k_ref, v_ref, kt_ref)
        dk_ref[...] = jnp.zeros_like(dk_ref)
        dv_ref[...] = jnp.zeros_like(dv_ref)
        for start, rows, length in row_tiles(prompt_total):
            at = pl.ds(pl.multiple_of(m * TOK_MB + start, 128), rows)
            inner = slice(start, start + rows)
            column = lax.broadcasted_iota(jnp.int32, (1, rows), 1)
            if start == 0:
                masked = 0
                reach = column + me * PROMPT_DEV
            else:
                masked = length - 256
                reach = column
            key = lax.broadcasted_iota(jnp.int32, (length - masked, rows), 0)
            back = None
            for h, (kv, half, pair) in enumerate(head_places(heads)):
                lanes = slice(pair * 128, (pair + 1) * 128)
                i = index[kv, half]
                q, do = q_ref[at, lanes], do_ref[at, lanes]
                if half == 0:
                    delta_pair = lax.dot_general(
                        half_rows,
                        do.astype(f32) * o_ref[at, lanes].astype(f32),
                        nt,
                        precision=lax.Precision.HIGHEST,
                        preferred_element_type=f32,
                    )
                delta = delta_pair[half : half + 1]
                lse = lse_ref[m, h : h + 1, inner]
                for low, high in ((0, masked), (masked, length)):
                    if low == high:
                        continue
                    s = lax.dot_general(k_ref[i, low:high], q, nt, preferred_element_type=f32)
                    if low == masked:
                        s = jnp.where(key <= reach, s, -1e30)
                    p = jnp.exp(s - lse)
                    dp_ = lax.dot_general(v_ref[i, low:high], do, nt, preferred_element_type=f32)
                    ds = (p * (dp_ - delta)).astype(bf16)
                    dv_ref[i, low:high] += jnp.dot(
                        p.astype(bf16), do, preferred_element_type=f32
                    )
                    dk_ref[i, low:high] += jnp.dot(ds, q, preferred_element_type=f32)
                    term = jnp.dot(kt_ref[i, :, low:high], ds, preferred_element_type=f32)
                    back = term if back is None else back + term
                if half == 1:
                    if start == 0:
                        table = pl.ds(pl.multiple_of(me * PROMPT_DEV, PROMPT_DEV), rows)
                    else:
                        table = pl.ds(prompt_total + start - PROMPT_DEV, rows)
                    to = (0, 1, 3)[pair] * 128
                    grad_ref[at, to : to + 128] = turn(
                        back.T, cos_ref[table], -sin_ref[table]
                    ).astype(bf16)
                    back = None
        lane = lax.broadcasted_iota(jnp.int32, (dk_ref.shape[1], 128), 1)

        def joined(acc):
            get = lambda place: acc[index[place]]
            return jnp.where(
                lane < HEAD_DIM,
                get((0, 0)) + pltpu.roll(get((0, 1)), HEAD_DIM, 1),
                get((1, 1)) + pltpu.roll(get((1, 0)), HEAD_DIM, 1),
            )

        dk = turn(joined(dk_ref) * HEAD_DIM**-0.5, cos_ref[...], -sin_ref[...])
        dv = joined(dv_ref)
        sent_ref[m, :, :128] = dk[:prompt_total].astype(bf16)
        sent_ref[m, :, 128:] = dv[:prompt_total].astype(bf16)
        every(m, lambda copy: copy.start())
        own = pl.ds(pl.multiple_of(m * TOK_MB + PROMPT_DEV, 128), CONT)
        put_both(own, dk[prompt_total:], dv[prompt_total:])
        return carry

    lax.fori_loop(0, MICRO, micro, 0)

    def collect(m, carry):
        every(m, lambda copy: copy.wait_recv())
        own = sent_ref[m, pl.ds(pl.multiple_of(me * PROMPT_DEV, PROMPT_DEV), PROMPT_DEV)]
        total = lax.fori_loop(
            1, n, lambda k, t: t + got_ref[m, k].astype(f32), own.astype(f32)
        )
        at = pl.ds(pl.multiple_of(m * TOK_MB, 128), PROMPT_DEV)
        put_both(at, total[:, :128], total[:, 128:])
        every(m, lambda copy: copy.wait_send())
        return carry

    lax.fori_loop(0, MICRO, collect, 0)


def attention_back_call(q, kv, prompts, do, o, lse, cosine, sine, n):
    count, width = q.shape
    keys = prompts.shape[1] + CONT
    heads = width // HEAD_DIM
    whole = pl.BlockSpec(memory_space=pltpu.VMEM)
    return pl.pallas_call(
        functools.partial(attention_back_kernel, heads, n),
        in_specs=[whole] * 8,
        out_specs=whole,
        out_shape=jax.ShapeDtypeStruct((count, width + 256), bf16),
        scratch_shapes=[
            pltpu.VMEM((4, keys, 128), bf16),
            pltpu.VMEM((4, keys, 128), bf16),
            pltpu.VMEM((4, 128, keys), bf16),
            pltpu.VMEM((4, keys, 128), f32),
            pltpu.VMEM((4, keys, 128), f32),
            pltpu.VMEM((MICRO, prompts.shape[1], 256), bf16),
            pltpu.VMEM((MICRO, n, PROMPT_DEV, 256), bf16),
            pltpu.SemaphoreType.DMA((MICRO, n)),
            pltpu.SemaphoreType.DMA((MICRO, n)),
        ],
        compiler_params=pltpu.CompilerParams(
            collective_id=4, has_side_effects=True, vmem_limit_bytes=56 * 2**20
        ),
        cost_estimate=pl.CostEstimate(
            flops=40 * count * keys * width,
            bytes_accessed=12 * count * width,
            transcendentals=count * keys * heads,
        ),
    )(q, kv, prompts, do, o, lse, cosine, sine)


def attend(queries, keys_all, values_all, allowed):
    factor = HEAD_DIM ** (-0.5)
    scores = jnp.einsum("tkgd,skd->kgts", queries, keys_all, preferred_element_type=f32) * factor
    scores = jnp.where(allowed, scores, -1e30)
    row_max = jnp.max(scores, axis=-1, keepdims=True)
    exponent = jnp.exp(scores - row_max)
    softened = exponent / jnp.sum(exponent, axis=-1, keepdims=True)
    soft_low = softened.astype(bf16)
    attended = jnp.einsum("kgts,skd->tkgd", soft_low, values_all, preferred_element_type=f32)
    return attended.astype(bf16), softened, soft_low


def attend_back(queries, keys_all, values_all, softened, soft_low, attended_grad):
    factor = HEAD_DIM ** (-0.5)
    soft_grad = jnp.einsum("tkgd,skd->kgts", attended_grad, values_all, preferred_element_type=f32)
    values_grad = jnp.einsum("kgts,tkgd->skd", soft_low, attended_grad, preferred_element_type=f32)
    row_delta = jnp.sum(softened * soft_grad, axis=-1, keepdims=True)
    scores_grad = (softened * (soft_grad - row_delta)).astype(bf16)
    queries_grad = (
        jnp.einsum("kgts,skd->tkgd", scores_grad, keys_all, preferred_element_type=f32) * factor
    )
    keys_grad = (
        jnp.einsum("kgts,tkgd->skd", scores_grad, queries, preferred_element_type=f32) * factor
    )
    return queries_grad, keys_grad, values_grad


def shards(
    tokens, cotangent, routes,
    inproj_weight, inproj_first, inproj_second,
    outproj_weight, outproj_first, outproj_second,
    gateup_weight, gateup_first, gateup_second,
    down_weight, down_first, down_second,
    router_weight, router_first, router_second,
    gains, gains_first, gains_second,
):
    n_dp = lax.axis_size("dp")
    n_tensor = lax.axis_size("tensor")
    depth = inproj_weight.shape[0]
    kv_local = inproj_weight.shape[1]
    hidden = down_weight.shape[1]
    group = max(1, 256 // hidden)
    groups = EXPERTS // group
    in_width = inproj_weight.shape[1] * inproj_weight.shape[2]
    out_width = outproj_weight.shape[0] * outproj_weight.shape[1]
    prompt_total = PROMPT_DEV * n_dp
    count = tokens.shape[0]

    def gateup_flat(w):
        w = w.reshape(groups, group, depth, 2, hidden)
        return w.transpose(2, 0, 3, 1, 4).reshape(depth, 2 * EXPERTS * hidden)

    def gateup_back(w):
        w = w.reshape(depth, groups, 2, group, hidden)
        return w.transpose(1, 3, 0, 2, 4).reshape(EXPERTS, depth, 2, hidden)

    query_width = GROUP * HEAD_DIM
    gains_high = gains.astype(bf16)
    gains_low = (gains - gains_high.astype(f32)).astype(bf16)
    attn_local = (
        inproj_weight.reshape(depth, in_width).astype(bf16),
        outproj_weight.reshape(out_width, depth).T.astype(bf16),
        jnp.concatenate(
            [
                router_weight.astype(bf16),
                gains_high.T,
                gains_low.T,
                jnp.zeros((depth, 128 - EXPERTS - 4), bf16),
            ],
            axis=1,
        ),
    )
    if hidden == 128:
        inproj_full, outproj_full, small_full, gu_local = gather(
            attn_local, gateup_weight.reshape(-1, hidden), n_dp, group, 5
        )
    else:
        inproj_full, outproj_full, small_full = gather(attn_local, None, n_dp, None, 5)
        gu_local = gateup_flat(gateup_weight.astype(bf16))
    down_local = down_weight.reshape(EXPERTS * hidden, depth).T.astype(bf16)
    gain_rows = small_full[:, EXPERTS : EXPERTS + 8].astype(f32).T

    device_index = lax.axis_index("dp")
    half_dim = HEAD_DIM // 2
    freqs = np.float32(10000.0) ** (-2.0 * np.arange(half_dim, dtype=np.float32) / HEAD_DIM)
    angles = np.arange(prompt_total + CONT, dtype=np.float32)[:, None] * freqs.astype(np.float32)
    cosine, sine = np.cos(angles), np.sin(angles)

    def of_rows(table):
        own = lax.dynamic_slice_in_dim(
            jnp.asarray(table), device_index * PROMPT_DEV, PROMPT_DEV, 0
        )
        return jnp.concatenate([own, table[prompt_total:]], axis=0)

    in_kernels = kv_local * HEAD_DIM == 128
    both_width = kv_local * 2 * HEAD_DIM
    if in_kernels:
        cos_all = np.concatenate([cosine] * 4, axis=1)
        sin_all = np.concatenate([-sine, sine] * 2, axis=1)
        normed_first, queries, both = project_call(
            tokens, gain_rows, inproj_full, cos_all, sin_all
        )
    else:
        cosine, sine = (jnp.tile(of_rows(t), (MICRO, 1))[:, None, :] for t in (cosine, sine))
        inputs = tokens.astype(f32)
        inverse_first = lax.rsqrt(jnp.mean(inputs * inputs, axis=-1, keepdims=True) + eps_norm)
        normed_first = (inputs * inverse_first * (gain_rows[0:1] + gain_rows[2:3])).astype(bf16)
        mixed = jnp.dot(normed_first, inproj_full, preferred_element_type=f32)
        mixed = mixed.reshape(count, kv_local, -1)
        queries = rotate(
            mixed[..., :query_width].reshape(count, -1, HEAD_DIM), cosine, sine
        ).astype(bf16)
        keys = rotate(mixed[..., query_width : query_width + HEAD_DIM], cosine, sine)
        both = jnp.concatenate(
            [keys.reshape(count, -1), mixed[..., query_width + HEAD_DIM :].reshape(count, -1)],
            axis=1,
        ).astype(bf16)
    if in_kernels:
        attended, lse, prompt_both, down_start = attention_call(
            queries, both, down_local[:, : down_local.shape[1] // 2], n_dp
        )
        down_start = down_start.reshape(n_dp * depth, -1)
        down_rest = down_local[:, down_local.shape[1] // 2 :]
    else:
        both = both.reshape(MICRO, TOK_MB, both_width)
        prompt_both = lax.all_gather(both[:, :PROMPT_DEV], "dp", axis=1, tiled=True)
        both_all = jnp.concatenate([prompt_both, both[:, PROMPT_DEV:]], axis=1)
        inner = jnp.arange(TOK_MB, dtype=jnp.int32)
        positions = jnp.where(
            inner < PROMPT_DEV, device_index * PROMPT_DEV + inner, prompt_total + inner - PROMPT_DEV
        )
        key_index = jnp.arange(prompt_total + CONT, dtype=jnp.int32)
        allowed = (key_index[None, :] <= positions[:, None]) & (
            (key_index[None, :] < prompt_total) | (inner[:, None] >= PROMPT_DEV)
        )
        kept = []
        attended = []
        for m in range(MICRO):
            q = queries[m * TOK_MB : (m + 1) * TOK_MB].reshape(TOK_MB, kv_local, GROUP, HEAD_DIM)
            k, v = (
                t.reshape(-1, kv_local, HEAD_DIM) for t in jnp.split(both_all[m], 2, axis=1)
            )
            out, softened, soft_low = attend(q, k, v, allowed)
            attended.append(out.reshape(TOK_MB, -1))
            kept.append((q, k, v, softened, soft_low))
        attended = jnp.concatenate(attended, axis=0)
    branch = lax.dot_general(
        attended, outproj_full, (((1,), (1,)), ((), ())), preferred_element_type=f32
    ).astype(bf16)
    branch, gu_full, down_rest = line_gather(
        branch, gu_local, down_rest if in_kernels else down_local, n_tensor, n_dp, 6
    )
    if not in_kernels:
        down_start, down_rest = jnp.split(down_rest, 2, axis=1)

    normed_second, gates_wide = route_call(tokens, branch, gain_rows, small_full, routes)
    active, hidden_grad, gate_grad = expert_call(
        normed_second, cotangent, gates_wide, gu_full, down_start, down_rest, group
    )
    contract_last = (((1,), (1,)), ((), ()))
    contract_first = (((0,), (0,)), ((), ()))
    rows_grad = lax.dot_general(
        hidden_grad, gu_full, contract_last, preferred_element_type=f32
    ).astype(bf16)
    summed, gateup_grad, down_grad, mixture = expert_grads_call(
        jnp.concatenate([rows_grad, gate_grad.astype(bf16)], axis=1),
        normed_second, cotangent, down_start, down_rest, hidden_grad, active, n_tensor, 2,
    )
    first_mixture = lax.psum(mixture[:TOK_MB], "tensor")
    model = tokens.shape[1]
    middle_grad, branch_own, attended_grad, logits_grad, gain_second_grad = middle_back_call(
        tokens, branch, summed, gates_wide, cotangent, gain_rows, small_full, outproj_full
    )
    middle_grad, attended_grad, down_grad, gateup_grad = lax.optimization_barrier(
        (middle_grad, attended_grad, down_grad, gateup_grad)
    )
    down_grad = lax.psum_scatter(down_grad, "dp", scatter_dimension=0, tiled=True)
    gateup_grad = lax.psum_scatter(gateup_grad, "dp", scatter_dimension=0, tiled=True)
    router_grad = lax.dot_general(
        normed_second, logits_grad, contract_first, preferred_element_type=f32
    ).astype(bf16)
    outproj_grad = lax.dot_general(
        branch_own, attended, contract_first, preferred_element_type=f32
    ).astype(bf16)
    if in_kernels:
        mixed_grad = attention_back_call(
            queries, both, prompt_both, attended_grad, attended, lse, cos_all, sin_all, n_dp
        )
    else:
        queries_grad, both_grad = [], []
        for m in range(MICRO):
            q, k, v, softened, soft_low = kept[m]
            dout = attended_grad[m * TOK_MB : (m + 1) * TOK_MB].reshape(q.shape)
            dq, dk, dv = attend_back(q, k, v, softened, soft_low, dout)
            queries_grad.append(dq.reshape(TOK_MB, -1, HEAD_DIM))
            both_grad.append(jnp.concatenate([t.reshape(-1, both_width // 2) for t in (dk, dv)], 1))
        queries_grad = rotate(jnp.concatenate(queries_grad, axis=0), cosine, -sine)
        both_grad = jnp.stack(both_grad)
        prompt_grad = lax.psum_scatter(
            both_grad[:, :prompt_total].astype(bf16), "dp", scatter_dimension=1, tiled=True
        )
        both_grad = jnp.concatenate(
            [prompt_grad.astype(f32), both_grad[:, prompt_total:]], axis=1
        ).reshape(count, both_width)
        keys_grad = rotate(
            both_grad[:, : both_width // 2].reshape(count, -1, HEAD_DIM), cosine, -sine
        )
        mixed_grad = jnp.concatenate(
            [
                t.reshape(count, kv_local, -1)
                for t in (queries_grad, keys_grad, both_grad[:, both_width // 2 :])
            ],
            axis=2,
        )
        mixed_grad = mixed_grad.reshape(count, -1).astype(bf16)
    normed_first_grad = lax.dot_general(
        mixed_grad, inproj_full, contract_last, preferred_element_type=f32
    ).astype(bf16)
    inproj_grad = lax.dot_general(
        normed_first, mixed_grad, contract_first, preferred_element_type=f32
    ).astype(bf16)
    attn_grad = [inproj_grad, outproj_grad, router_grad]
    if in_width % 128 or out_width % 128:
        attn_grad = [jnp.concatenate(attn_grad, axis=1)]
    gateup_state = (gateup_weight, gateup_first, gateup_second)
    down_state = (down_weight, down_first, down_second)
    if hidden == 128:
        gateup_next, down_next = expert_adam(
            gateup_state, gateup_grad, down_state, down_grad, group
        )
    else:
        down_next = adam_update(
            *down_state, down_grad.T.reshape(down_weight.shape).astype(f32), weight_decay, 0.05
        )
        gateup_next = adam_update(
            *gateup_state, gateup_back(gateup_grad).astype(f32), weight_decay, 0.05
        )
    tokens_grad, attn_grad, gains_grad, second_mixture = last_call(
        normed_first_grad, tokens, middle_grad, mixture, gain_rows,
        attn_grad, gain_second_grad, n_tensor, n_dp, 7,
    )
    first_mixture, tokens_grad = lax.optimization_barrier((first_mixture, tokens_grad))
    block_out = block_out_call(tokens, branch, first_mixture, second_mixture)
    split = (in_width, in_width + out_width, in_width + out_width + EXPERTS)
    inproj_grad, outproj_grad, router_grad = (
        attn_grad[:, : split[0]],
        attn_grad[:, split[0] : split[1]],
        attn_grad[:, split[1] : split[2]],
    )
    updates = (
        adam_update(
            inproj_weight, inproj_first, inproj_second,
            inproj_grad.reshape(inproj_weight.shape), weight_decay, 0.05,
        ),
        adam_update(
            outproj_weight, outproj_first, outproj_second,
            outproj_grad.T.reshape(outproj_weight.shape), weight_decay, 0.3,
        ),
        gateup_next,
        down_next,
        adam_update(router_weight, router_first, router_second, router_grad, weight_decay, 0.05),
        adam_update(gains, gains_first, gains_second, gains_grad, 0.0, 0.4),
    )
    return (block_out, tokens_grad) + sum(updates, ())


def solution(mesh):
    row = P("dp", None)
    inproj = P("dp", "tensor", None)
    outproj = P("tensor", None, "dp")
    gateup = P(None, "dp", None, "tensor")
    down = P(None, "tensor", "dp")
    gain = P(None, "dp")
    weights = (inproj,) * 3 + (outproj,) * 3 + (gateup,) * 3 + (down,) * 3 + (row,) * 3 + (gain,) * 3
    return jax.shard_map(
        shards,
        mesh=mesh,
        in_specs=(row, row, row) + weights,
        out_specs=(row, row) + weights,
        check_vma=False,
    )
```
